32 devices in a mesh: wide: 8 (over z, y), narrow: 4 (over x, core).
Axes of the slice: x: 2, y: 2, z: 4, core: 2. Of those that a mesh axis runs over, the one named last changes fastest.
Arguments:
- tag_states: bfloat16 [96, 512, 512], P(('wide', 'narrow')), may hold values from -6 to 6
- image_memory: bfloat16 [96, 784, 512], P(('wide', 'narrow')), may hold values from -6 to 6
- tag_lengths: int32 [96], P(('wide', 'narrow')), may hold values from 20 to 512, as said below
- w_self: bfloat16 [512, 1536], P(('wide', 'narrow')), may hold values from -0.25 to 0.25
- w_cross: bfloat16 [512, 1536], P(('wide', 'narrow')), may hold values from -0.25 to 0.25
- w_proj: bfloat16 [2, 512, 512], P(None, ('wide', 'narrow')), may hold values from -1 to 1
- w_in: bfloat16 [512, 1024], P(('wide', 'narrow')), may hold values from -0.25 to 0.25
- b_in: bfloat16 [1024], P(('wide', 'narrow')), may hold values from -1.75 to 1.75
- w_out: bfloat16 [1024, 512], P(('wide', 'narrow')), may hold values from -0.1875 to 0.1875
- ln_gains: bfloat16 [3, 512], P(None, ('wide', 'narrow')), may hold values from 0.099609375 to 1.8984375
- biases: bfloat16 [10, 512], P(None, ('wide', 'narrow')), may hold values from -1.75 to 1.75
- out_grad: bfloat16 [96, 512, 512], P(('wide', 'narrow')), may hold values from -6 to 6
Outputs:
- layer_out: bfloat16 [96, 512, 512], P(('wide', 'narrow'))
- grad_tags: float32 [96, 512, 512], P(('wide', 'narrow'))
- grad_memory: float32 [96, 784, 512], P(('wide', 'narrow'))
- grad_w_self: float32 [512, 1536], P(('wide', 'narrow'))
- grad_w_cross: float32 [512, 1536], P(('wide', 'narrow'))
- grad_w_proj: float32 [2, 512, 512], P(None, ('wide', 'narrow'))
- grad_w_in: float32 [512, 1024], P(('wide', 'narrow'))
- grad_b_in: float32 [1024], P(('wide', 'narrow'))
- grad_w_out: float32 [1024, 512], P(('wide', 'narrow'))
- grad_gains: float32 [3, 512], P(None, ('wide', 'narrow'))
- grad_biases: float32 [10, 512], P(None, ('wide', 'narrow'))
The draws below stay inside these ranges and needn't reach their ends.
Inputs may be any that keep to these rules, and one draw needn't show every extreme that they name: `tag_lengths`: each image's number of tags; some image has exactly 512 and some exactly 20.
All inputs are finite; a program needn't handle non-finite values.
Results may differ from the reference program's by a relative error of at most 0.02.
Values may be sent and summed in bfloat16 or wider, within the bound.
A program may use at most 256 MiB of HBM per device.

```python
import jax
import jax.numpy as jnp
from jax import lax

D = 512
HEADS = 8
HEAD_DIM = 64
FF = 1024
TAG_LEN = 512
MIN_TAGS = 20
MEM_LEN = 784
IMG_DEV = 3
IMAGES = 96


def draw_tag_lengths(key, part):
    key = jax.random.fold_in(key, 11)
    first, second, third = jax.random.split(key, 3)
    counts = jax.random.randint(first, (IMAGES,), MIN_TAGS, TAG_LEN + 1)
    longest = jax.random.randint(second, (), 0, IMAGES)
    shortest = (longest + 1 + jax.random.randint(third, (), 0, IMAGES - 1)) % IMAGES
    counts = counts.at[longest].set(TAG_LEN).at[shortest].set(MIN_TAGS)
    return counts.astype(jnp.int32)


def steps_of(rng, extent, cuts, low, high):
    level = 1.0
    for position, blocks in cuts:
        steps = jax.random.uniform(jax.random.fold_in(jax.random.fold_in(rng, 6), position), (blocks,), jnp.float32, low / len(cuts), high / len(cuts))
        level = level * jnp.repeat(jnp.exp(steps), extent[position] // blocks).reshape((-1,) + (1,) * (len(extent) - 1 - position))
    return level


def scatter_about(own_key, dims, scale, limit, cuts=(), kind=jnp.bfloat16):
    values = scale * jax.random.normal(own_key, dims, jnp.float32)
    if cuts:
        values = values * steps_of(own_key, dims, cuts, -0.22, 0.18)
    return jnp.clip(values, -limit, limit).astype(kind)


def setup_inputs(seed: int = 0) -> dict:
    keys = jax.random.split(jax.random.key(seed), 13)
    tag_states = scatter_about(keys[0], (IMAGES, TAG_LEN, D), 1.0, 6.0, ((0, 32),))
    image_memory = scatter_about(keys[1], (IMAGES, MEM_LEN, D), 1.0, 6.0, ((0, 32),))
    tag_lengths = draw_tag_lengths(jax.random.fold_in(keys[12], 71), 0)
    w_self = scatter_about(keys[3], (D, 3 * D), D ** -0.5, 0.25, ((0, 32),))
    w_cross = scatter_about(keys[4], (D, 3 * D), D ** -0.5, 0.25, ((0, 32),))
    w_proj = scatter_about(keys[5], (2, D, D), (D // 16) ** -0.5, 1.0, ((1, 32),))
    w_in = scatter_about(keys[6], (D, FF), D ** -0.5, 0.25, ((0, 32),))
    b_in = scatter_about(keys[7], (FF,), 0.3, 1.75, ((0, 32),))
    w_out = scatter_about(keys[8], (FF, D), FF ** -0.5, 0.1875, ((0, 32),))
    ln_gains = jnp.clip(1.0 + 0.18 * jax.random.normal(keys[9], (3, D), jnp.float32), 0.099609375, 1.8984375).astype(jnp.bfloat16)
    biases = scatter_about(keys[10], (10, D), 0.3, 1.75, ((1, 32),))
    out_grad = scatter_about(keys[11], (IMAGES, TAG_LEN, D), 1.0, 6.0, ((0, 32),))
    return {"tag_states": tag_states, "image_memory": image_memory, "tag_lengths": tag_lengths, "w_self": w_self, "w_cross": w_cross, "w_proj": w_proj, "w_in": w_in, "b_in": b_in, "w_out": w_out, "ln_gains": ln_gains, "biases": biases, "out_grad": out_grad}


epsilon = 1e-05
masked_fill = -1000000000.0

@jax.custom_vjp
def low(v):
    return lax.optimization_barrier(v.astype(jnp.bfloat16)).astype(jnp.float32)

@jax.custom_vjp
def low_back(v):
    return v

def low_keep(v):
    return (low(v), None)

def low_pass(kept, grad):
    return (grad,)

def back_keep(v):
    return (v, None)

def back_low(kept, grad):
    return (low(grad),)
low.defvjp(low_keep, low_pass)
low_back.defvjp(back_keep, back_low)

def matmul(left, right):
    return jnp.dot(left, right, precision=lax.Precision.HIGHEST)

def layer_norm(resid, gain, shift):
    centred = resid - lax.optimization_barrier(jnp.mean(resid, -1, keepdims=True))
    spread = lax.optimization_barrier(jnp.mean(centred * centred, -1, keepdims=True))
    return centred * lax.rsqrt(spread + epsilon) * gain + shift

def attend(queries, key_rows, value_rows, allowed):
    images = queries.shape[0]
    q_heads = queries.reshape(images, queries.shape[1], HEADS, HEAD_DIM)
    k_heads = key_rows.reshape(images, key_rows.shape[1], HEADS, HEAD_DIM)
    v_heads = value_rows.reshape(images, value_rows.shape[1], HEADS, HEAD_DIM)
    scores = jnp.einsum('gqhd,gkhd->ghqk', q_heads, k_heads, precision=lax.Precision.HIGHEST) * HEAD_DIM ** (-0.5)
    scores = low_back(scores)
    scores = jnp.where(allowed[:, None], scores, masked_fill)
    softmax_w = jax.nn.softmax(scores, axis=-1)
    mixed_out = jnp.einsum('ghqk,gkhd->gqhd', low(softmax_w), v_heads, precision=lax.Precision.HIGHEST)
    return mixed_out.reshape(images, queries.shape[1], HEADS * HEAD_DIM)

def layer_fn(weights, states, memory, tag_counts):
    w_self, w_cross, w_proj, w_in, b_in, w_out, ln_gains, biases = weights
    images, tag_len, model_width = states.shape
    memory_len = memory.shape[1]
    zero_row = jnp.zeros((model_width,), jnp.float32)
    query_pos = lax.broadcasted_iota(jnp.int32, (tag_len, tag_len), 0)
    key_pos = lax.broadcasted_iota(jnp.int32, (tag_len, tag_len), 1)
    allowed_self = (key_pos <= query_pos)[None] & (key_pos[None] < tag_counts[:, None, None])
    valid_rows = (query_pos[:, 0][None] < tag_counts[:, None]).astype(jnp.float32).reshape(images * tag_len, 1)
    tag_rows = states.reshape(images * tag_len, model_width)
    mem_rows = memory.reshape(images * memory_len, model_width)
    self_bias = jnp.concatenate([biases[0], zero_row, biases[1]])
    qkv_rows = low(low_back(matmul(tag_rows, w_self) + self_bias)).reshape(images, tag_len, 3 * model_width)
    self_mix = attend(qkv_rows[..., :model_width], qkv_rows[..., model_width:2 * model_width], qkv_rows[..., 2 * model_width:], allowed_self)
    self_mix = low(low_back(self_mix.reshape(images * tag_len, model_width)))
    branch_one = low_back(matmul(self_mix, w_proj[0]) + biases[2])
    normed_one = layer_norm(tag_rows + branch_one, ln_gains[0], biases[6])
    cross_q = low(low_back(matmul(low(normed_one), w_cross[:, :model_width]) + biases[3]))
    cross_kv = low(low_back(matmul(mem_rows, w_cross[:, model_width:]) + jnp.concatenate([zero_row, biases[4]])))
    cross_kv = cross_kv.reshape(images, memory_len, 2 * model_width)
    all_pairs = jnp.ones((images, tag_len, memory_len), bool)
    cross_mix = attend(cross_q.reshape(images, tag_len, model_width), cross_kv[..., :model_width], cross_kv[..., model_width:], all_pairs)
    cross_mix = low(low_back(cross_mix.reshape(images * tag_len, model_width)))
    branch_two = low_back(matmul(cross_mix, w_proj[1]) + biases[5])
    normed_two = layer_norm(normed_one + branch_two, ln_gains[1], biases[7])
    inner_pre = low_back(matmul(low(normed_two), w_in) + b_in)
    activated = low(jax.nn.gelu(inner_pre))
    branch_three = low_back(matmul(activated, w_out) + biases[9])
    result = layer_norm(normed_two + branch_three, ln_gains[2], biases[8]) * valid_rows
    return result.reshape(images, tag_len, model_width)

def reference(tag_states, image_memory, tag_lengths, w_self, w_cross, w_proj, w_in, b_in, w_out, ln_gains, biases, out_grad):
    weights = tuple((tensor.astype(jnp.float32) for tensor in (w_self, w_cross, w_proj, w_in, b_in, w_out, ln_gains, biases)))
    groups = tag_states.shape[0] // IMG_DEV
    tag_len = tag_states.shape[1]
    memory_len = image_memory.shape[1]
    model_width = tag_states.shape[2]

    def group_step(summed, pieces):
        states, memory, tag_counts, grad_now = pieces

        def apply_layer(params, state_f, memory_f):
            return layer_fn(params, state_f, memory_f, tag_counts)
        result, pull_back = jax.vjp(apply_layer, weights, states.astype(jnp.float32), memory.astype(jnp.float32))
        grad_params, grad_state, grad_mem = pull_back(grad_now.astype(jnp.float32))
        summed = jax.tree.map(jnp.add, summed, grad_params)
        return (summed, (result.astype(jnp.bfloat16), grad_state, grad_mem))
    initial = tuple((jnp.zeros(tensor.shape, jnp.float32) for tensor in weights))
    pieces = (tag_states.reshape(groups, IMG_DEV, tag_len, model_width), image_memory.reshape(groups, IMG_DEV, memory_len, model_width), tag_lengths.astype(jnp.int32).reshape(groups, IMG_DEV), out_grad.reshape(groups, IMG_DEV, tag_len, model_width))
    summed, stacked = lax.scan(group_step, initial, pieces)
    layer_out = stacked[0].reshape(groups * IMG_DEV, tag_len, model_width)
    grad_tags = stacked[1].reshape(groups * IMG_DEV, tag_len, model_width)
    grad_memory = stacked[2].reshape(groups * IMG_DEV, memory_len, model_width)
    return (layer_out, grad_tags, grad_memory, summed[0], summed[1], summed[2], summed[3], summed[4], summed[5], summed[6], summed[7])
```

```python
import functools

import jax
import jax.numpy as jnp
from jax import lax
from jax.experimental import pallas as pl
from jax.experimental.pallas import tpu as pltpu
from jax.sharding import PartitionSpec as P


MESH = pl.DeviceIdType.MESH
f32, bf16 = jnp.float32, jnp.bfloat16


def grid_of(mesh_wide, mesh_narrow):
    outer = 4
    return outer, mesh_wide // outer, mesh_narrow // 2


def place(dims):
    outer, inner, across = dims
    wide, narrow = lax.axis_index("wide"), lax.axis_index("narrow")
    return wide // inner, lax.rem(wide, inner), narrow // 2, lax.rem(narrow, 2)


def device(dims, a, b, x, c):
    return {"wide": a * dims[1] + b, "narrow": x * 2 + c}


def greet(dims, me):
    a, b, x, c = me
    outer, inner, across = dims
    barrier = pltpu.get_barrier_semaphore()
    peers = [(lax.rem(a + k, outer), b, x, c) for k in range(1, outer)]
    peers += [(a, lax.rem(b + k, inner), x, c) for k in range(1, inner)]
    peers += [(a, b, lax.rem(x + k, across), c) for k in range(1, across)]
    peers += [(a, b, x, 1 - c)]
    for peer in peers:
        pl.semaphore_signal(barrier, inc=1, device_id=device(dims, *peer), device_id_type=MESH)
    pl.semaphore_wait(barrier, len(peers))


ALL = slice(None)


def gather_kernel(dims, leads, *refs):
    count = len(leads)
    shards, outs = refs[:count], refs[count : 2 * count]
    local_sem, send_sem, recv_sem = refs[2 * count :]
    outer, inner, across = dims
    me = place(dims)
    a, b, x, c = me
    greet(dims, me)

    def cell(ref, lead, *index):
        return ref.at[(ALL,) * lead + index]

    def remote(g, slot, src, dst, peer):
        return pltpu.make_async_remote_copy(
            src_ref=src, dst_ref=dst, send_sem=send_sem.at[g, slot], recv_sem=recv_sem.at[g, slot],
            device_id=device(dims, *peer), device_id_type=MESH)

    n_in, n_ac = inner - 1, across - 1

    def first(g):
        lead = leads[g]
        mine = cell(outs[g], lead, a, b, x, c)
        return [remote(g, k - 1, shards[g], mine, (lax.rem(a + k, outer), b, x, c)) for k in range(1, outer)]

    def keep(g):
        return pltpu.make_async_copy(shards[g], cell(outs[g], leads[g], a, b, x, c), local_sem.at[g])

    base = outer - 1

    def via_inner(g, core):
        lead = leads[g]
        column = ALL if core == 0 else x
        piece = cell(outs[g], lead, ALL, b, column, c)
        return [remote(g, base + k - 1, piece, piece, (a, lax.rem(b + k, inner), x, c)) for k in range(1, inner)]

    def via_across(g, core):
        lead = leads[g]
        row = b if core == 0 else ALL
        piece = cell(outs[g], lead, ALL, row, x, c)
        return [remote(g, base + n_in + k - 1, piece, piece, (a, b, lax.rem(x + k, across), c)) for k in range(1, across)]

    share = base + n_in + n_ac

    def to_partner(g, core, holder):
        lead = leads[g]
        def piece(slot, row, column):
            ref = cell(outs[g], lead, ALL, row, column, holder)
            return remote(g, share + slot, ref, ref, (a, b, x, 1 - c))
        own = [piece(0, b, x)]
        by_inner = [piece(1 + k - 1, lax.rem(b + k, inner), ALL if core == 0 else x) for k in range(1, inner)]
        by_across = [piece(1 + n_in + k - 1, b if core == 0 else ALL, lax.rem(x + k, across)) for k in range(1, across)]
        return (own, by_across, by_inner) if core == 0 else (own, by_inner, by_across)

    def start(copies):
        for copy in copies:
            copy.start()

    def arrived(copies):
        for copy in copies:
            copy.wait_recv()

    for g in range(count):
        keep(g).start()
        start(first(g))

    def body(core):
        second, third = (via_across, via_inner) if core == 0 else (via_inner, via_across)
        for step in range(count + 2):
            g = step
            if g < count:
                keep(g).wait()
                arrived(first(g))
                start(second(g, core))
                start(to_partner(g, core, c)[0])
            g = step - 1
            if 0 <= g < count:
                arrived(second(g, core))
                start(third(g, core))
                start(to_partner(g, core, c)[1])
            g = step - 2
            if 0 <= g < count:
                arrived(third(g, core))
                start(to_partner(g, core, c)[2])
        for g in range(count):
            for group in to_partner(g, 1 - core, 1 - c):
                arrived(group)
        for g in range(count):
            for copy in first(g) + second(g, core) + third(g, core):
                copy.wait_send()
            for group in to_partner(g, core, c):
                for copy in group:
                    copy.wait_send()

    @pl.when(c == 0)
    def _():
        body(0)

    @pl.when(c == 1)
    def _():
        body(1)


def gather(dims, shards, leads):
    outer, inner, across = dims
    def shape(s, lead):
        return jax.ShapeDtypeStruct(s.shape[:lead] + (outer, inner, across, 2) + s.shape[lead:], s.dtype)
    slots = (outer - 1) + 2 * (inner - 1) + 2 * (across - 1) + 1
    n = len(shards)
    return pl.pallas_call(
        functools.partial(gather_kernel, dims, leads),
        out_shape=[shape(s, l) for s, l in zip(shards, leads)],
        in_specs=[pl.BlockSpec(memory_space=pl.ANY)] * n,
        out_specs=[pl.BlockSpec(memory_space=pl.ANY)] * n,
        scratch_shapes=[pltpu.SemaphoreType.DMA((n,)), pltpu.SemaphoreType.DMA((n, slots)), pltpu.SemaphoreType.DMA((n, slots))],
        compiler_params=pltpu.CompilerParams(collective_id=0, has_side_effects=True),
        name="gather_weights",
    )(*shards)


def scatter_kernel(dims, leads, *refs):
    count = len(leads)
    grads, outs = refs[:count], refs[count : 2 * count]
    rest = refs[2 * count :]
    r0, r1i, r1a, r2a, r2i, r3 = (rest[k * count : (k + 1) * count] for k in range(6))
    send_sem, recv_sem = rest[6 * count :]
    outer, inner, across = dims
    me = place(dims)
    a, b, x, c = me
    greet(dims, me)
    n_in, n_ac = inner - 1, across - 1

    def cell(ref, lead, *index):
        return ref.at[(ALL,) * lead + index]

    def remote(g, slot, src, dst, peer):
        return pltpu.make_async_remote_copy(
            src_ref=src, dst_ref=dst, send_sem=send_sem.at[g, slot], recv_sem=recv_sem.at[g, slot],
            device_id=device(dims, *peer), device_id_type=MESH)

    def swap(g):
        return [remote(g, 0, cell(grads[g], leads[g], ALL, ALL, ALL, 1 - c), r0[g], (a, b, x, 1 - c))]

    def via_inner(g, core):
        lead = leads[g]
        res = []
        for k in range(1, inner):
            peer = lax.rem(b + k, inner)
            if core == 0:
                src, dst = cell(r0[g], lead, ALL, peer), r1i[g].at[k - 1]
            else:
                src, dst = cell(r1a[g].at[0], lead, ALL, peer), r2i[g].at[k - 1]
            res.append(remote(g, k, src, dst, (a, peer, x, c)))
        return res

    def via_across(g, core):
        lead = leads[g]
        res = []
        for k in range(1, across):
            peer = lax.rem(x + k, across)
            if core == 1:
                src, dst = cell(r0[g], lead, ALL, ALL, peer), r1a[g].at[k - 1]
            else:
                src, dst = cell(r1i[g].at[0], lead, ALL, peer), r2a[g].at[k - 1]
            res.append(remote(g, 1 + n_in + k - 1, src, dst, (a, b, peer, c)))
        return res

    def last(g, core):
        lead = leads[g]
        held = (r2a if core == 0 else r2i)[g].at[0]
        res = []
        for k in range(1, outer):
            peer = lax.rem(a + k, outer)
            res.append(remote(g, 1 + n_in + n_ac + k - 1, cell(held, lead, peer), r3[g].at[k - 1], (peer, b, x, c)))
        return res

    def start(copies):
        for copy in copies:
            copy.start()

    def arrived(copies):
        for copy in copies:
            copy.wait_recv()

    def up(v):
        return v.astype(f32)

    for g in range(count):
        start(swap(g))

    def body(core):
        second, third = (via_inner, via_across) if core == 0 else (via_across, via_inner)
        def at(lead, *index):
            return (ALL,) * lead + index
        for step in range(count + 3):
            g = step
            if g < count:
                arrived(swap(g))
                lead = leads[g]
                r0[g][...] = (up(grads[g][at(lead, ALL, ALL, ALL, c)]) + up(r0[g][...])).astype(bf16)
                start(second(g, core))
            g = step - 1
            if 0 <= g < count:
                arrived(second(g, core))
                lead = leads[g]
                if core == 0:
                    total = up(r0[g][at(lead, ALL, b)])
                    held = r1i[g]
                else:
                    total = up(r0[g][at(lead, ALL, ALL, x)])
                    held = r1a[g]
                for k in range(held.shape[0]):
                    total = total + up(held[k])
                held[0] = total.astype(bf16)
                start(third(g, core))
            g = step - 2
            if 0 <= g < count:
                arrived(third(g, core))
                lead = leads[g]
                if core == 0:
                    total = up(r1i[g][(0,) + at(lead, ALL, x)])
                    held = r2a[g]
                else:
                    total = up(r1a[g][(0,) + at(lead, ALL, b)])
                    held = r2i[g]
                for k in range(held.shape[0]):
                    total = total + up(held[k])
                held[0] = total.astype(bf16)
                start(last(g, core))
            g = step - 3
            if 0 <= g < count:
                arrived(last(g, core))
                lead = leads[g]
                held = (r2a if core == 0 else r2i)[g]
                total = up(held[(0,) + at(lead, a)])
                for k in range(outer - 1):
                    total = total + up(r3[g][k])
                outs[g][...] = total
        for g in range(count):
            for copy in swap(g) + second(g, core) + third(g, core) + last(g, core):
                copy.wait_send()

    @pl.when(c == 0)
    def _():
        body(0)

    @pl.when(c == 1)
    def _():
        body(1)


def scatter(dims, grads, leads):
    outer, inner, across = dims
    n = len(grads)
    outs, shapes = [], [[] for _ in range(6)]
    for g, lead in zip(grads, leads):
        head, tail = g.shape[:lead], g.shape[lead + 4 :]
        outs.append(jax.ShapeDtypeStruct(head + tail, f32))
        shapes[0].append(head + (outer, inner, across) + tail)
        shapes[1].append((inner - 1,) + head + (outer, across) + tail)
        shapes[2].append((across - 1,) + head + (outer, inner) + tail)
        shapes[3].append((across - 1,) + head + (outer,) + tail)
        shapes[4].append((inner - 1,) + head + (outer,) + tail)
        shapes[5].append((outer - 1,) + head + tail)
    slots = 1 + (inner - 1) + (across - 1) + (outer - 1)
    return pl.pallas_call(
        functools.partial(scatter_kernel, dims, leads),
        out_shape=outs,
        in_specs=[pl.BlockSpec(memory_space=pltpu.VMEM)] * n,
        out_specs=[pl.BlockSpec(memory_space=pltpu.VMEM)] * n,
        scratch_shapes=[pltpu.VMEM(s, bf16) for group in shapes for s in group]
        + [pltpu.SemaphoreType.DMA((n, slots)), pltpu.SemaphoreType.DMA((n, slots))],
        compiler_params=pltpu.CompilerParams(collective_id=1, has_side_effects=True, vmem_limit_bytes=48 * 2**20),
        name="scatter_grads",
    )(*grads)

HEADS, HEAD_DIM = 8, 64
EPS = 1e-5
MASKED = -1e9
MIB = 2**20


def dot(left, right, left_dim, right_dim):
    return lax.dot_general(left, right, (((left_dim,), (right_dim,)), ((), ())), preferred_element_type=f32)


def full(shape):
    return pl.BlockSpec(shape, lambda i: (0,) * len(shape))


def image(shape):
    return pl.BlockSpec((1,) + shape, lambda i: (i,) + (0,) * len(shape))


def with_ones(rows):
    return jnp.concatenate([rows, jnp.ones((16, rows.shape[1]), bf16)], 0)


def with_delta(rows, delta):
    high = delta.astype(bf16).astype(f32)
    low = delta - high
    at = lax.broadcasted_iota(jnp.int32, (16, rows.shape[1]), 0)
    extra = jnp.where(at == 0, -high, jnp.where(at == 1, -low, 0.0))
    return jnp.concatenate([rows, extra.astype(bf16)], 0)


def self_forward(lens, x_ref, mem_ref, w_self, w_cross, bias_qkv, bias_kv,
                 qkv_ref, ckv_ref, near_ref, far_ref, inv_ref, mix_ref, wt_self, wt_cross):
    width = x_ref.shape[2]
    tags = x_ref.shape[1]
    half = tags // 2
    i = pl.program_id(0)

    @pl.when(i == 0)
    def _():
        wt_self[...] = w_self[...].T
        wt_cross[...] = w_cross[...].T

    ckv = dot(wt_cross[width:], mem_ref[0], 1, 1) + bias_kv[...]
    ckv_ref[0] = ckv.astype(bf16).reshape(ckv_ref.shape[1:])
    qkv = dot(wt_self[...], x_ref[0], 1, 1) + bias_qkv[...]
    q = qkv[:width].astype(bf16) * bf16(HEAD_DIM ** -0.5)
    qkv_ref[0, :HEADS] = q.reshape(HEADS, HEAD_DIM, tags)
    qkv_ref[0, HEADS:] = qkv[width:].astype(bf16).reshape(2 * HEADS, HEAD_DIM, tags)
    last = lens[i] - 1

    def head(h, _):
        qt, kt, vt = qkv_ref[0, h], qkv_ref[0, HEADS + h], with_ones(qkv_ref[0, 2 * HEADS + h])

        def part(keys, first, out):
            s = dot(kt[:, :keys], qt[:, first : first + half], 0, 0)
            key_at = lax.broadcasted_iota(jnp.int32, (keys, half), 0)
            query_at = lax.broadcasted_iota(jnp.int32, (1, half), 1) + first
            s = jnp.where(key_at <= jnp.minimum(query_at, last), s, MASKED)
            e = jnp.exp(s - jnp.max(s, 0, keepdims=True)).astype(bf16)
            out[0, h] = e
            mixed = dot(vt[:, :keys], e, 1, 0)
            inv = 1.0 / mixed[HEAD_DIM : HEAD_DIM + 1]
            inv_ref[0, pl.ds(h, 1), first : first + half] = inv
            mix_ref[0, h, :, first : first + half] = (mixed[:HEAD_DIM] * inv).astype(bf16)

        part(half, 0, near_ref)
        part(tags, half, far_ref)
        return 0

    lax.fori_loop(0, HEADS, head, 0)


def run_self_forward(lens, x, mem, w_self, w_cross, bias_qkv, bias_kv):
    images, tags, width = x.shape
    cells = mem.shape[1]
    half = tags // 2
    sds = jax.ShapeDtypeStruct
    return pl.pallas_call(
        self_forward,
        grid_spec=pltpu.PrefetchScalarGridSpec(
            num_scalar_prefetch=1,
            grid=(images,),
            in_specs=[pl.BlockSpec((1, tags, width), lambda i, n: (i, 0, 0)), pl.BlockSpec((1, cells, width), lambda i, n: (i, 0, 0))]
            + [pl.BlockSpec(v.shape, lambda i, n: (0, 0)) for v in (w_self, w_cross, bias_qkv, bias_kv)],
            out_specs=[
                pl.BlockSpec((1, 3 * HEADS, HEAD_DIM, tags), lambda i, n: (i, 0, 0, 0)),
                pl.BlockSpec((1, 2 * HEADS, HEAD_DIM, cells), lambda i, n: (i, 0, 0, 0)),
                pl.BlockSpec((1, HEADS, half, half), lambda i, n: (i, 0, 0, 0)),
                pl.BlockSpec((1, HEADS, tags, half), lambda i, n: (i, 0, 0, 0)),
                pl.BlockSpec((1, HEADS, tags), lambda i, n: (i, 0, 0)),
                pl.BlockSpec((1, HEADS, HEAD_DIM, tags), lambda i, n: (i, 0, 0, 0)),
                pl.BlockSpec((3 * width, width), lambda i, n: (0, 0)),
                pl.BlockSpec((3 * width, width), lambda i, n: (0, 0)),
            ],
        ),
        out_shape=[
            sds((images, 3 * HEADS, HEAD_DIM, tags), bf16),
            sds((images, 2 * HEADS, HEAD_DIM, cells), bf16),
            sds((images, HEADS, half, half), bf16),
            sds((images, HEADS, tags, half), bf16),
            sds((images, HEADS, tags), f32),
            sds((images, HEADS, HEAD_DIM, tags), bf16),
            sds((3 * width, width), bf16),
            sds((3 * width, width), bf16),
        ],
        compiler_params=pltpu.CompilerParams(vmem_limit_bytes=58 * MIB),
        name="self_forward",
    )(lens, x, mem, w_self, w_cross, bias_qkv, bias_kv)


def norm(resid):
    centred = resid - jnp.mean(resid, -1, keepdims=True)
    scale = lax.rsqrt(jnp.mean(centred * centred, -1, keepdims=True) + EPS)
    return centred * scale, scale


def norm_back(grad, normed, scale, gain):
    scaled = grad * gain
    mean_one = jnp.mean(scaled, -1, keepdims=True)
    mean_two = jnp.mean(scaled * normed, -1, keepdims=True)
    return scale * (scaled - mean_one - normed * mean_two)


def column_sums(rows):
    return jnp.sum(rows, 0, keepdims=True)


def lane_groups(rows):
    total = rows[:, :128]
    for k in range(1, rows.shape[1] // 128):
        total = total + rows[:, 128 * k : 128 * (k + 1)]
    return total


def middle(lens, x_ref, mem_ref, gout_ref, mix_one, ckv_ref, wt_q, w_proj, w_in, w_out, bias_q, vectors, b_in,
           out_ref, g_resid, g_mix, dkv_ref, gw_cross, gw_proj, gw_in, gw_out, g_vec, g_bin,
           e_ref, q_ref, inv_ref, mix_two, gmix_two, dq_ref, acc_cross, acc_proj, acc_in, acc_out, acc_vec, acc_bin, acc_col,
           n_one, n_two):
    tags, width = x_ref.shape[1:]
    cells = mem_ref.shape[1]
    i = pl.program_id(0)
    count = pl.num_programs(0)

    @pl.when(i == 0)
    def _():
        for ref in (acc_cross, acc_proj, acc_in, acc_out, acc_vec, acc_bin, acc_col):
            ref[...] = jnp.zeros_like(ref)

    def vec(k):
        return vectors[k : k + 1, :]

    def add(k, value):
        acc_vec[k : k + 1, :] += value

    mix_one_t = mix_one[0].reshape(width, tags)
    resid = x_ref[0].astype(f32) + dot(mix_one_t, w_proj[0], 0, 0) + vec(2)
    normed, scale_one = norm(resid)
    n_one[...] = normed
    one = normed * vec(10) + vec(6)
    one_low = one.astype(bf16)
    cq = (dot(wt_q[...], one_low, 1, 1) + bias_q[...]).astype(bf16) * bf16(HEAD_DIM ** -0.5)
    q_ref[...] = cq.reshape(q_ref.shape)

    def forward(h, _):
        s = dot(ckv_ref[0, h], q_ref[h], 0, 0)
        e = jnp.exp(s - jnp.max(s, 0, keepdims=True)).astype(bf16)
        e_ref[h] = e
        mixed = dot(with_ones(ckv_ref[0, HEADS + h]), e, 1, 0)
        inv = 1.0 / mixed[HEAD_DIM : HEAD_DIM + 1]
        inv_ref[pl.ds(h, 1), :] = inv
        mix_two[h] = (mixed[:HEAD_DIM] * inv).astype(bf16)
        return 0

    lax.fori_loop(0, HEADS, forward, 0)
    mix_two_t = mix_two[...].reshape(width, tags)
    resid = one + dot(mix_two_t, w_proj[1], 0, 0) + vec(5)
    normed, scale_two = norm(resid)
    n_two[...] = normed
    two = normed * vec(11) + vec(7)
    two_low = two.astype(bf16)
    inner = dot(two_low, w_in[...], 1, 0) + b_in[...]
    root = 0.7978845608028654
    square = inner * inner
    tanh = jnp.tanh(root * inner * (1.0 + 0.044715 * square))
    act = (0.5 * inner * (1.0 + tanh)).astype(bf16)
    slope = 0.5 * (1.0 + tanh) + 0.5 * inner * (1.0 - tanh * tanh) * (root * (1.0 + 3 * 0.044715 * square))
    resid = two + dot(act, w_out[...], 1, 0) + vec(9)
    three, scale_three = norm(resid)
    valid = lax.broadcasted_iota(jnp.int32, (tags, 1), 0) < lens[i]
    out_ref[0] = jnp.where(valid, three * vec(12) + vec(8), 0.0).astype(bf16)

    grad = jnp.where(valid, gout_ref[0].astype(f32), 0.0)
    add(12, column_sums(grad * three))
    add(8, column_sums(grad))
    g_three = norm_back(grad, three, scale_three, vec(12))
    g_low = g_three.astype(bf16)
    add(9, column_sums(g_three))
    acc_out[...] += dot(act, g_low, 0, 0)
    g_inner = dot(g_low, w_out[...], 1, 1) * slope
    acc_bin[...] += column_sums(g_inner)
    g_inner = g_inner.astype(bf16)
    acc_in[...] += dot(two_low, g_inner, 0, 0)
    g_two = g_three + dot(g_inner, w_in[...], 1, 1)
    add(11, column_sums(g_two * n_two[...]))
    add(7, column_sums(g_two))
    g_two = norm_back(g_two, n_two[...], scale_two, vec(11))
    add(5, column_sums(g_two))
    g_low = g_two.astype(bf16)
    acc_proj[1] += dot(mix_two_t, g_low, 1, 0)
    gmix_two[...] = dot(w_proj[1], g_low, 1, 1).astype(bf16).reshape(gmix_two.shape)

    def backward(h, _):
        grad = gmix_two[h].astype(f32)
        inv = inv_ref[pl.ds(h, 1), :]
        delta = jnp.sum(grad * mix_two[h].astype(f32), 0, keepdims=True) * inv
        grad = (grad * inv).astype(bf16)
        e = e_ref[h]
        dp = dot(with_ones(ckv_ref[0, HEADS + h]), with_delta(grad, delta), 0, 0)
        ds = e * dp.astype(bf16)
        dkv_ref[0, HEADS + h] = dot(grad, e, 1, 1).astype(bf16)
        dkv_ref[0, h] = dot(q_ref[h], ds, 1, 1).astype(bf16)
        dq_ref[h] = (dot(ckv_ref[0, h], ds, 1, 0) * HEAD_DIM ** -0.5).astype(bf16)
        return 0

    lax.fori_loop(0, HEADS, backward, 0)
    dq = dq_ref[...].reshape(width, tags)
    dkv = dkv_ref[0].reshape(2 * width, cells)
    acc_col[0] += lane_groups(dq.astype(f32))
    body = cells // 128 * 128
    dv = dkv[width:].astype(f32)
    acc_col[1] += lane_groups(dv[:, :body])
    if body < cells:
        acc_col[1, :, : cells - body] += dv[:, body:]
    acc_cross[:width] += dot(dq, one_low, 1, 0)
    acc_cross[width:] += dot(dkv, mem_ref[0], 1, 0)
    g_one = g_two + dot(dq, wt_q[...], 0, 0)
    add(10, column_sums(g_one * n_one[...]))
    add(6, column_sums(g_one))
    g_one = norm_back(g_one, n_one[...], scale_one, vec(10))
    add(2, column_sums(g_one))
    g_resid[0] = g_one
    g_low = g_one.astype(bf16)
    acc_proj[0] += dot(mix_one_t, g_low, 1, 0)
    g_mix[0] = dot(w_proj[0], g_low, 1, 1).astype(bf16).reshape(g_mix.shape[1:])

    @pl.when(i == count - 1)
    def _():
        gw_cross[...] = acc_cross[...].astype(bf16).T
        gw_proj[...] = acc_proj[...].astype(bf16)
        gw_in[...] = acc_in[...].astype(bf16)
        gw_out[...] = acc_out[...].astype(bf16)
        add(3, column_sums(acc_col[0].T))
        add(4, column_sums(acc_col[1].T))
        g_vec[...] = acc_vec[...]
        g_bin[...] = acc_bin[...]


def run_middle(lens, x, mem, gout, mix_one, ckv, wt_cross, w_proj, w_in, w_out, bias_q, vectors, b_in):
    images, tags, width = x.shape
    cells = mem.shape[1]
    hidden = w_in.shape[1]
    sds = jax.ShapeDtypeStruct

    def per(*shape):
        return pl.BlockSpec((1,) + shape, lambda i, n: (i,) + (0,) * len(shape))

    def one(*shape):
        return pl.BlockSpec(shape, lambda i, n: (0,) * len(shape))

    return pl.pallas_call(
        middle,
        grid_spec=pltpu.PrefetchScalarGridSpec(
            num_scalar_prefetch=1,
            grid=(images,),
            in_specs=[
                per(tags, width), per(cells, width), per(tags, width), per(HEADS, HEAD_DIM, tags), per(2 * HEADS, HEAD_DIM, cells),
                one(width, width), one(2, width, width), one(width, hidden), one(hidden, width), one(width, 1), one(16, width), one(1, hidden),
            ],
            out_specs=[
                per(tags, width), per(tags, width), per(HEADS, HEAD_DIM, tags), per(2 * HEADS, HEAD_DIM, cells),
                one(width, 3 * width), one(2, width, width), one(width, hidden), one(hidden, width), one(16, width), one(1, hidden),
            ],
            scratch_shapes=[
                pltpu.VMEM((HEADS, cells, tags), bf16),
                pltpu.VMEM((HEADS, HEAD_DIM, tags), bf16),
                pltpu.VMEM((HEADS, tags), f32),
                pltpu.VMEM((HEADS, HEAD_DIM, tags), bf16),
                pltpu.VMEM((HEADS, HEAD_DIM, tags), bf16),
                pltpu.VMEM((HEADS, HEAD_DIM, tags), bf16),
                pltpu.VMEM((3 * width, width), f32),
                pltpu.VMEM((2, width, width), f32),
                pltpu.VMEM((width, hidden), f32),
                pltpu.VMEM((hidden, width), f32),
                pltpu.VMEM((16, width), f32),
                pltpu.VMEM((1, hidden), f32),
                pltpu.VMEM((2, width, 128), f32),
                pltpu.VMEM((tags, width), f32),
                pltpu.VMEM((tags, width), f32),
            ],
        ),
        out_shape=[
            sds((images, tags, width), bf16), sds((images, tags, width), f32), sds((images, HEADS, HEAD_DIM, tags), bf16),
            sds((images, 2 * HEADS, HEAD_DIM, cells), bf16),
            sds((width, 3 * width), bf16), sds((2, width, width), bf16), sds((width, hidden), bf16), sds((hidden, width), bf16),
            sds((16, width), f32), sds((1, hidden), f32),
        ],
        compiler_params=pltpu.CompilerParams(vmem_limit_bytes=62 * MIB),
        name="middle",
    )(lens, x, mem, gout, mix_one, ckv, wt_cross, w_proj, w_in, w_out, bias_q, vectors, b_in)


def self_backward(x_ref, qkv_ref, near_ref, far_ref, inv_ref, mix_ref, gmix_ref, g_resid, dkv_ref, wt_self, wt_cross,
                  g_tags, g_mem, gw_self, g_col, d_ref, acc, acc_col):
    tags, width = x_ref.shape[1:]
    half = tags // 2
    i = pl.program_id(0)

    @pl.when(i == 0)
    def _():
        acc[...] = jnp.zeros_like(acc)
        acc_col[...] = jnp.zeros_like(acc_col)

    def head(h, _):
        grad = gmix_ref[0, h].astype(f32)
        inv = inv_ref[0, pl.ds(h, 1), :]
        delta = jnp.sum(grad * mix_ref[0, h].astype(f32), 0, keepdims=True) * inv
        grad = (grad * inv).astype(bf16)
        ext = with_delta(grad, delta)
        qt, kt, vt = qkv_ref[0, h], qkv_ref[0, HEADS + h], with_ones(qkv_ref[0, 2 * HEADS + h])
        near, far = near_ref[0, h], far_ref[0, h]
        ds_near = near * dot(vt[:, :half], ext[:, :half], 0, 0).astype(bf16)
        ds_far = far * dot(vt, ext[:, half:], 0, 0).astype(bf16)
        dv = dot(grad[:, half:], far, 1, 1)
        dk = dot(qt[:, half:], ds_far, 1, 1)
        d_ref[2 * HEADS + h, :, half:] = dv[:, half:].astype(bf16)
        d_ref[2 * HEADS + h, :, :half] = (dv[:, :half] + dot(grad[:, :half], near, 1, 1)).astype(bf16)
        d_ref[HEADS + h, :, half:] = dk[:, half:].astype(bf16)
        d_ref[HEADS + h, :, :half] = (dk[:, :half] + dot(qt[:, :half], ds_near, 1, 1)).astype(bf16)
        d_ref[h, :, :half] = (dot(kt[:, :half], ds_near, 1, 0) * HEAD_DIM ** -0.5).astype(bf16)
        d_ref[h, :, half:] = (dot(kt, ds_far, 1, 0) * HEAD_DIM ** -0.5).astype(bf16)
        return 0

    lax.fori_loop(0, HEADS, head, 0)
    d = d_ref[...].reshape(3 * width, tags)
    acc_col[0] += lane_groups(d[:width].astype(f32))
    acc_col[1] += lane_groups(d[2 * width :].astype(f32))
    acc[...] += dot(d, x_ref[0], 1, 0)
    g_tags[0] = g_resid[0] + dot(d, wt_self[...], 0, 0)
    g_mem[0] = dot(dkv_ref[0].reshape(2 * width, -1), wt_cross[width:], 0, 0)

    @pl.when(i == pl.num_programs(0) - 1)
    def _():
        gw_self[...] = acc[...].astype(bf16).T
        g_col[0:1] = column_sums(acc_col[0].T)
        g_col[1:2] = column_sums(acc_col[1].T)


def run_self_backward(x, qkv, near, far, inv, mix, gmix, g_resid, dkv, wt_self, wt_cross):
    images, tags, width = x.shape
    cells = dkv.shape[3]
    half = tags // 2
    sds = jax.ShapeDtypeStruct

    def per(*shape):
        return pl.BlockSpec((1,) + shape, lambda i: (i,) + (0,) * len(shape))

    def one(*shape):
        return pl.BlockSpec(shape, lambda i: (0,) * len(shape))

    return pl.pallas_call(
        self_backward,
        grid=(images,),
        in_specs=[per(tags, width), per(3 * HEADS, HEAD_DIM, tags), per(HEADS, half, half), per(HEADS, tags, half), per(HEADS, tags),
                  per(HEADS, HEAD_DIM, tags), per(HEADS, HEAD_DIM, tags), per(tags, width), per(2 * HEADS, HEAD_DIM, cells),
                  one(3 * width, width), one(3 * width, width)],
        out_specs=[per(tags, width), per(cells, width), one(width, 3 * width), one(8, width)],
        out_shape=[sds((images, tags, width), f32), sds((images, cells, width), f32), sds((width, 3 * width), bf16), sds((8, width), f32)],
        scratch_shapes=[pltpu.VMEM((3 * HEADS, HEAD_DIM, tags), bf16), pltpu.VMEM((3 * width, width), f32), pltpu.VMEM((2, width, 128), f32)],
        compiler_params=pltpu.CompilerParams(vmem_limit_bytes=60 * MIB),
        name="self_backward",
    )(x, qkv, near, far, inv, mix, gmix, g_resid, dkv, wt_self, wt_cross)


def layer(lens, x, mem, gout, w_self, w_cross, w_proj, w_in, w_out, vectors, b_in):
    width = x.shape[2]
    zero = jnp.zeros((width,), f32)
    bias_qkv = jnp.concatenate([vectors[0], zero, vectors[1]])[:, None]
    bias_kv = jnp.concatenate([zero, vectors[4]])[:, None]
    bias_q = vectors[3][:, None]
    qkv, ckv, near, far, inv, mix, wt_self, wt_cross = run_self_forward(lens, x, mem, w_self, w_cross, bias_qkv, bias_kv)
    out, g_resid, gmix, dkv, gw_cross, gw_proj, gw_in, gw_out, g_vec, g_bin = run_middle(
        lens, x, mem, gout, mix, ckv, wt_cross, w_proj, w_in, w_out, bias_q, vectors, b_in)
    g_tags, g_mem, gw_self, g_col = run_self_backward(x, qkv, near, far, inv, mix, gmix, g_resid, dkv, wt_self, wt_cross)
    g_vec = g_vec.at[0:2].set(g_col[0:2])
    return out, g_tags, g_mem, gw_self, gw_cross, gw_proj, gw_in, gw_out, g_vec, g_bin


AXES = ("wide", "narrow")
LEADS = (0, 0, 1, 0, 0, 0)


def fold(block, rows, columns):
    if rows % 16 == 0:
        return block
    return block.reshape(block.shape[:-2] + (16, rows * columns // 16))


def per_device(dims, tag_states, image_memory, tag_lengths, w_self, w_cross, w_proj, w_in, b_in, w_out, ln_gains, biases, out_grad):
    cells = dims + (2,)
    devices = dims[0] * dims[1] * dims[2] * 2
    width = tag_states.shape[2]
    lanes, hidden_lanes = biases.shape[1], b_in.shape[0]
    small = jnp.concatenate(
        [
            jnp.pad(jnp.concatenate([biases, ln_gains]), ((0, 0), (0, 128 - lanes))),
            jnp.pad(b_in[None], ((0, 2), (0, 128 - hidden_lanes))),
        ]
    )
    shards = (w_self, w_cross, w_proj, w_in, w_out, small)
    gathered = gather(dims, [fold(s, *s.shape[-2:]) for s in shards], LEADS)

    def whole(held, shard):
        lead = shard.shape[:-2]
        rows, columns = shard.shape[-2:]
        return held.reshape(lead + (devices * rows, columns))

    full_self, full_cross, full_proj, full_in, full_out, full_small = [whole(h, s) for h, s in zip(gathered, shards)]
    by_device = full_small.reshape(devices, 16, 128)
    vectors = by_device[:, :, :lanes].transpose(1, 0, 2).reshape(16, width).astype(f32)
    hidden_bias = by_device[:, 13, :hidden_lanes].reshape(1, -1).astype(f32)
    layer_out, grad_tags, grad_memory, g_self, g_cross, g_proj, g_in, g_out, g_vec, g_bin = layer(
        tag_lengths, tag_states, image_memory, out_grad, full_self, full_cross, full_proj, full_in, full_out, vectors, hidden_bias)
    g_small = jnp.pad(g_vec.reshape(16, devices, lanes).transpose(1, 0, 2)[:, :13], ((0, 0), (0, 0), (0, 128 - lanes)))
    g_hidden = jnp.pad(g_bin.reshape(devices, 1, hidden_lanes), ((0, 0), (0, 2), (0, 128 - hidden_lanes)))
    g_small = jnp.concatenate([g_small, g_hidden], 1).astype(bf16).reshape(devices * 16, 128)

    def parts(grad, shard):
        lead = shard.shape[:-2]
        rows, columns = shard.shape[-2:]
        return fold(grad.reshape(lead + cells + (rows, columns)), rows, columns)

    shares = scatter(dims, [parts(g, s) for g, s in zip((g_self, g_cross, g_proj, g_in, g_out, g_small), shards)], LEADS)
    s_self, s_cross, s_proj, s_in, s_out, s_small = [v.reshape(s.shape) for v, s in zip(shares, shards)]
    return (layer_out, grad_tags, grad_memory, s_self, s_cross, s_proj, s_in, s_small[13, :hidden_lanes], s_out,
            s_small[10:13, :lanes], s_small[:10, :lanes])


def solution(mesh):
    dims = grid_of(mesh.shape["wide"], mesh.shape["narrow"])
    rows, matrix, stack, columns = P(AXES, None, None), P(AXES, None), P(None, AXES, None), P(None, AXES)
    return jax.shard_map(
        functools.partial(per_device, dims),
        mesh=mesh,
        in_specs=(rows, rows, P(AXES), matrix, matrix, stack, matrix, P(AXES), matrix, columns, columns, rows),
        out_specs=(rows, rows, rows, matrix, matrix, stack, matrix, P(AXES), matrix, columns, columns),
        check_vma=False,
    )
```

```python
import functools

import jax
import jax.numpy as jnp
from jax import lax
from jax.experimental import pallas as pl
from jax.experimental.pallas import tpu as pltpu
from jax.sharding import PartitionSpec as P


MESH = pl.DeviceIdType.MESH
f32, bf16 = jnp.float32, jnp.bfloat16


def grid_of(mesh_wide, mesh_narrow):
    outer = 4
    return outer, mesh_wide // outer, mesh_narrow // 2


def place(dims):
    outer, inner, across = dims
    wide, narrow = lax.axis_index("wide"), lax.axis_index("narrow")
    return wide // inner, lax.rem(wide, inner), narrow // 2, lax.rem(narrow, 2)


def device(dims, a, b, x, c):
    return {"wide": a * dims[1] + b, "narrow": x * 2 + c}


def greet(dims, me):
    a, b, x, c = me
    outer, inner, across = dims
    barrier = pltpu.get_barrier_semaphore()
    peers = [(lax.rem(a + k, outer), b, x, c) for k in range(1, outer)]
    peers += [(a, lax.rem(b + k, inner), x, c) for k in range(1, inner)]
    peers += [(a, b, lax.rem(x + k, across), c) for k in range(1, across)]
    peers += [(a, b, x, 1 - c)]
    for peer in peers:
        pl.semaphore_signal(barrier, inc=1, device_id=device(dims, *peer), device_id_type=MESH)
    pl.semaphore_wait(barrier, len(peers))


ALL = slice(None)


def gather_kernel(dims, leads, *refs):
    count = len(leads)
    shards, outs = refs[:count], refs[count : 2 * count]
    local_sem, send_sem, recv_sem = refs[2 * count :]
    outer, inner, across = dims
    me = place(dims)
    a, b, x, c = me
    greet(dims, me)

    def cell(ref, lead, *index):
        return ref.at[(ALL,) * lead + index]

    def remote(g, slot, src, dst, peer):
        return pltpu.make_async_remote_copy(
            src_ref=src, dst_ref=dst, send_sem=send_sem.at[g, slot], recv_sem=recv_sem.at[g, slot],
            device_id=device(dims, *peer), device_id_type=MESH)

    n_in, n_ac = inner - 1, across - 1

    def first(g):
        lead = leads[g]
        mine = cell(outs[g], lead, a, b, x, c)
        return [remote(g, k - 1, shards[g], mine, (lax.rem(a + k, outer), b, x, c)) for k in range(1, outer)]

    def keep(g):
        return pltpu.make_async_copy(shards[g], cell(outs[g], leads[g], a, b, x, c), local_sem.at[g])

    base = outer - 1

    def via_inner(g, core):
        lead = leads[g]
        column = ALL if core == 0 else x
        piece = cell(outs[g], lead, ALL, b, column, c)
        return [remote(g, base + k - 1, piece, piece, (a, lax.rem(b + k, inner), x, c)) for k in range(1, inner)]

    def via_across(g, core):
        lead = leads[g]
        row = b if core == 0 else ALL
        piece = cell(outs[g], lead, ALL, row, x, c)
        return [remote(g, base + n_in + k - 1, piece, piece, (a, b, lax.rem(x + k, across), c)) for k in range(1, across)]

    share = base + n_in + n_ac

    def to_partner(g, core, holder):
        lead = leads[g]
        def piece(slot, row, column):
            ref = cell(outs[g], lead, ALL, row, column, holder)
            return remote(g, share + slot, ref, ref, (a, b, x, 1 - c))
        own = [piece(0, b, x)]
        by_inner = [piece(1 + k - 1, lax.rem(b + k, inner), ALL if core == 0 else x) for k in range(1, inner)]
        by_across = [piece(1 + n_in + k - 1, b if core == 0 else ALL, lax.rem(x + k, across)) for k in range(1, across)]
        return (own, by_across, by_inner) if core == 0 else (own, by_inner, by_across)

    def start(copies):
        for copy in copies:
            copy.start()

    def arrived(copies):
        for copy in copies:
            copy.wait_recv()

    for g in range(count):
        keep(g).start()
        start(first(g))

    def body(core):
        second, third = (via_across, via_inner) if core == 0 else (via_inner, via_across)
        for step in range(count + 2):
            g = step
            if g < count:
                keep(g).wait()
                arrived(first(g))
                start(second(g, core))
                start(to_partner(g, core, c)[0])
            g = step - 1
            if 0 <= g < count:
                arrived(second(g, core))
                start(third(g, core))
                start(to_partner(g, core, c)[1])
            g = step - 2
            if 0 <= g < count:
                arrived(third(g, core))
                start(to_partner(g, core, c)[2])
        for g in range(count):
            for group in to_partner(g, 1 - core, 1 - c):
                arrived(group)
        for g in range(count):
            for copy in first(g) + second(g, core) + third(g, core):
                copy.wait_send()
            for group in to_partner(g, core, c):
                for copy in group:
                    copy.wait_send()

    @pl.when(c == 0)
    def _():
        body(0)

    @pl.when(c == 1)
    def _():
        body(1)


def gather(dims, shards, leads):
    outer, inner, across = dims
    def shape(s, lead):
        return jax.ShapeDtypeStruct(s.shape[:lead] + (outer, inner, across, 2) + s.shape[lead:], s.dtype)
    slots = (outer - 1) + 2 * (inner - 1) + 2 * (across - 1) + 1
    n = len(shards)
    return pl.pallas_call(
        functools.partial(gather_kernel, dims, leads),
        out_shape=[shape(s, l) for s, l in zip(shards, leads)],
        in_specs=[pl.BlockSpec(memory_space=pl.ANY)] * n,
        out_specs=[pl.BlockSpec(memory_space=pl.ANY)] * n,
        scratch_shapes=[pltpu.SemaphoreType.DMA((n,)), pltpu.SemaphoreType.DMA((n, slots)), pltpu.SemaphoreType.DMA((n, slots))],
        compiler_params=pltpu.CompilerParams(collective_id=0, has_side_effects=True),
        name="gather_weights",
    )(*shards)


def scatter_kernel(dims, leads, *refs):
    count = len(leads)
    grads, outs = refs[:count], refs[count : 2 * count]
    rest = refs[2 * count :]
    r0, r1i, r1a, r2a, r2i, r3 = (rest[k * count : (k + 1) * count] for k in range(6))
    send_sem, recv_sem = rest[6 * count :]
    outer, inner, across = dims
    me = place(dims)
    a, b, x, c = me
    greet(dims, me)
    n_in, n_ac = inner - 1, across - 1

    def cell(ref, lead, *index):
        return ref.at[(ALL,) * lead + index]

    def remote(g, slot, src, dst, peer):
        return pltpu.make_async_remote_copy(
            src_ref=src, dst_ref=dst, send_sem=send_sem.at[g, slot], recv_sem=recv_sem.at[g, slot],
            device_id=device(dims, *peer), device_id_type=MESH)

    def swap(g):
        return [remote(g, 0, cell(grads[g], leads[g], ALL, ALL, ALL, 1 - c), r0[g], (a, b, x, 1 - c))]

    def via_inner(g, core):
        lead = leads[g]
        res = []
        for k in range(1, inner):
            peer = lax.rem(b + k, inner)
            if core == 0:
                src, dst = cell(r0[g], lead, ALL, peer), r1i[g].at[k - 1]
            else:
                src, dst = cell(r1a[g].at[0], lead, ALL, peer), r2i[g].at[k - 1]
            res.append(remote(g, k, src, dst, (a, peer, x, c)))
        return res

    def via_across(g, core):
        lead = leads[g]
        res = []
        for k in range(1, across):
            peer = lax.rem(x + k, across)
            if core == 1:
                src, dst = cell(r0[g], lead, ALL, ALL, peer), r1a[g].at[k - 1]
            else:
                src, dst = cell(r1i[g].at[0], lead, ALL, peer), r2a[g].at[k - 1]
            res.append(remote(g, 1 + n_in + k - 1, src, dst, (a, b, peer, c)))
        return res

    def last(g, core):
        lead = leads[g]
        held = (r2a if core == 0 else r2i)[g].at[0]
        res = []
        for k in range(1, outer):
            peer = lax.rem(a + k, outer)
            res.append(remote(g, 1 + n_in + n_ac + k - 1, cell(held, lead, peer), r3[g].at[k - 1], (peer, b, x, c)))
        return res

    def start(copies):
        for copy in copies:
            copy.start()

    def arrived(copies):
        for copy in copies:
            copy.wait_recv()

    def up(v):
        return v.astype(f32)

    for g in range(count):
        start(swap(g))

    def body(core):
        second, third = (via_inner, via_across) if core == 0 else (via_across, via_inner)
        def at(lead, *index):
            return (ALL,) * lead + index
        for step in range(count + 3):
            g = step
            if g < count:
                arrived(swap(g))
                lead = leads[g]
                r0[g][...] = (up(grads[g][at(lead, ALL, ALL, ALL, c)]) + up(r0[g][...])).astype(bf16)
                start(second(g, core))
            g = step - 1
            if 0 <= g < count:
                arrived(second(g, core))
                lead = leads[g]
                if core == 0:
                    total = up(r0[g][at(lead, ALL, b)])
                    held = r1i[g]
                else:
                    total = up(r0[g][at(lead, ALL, ALL, x)])
                    held = r1a[g]
                for k in range(held.shape[0]):
                    total = total + up(held[k])
                held[0] = total.astype(bf16)
                start(third(g, core))
            g = step - 2
            if 0 <= g < count:
                arrived(third(g, core))
                lead = leads[g]
                if core == 0:
                    total = up(r1i[g][(0,) + at(lead, ALL, x)])
                    held = r2a[g]
                else:
                    total = up(r1a[g][(0,) + at(lead, ALL, b)])
                    held = r2i[g]
                for k in range(held.shape[0]):
                    total = total + up(held[k])
                held[0] = total.astype(bf16)
                start(last(g, core))
            g = step - 3
            if 0 <= g < count:
                arrived(last(g, core))
                lead = leads[g]
                held = (r2a if core == 0 else r2i)[g]
                total = up(held[(0,) + at(lead, a)])
                for k in range(outer - 1):
                    total = total + up(r3[g][k])
                outs[g][...] = total
        for g in range(count):
            for copy in swap(g) + second(g, core) + third(g, core) + last(g, core):
                copy.wait_send()

    @pl.when(c == 0)
    def _():
        body(0)

    @pl.when(c == 1)
    def _():
        body(1)


def scatter(dims, grads, leads):
    outer, inner, across = dims
    n = len(grads)
    outs, shapes = [], [[] for _ in range(6)]
    for g, lead in zip(grads, leads):
        head, tail = g.shape[:lead], g.shape[lead + 4 :]
        outs.append(jax.ShapeDtypeStruct(head + tail, f32))
        shapes[0].append(head + (outer, inner, across) + tail)
        shapes[1].append((inner - 1,) + head + (outer, across) + tail)
        shapes[2].append((across - 1,) + head + (outer, inner) + tail)
        shapes[3].append((across - 1,) + head + (outer,) + tail)
        shapes[4].append((inner - 1,) + head + (outer,) + tail)
        shapes[5].append((outer - 1,) + head + tail)
    slots = 1 + (inner - 1) + (across - 1) + (outer - 1)
    return pl.pallas_call(
        functools.partial(scatter_kernel, dims, leads),
        out_shape=outs,
        in_specs=[pl.BlockSpec(memory_space=pltpu.VMEM)] * n,
        out_specs=[pl.BlockSpec(memory_space=pltpu.VMEM)] * n,
        scratch_shapes=[pltpu.VMEM(s, bf16) for group in shapes for s in group]
        + [pltpu.SemaphoreType.DMA((n, slots)), pltpu.SemaphoreType.DMA((n, slots))],
        compiler_params=pltpu.CompilerParams(collective_id=1, has_side_effects=True, vmem_limit_bytes=48 * 2**20),
        name="scatter_grads",
    )(*grads)

HEADS, HEAD_DIM = 8, 64
EPS = 1e-5
MASKED = -1e9
MIB = 2**20


def dot(left, right, left_dim, right_dim):
    return lax.dot_general(left, right, (((left_dim,), (right_dim,)), ((), ())), preferred_element_type=f32)


def full(shape):
    return pl.BlockSpec(shape, lambda i: (0,) * len(shape))


def image(shape):
    return pl.BlockSpec((1,) + shape, lambda i: (i,) + (0,) * len(shape))


def with_ones(rows):
    return jnp.concatenate([rows, jnp.ones((16, rows.shape[1]), bf16)], 0)


def with_delta(rows, delta):
    high = delta.astype(bf16).astype(f32)
    low = delta - high
    at = lax.broadcasted_iota(jnp.int32, (16, rows.shape[1]), 0)
    extra = jnp.where(at == 0, -high, jnp.where(at == 1, -low, 0.0))
    return jnp.concatenate([rows, extra.astype(bf16)], 0)


def self_forward(lens, x_ref, mem_ref, w_self, w_cross, bias_qkv, bias_kv,
                 qkv_ref, ckv_ref, near_ref, far_ref, inv_ref, mix_ref, wt_self, wt_cross):
    width = x_ref.shape[2]
    tags = x_ref.shape[1]
    half = tags // 2
    i = pl.program_id(0)

    @pl.when(i == 0)
    def _():
        wt_self[...] = w_self[...].T
        wt_cross[...] = w_cross[...].T

    ckv = dot(wt_cross[width:], mem_ref[0], 1, 1) + bias_kv[...]
    ckv_ref[0] = ckv.astype(bf16).reshape(ckv_ref.shape[1:])
    qkv = dot(wt_self[...], x_ref[0], 1, 1) + bias_qkv[...]
    q = qkv[:width].astype(bf16) * bf16(HEAD_DIM ** -0.5)
    qkv_ref[0, :HEADS] = q.reshape(HEADS, HEAD_DIM, tags)
    qkv_ref[0, HEADS:] = qkv[width:].astype(bf16).reshape(2 * HEADS, HEAD_DIM, tags)
    last = lens[i] - 1

    def head(h, _):
        qt, kt, vt = qkv_ref[0, h], qkv_ref[0, HEADS + h], with_ones(qkv_ref[0, 2 * HEADS + h])

        def part(keys, first, out):
            s = dot(kt[:, :keys], qt[:, first : first + half], 0, 0)
            key_at = lax.broadcasted_iota(jnp.int32, (keys, half), 0)
            query_at = lax.broadcasted_iota(jnp.int32, (1, half), 1) + first
            s = jnp.where(key_at <= jnp.minimum(query_at, last), s, MASKED)
            e = jnp.exp(s - jnp.max(s, 0, keepdims=True)).astype(bf16)
            out[0, h] = e
            mixed = dot(vt[:, :keys], e, 1, 0)
            inv = 1.0 / mixed[HEAD_DIM : HEAD_DIM + 1]
            inv_ref[0, pl.ds(h, 1), first : first + half] = inv
            mix_ref[0, h, :, first : first + half] = (mixed[:HEAD_DIM] * inv).astype(bf16)

        part(half, 0, near_ref)
        part(tags, half, far_ref)
        return 0

    lax.fori_loop(0, HEADS, head, 0)


def run_self_forward(lens, x, mem, w_self, w_cross, bias_qkv, bias_kv):
    images, tags, width = x.shape
    cells = mem.shape[1]
    half = tags // 2
    sds = jax.ShapeDtypeStruct
    return pl.pallas_call(
        self_forward,
        grid_spec=pltpu.PrefetchScalarGridSpec(
            num_scalar_prefetch=1,
            grid=(images,),
            in_specs=[pl.BlockSpec((1, tags, width), lambda i, n: (i, 0, 0)), pl.BlockSpec((1, cells, width), lambda i, n: (i, 0, 0))]
            + [pl.BlockSpec(v.shape, lambda i, n: (0, 0)) for v in (w_self, w_cross, bias_qkv, bias_kv)],
            out_specs=[
                pl.BlockSpec((1, 3 * HEADS, HEAD_DIM, tags), lambda i, n: (i, 0, 0, 0)),
                pl.BlockSpec((1, 2 * HEADS, HEAD_DIM, cells), lambda i, n: (i, 0, 0, 0)),
                pl.BlockSpec((1, HEADS, half, half), lambda i, n: (i, 0, 0, 0)),
                pl.BlockSpec((1, HEADS, tags, half), lambda i, n: (i, 0, 0, 0)),
                pl.BlockSpec((1, HEADS, tags), lambda i, n: (i, 0, 0)),
                pl.BlockSpec((1, HEADS, HEAD_DIM, tags), lambda i, n: (i, 0, 0, 0)),
                pl.BlockSpec((3 * width, width), lambda i, n: (0, 0)),
                pl.BlockSpec((3 * width, width), lambda i, n: (0, 0)),
            ],
        ),
        out_shape=[
            sds((images, 3 * HEADS, HEAD_DIM, tags), bf16),
            sds((images, 2 * HEADS, HEAD_DIM, cells), bf16),
            sds((images, HEADS, half, half), bf16),
            sds((images, HEADS, tags, half), bf16),
            sds((images, HEADS, tags), f32),
            sds((images, HEADS, HEAD_DIM, tags), bf16),
            sds((3 * width, width), bf16),
            sds((3 * width, width), bf16),
        ],
        compiler_params=pltpu.CompilerParams(vmem_limit_bytes=58 * MIB),
        name="self_forward",
    )(lens, x, mem, w_self, w_cross, bias_qkv, bias_kv)


def norm(resid):
    centred = resid - jnp.mean(resid, -1, keepdims=True)
    scale = lax.rsqrt(jnp.mean(centred * centred, -1, keepdims=True) + EPS)
    return centred * scale, scale


def norm_back(grad, normed, scale, gain):
    scaled = grad * gain
    mean_one = jnp.mean(scaled, -1, keepdims=True)
    mean_two = jnp.mean(scaled * normed, -1, keepdims=True)
    return scale * (scaled - mean_one - normed * mean_two)


def column_sums(rows):
    return jnp.sum(rows, 0, keepdims=True)


def lane_groups(rows):
    total = rows[:, :128]
    for k in range(1, rows.shape[1] // 128):
        total = total + rows[:, 128 * k : 128 * (k + 1)]
    return total


def middle(lens, x_ref, mem_ref, gout_ref, mix_one, ckv_ref, wt_q, w_proj, w_in, w_out, bias_q, vectors, b_in,
           out_ref, g_resid, g_mix, dkv_ref, gw_cross, gw_proj, gw_in, gw_out, g_vec, g_bin,
           e_ref, q_ref, inv_ref, mix_two, gmix_two, dq_ref, acc_cross, acc_proj, acc_in, acc_out, acc_vec, acc_bin, acc_col,
           n_one, n_two):
    tags, width = x_ref.shape[1:]
    cells = mem_ref.shape[1]
    i = pl.program_id(0)
    count = pl.num_programs(0)

    @pl.when(i == 0)
    def _():
        for ref in (acc_cross, acc_proj, acc_in, acc_out, acc_vec, acc_bin, acc_col):
            ref[...] = jnp.zeros_like(ref)

    def vec(k):
        return vectors[k : k + 1, :]

    def add(k, value):
        acc_vec[k : k + 1, :] += value

    mix_one_t = mix_one[0].reshape(width, tags)
    resid = x_ref[0].astype(f32) + dot(mix_one_t, w_proj[0], 0, 0) + vec(2)
    normed, scale_one = norm(resid)
    n_one[...] = normed
    one = normed * vec(10) + vec(6)
    one_low = one.astype(bf16)
    cq = (dot(wt_q[...], one_low, 1, 1) + bias_q[...]).astype(bf16) * bf16(HEAD_DIM ** -0.5)
    q_ref[...] = cq.reshape(q_ref.shape)

    def forward(h, _):
        s = dot(ckv_ref[0, h], q_ref[h], 0, 0)
        e = jnp.exp(s - jnp.max(s, 0, keepdims=True)).astype(bf16)
        e_ref[h] = e
        mixed = dot(with_ones(ckv_ref[0, HEADS + h]), e, 1, 0)
        inv = 1.0 / mixed[HEAD_DIM : HEAD_DIM + 1]
        inv_ref[pl.ds(h, 1), :] = inv
        mix_two[h] = (mixed[:HEAD_DIM] * inv).astype(bf16)
        return 0

    lax.fori_loop(0, HEADS, forward, 0)
    mix_two_t = mix_two[...].reshape(width, tags)
    resid = one + dot(mix_two_t, w_proj[1], 0, 0) + vec(5)
    normed, scale_two = norm(resid)
    n_two[...] = normed
    two = normed * vec(11) + vec(7)
    two_low = two.astype(bf16)
    inner = dot(two_low, w_in[...], 1, 0) + b_in[...]
    root = 0.7978845608028654
    square = inner * inner
    tanh = jnp.tanh(root * inner * (1.0 + 0.044715 * square))
    act = (0.5 * inner * (1.0 + tanh)).astype(bf16)
    slope = 0.5 * (1.0 + tanh) + 0.5 * inner * (1.0 - tanh * tanh) * (root * (1.0 + 3 * 0.044715 * square))
    resid = two + dot(act, w_out[...], 1, 0) + vec(9)
    three, scale_three = norm(resid)
    valid = lax.broadcasted_iota(jnp.int32, (tags, 1), 0) < lens[i]
    out_ref[0] = jnp.where(valid, three * vec(12) + vec(8), 0.0).astype(bf16)

    grad = jnp.where(valid, gout_ref[0].astype(f32), 0.0)
    add(12, column_sums(grad * three))
    add(8, column_sums(grad))
    g_three = norm_back(grad, three, scale_three, vec(12))
    g_low = g_three.astype(bf16)
    add(9, column_sums(g_three))
    acc_out[...] += dot(act, g_low, 0, 0)
    g_inner = dot(g_low, w_out[...], 1, 1) * slope
    acc_bin[...] += column_sums(g_inner)
    g_inner = g_inner.astype(bf16)
    acc_in[...] += dot(two_low, g_inner, 0, 0)
    g_two = g_three + dot(g_inner, w_in[...], 1, 1)
    add(11, column_sums(g_two * n_two[...]))
    add(7, column_sums(g_two))
    g_two = norm_back(g_two, n_two[...], scale_two, vec(11))
    add(5, column_sums(g_two))
    g_low = g_two.astype(bf16)
    acc_proj[1] += dot(mix_two_t, g_low, 1, 0)
    gmix_two[...] = dot(w_proj[1], g_low, 1, 1).astype(bf16).reshape(gmix_two.shape)

    def backward(h, _):
        grad = gmix_two[h].astype(f32)
        inv = inv_ref[pl.ds(h, 1), :]
        delta = jnp.sum(grad * mix_two[h].astype(f32), 0, keepdims=True) * inv
        grad = (grad * inv).astype(bf16)
        e = e_ref[h]
        dp = dot(with_ones(ckv_ref[0, HEADS + h]), with_delta(grad, delta), 0, 0)
        ds = e * dp.astype(bf16)
        dkv_ref[0, HEADS + h] = dot(grad, e, 1, 1).astype(bf16)
        dkv_ref[0, h] = dot(q_ref[h], ds, 1, 1).astype(bf16)
        dq_ref[h] = (dot(ckv_ref[0, h], ds, 1, 0) * HEAD_DIM ** -0.5).astype(bf16)
        return 0

    lax.fori_loop(0, HEADS, backward, 0)
    dq = dq_ref[...].reshape(width, tags)
    dkv = dkv_ref[0].reshape(2 * width, cells)
    acc_col[0] += lane_groups(dq.astype(f32))
    body = cells // 128 * 128
    dv = dkv[width:].astype(f32)
    acc_col[1] += lane_groups(dv[:, :body])
    if body < cells:
        acc_col[1, :, : cells - body] += dv[:, body:]
    acc_cross[:width] += dot(dq, one_low, 1, 0)
    acc_cross[width:] += dot(dkv, mem_ref[0], 1, 0)
    g_one = g_two + dot(dq, wt_q[...], 0, 0)
    add(10, column_sums(g_one * n_one[...]))
    add(6, column_sums(g_one))
    g_one = norm_back(g_one, n_one[...], scale_one, vec(10))
    add(2, column_sums(g_one))
    g_resid[0] = g_one
    g_low = g_one.astype(bf16)
    acc_proj[0] += dot(mix_one_t, g_low, 1, 0)
    g_mix[0] = dot(w_proj[0], g_low, 1, 1).astype(bf16).reshape(g_mix.shape[1:])

    @pl.when(i == count - 1)
    def _():
        gw_cross[...] = acc_cross[...].astype(bf16).T
        gw_proj[...] = acc_proj[...].astype(bf16)
        gw_in[...] = acc_in[...].astype(bf16)
        gw_out[...] = acc_out[...].astype(bf16)
        add(3, column_sums(acc_col[0].T))
        add(4, column_sums(acc_col[1].T))
        g_vec[...] = acc_vec[...]
        g_bin[...] = acc_bin[...]


def run_middle(lens, x, mem, gout, mix_one, ckv, wt_cross, w_proj, w_in, w_out, bias_q, vectors, b_in):
    images, tags, width = x.shape
    cells = mem.shape[1]
    hidden = w_in.shape[1]
    sds = jax.ShapeDtypeStruct

    def per(*shape):
        return pl.BlockSpec((1,) + shape, lambda i, n: (i,) + (0,) * len(shape))

    def one(*shape):
        return pl.BlockSpec(shape, lambda i, n: (0,) * len(shape))

    return pl.pallas_call(
        middle,
        grid_spec=pltpu.PrefetchScalarGridSpec(
            num_scalar_prefetch=1,
            grid=(images,),
            in_specs=[
                per(tags, width), per(cells, width), per(tags, width), per(HEADS, HEAD_DIM, tags), per(2 * HEADS, HEAD_DIM, cells),
                one(width, width), one(2, width, width), one(width, hidden), one(hidden, width), one(width, 1), one(16, width), one(1, hidden),
            ],
            out_specs=[
                per(tags, width), per(tags, width), per(HEADS, HEAD_DIM, tags), per(2 * HEADS, HEAD_DIM, cells),
                one(width, 3 * width), one(2, width, width), one(width, hidden), one(hidden, width), one(16, width), one(1, hidden),
            ],
            scratch_shapes=[
                pltpu.VMEM((HEADS, cells, tags), bf16),
                pltpu.VMEM((HEADS, HEAD_DIM, tags), bf16),
                pltpu.VMEM((HEADS, tags), f32),
                pltpu.VMEM((HEADS, HEAD_DIM, tags), bf16),
                pltpu.VMEM((HEADS, HEAD_DIM, tags), bf16),
                pltpu.VMEM((HEADS, HEAD_DIM, tags), bf16),
                pltpu.VMEM((3 * width, width), f32),
                pltpu.VMEM((2, width, width), f32),
                pltpu.VMEM((width, hidden), f32),
                pltpu.VMEM((hidden, width), f32),
                pltpu.VMEM((16, width), f32),
                pltpu.VMEM((1, hidden), f32),
                pltpu.VMEM((2, width, 128), f32),
                pltpu.VMEM((tags, width), f32),
                pltpu.VMEM((tags, width), f32),
            ],
        ),
        out_shape=[
            sds((images, tags, width), bf16), sds((images, tags, width), f32), sds((images, HEADS, HEAD_DIM, tags), bf16),
            sds((images, 2 * HEADS, HEAD_DIM, cells), bf16),
            sds((width, 3 * width), bf16), sds((2, width, width), bf16), sds((width, hidden), bf16), sds((hidden, width), bf16),
            sds((16, width), f32), sds((1, hidden), f32),
        ],
        compiler_params=pltpu.CompilerParams(vmem_limit_bytes=62 * MIB),
        name="middle",
    )(lens, x, mem, gout, mix_one, ckv, wt_cross, w_proj, w_in, w_out, bias_q, vectors, b_in)


def self_backward(x_ref, qkv_ref, near_ref, far_ref, inv_ref, mix_ref, gmix_ref, g_resid, dkv_ref, wt_self, wt_cross,
                  g_tags, g_mem, gw_self, g_col, d_ref, acc, acc_col):
    tags, width = x_ref.shape[1:]
    half = tags // 2
    i = pl.program_id(0)

    @pl.when(i == 0)
    def _():
        acc[...] = jnp.zeros_like(acc)
        acc_col[...] = jnp.zeros_like(acc_col)

    def head(h, _):
        grad = gmix_ref[0, h].astype(f32)
        inv = inv_ref[0, pl.ds(h, 1), :]
        delta = jnp.sum(grad * mix_ref[0, h].astype(f32), 0, keepdims=True) * inv
        grad = (grad * inv).astype(bf16)
        ext = with_delta(grad, delta)
        qt, kt, vt = qkv_ref[0, h], qkv_ref[0, HEADS + h], with_ones(qkv_ref[0, 2 * HEADS + h])
        near, far = near_ref[0, h], far_ref[0, h]
        ds_near = near * dot(vt[:, :half], ext[:, :half], 0, 0).astype(bf16)
        ds_far = far * dot(vt, ext[:, half:], 0, 0).astype(bf16)
        dv = dot(grad[:, half:], far, 1, 1)
        dk = dot(qt[:, half:], ds_far, 1, 1)
        d_ref[2 * HEADS + h, :, half:] = dv[:, half:].astype(bf16)
        d_ref[2 * HEADS + h, :, :half] = (dv[:, :half] + dot(grad[:, :half], near, 1, 1)).astype(bf16)
        d_ref[HEADS + h, :, half:] = dk[:, half:].astype(bf16)
        d_ref[HEADS + h, :, :half] = (dk[:, :half] + dot(qt[:, :half], ds_near, 1, 1)).astype(bf16)
        d_ref[h, :, :half] = (dot(kt[:, :half], ds_near, 1, 0) * HEAD_DIM ** -0.5).astype(bf16)
        d_ref[h, :, half:] = (dot(kt, ds_far, 1, 0) * HEAD_DIM ** -0.5).astype(bf16)
        return 0

    lax.fori_loop(0, HEADS, head, 0)
    d = d_ref[...].reshape(3 * width, tags)
    acc_col[0] += lane_groups(d[:width].astype(f32))
    acc_col[1] += lane_groups(d[2 * width :].astype(f32))
    acc[...] += dot(d, x_ref[0], 1, 0)
    g_tags[0] = g_resid[0] + dot(d, wt_self[...], 0, 0)
    g_mem[0] = dot(dkv_ref[0].reshape(2 * width, -1), wt_cross[width:], 0, 0)

    @pl.when(i == pl.num_programs(0) - 1)
    def _():
        gw_self[...] = acc[...].astype(bf16).T
        g_col[0:1] = column_sums(acc_col[0].T)
        g_col[1:2] = column_sums(acc_col[1].T)


def run_self_backward(x, qkv, near, far, inv, mix, gmix, g_resid, dkv, wt_self, wt_cross):
    images, tags, width = x.shape
    cells = dkv.shape[3]
    half = tags // 2
    sds = jax.ShapeDtypeStruct

    def per(*shape):
        return pl.BlockSpec((1,) + shape, lambda i: (i,) + (0,) * len(shape))

    def one(*shape):
        return pl.BlockSpec(shape, lambda i: (0,) * len(shape))

    return pl.pallas_call(
        self_backward,
        grid=(images,),
        in_specs=[per(tags, width), per(3 * HEADS, HEAD_DIM, tags), per(HEADS, half, half), per(HEADS, tags, half), per(HEADS, tags),
                  per(HEADS, HEAD_DIM, tags), per(HEADS, HEAD_DIM, tags), per(tags, width), per(2 * HEADS, HEAD_DIM, cells),
                  one(3 * width, width), one(3 * width, width)],
        out_specs=[per(tags, width), per(cells, width), one(width, 3 * width), one(8, width)],
        out_shape=[sds((images, tags, width), f32), sds((images, cells, width), f32), sds((width, 3 * width), bf16), sds((8, width), f32)],
        scratch_shapes=[pltpu.VMEM((3 * HEADS, HEAD_DIM, tags), bf16), pltpu.VMEM((3 * width, width), f32), pltpu.VMEM((2, width, 128), f32)],
        compiler_params=pltpu.CompilerParams(vmem_limit_bytes=60 * MIB),
        name="self_backward",
    )(x, qkv, near, far, inv, mix, gmix, g_resid, dkv, wt_self, wt_cross)


def layer(lens, x, mem, gout, w_self, w_cross, w_proj, w_in, w_out, vectors, b_in):
    width = x.shape[2]
    zero = jnp.zeros((width,), f32)
    bias_qkv = jnp.concatenate([vectors[0], zero, vectors[1]])[:, None]
    bias_kv = jnp.concatenate([zero, vectors[4]])[:, None]
    bias_q = vectors[3][:, None]
    qkv, ckv, near, far, inv, mix, wt_self, wt_cross = run_self_forward(lens, x, mem, w_self, w_cross, bias_qkv, bias_kv)
    out, g_resid, gmix, dkv, gw_cross, gw_proj, gw_in, gw_out, g_vec, g_bin = run_middle(
        lens, x, mem, gout, mix, ckv, wt_cross, w_proj, w_in, w_out, bias_q, vectors, b_in)
    g_tags, g_mem, gw_self, g_col = run_self_backward(x, qkv, near, far, inv, mix, gmix, g_resid, dkv, wt_self, wt_cross)
    g_vec = g_vec.at[0:2].set(g_col[0:2])
    return out, g_tags, g_mem, gw_self, gw_cross, gw_proj, gw_in, gw_out, g_vec, g_bin


ALL = slice(None)


class Gathering:
    def __init__(self, dims, me, shard, held, lead, sems):
        self.dims, self.me, self.shard, self.held, self.lead = dims, me, shard, held, lead
        self.local, self.send, self.recv = sems

    def cell(self, *index):
        return self.held.at[(ALL,) * self.lead + index]

    def remote(self, slot, src, dst, peer):
        return pltpu.make_async_remote_copy(
            src_ref=src, dst_ref=dst, send_sem=self.send.at[slot], recv_sem=self.recv.at[slot],
            device_id=device(self.dims, *peer), device_id_type=MESH)

    def keep(self):
        return pltpu.make_async_copy(self.shard, self.cell(*self.me), self.local)

    def first(self):
        a, b, x, c = self.me
        outer = self.dims[0]
        return [self.remote(k - 1, self.shard, self.cell(a, b, x, c), (lax.rem(a + k, outer), b, x, c)) for k in range(1, outer)]

    def along_inner(self, core):
        a, b, x, c = self.me
        outer, inner, _ = self.dims
        piece = self.cell(ALL, b, ALL if core == 0 else x, c)
        return [self.remote(outer - 2 + k, piece, piece, (a, lax.rem(b + k, inner), x, c)) for k in range(1, inner)]

    def along_across(self, core):
        a, b, x, c = self.me
        outer, inner, across = self.dims
        piece = self.cell(ALL, b if core == 0 else ALL, x, c)
        return [self.remote(outer + inner - 3 + k, piece, piece, (a, b, lax.rem(x + k, across), c)) for k in range(1, across)]

    def second(self, core):
        return self.along_across(core) if core == 0 else self.along_inner(core)

    def third(self, core):
        return self.along_inner(core) if core == 0 else self.along_across(core)

    def handed(self, core, holder):
        a, b, x, c = self.me
        outer, inner, across = self.dims
        base = outer + inner + across - 3

        def piece(slot, row, column):
            ref = self.cell(ALL, row, column, holder)
            return self.remote(base + slot, ref, ref, (a, b, x, 1 - c))

        own = [piece(0, b, x)]
        by_inner = [piece(k, lax.rem(b + k, inner), ALL if core == 0 else x) for k in range(1, inner)]
        by_across = [piece(inner - 1 + k, b if core == 0 else ALL, lax.rem(x + k, across)) for k in range(1, across)]
        return (own, by_across, by_inner) if core == 0 else (own, by_inner, by_across)

    def begin(self):
        self.keep().start()
        for copy in self.first():
            copy.start()

    def each_core(self, act):
        for core in (0, 1):
            pl.when(self.me[3] == core)(functools.partial(act, core))

    def advance(self, stage):
        def act(core):
            if stage == 1:
                self.keep().wait()
            for copy in (self.first(), self.second(core), self.third(core))[stage - 1]:
                copy.wait_recv()
            following = (self.second(core), self.third(core), [])[stage - 1]
            for copy in following + self.handed(core, self.me[3])[stage - 1]:
                copy.start()
        self.each_core(act)

    def finish(self):
        def act(core):
            for group in self.handed(1 - core, 1 - self.me[3]):
                for copy in group:
                    copy.wait_recv()
        self.each_core(act)

    def drain(self):
        def act(core):
            for copy in self.first() + self.second(core) + self.third(core) + sum(self.handed(core, self.me[3]), []):
                copy.wait_send()
        self.each_core(act)


def gather_slots(dims):
    outer, inner, across = dims
    return outer + 2 * (inner + across) - 4


def spread(held, row_lanes, width, rows):
    devices = held.shape[0] // 16
    lane = lax.broadcasted_iota(jnp.int32, (128, width), 0)
    at = lax.broadcasted_iota(jnp.int32, (128, width), 1)
    pick = jnp.where((lax.rem(at, row_lanes) == lane), 1.0, 0.0).astype(bf16)
    wide = dot(held, pick, 1, 0)
    owner = lax.broadcasted_iota(jnp.int32, (devices * 16, width), 0) // 16
    at = lax.broadcasted_iota(jnp.int32, (devices * 16, width), 1)
    wide = jnp.where(at // row_lanes == owner, wide, 0.0)
    return jnp.sum(wide.reshape(devices, 16, width), 0)


def opening(dims, lens, x_ref, mem_ref, b_ref, g_ref, h_ref, s_cross, s_self, s_proj, s_in, s_out,
            qkv_ref, ckv_ref, near_ref, far_ref, inv_ref, mix_ref, wt_self, wt_cross, vec_ref, bin_ref, o_proj, o_in, o_out,
            small, small_low, h_small, h_kv, h_self, h_q, cols, local, send, recv):
    width = x_ref.shape[2]
    tags = x_ref.shape[1]
    half = tags // 2
    step = pl.program_id(0)
    images = pl.num_programs(0) // 2
    me = place(dims)
    s_kv, s_q = s_cross.at[:, width:], s_cross.at[:, :width]
    pairs = ((small_low, h_small, 0), (s_kv, h_kv, 0), (s_self, h_self, 0), (s_q, h_q, 0), (s_proj, o_proj, 1), (s_in, o_in, 0), (s_out, o_out, 0))
    gs = [Gathering(dims, me, shard, held, lead, (local.at[k], send.at[k], recv.at[k])) for k, (shard, held, lead) in enumerate(pairs)]
    g_small, g_kv, g_self, g_q, g_proj, g_in, g_out = gs

    @pl.when(step == 0)
    def _():
        small[...] = jnp.zeros_like(small)
        small[0:10, : b_ref.shape[1]] = b_ref[...].astype(f32)
        small[10:13, : g_ref.shape[1]] = g_ref[...].astype(f32)
        small[13:14, : h_ref.shape[1]] = h_ref[...].astype(f32)
        small_low[...] = small[...].astype(bf16)
        greet(dims, me)
        g_small.begin()
        g_kv.begin()
        g_self.begin()
        g_small.advance(1)
        g_kv.advance(1)
        g_q.begin()
        g_proj.begin()
        g_small.advance(2)
        g_kv.advance(2)
        g_self.advance(1)
        g_small.advance(3)
        g_kv.advance(3)
        g_in.begin()
        g_self.advance(2)
        g_out.begin()
        g_small.finish()
        vectors = spread(h_small[...].reshape(-1, 128), b_ref.shape[1], width, 16)
        vec_ref[...] = vectors
        bin_ref[...] = spread(h_small[...].reshape(-1, 128), h_ref.shape[1], bin_ref.shape[1], 16)[13:14]
        cols[...] = vectors.T
        g_kv.finish()
        wt_cross[width:] = h_kv[...].reshape(width, 2 * width).T

    @pl.when(step < images)
    def _():
        kv = dot(wt_cross[width:], mem_ref[0], 1, 1)
        heads = ckv_ref.shape[1] // 2
        ckv_ref[0, :heads] = kv[:width].astype(bf16).reshape(heads, HEAD_DIM, -1)
        ckv_ref[0, heads:] = (kv[width:] + cols[:, 4:5]).astype(bf16).reshape(heads, HEAD_DIM, -1)

    @pl.when(step == 0)
    def _():
        g_self.advance(3)
        g_q.advance(1)
        g_proj.advance(1)

    @pl.when(step == 1)
    def _():
        g_q.advance(2)
        g_proj.advance(2)
        g_in.advance(1)

    @pl.when(step == 2)
    def _():
        g_q.advance(3)
        g_proj.advance(3)
        g_in.advance(2)
        g_out.advance(1)

    @pl.when(step == images)
    def _():
        g_self.finish()
        wt_self[...] = h_self[...].reshape(width, 3 * width).T

    @pl.when(step >= images)
    def _():
        qkv = dot(wt_self[...], x_ref[0], 1, 1)
        qkv_ref[0, :HEADS] = ((qkv[:width] + cols[:, 0:1]).astype(bf16) * bf16(HEAD_DIM ** -0.5)).reshape(HEADS, HEAD_DIM, tags)
        qkv_ref[0, HEADS : 2 * HEADS] = qkv[width : 2 * width].astype(bf16).reshape(HEADS, HEAD_DIM, tags)
        qkv_ref[0, 2 * HEADS :] = (qkv[2 * width :] + cols[:, 1:2]).astype(bf16).reshape(HEADS, HEAD_DIM, tags)

    @pl.when(step == images)
    def _():
        g_in.advance(3)
        g_out.advance(2)

    def head(h, _):
        qt, kt, vt = qkv_ref[0, h], qkv_ref[0, HEADS + h], with_ones(qkv_ref[0, 2 * HEADS + h])
        last = lens[jnp.maximum(step - images, 0)] - 1

        def part(keys, first, out):
            s = dot(kt[:, :keys], qt[:, first : first + half], 0, 0)
            key_at = lax.broadcasted_iota(jnp.int32, (keys, half), 0)
            query_at = lax.broadcasted_iota(jnp.int32, (1, half), 1) + first
            s = jnp.where(key_at <= jnp.minimum(query_at, last), s, MASKED)
            e = jnp.exp(s - jnp.max(s, 0, keepdims=True)).astype(bf16)
            out[0, h] = e
            mixed = dot(vt[:, :keys], e, 1, 0)
            inv = 1.0 / mixed[HEAD_DIM : HEAD_DIM + 1]
            inv_ref[0, pl.ds(h, 1), first : first + half] = inv
            mix_ref[0, h, :, first : first + half] = (mixed[:HEAD_DIM] * inv).astype(bf16)

        part(half, 0, near_ref)
        part(tags, half, far_ref)
        return 0

    @pl.when(step >= images)
    def _():
        lax.fori_loop(0, HEADS, head, 0)

    @pl.when(step == images)
    def _():
        g_out.advance(3)

    @pl.when(step == 2 * images - 1)
    def _():
        g_q.finish()
        wt_cross[:width] = h_q[...].reshape(width, width).T
        for g in (g_proj, g_in, g_out):
            g.finish()
        for g in gs:
            g.drain()


def run_opening(dims, lens, x, mem, biases, gains, b_in, shards):
    images, tags, width = x.shape
    cells = mem.shape[1]
    half = tags // 2
    hidden = b_in.shape[1] * dims[0] * dims[1] * dims[2] * 2
    sds = jax.ShapeDtypeStruct

    def early(*shape):
        return pl.BlockSpec((1,) + shape, lambda i: (jnp.minimum(i, images - 1),) + (0,) * len(shape))

    def late(*shape):
        return pl.BlockSpec((1,) + shape, lambda i: (jnp.maximum(i - images, 0),) + (0,) * len(shape))

    def one(*shape):
        return pl.BlockSpec(shape, lambda i: (0,) * len(shape))

    def held(shard, lead):
        return shard.shape[:lead] + dims + (2,) + shard.shape[lead:]

    s_cross, s_self, s_proj, s_in, s_out = shards
    rows = s_cross.shape[0]
    cell = dims + (2, rows)
    anywhere = pl.BlockSpec(memory_space=pl.ANY)
    n = len(shards) + 2
    slots = gather_slots(dims)
    return pl.pallas_call(
        functools.partial(opening, dims),
        grid=(2 * images,),
        in_specs=[pl.BlockSpec(memory_space=pltpu.SMEM), late(tags, width), early(cells, width), one(*biases.shape), one(*gains.shape), one(*b_in.shape)]
        + [anywhere] * len(shards),
        out_specs=[
            late(3 * HEADS, HEAD_DIM, tags), early(2 * HEADS, HEAD_DIM, cells), late(HEADS, half, half), late(HEADS, tags, half),
            late(HEADS, tags), late(HEADS, HEAD_DIM, tags), one(3 * width, width), one(3 * width, width), one(16, width), one(1, hidden),
            anywhere, anywhere, anywhere,
        ],
        out_shape=[
            sds((images, 3 * HEADS, HEAD_DIM, tags), bf16),
            sds((images, 2 * HEADS, HEAD_DIM, cells), bf16),
            sds((images, HEADS, half, half), bf16),
            sds((images, HEADS, tags, half), bf16),
            sds((images, HEADS, tags), f32),
            sds((images, HEADS, HEAD_DIM, tags), bf16),
            sds((3 * width, width), bf16),
            sds((3 * width, width), bf16),
            sds((16, width), f32),
            sds((1, hidden), f32),
            sds(held(s_proj, 1), bf16),
            sds(held(s_in, 0), bf16),
            sds(held(s_out, 0), bf16),
        ],
        scratch_shapes=[
            pltpu.VMEM((16, 128), f32), pltpu.VMEM((16, 128), bf16), pltpu.VMEM(dims + (2, 16, 128), bf16),
            pltpu.VMEM(cell + (2 * width,), bf16), pltpu.VMEM(cell + (3 * width,), bf16), pltpu.VMEM(cell + (width,), bf16),
            pltpu.VMEM((width, 16), f32),
            pltpu.SemaphoreType.DMA((n,)), pltpu.SemaphoreType.DMA((n, slots)), pltpu.SemaphoreType.DMA((n, slots)),
        ],
        compiler_params=pltpu.CompilerParams(collective_id=0, has_side_effects=True, vmem_limit_bytes=58 * MIB),
        name="opening",
    )(lens, x, mem, biases, gains, b_in, *shards)


AXES = ("wide", "narrow")
LEADS = (0, 0, 1, 0, 0, 0)


def fold(block, rows, columns):
    if rows % 16 == 0:
        return block
    return block.reshape(block.shape[:-2] + (16, rows * columns // 16))


def per_device(dims, tag_states, image_memory, tag_lengths, w_self, w_cross, w_proj, w_in, b_in, w_out, ln_gains, biases, out_grad):
    cells = dims + (2,)
    fused = w_self.shape[0] % 16 == 0
    devices = dims[0] * dims[1] * dims[2] * 2
    width = tag_states.shape[2]
    lanes, hidden_lanes = biases.shape[1], b_in.shape[0]
    if fused:
        qkv, ckv, near, far, inv, mix, wt_self, wt_cross, vectors, hidden_bias, full_proj, full_in, full_out = run_opening(
            dims, tag_lengths, tag_states, image_memory, biases, ln_gains, b_in[None], (w_cross, w_self, w_proj, w_in, w_out))
        full_proj, full_in, full_out = full_proj.reshape(2, width, width), full_in.reshape(width, -1), full_out.reshape(-1, width)
        layer_out, g_resid, gmix, dkv, g_cross, g_proj, g_in, g_out, g_vec, g_bin = run_middle(
            tag_lengths, tag_states, image_memory, out_grad, mix, ckv, wt_cross, full_proj, full_in, full_out, vectors[3][:, None], vectors, hidden_bias)
        grad_tags, grad_memory, g_self, g_col = run_self_backward(tag_states, qkv, near, far, inv, mix, gmix, g_resid, dkv, wt_self, wt_cross)
        g_vec = g_vec.at[0:2].set(g_col[0:2])
    else:
        small = jnp.concatenate(
            [
                jnp.pad(jnp.concatenate([biases, ln_gains]), ((0, 0), (0, 128 - lanes))),
                jnp.pad(b_in[None], ((0, 2), (0, 128 - hidden_lanes))),
            ]
        )
        shards = (w_self, w_cross, w_proj, w_in, w_out, small)
        gathered = gather(dims, [fold(s, *s.shape[-2:]) for s in shards], LEADS)

        def whole(held, shard):
            lead = shard.shape[:-2]
            rows, columns = shard.shape[-2:]
            return held.reshape(lead + (devices * rows, columns))

        full_self, full_cross, full_proj, full_in, full_out, full_small = [whole(h, s) for h, s in zip(gathered, shards)]
        by_device = full_small.reshape(devices, 16, 128)
        vectors = by_device[:, :, :lanes].transpose(1, 0, 2).reshape(16, width).astype(f32)
        hidden_bias = by_device[:, 13, :hidden_lanes].reshape(1, -1).astype(f32)
        layer_out, grad_tags, grad_memory, g_self, g_cross, g_proj, g_in, g_out, g_vec, g_bin = layer(
            tag_lengths, tag_states, image_memory, out_grad, full_self, full_cross, full_proj, full_in, full_out, vectors, hidden_bias)
    g_small = jnp.pad(g_vec.reshape(16, devices, lanes).transpose(1, 0, 2)[:, :13], ((0, 0), (0, 0), (0, 128 - lanes)))
    g_hidden = jnp.pad(g_bin.reshape(devices, 1, hidden_lanes), ((0, 0), (0, 2), (0, 128 - hidden_lanes)))
    g_small = jnp.concatenate([g_small, g_hidden], 1).astype(bf16).reshape(devices * 16, 128)

    def parts(grad, shard):
        lead = shard.shape[:-2]
        rows, columns = shard.shape[-2:]
        return fold(grad.reshape(lead + cells + (rows, columns)), rows, columns)

    shards = (w_self, w_cross, w_proj, w_in, w_out, jax.ShapeDtypeStruct((16, 128), bf16))
    shares = scatter(dims, [parts(g, s) for g, s in zip((g_self, g_cross, g_proj, g_in, g_out, g_small), shards)], LEADS)
    s_self, s_cross, s_proj, s_in, s_out, s_small = [v.reshape(s.shape) for v, s in zip(shares, shards)]
    return (layer_out, grad_tags, grad_memory, s_self, s_cross, s_proj, s_in, s_small[13, :hidden_lanes], s_out,
            s_small[10:13, :lanes], s_small[:10, :lanes])


def solution(mesh):
    dims = grid_of(mesh.shape["wide"], mesh.shape["narrow"])
    rows, matrix, stack, columns = P(AXES, None, None), P(AXES, None), P(None, AXES, None), P(None, AXES)
    return jax.shard_map(
        functools.partial(per_device, dims),
        mesh=mesh,
        in_specs=(rows, rows, P(AXES), matrix, matrix, stack, matrix, P(AXES), matrix, columns, columns, rows),
        out_specs=(rows, rows, rows, matrix, matrix, stack, matrix, P(AXES), matrix, columns, columns),
        check_vma=False,
    )
```

```python
import functools

import jax
import jax.numpy as jnp
from jax import lax
from jax.experimental import pallas as pl
from jax.experimental.pallas import tpu as pltpu
from jax.sharding import PartitionSpec as P


MESH = pl.DeviceIdType.MESH
f32, bf16 = jnp.float32, jnp.bfloat16


def grid_of(mesh_wide, mesh_narrow):
    outer = 4
    return outer, mesh_wide // outer, mesh_narrow // 2


def place(dims):
    outer, inner, across = dims
    wide, narrow = lax.axis_index("wide"), lax.axis_index("narrow")
    return wide // inner, lax.rem(wide, inner), narrow // 2, lax.rem(narrow, 2)


def device(dims, a, b, x, c):
    return {"wide": a * dims[1] + b, "narrow": x * 2 + c}


def greet(dims, me):
    a, b, x, c = me
    outer, inner, across = dims
    barrier = pltpu.get_barrier_semaphore()
    peers = [(lax.rem(a + k, outer), b, x, c) for k in range(1, outer)]
    peers += [(a, lax.rem(b + k, inner), x, c) for k in range(1, inner)]
    peers += [(a, b, lax.rem(x + k, across), c) for k in range(1, across)]
    peers += [(a, b, x, 1 - c)]
    for peer in peers:
        pl.semaphore_signal(barrier, inc=1, device_id=device(dims, *peer), device_id_type=MESH)
    pl.semaphore_wait(barrier, len(peers))


ALL = slice(None)


def gather_kernel(dims, leads, *refs):
    count = len(leads)
    shards, outs = refs[:count], refs[count : 2 * count]
    local_sem, send_sem, recv_sem = refs[2 * count :]
    outer, inner, across = dims
    me = place(dims)
    a, b, x, c = me
    greet(dims, me)

    def cell(ref, lead, *index):
        return ref.at[(ALL,) * lead + index]

    def remote(g, slot, src, dst, peer):
        return pltpu.make_async_remote_copy(
            src_ref=src, dst_ref=dst, send_sem=send_sem.at[g, slot], recv_sem=recv_sem.at[g, slot],
            device_id=device(dims, *peer), device_id_type=MESH)

    n_in, n_ac = inner - 1, across - 1

    def first(g):
        lead = leads[g]
        mine = cell(outs[g], lead, a, b, x, c)
        return [remote(g, k - 1, shards[g], mine, (lax.rem(a + k, outer), b, x, c)) for k in range(1, outer)]

    def keep(g):
        return pltpu.make_async_copy(shards[g], cell(outs[g], leads[g], a, b, x, c), local_sem.at[g])

    base = outer - 1

    def via_inner(g, core):
        lead = leads[g]
        column = ALL if core == 0 else x
        piece = cell(outs[g], lead, ALL, b, column, c)
        return [remote(g, base + k - 1, piece, piece, (a, lax.rem(b + k, inner), x, c)) for k in range(1, inner)]

    def via_across(g, core):
        lead = leads[g]
        row = b if core == 0 else ALL
        piece = cell(outs[g], lead, ALL, row, x, c)
        return [remote(g, base + n_in + k - 1, piece, piece, (a, b, lax.rem(x + k, across), c)) for k in range(1, across)]

    share = base + n_in + n_ac

    def to_partner(g, core, holder):
        lead = leads[g]
        def piece(slot, row, column):
            ref = cell(outs[g], lead, ALL, row, column, holder)
            return remote(g, share + slot, ref, ref, (a, b, x, 1 - c))
        own = [piece(0, b, x)]
        by_inner = [piece(1 + k - 1, lax.rem(b + k, inner), ALL if core == 0 else x) for k in range(1, inner)]
        by_across = [piece(1 + n_in + k - 1, b if core == 0 else ALL, lax.rem(x + k, across)) for k in range(1, across)]
        return (own, by_across, by_inner) if core == 0 else (own, by_inner, by_across)

    def start(copies):
        for copy in copies:
            copy.start()

    def arrived(copies):
        for copy in copies:
            copy.wait_recv()

    for g in range(count):
        keep(g).start()
        start(first(g))

    def body(core):
        second, third = (via_across, via_inner) if core == 0 else (via_inner, via_across)
        for step in range(count + 2):
            g = step
            if g < count:
                keep(g).wait()
                arrived(first(g))
                start(second(g, core))
                start(to_partner(g, core, c)[0])
            g = step - 1
            if 0 <= g < count:
                arrived(second(g, core))
                start(third(g, core))
                start(to_partner(g, core, c)[1])
            g = step - 2
            if 0 <= g < count:
                arrived(third(g, core))
                start(to_partner(g, core, c)[2])
        for g in range(count):
            for group in to_partner(g, 1 - core, 1 - c):
                arrived(group)
        for g in range(count):
            for copy in first(g) + second(g, core) + third(g, core):
                copy.wait_send()
            for group in to_partner(g, core, c):
                for copy in group:
                    copy.wait_send()

    @pl.when(c == 0)
    def _():
        body(0)

    @pl.when(c == 1)
    def _():
        body(1)


def gather(dims, shards, leads):
    outer, inner, across = dims
    def shape(s, lead):
        return jax.ShapeDtypeStruct(s.shape[:lead] + (outer, inner, across, 2) + s.shape[lead:], s.dtype)
    slots = (outer - 1) + 2 * (inner - 1) + 2 * (across - 1) + 1
    n = len(shards)
    return pl.pallas_call(
        functools.partial(gather_kernel, dims, leads),
        out_shape=[shape(s, l) for s, l in zip(shards, leads)],
        in_specs=[pl.BlockSpec(memory_space=pl.ANY)] * n,
        out_specs=[pl.BlockSpec(memory_space=pl.ANY)] * n,
        scratch_shapes=[pltpu.SemaphoreType.DMA((n,)), pltpu.SemaphoreType.DMA((n, slots)), pltpu.SemaphoreType.DMA((n, slots))],
        compiler_params=pltpu.CompilerParams(collective_id=0, has_side_effects=True),
        name="gather_weights",
    )(*shards)


def scatter_kernel(dims, leads, *refs):
    count = len(leads)
    grads, outs = refs[:count], refs[count : 2 * count]
    rest = refs[2 * count :]
    r0, r1i, r1a, r2a, r2i, r3 = (rest[k * count : (k + 1) * count] for k in range(6))
    send_sem, recv_sem = rest[6 * count :]
    outer, inner, across = dims
    me = place(dims)
    a, b, x, c = me
    greet(dims, me)
    n_in, n_ac = inner - 1, across - 1

    def cell(ref, lead, *index):
        return ref.at[(ALL,) * lead + index]

    def remote(g, slot, src, dst, peer):
        return pltpu.make_async_remote_copy(
            src_ref=src, dst_ref=dst, send_sem=send_sem.at[g, slot], recv_sem=recv_sem.at[g, slot],
            device_id=device(dims, *peer), device_id_type=MESH)

    def swap(g):
        return [remote(g, 0, cell(grads[g], leads[g], ALL, ALL, ALL, 1 - c), r0[g], (a, b, x, 1 - c))]

    def via_inner(g, core):
        lead = leads[g]
        res = []
        for k in range(1, inner):
            peer = lax.rem(b + k, inner)
            if core == 0:
                src, dst = cell(r0[g], lead, ALL, peer), r1i[g].at[k - 1]
            else:
                src, dst = cell(r1a[g].at[0], lead, ALL, peer), r2i[g].at[k - 1]
            res.append(remote(g, k, src, dst, (a, peer, x, c)))
        return res

    def via_across(g, core):
        lead = leads[g]
        res = []
        for k in range(1, across):
            peer = lax.rem(x + k, across)
            if core == 1:
                src, dst = cell(r0[g], lead, ALL, ALL, peer), r1a[g].at[k - 1]
            else:
                src, dst = cell(r1i[g].at[0], lead, ALL, peer), r2a[g].at[k - 1]
            res.append(remote(g, 1 + n_in + k - 1, src, dst, (a, b, peer, c)))
        return res

    def last(g, core):
        lead = leads[g]
        held = (r2a if core == 0 else r2i)[g].at[0]
        res = []
        for k in range(1, outer):
            peer = lax.rem(a + k, outer)
            res.append(remote(g, 1 + n_in + n_ac + k - 1, cell(held, lead, peer), r3[g].at[k - 1], (peer, b, x, c)))
        return res

    def start(copies):
        for copy in copies:
            copy.start()

    def arrived(copies):
        for copy in copies:
            copy.wait_recv()

    def up(v):
        return v.astype(f32)

    for g in range(count):
        start(swap(g))

    def body(core):
        second, third = (via_inner, via_across) if core == 0 else (via_across, via_inner)
        def at(lead, *index):
            return (ALL,) * lead + index
        for step in range(count + 3):
            g = step
            if g < count:
                arrived(swap(g))
                lead = leads[g]
                r0[g][...] = (up(grads[g][at(lead, ALL, ALL, ALL, c)]) + up(r0[g][...])).astype(bf16)
                start(second(g, core))
            g = step - 1
            if 0 <= g < count:
                arrived(second(g, core))
                lead = leads[g]
                if core == 0:
                    total = up(r0[g][at(lead, ALL, b)])
                    held = r1i[g]
                else:
                    total = up(r0[g][at(lead, ALL, ALL, x)])
                    held = r1a[g]
                for k in range(held.shape[0]):
                    total = total + up(held[k])
                held[0] = total.astype(bf16)
                start(third(g, core))
            g = step - 2
            if 0 <= g < count:
                arrived(third(g, core))
                lead = leads[g]
                if core == 0:
                    total = up(r1i[g][(0,) + at(lead, ALL, x)])
                    held = r2a[g]
                else:
                    total = up(r1a[g][(0,) + at(lead, ALL, b)])
                    held = r2i[g]
                for k in range(held.shape[0]):
                    total = total + up(held[k])
                held[0] = total.astype(bf16)
                start(last(g, core))
            g = step - 3
            if 0 <= g < count:
                arrived(last(g, core))
                lead = leads[g]
                held = (r2a if core == 0 else r2i)[g]
                total = up(held[(0,) + at(lead, a)])
                for k in range(outer - 1):
                    total = total + up(r3[g][k])
                outs[g][...] = total
        for g in range(count):
            for copy in swap(g) + second(g, core) + third(g, core) + last(g, core):
                copy.wait_send()

    @pl.when(c == 0)
    def _():
        body(0)

    @pl.when(c == 1)
    def _():
        body(1)


def scatter(dims, grads, leads):
    outer, inner, across = dims
    n = len(grads)
    outs, shapes = [], [[] for _ in range(6)]
    for g, lead in zip(grads, leads):
        head, tail = g.shape[:lead], g.shape[lead + 4 :]
        outs.append(jax.ShapeDtypeStruct(head + tail, f32))
        shapes[0].append(head + (outer, inner, across) + tail)
        shapes[1].append((inner - 1,) + head + (outer, across) + tail)
        shapes[2].append((across - 1,) + head + (outer, inner) + tail)
        shapes[3].append((across - 1,) + head + (outer,) + tail)
        shapes[4].append((inner - 1,) + head + (outer,) + tail)
        shapes[5].append((outer - 1,) + head + tail)
    slots = 1 + (inner - 1) + (across - 1) + (outer - 1)
    return pl.pallas_call(
        functools.partial(scatter_kernel, dims, leads),
        out_shape=outs,
        in_specs=[pl.BlockSpec(memory_space=pltpu.VMEM)] * n,
        out_specs=[pl.BlockSpec(memory_space=pltpu.VMEM)] * n,
        scratch_shapes=[pltpu.VMEM(s, bf16) for group in shapes for s in group]
        + [pltpu.SemaphoreType.DMA((n, slots)), pltpu.SemaphoreType.DMA((n, slots))],
        compiler_params=pltpu.CompilerParams(collective_id=1, has_side_effects=True, vmem_limit_bytes=48 * 2**20),
        name="scatter_grads",
    )(*grads)

HEADS, HEAD_DIM = 8, 64
EPS = 1e-5
MASKED = -1e9
TAME = 30.0
MIB = 2**20


def dot(left, right, left_dim, right_dim):
    return lax.dot_general(left, right, (((left_dim,), (right_dim,)), ((), ())), preferred_element_type=f32)


def full(shape):
    return pl.BlockSpec(shape, lambda i: (0,) * len(shape))


def image(shape):
    return pl.BlockSpec((1,) + shape, lambda i: (i,) + (0,) * len(shape))


def with_ones(rows):
    return jnp.concatenate([rows, jnp.ones((16, rows.shape[1]), bf16)], 0)


def with_delta(rows, delta):
    high = delta.astype(bf16).astype(f32)
    low = delta - high
    at = lax.broadcasted_iota(jnp.int32, (16, rows.shape[1]), 0)
    extra = jnp.where(at == 0, -high, jnp.where(at == 1, -low, 0.0))
    return jnp.concatenate([rows, extra.astype(bf16)], 0)


def self_forward(lens, x_ref, mem_ref, w_self, w_cross, bias_qkv, bias_kv,
                 qkv_ref, ckv_ref, near_ref, far_ref, inv_ref, mix_ref, wt_self, wt_cross):
    width = x_ref.shape[2]
    tags = x_ref.shape[1]
    half = tags // 2
    i = pl.program_id(0)

    @pl.when(i == 0)
    def _():
        wt_self[...] = w_self[...].T
        wt_cross[...] = w_cross[...].T

    ckv = dot(wt_cross[width:], mem_ref[0], 1, 1) + bias_kv[...]
    ckv_ref[0] = ckv.astype(bf16).reshape(ckv_ref.shape[1:])
    qkv = dot(wt_self[...], x_ref[0], 1, 1) + bias_qkv[...]
    q = qkv[:width].astype(bf16) * bf16(HEAD_DIM ** -0.5)
    qkv_ref[0, :HEADS] = q.reshape(HEADS, HEAD_DIM, tags)
    qkv_ref[0, HEADS:] = qkv[width:].astype(bf16).reshape(2 * HEADS, HEAD_DIM, tags)
    last = lens[i] - 1

    def head(h, _):
        qt, kt, vt = qkv_ref[0, h], qkv_ref[0, HEADS + h], with_ones(qkv_ref[0, 2 * HEADS + h])

        def part(keys, first, out):
            s = dot(kt[:, :keys], qt[:, first : first + half], 0, 0)
            key_at = lax.broadcasted_iota(jnp.int32, (keys, half), 0)
            query_at = lax.broadcasted_iota(jnp.int32, (1, half), 1) + first
            s = jnp.where(key_at <= jnp.minimum(query_at, last), s, MASKED)
            e = jnp.exp(s - jnp.max(s, 0, keepdims=True)).astype(bf16)
            out[0, h] = e
            mixed = dot(vt[:, :keys], e, 1, 0)
            inv = 1.0 / mixed[HEAD_DIM : HEAD_DIM + 1]
            inv_ref[0, pl.ds(h, 1), first : first + half] = inv
            mix_ref[0, h, :, first : first + half] = (mixed[:HEAD_DIM] * inv).astype(bf16)

        part(half, 0, near_ref)
        part(tags, half, far_ref)
        return 0

    lax.fori_loop(0, HEADS, head, 0)


def run_self_forward(lens, x, mem, w_self, w_cross, bias_qkv, bias_kv):
    images, tags, width = x.shape
    cells = mem.shape[1]
    half = tags // 2
    sds = jax.ShapeDtypeStruct
    return pl.pallas_call(
        self_forward,
        grid_spec=pltpu.PrefetchScalarGridSpec(
            num_scalar_prefetch=1,
            grid=(images,),
            in_specs=[pl.BlockSpec((1, tags, width), lambda i, n: (i, 0, 0)), pl.BlockSpec((1, cells, width), lambda i, n: (i, 0, 0))]
            + [pl.BlockSpec(v.shape, lambda i, n: (0, 0)) for v in (w_self, w_cross, bias_qkv, bias_kv)],
            out_specs=[
                pl.BlockSpec((1, 3 * HEADS, HEAD_DIM, tags), lambda i, n: (i, 0, 0, 0)),
                pl.BlockSpec((1, 2 * HEADS, HEAD_DIM, cells), lambda i, n: (i, 0, 0, 0)),
                pl.BlockSpec((1, HEADS, half, half), lambda i, n: (i, 0, 0, 0)),
                pl.BlockSpec((1, HEADS, tags, half), lambda i, n: (i, 0, 0, 0)),
                pl.BlockSpec((1, HEADS, tags), lambda i, n: (i, 0, 0)),
                pl.BlockSpec((1, HEADS, HEAD_DIM, tags), lambda i, n: (i, 0, 0, 0)),
                pl.BlockSpec((3 * width, width), lambda i, n: (0, 0)),
                pl.BlockSpec((3 * width, width), lambda i, n: (0, 0)),
            ],
        ),
        out_shape=[
            sds((images, 3 * HEADS, HEAD_DIM, tags), bf16),
            sds((images, 2 * HEADS, HEAD_DIM, cells), bf16),
            sds((images, HEADS, half, half), bf16),
            sds((images, HEADS, tags, half), bf16),
            sds((images, HEADS, tags), f32),
            sds((images, HEADS, HEAD_DIM, tags), bf16),
            sds((3 * width, width), bf16),
            sds((3 * width, width), bf16),
        ],
        compiler_params=pltpu.CompilerParams(vmem_limit_bytes=58 * MIB),
        name="self_forward",
    )(lens, x, mem, w_self, w_cross, bias_qkv, bias_kv)


def norm(resid):
    centred = resid - jnp.mean(resid, -1, keepdims=True)
    scale = lax.rsqrt(jnp.mean(centred * centred, -1, keepdims=True) + EPS)
    return centred * scale, scale


def norm_back(grad, normed, scale, gain):
    scaled = grad * gain
    mean_one = jnp.mean(scaled, -1, keepdims=True)
    mean_two = jnp.mean(scaled * normed, -1, keepdims=True)
    return scale * (scaled - mean_one - normed * mean_two)


def column_sums(rows):
    return jnp.sum(rows, 0, keepdims=True)


def lane_groups(rows):
    total = rows[:, :128]
    for k in range(1, rows.shape[1] // 128):
        total = total + rows[:, 128 * k : 128 * (k + 1)]
    return total


def cross_back(h, e, keys, values, queries, grad, mixed, inv):
    grad = grad.astype(f32)
    delta = jnp.sum(grad * mixed.astype(f32), 0, keepdims=True) * inv
    grad = (grad * inv).astype(bf16)
    dp = dot(with_ones(values), with_delta(grad, delta), 0, 0)
    ds = e * dp.astype(bf16)
    dv = dot(grad, e, 1, 1).astype(bf16)
    dk = dot(queries, ds, 1, 1).astype(bf16)
    dq = (dot(keys, ds, 1, 0) * HEAD_DIM ** -0.5).astype(bf16)
    return dq, dk, dv


def memory_lanes(rows):
    cells = rows.shape[1]
    body = cells // 128 * 128
    total = lane_groups(rows[:, :body])
    if body < cells:
        total = total + jnp.concatenate([rows[:, body:], jnp.zeros((rows.shape[0], 128 - cells + body), f32)], 1)
    return total


def middle(held_back, lens, x_ref, mem_ref, gout_ref, mix_one, ckv_ref, wt_cross, w_proj, w_in, w_out, vectors, b_in,
           out_ref, g_resid, g_mix, g_mem, gw_cross, gw_proj, gw_in, gw_out, g_vec, g_bin, *rest):
    if held_back:
        o_scale, o_e, o_q, o_inv, o_mix, o_gmix, o_one, o_two, o_cross, o_proj = rest[:10]
        gone = rest[-1]
        rest = rest[10:-1]
    middle_body(held_back and (o_scale, o_e, o_q, o_inv, o_mix, o_gmix, o_one, o_two, o_cross, o_proj, gone),
                lens, x_ref, mem_ref, gout_ref, mix_one, ckv_ref, wt_cross, w_proj, w_in, w_out, vectors, b_in,
                out_ref, g_resid, g_mix, g_mem, gw_cross, gw_proj, gw_in, gw_out, g_vec, g_bin, *rest)


def middle_body(held_back, lens, x_ref, mem_ref, gout_ref, mix_one, ckv_ref, wt_cross, w_proj, w_in, w_out, vectors, b_in,
           out_ref, g_resid, g_mix, g_mem, gw_cross, gw_proj, gw_in, gw_out, g_vec, g_bin,
           dkv_ref, cols,
           e_ref, q_ref, inv_ref, mix_two, gmix_two, dq_ref, acc_cross, acc_proj, acc_in, acc_out, acc_vec, acc_bin, acc_col,
           n_one, n_two):
    tags, width = x_ref.shape[1:]
    cells = mem_ref.shape[1]
    i = pl.program_id(0)
    count = pl.num_programs(0)

    @pl.when(i == 0)
    def _():
        for ref in (acc_cross, acc_proj, acc_in, acc_out, acc_vec, acc_bin, acc_col):
            ref[...] = jnp.zeros_like(ref)
        cols[...] = vectors[...].T

    def vec(k):
        return vectors[k : k + 1, :]

    def add(k, value):
        acc_vec[k : k + 1, :] += value

    if held_back:
        scale_out, *places, gone = held_back
        sources = (e_ref, q_ref, inv_ref, mix_two, gmix_two, n_one, n_two, acc_cross, acc_proj.at[0])
        copies = [pltpu.make_async_copy(src, dst, gone.at[k]) for k, (src, dst) in enumerate(zip(sources, places))]

    def leave(*numbers):
        if held_back:
            @pl.when(i == count - 1)
            def _():
                for number in numbers:
                    copies[number].start()

    leave(7, 8)
    mix_one_t = mix_one[0].reshape(width, tags)
    resid = x_ref[0].astype(f32) + dot(mix_one_t, w_proj[0], 0, 0) + vec(2)
    normed, scale_one = norm(resid)
    n_one[...] = normed
    one = normed * vec(10) + vec(6)
    one_low = one.astype(bf16)
    cq = (dot(wt_cross[:width], one_low, 1, 1) + cols[:, 3:4]).astype(bf16) * bf16(HEAD_DIM ** -0.5)
    q_ref[...] = cq.reshape(q_ref.shape)
    leave(1, 5)

    keys = ckv_ref[0, :HEADS].astype(f32)
    queries = q_ref[...].astype(f32)
    bound = jnp.max(jnp.sum(keys * keys, 1)) * jnp.max(jnp.sum(queries * queries, 1))
    tame = bound < TAME * TAME

    def forward(shifted, h, _):
        s = dot(ckv_ref[0, h], q_ref[h], 0, 0)
        if shifted:
            s = s - jnp.max(s, 0, keepdims=True)
        e = jnp.exp(s).astype(bf16)
        e_ref[h] = e
        mixed = dot(with_ones(ckv_ref[0, HEADS + h]), e, 1, 0)
        inv = 1.0 / mixed[HEAD_DIM : HEAD_DIM + 1]
        inv_ref[pl.ds(h, 1), :] = inv
        mix_two[h] = (mixed[:HEAD_DIM] * inv).astype(bf16)
        return 0

    @pl.when(tame)
    def _():
        lax.fori_loop(0, HEADS, functools.partial(forward, False), 0, unroll=4)

    @pl.when(jnp.logical_not(tame))
    def _():
        lax.fori_loop(0, HEADS, functools.partial(forward, True), 0)

    leave(0, 2, 3)
    mix_two_t = mix_two[...].reshape(width, tags)
    resid = one + dot(mix_two_t, w_proj[1], 0, 0) + vec(5)
    normed, scale_two = norm(resid)
    n_two[...] = normed
    two = normed * vec(11) + vec(7)
    two_low = two.astype(bf16)
    inner = dot(two_low, w_in[...], 1, 0) + b_in[...]
    root = 0.7978845608028654
    square = inner * inner
    tanh = jnp.tanh(root * inner * (1.0 + 0.044715 * square))
    act = (0.5 * inner * (1.0 + tanh)).astype(bf16)
    slope = 0.5 * (1.0 + tanh) + 0.5 * inner * (1.0 - tanh * tanh) * (root * (1.0 + 3 * 0.044715 * square))
    resid = two + dot(act, w_out[...], 1, 0) + vec(9)
    three, scale_three = norm(resid)
    valid = lax.broadcasted_iota(jnp.int32, (tags, 1), 0) < lens[i]
    out_ref[0] = jnp.where(valid, three * vec(12) + vec(8), 0.0).astype(bf16)

    grad = jnp.where(valid, gout_ref[0].astype(f32), 0.0)
    add(12, column_sums(grad * three))
    add(8, column_sums(grad))
    g_three = norm_back(grad, three, scale_three, vec(12))
    g_low = g_three.astype(bf16)
    add(9, column_sums(g_three))
    acc_out[...] += dot(act, g_low, 0, 0)
    g_inner = dot(g_low, w_out[...], 1, 1) * slope
    acc_bin[...] += column_sums(g_inner)
    g_inner = g_inner.astype(bf16)
    acc_in[...] += dot(two_low, g_inner, 0, 0)
    g_two = g_three + dot(g_inner, w_in[...], 1, 1)
    add(11, column_sums(g_two * n_two[...]))
    add(7, column_sums(g_two))
    g_two = norm_back(g_two, n_two[...], scale_two, vec(11))
    add(5, column_sums(g_two))
    g_low = g_two.astype(bf16)
    acc_proj[1] += dot(mix_two_t, g_low, 1, 0)
    gmix_two[...] = dot(w_proj[1], g_low, 1, 1).astype(bf16).reshape(gmix_two.shape)

    def rest_of_image():
        def backward(h, _):
            dq_ref[h], dkv_ref[h], dkv_ref[HEADS + h] = cross_back(
                h, e_ref[h], ckv_ref[0, h], ckv_ref[0, HEADS + h], q_ref[h], gmix_two[h], mix_two[h], inv_ref[pl.ds(h, 1), :])
            return 0

        lax.fori_loop(0, HEADS, backward, 0, unroll=4)
        dq = dq_ref[...].reshape(width, tags)
        dkv = dkv_ref[...].reshape(2 * width, cells)
        acc_col[0] += lane_groups(dq.astype(f32))
        acc_col[1] += memory_lanes(dkv[width:].astype(f32))
        acc_cross[:width] += dot(dq, one_low, 1, 0)
        acc_cross[width:] += dot(dkv, mem_ref[0], 1, 0)
        g_mem[0] = dot(dkv, wt_cross[width:], 0, 0)
        g_one = g_two + dot(dq, wt_cross[:width], 0, 0)
        add(10, column_sums(g_one * n_one[...]))
        add(6, column_sums(g_one))
        g_one = norm_back(g_one, n_one[...], scale_one, vec(10))
        add(2, column_sums(g_one))
        g_resid[0] = g_one
        g_low = g_one.astype(bf16)
        acc_proj[0] += dot(mix_one_t, g_low, 1, 0)
        g_mix[0] = dot(w_proj[0], g_low, 1, 1).astype(bf16).reshape(g_mix.shape[1:])

    if held_back:
        pl.when(i < count - 1)(rest_of_image)

        @pl.when(i == count - 1)
        def _():
            n_two[...] = g_two
            scale_out[...] = scale_one

        leave(4, 6)
    else:
        rest_of_image()

    @pl.when(i == count - 1)
    def _():
        if held_back:
            gw_proj[...] = acc_proj[1].astype(bf16)
        else:
            gw_cross[...] = acc_cross[...].astype(bf16).T
            gw_proj[...] = acc_proj[...].astype(bf16)
        gw_in[...] = acc_in[...].astype(bf16)
        gw_out[...] = acc_out[...].astype(bf16)
        add(3, column_sums(acc_col[0].T))
        add(4, column_sums(acc_col[1].T))
        g_vec[...] = acc_vec[...]
        g_bin[...] = acc_bin[...]
        if held_back:
            for copy in copies:
                copy.wait()


def run_middle(lens, x, mem, gout, mix_one, ckv, wt_cross, w_proj, w_in, w_out, vectors, b_in, held_back=False):
    images, tags, width = x.shape
    cells = mem.shape[1]
    hidden = w_in.shape[1]
    sds = jax.ShapeDtypeStruct

    def per(*shape):
        return pl.BlockSpec((1,) + shape, lambda i, n: (i,) + (0,) * len(shape))

    def one(*shape):
        return pl.BlockSpec(shape, lambda i, n: (0,) * len(shape), pipeline_mode=pl.Buffered(1))

    def out(*shape):
        return pl.BlockSpec(shape, lambda i, n: (0,) * len(shape))

    def early(*shape):
        return pl.BlockSpec((1,) + shape, lambda i, n: (jnp.minimum(i, images - 2),) + (0,) * len(shape)) if held_back else per(*shape)

    done = images - 1 if held_back else images
    out_specs = [
        per(tags, width), early(tags, width), early(HEADS, HEAD_DIM, tags), early(cells, width),
        out(width, 3 * width), out(2, width, width), out(width, hidden), out(hidden, width), out(16, width), out(1, hidden),
    ]
    out_shape = [
        sds((images, tags, width), bf16), sds((done, tags, width), f32), sds((done, HEADS, HEAD_DIM, tags), bf16),
        sds((images, cells, width), f32),
        sds((width, 3 * width), bf16), sds((2, width, width), bf16), sds((width, hidden), bf16), sds((hidden, width), bf16),
        sds((16, width), f32), sds((1, hidden), f32),
    ]
    scratch = [
        pltpu.VMEM((2 * HEADS, HEAD_DIM, cells), bf16),
        pltpu.VMEM((width, 16), f32),
        pltpu.VMEM((HEADS, cells, tags), bf16),
        pltpu.VMEM((HEADS, HEAD_DIM, tags), bf16),
        pltpu.VMEM((HEADS, tags), f32),
        pltpu.VMEM((HEADS, HEAD_DIM, tags), bf16),
        pltpu.VMEM((HEADS, HEAD_DIM, tags), bf16),
        pltpu.VMEM((HEADS, HEAD_DIM, tags), bf16),
        pltpu.VMEM((3 * width, width), f32),
        pltpu.VMEM((2, width, width), f32),
        pltpu.VMEM((width, hidden), f32),
        pltpu.VMEM((hidden, width), f32),
        pltpu.VMEM((16, width), f32),
        pltpu.VMEM((1, hidden), f32),
        pltpu.VMEM((2, width, 128), f32),
        pltpu.VMEM((tags, width), f32),
        pltpu.VMEM((tags, width), f32),
    ]
    if held_back:
        out_specs[4], out_shape[4] = out(8, 128), sds((8, 128), bf16)
        out_specs[5], out_shape[5] = out(width, width), sds((width, width), bf16)
        kept = [((HEADS, cells, tags), bf16), ((HEADS, HEAD_DIM, tags), bf16), ((HEADS, tags), f32), ((HEADS, HEAD_DIM, tags), bf16),
                ((HEADS, HEAD_DIM, tags), bf16), ((tags, width), f32), ((tags, width), f32), ((3 * width, width), f32), ((width, width), f32)]
        out_specs += [out(tags, 1)] + [pl.BlockSpec(memory_space=pl.ANY)] * len(kept)
        out_shape += [sds((tags, 1), f32)] + [sds(*k) for k in kept]
        scratch.append(pltpu.SemaphoreType.DMA((len(kept),)))
    return pl.pallas_call(
        functools.partial(middle, held_back),
        grid_spec=pltpu.PrefetchScalarGridSpec(
            num_scalar_prefetch=1,
            grid=(images,),
            in_specs=[
                per(tags, width), per(cells, width), per(tags, width), per(HEADS, HEAD_DIM, tags), per(2 * HEADS, HEAD_DIM, cells),
                one(3 * width, width), one(2, width, width), one(width, hidden), one(hidden, width), one(16, width), one(1, hidden),
            ],
            out_specs=out_specs,
            scratch_shapes=scratch,
        ),
        out_shape=out_shape,
        compiler_params=pltpu.CompilerParams(vmem_limit_bytes=62 * MIB),
        name="middle",
    )(lens, x, mem, gout, mix_one, ckv, wt_cross, w_proj, w_in, w_out, vectors, b_in)


def self_backward(x_ref, qkv_ref, near_ref, far_ref, inv_ref, mix_ref, gmix_ref, g_resid, wt_self,
                  g_tags, gw_self, g_col, d_ref, acc, acc_col):
    tags, width = x_ref.shape[1:]
    half = tags // 2
    i = pl.program_id(0)

    @pl.when(i == 0)
    def _():
        acc[...] = jnp.zeros_like(acc)
        acc_col[...] = jnp.zeros_like(acc_col)

    def head(h, _):
        grad = gmix_ref[0, h].astype(f32)
        inv = inv_ref[0, pl.ds(h, 1), :]
        delta = jnp.sum(grad * mix_ref[0, h].astype(f32), 0, keepdims=True) * inv
        grad = (grad * inv).astype(bf16)
        ext = with_delta(grad, delta)
        qt, kt, vt = qkv_ref[0, h], qkv_ref[0, HEADS + h], with_ones(qkv_ref[0, 2 * HEADS + h])
        near, far = near_ref[0, h], far_ref[0, h]
        ds_near = near * dot(vt[:, :half], ext[:, :half], 0, 0).astype(bf16)
        ds_far = far * dot(vt, ext[:, half:], 0, 0).astype(bf16)
        dv = dot(grad[:, half:], far, 1, 1)
        dk = dot(qt[:, half:], ds_far, 1, 1)
        d_ref[2 * HEADS + h, :, half:] = dv[:, half:].astype(bf16)
        d_ref[2 * HEADS + h, :, :half] = (dv[:, :half] + dot(grad[:, :half], near, 1, 1)).astype(bf16)
        d_ref[HEADS + h, :, half:] = dk[:, half:].astype(bf16)
        d_ref[HEADS + h, :, :half] = (dk[:, :half] + dot(qt[:, :half], ds_near, 1, 1)).astype(bf16)
        d_ref[h, :, :half] = (dot(kt[:, :half], ds_near, 1, 0) * HEAD_DIM ** -0.5).astype(bf16)
        d_ref[h, :, half:] = (dot(kt, ds_far, 1, 0) * HEAD_DIM ** -0.5).astype(bf16)
        return 0

    lax.fori_loop(0, HEADS, head, 0)
    d = d_ref[...].reshape(3 * width, tags)
    acc_col[0] += lane_groups(d[:width].astype(f32))
    acc_col[1] += lane_groups(d[2 * width :].astype(f32))
    acc[...] += dot(d, x_ref[0], 1, 0)
    g_tags[0] = g_resid[0] + dot(d, wt_self[...], 0, 0)

    @pl.when(i == pl.num_programs(0) - 1)
    def _():
        gw_self[...] = acc[...].astype(bf16).T
        g_col[0:1] = column_sums(acc_col[0].T)
        g_col[1:2] = column_sums(acc_col[1].T)


def run_self_backward(x, qkv, near, far, inv, mix, gmix, g_resid, wt_self):
    images, tags, width = x.shape
    half = tags // 2
    sds = jax.ShapeDtypeStruct

    def per(*shape):
        return pl.BlockSpec((1,) + shape, lambda i: (i,) + (0,) * len(shape))

    def one(*shape):
        return pl.BlockSpec(shape, lambda i: (0,) * len(shape))

    return pl.pallas_call(
        self_backward,
        grid=(images,),
        in_specs=[per(tags, width), per(3 * HEADS, HEAD_DIM, tags), per(HEADS, half, half), per(HEADS, tags, half), per(HEADS, tags),
                  per(HEADS, HEAD_DIM, tags), per(HEADS, HEAD_DIM, tags), per(tags, width),
                  one(3 * width, width)],
        out_specs=[per(tags, width), one(width, 3 * width), one(8, width)],
        out_shape=[sds((images, tags, width), f32), sds((width, 3 * width), bf16), sds((8, width), f32)],
        scratch_shapes=[pltpu.VMEM((3 * HEADS, HEAD_DIM, tags), bf16), pltpu.VMEM((3 * width, width), f32), pltpu.VMEM((2, width, 128), f32)],
        compiler_params=pltpu.CompilerParams(vmem_limit_bytes=60 * MIB),
        name="self_backward",
    )(x, qkv, near, far, inv, mix, gmix, g_resid, wt_self)


def layer(lens, x, mem, gout, w_self, w_cross, w_proj, w_in, w_out, vectors, b_in):
    width = x.shape[2]
    zero = jnp.zeros((width,), f32)
    bias_qkv = jnp.concatenate([vectors[0], zero, vectors[1]])[:, None]
    bias_kv = jnp.concatenate([zero, vectors[4]])[:, None]
    qkv, ckv, near, far, inv, mix, wt_self, wt_cross = run_self_forward(lens, x, mem, w_self, w_cross, bias_qkv, bias_kv)
    out, g_resid, gmix, g_mem, gw_cross, gw_proj, gw_in, gw_out, g_vec, g_bin = run_middle(
        lens, x, mem, gout, mix, ckv, wt_cross, w_proj, w_in, w_out, vectors, b_in)
    g_tags, gw_self, g_col = run_self_backward(x, qkv, near, far, inv, mix, gmix, g_resid, wt_self)
    g_vec = g_vec.at[0:2].set(g_col[0:2])
    return out, g_tags, g_mem, gw_self, gw_cross, gw_proj, gw_in, gw_out, g_vec, g_bin


ALL = slice(None)


SMALL, SELF, PROJ, CROSS, IN, OUT = range(6)
PLAN = (
    ((SMALL, 0), (SELF, 0), (PROJ, 0), (CROSS, 0), (IN, 0), (OUT, 0),
     (SMALL, 1), (SELF, 1), (SMALL, 2), (PROJ, 1), (SELF, 2), (SMALL, 3), (CROSS, 1), (PROJ, 2), (IN, 1), (SELF, 3), (CROSS, 2), (OUT, 1),
     (PROJ, 3), (SMALL, 4), (SELF, 4)),
    ((IN, 2),),
    ((OUT, 2),),
    ((CROSS, 3),),
    ((IN, 3),),
    ((OUT, 3),),
    (),
    ((CROSS, 4),),
    ((PROJ, 4), (IN, 4), (OUT, 4)),
)
MEANTIME = {2: (0, 2), 3: (1, 0), 4: (1, 3), 5: (2, 2)}


class Gathering:
    def __init__(self, dims, me, shard, held, lead, sems):
        self.dims, self.me, self.shard, self.held, self.lead = dims, me, shard, held, lead
        self.local, self.send, self.recv = sems

    def cell(self, *index):
        return self.held.at[(ALL,) * self.lead + index]

    def remote(self, slot, src, dst, peer):
        return pltpu.make_async_remote_copy(
            src_ref=src, dst_ref=dst, send_sem=self.send.at[slot], recv_sem=self.recv.at[slot],
            device_id=device(self.dims, *peer), device_id_type=MESH)

    def keep(self):
        return pltpu.make_async_copy(self.shard, self.cell(*self.me), self.local)

    def first(self):
        a, b, x, c = self.me
        outer = self.dims[0]
        return [self.remote(k - 1, self.shard, self.cell(a, b, x, c), (lax.rem(a + k, outer), b, x, c)) for k in range(1, outer)]

    def along_inner(self, core):
        a, b, x, c = self.me
        outer, inner, _ = self.dims
        piece = self.cell(ALL, b, ALL if core == 0 else x, c)
        return [self.remote(outer - 2 + k, piece, piece, (a, lax.rem(b + k, inner), x, c)) for k in range(1, inner)]

    def along_across(self, core):
        a, b, x, c = self.me
        outer, inner, across = self.dims
        piece = self.cell(ALL, b if core == 0 else ALL, x, c)
        return [self.remote(outer + inner - 3 + k, piece, piece, (a, b, lax.rem(x + k, across), c)) for k in range(1, across)]

    def second(self, core):
        return self.along_across(core) if core == 0 else self.along_inner(core)

    def third(self, core):
        return self.along_inner(core) if core == 0 else self.along_across(core)

    def handed(self, core, holder):
        a, b, x, c = self.me
        outer, inner, across = self.dims
        base = outer + inner + across - 3

        def piece(slot, row, column):
            ref = self.cell(ALL, row, column, holder)
            return self.remote(base + slot, ref, ref, (a, b, x, 1 - c))

        own = [piece(0, b, x)]
        by_inner = [piece(k, lax.rem(b + k, inner), ALL if core == 0 else x) for k in range(1, inner)]
        by_across = [piece(inner - 1 + k, b if core == 0 else ALL, lax.rem(x + k, across)) for k in range(1, across)]
        return (own, by_across, by_inner) if core == 0 else (own, by_inner, by_across)

    def begin(self):
        self.keep().start()
        for copy in self.first():
            copy.start()

    def each_core(self, act):
        for core in (0, 1):
            pl.when(self.me[3] == core)(functools.partial(act, core))

    def advance(self, stage):
        def act(core):
            if stage == 1:
                self.keep().wait()
            for copy in (self.first(), self.second(core), self.third(core))[stage - 1]:
                copy.wait_recv()
            following = (self.second(core), self.third(core), [])[stage - 1]
            for copy in following + self.handed(core, self.me[3])[stage - 1]:
                copy.start()
        self.each_core(act)

    def finish(self):
        def act(core):
            for group in self.handed(1 - core, 1 - self.me[3]):
                for copy in group:
                    copy.wait_recv()
        self.each_core(act)

    def drain(self):
        def act(core):
            for copy in self.first() + self.second(core) + self.third(core) + sum(self.handed(core, self.me[3]), []):
                copy.wait_send()
        self.each_core(act)


def gather_slots(dims):
    outer, inner, across = dims
    return outer + 2 * (inner + across) - 4


def spread(held, row_lanes, width, rows):
    devices = held.shape[0] // 16
    lane = lax.broadcasted_iota(jnp.int32, (128, width), 0)
    at = lax.broadcasted_iota(jnp.int32, (128, width), 1)
    pick = jnp.where((lax.rem(at, row_lanes) == lane), 1.0, 0.0).astype(bf16)
    wide = dot(held, pick, 1, 0)
    owner = lax.broadcasted_iota(jnp.int32, (devices * 16, width), 0) // 16
    at = lax.broadcasted_iota(jnp.int32, (devices * 16, width), 1)
    wide = jnp.where(at // row_lanes == owner, wide, 0.0)
    return jnp.sum(wide.reshape(devices, 16, width), 0)


def opening(dims, lens, x_ref, mem_ref, b_ref, g_ref, h_ref, s_cross, s_self, s_proj, s_in, s_out,
            qkv_ref, ckv_ref, near_ref, far_ref, inv_ref, mix_ref, out_self, out_cross, vec_ref, bin_ref, o_proj, o_in, o_out,
            small, small_low, h_small, h_self, h_cross, wt_self, wt_cross, cols, near_a, far_a, near_b, far_b, gone, local, send, recv):
    width = x_ref.shape[2]
    tags = x_ref.shape[1]
    half = tags // 2
    step = pl.program_id(0)
    images = pl.num_programs(0) // 2
    me = place(dims)
    pairs = ((small_low, h_small, 0), (s_self, h_self, 0), (s_proj, o_proj, 1), (s_cross, h_cross, 0), (s_in, o_in, 0), (s_out, o_out, 0))
    gs = [Gathering(dims, me, shard, held, lead, (local.at[k], send.at[k], recv.at[k])) for k, (shard, held, lead) in enumerate(pairs)]
    keep_self = pltpu.make_async_copy(wt_self, out_self, gone.at[0])
    keep_cross = pltpu.make_async_copy(wt_cross, out_cross, gone.at[1])

    def play(slot):
        for item, stage in PLAN[slot]:
            item = gs[item]
            item.begin() if stage == 0 else item.finish() if stage == 4 else item.advance(stage)

    def slot_at(number, slot):
        @pl.when(step == number)
        def _():
            play(slot)

    @pl.when(step == 0)
    def _():
        small[...] = jnp.zeros_like(small)
        small[0:10, : b_ref.shape[1]] = b_ref[...].astype(f32)
        small[10:13, : g_ref.shape[1]] = g_ref[...].astype(f32)
        small[13:14, : h_ref.shape[1]] = h_ref[...].astype(f32)
        small_low[...] = small[...].astype(bf16)
        greet(dims, me)
        play(0)
        vectors = spread(h_small[...].reshape(-1, 128), b_ref.shape[1], width, 16)
        vec_ref[...] = vectors
        bin_ref[...] = spread(h_small[...].reshape(-1, 128), h_ref.shape[1], bin_ref.shape[1], 16)[13:14]
        cols[...] = vectors.T
        wt_self[...] = h_self[...].reshape(width, 3 * width).T
        keep_self.start()

    @pl.when(step < images)
    def _():
        qkv = dot(wt_self[...], x_ref[0], 1, 1)
        qkv_ref[0, :HEADS] = ((qkv[:width] + cols[:, 0:1]).astype(bf16) * bf16(HEAD_DIM ** -0.5)).reshape(HEADS, HEAD_DIM, tags)
        qkv_ref[0, HEADS : 2 * HEADS] = qkv[width : 2 * width].astype(bf16).reshape(HEADS, HEAD_DIM, tags)
        qkv_ref[0, 2 * HEADS :] = (qkv[2 * width :] + cols[:, 1:2]).astype(bf16).reshape(HEADS, HEAD_DIM, tags)

    last = lens[jnp.minimum(step, images - 1)] - 1

    def scores(h, near, far):
        qt, kt = qkv_ref[0, h], qkv_ref[0, HEADS + h]

        def part(keys, first, held):
            s = dot(kt[:, :keys], qt[:, first : first + half], 0, 0)
            key_at = lax.broadcasted_iota(jnp.int32, (keys, half), 0)
            query_at = lax.broadcasted_iota(jnp.int32, (1, half), 1) + first
            s = jnp.where(key_at <= jnp.minimum(query_at, last), s, MASKED)
            held[...] = s
            return jnp.max(s, 0, keepdims=True)

        return part(half, 0, near), part(tags, half, far)

    def mix(h, near, far, tops):
        vt = with_ones(qkv_ref[0, 2 * HEADS + h])

        def part(keys, first, held, top, out):
            e = jnp.exp(held[...] - top).astype(bf16)
            out[0, h] = e
            mixed = dot(vt[:, :keys], e, 1, 0)
            inv = 1.0 / mixed[HEAD_DIM : HEAD_DIM + 1]
            inv_ref[0, pl.ds(h, 1), first : first + half] = inv
            mix_ref[0, h, :, first : first + half] = (mixed[:HEAD_DIM] * inv).astype(bf16)

        part(half, 0, near, tops[0], near_ref)
        part(tags, half, far, tops[1], far_ref)

    def pair(p, tops):
        h = 2 * p
        for slot, (image, number) in MEANTIME.items():
            pl.when(jnp.logical_and(step == image, p == number))(functools.partial(play, slot))
        following = scores(h + 1, near_b, far_b)
        mix(h, near_a, far_a, tops)
        tops = scores(jnp.minimum(h + 2, HEADS - 1), near_a, far_a)
        mix(h + 1, near_b, far_b, following)
        return tops

    slot_at(0, 1)

    @pl.when(step < images)
    def _():
        lax.fori_loop(0, HEADS // 2, pair, scores(0, near_a, far_a))

    @pl.when(step == images)
    def _():
        play(7)
        wt_cross[...] = h_cross[...].reshape(width, 3 * width).T
        keep_cross.start()

    @pl.when(step >= images)
    def _():
        kv = dot(wt_cross[width:], mem_ref[0], 1, 1)
        ckv_ref[0, :HEADS] = kv[:width].astype(bf16).reshape(HEADS, HEAD_DIM, -1)
        ckv_ref[0, HEADS:] = (kv[width:] + cols[:, 4:5]).astype(bf16).reshape(HEADS, HEAD_DIM, -1)

    @pl.when(step == 2 * images - 1)
    def _():
        play(8)
        for g in gs:
            g.drain()
        keep_self.wait()
        keep_cross.wait()


def run_opening(dims, lens, x, mem, biases, gains, b_in, shards):
    images, tags, width = x.shape
    cells = mem.shape[1]
    half = tags // 2
    hidden = b_in.shape[1] * dims[0] * dims[1] * dims[2] * 2
    sds = jax.ShapeDtypeStruct

    def early(*shape):
        return pl.BlockSpec((1,) + shape, lambda i: (jnp.minimum(i, images - 1),) + (0,) * len(shape))

    def late(*shape):
        return pl.BlockSpec((1,) + shape, lambda i: (jnp.maximum(i - images, 0),) + (0,) * len(shape))

    def one(*shape):
        return pl.BlockSpec(shape, lambda i: (0,) * len(shape))

    def held(shard, lead):
        return shard.shape[:lead] + dims + (2,) + shard.shape[lead:]

    s_cross, s_self, s_proj, s_in, s_out = shards
    rows = s_cross.shape[0]
    cell = dims + (2, rows)
    anywhere = pl.BlockSpec(memory_space=pl.ANY)
    n = len(shards) + 1
    slots = gather_slots(dims)
    return pl.pallas_call(
        functools.partial(opening, dims),
        grid=(2 * images,),
        in_specs=[pl.BlockSpec(memory_space=pltpu.SMEM), early(tags, width), late(cells, width), one(*biases.shape), one(*gains.shape), one(*b_in.shape)]
        + [anywhere] * len(shards),
        out_specs=[
            early(3 * HEADS, HEAD_DIM, tags), late(2 * HEADS, HEAD_DIM, cells), early(HEADS, half, half), early(HEADS, tags, half),
            early(HEADS, tags), early(HEADS, HEAD_DIM, tags), anywhere, anywhere, one(16, width), one(1, hidden),
            anywhere, anywhere, anywhere,
        ],
        out_shape=[
            sds((images, 3 * HEADS, HEAD_DIM, tags), bf16),
            sds((images, 2 * HEADS, HEAD_DIM, cells), bf16),
            sds((images, HEADS, half, half), bf16),
            sds((images, HEADS, tags, half), bf16),
            sds((images, HEADS, tags), f32),
            sds((images, HEADS, HEAD_DIM, tags), bf16),
            sds((3 * width, width), bf16),
            sds((3 * width, width), bf16),
            sds((16, width), f32),
            sds((1, hidden), f32),
            sds(held(s_proj, 1), bf16),
            sds(held(s_in, 0), bf16),
            sds(held(s_out, 0), bf16),
        ],
        scratch_shapes=[
            pltpu.VMEM((16, 128), f32), pltpu.VMEM((16, 128), bf16), pltpu.VMEM(dims + (2, 16, 128), bf16),
            pltpu.VMEM(cell + (3 * width,), bf16), pltpu.VMEM(cell + (3 * width,), bf16),
            pltpu.VMEM((3 * width, width), bf16), pltpu.VMEM((3 * width, width), bf16),
            pltpu.VMEM((width, 16), f32), pltpu.VMEM((half, half), f32), pltpu.VMEM((tags, half), f32), pltpu.VMEM((half, half), f32), pltpu.VMEM((tags, half), f32),
            pltpu.SemaphoreType.DMA((2,)),
            pltpu.SemaphoreType.DMA((n,)), pltpu.SemaphoreType.DMA((n, slots)), pltpu.SemaphoreType.DMA((n, slots)),
        ],
        compiler_params=pltpu.CompilerParams(collective_id=0, has_side_effects=True, vmem_limit_bytes=58 * MIB),
        name="opening",
    )(lens, x, mem, biases, gains, b_in, *shards)


class Scattering:
    def __init__(self, dims, me, grads, out, lead, held, sems):
        self.dims, self.me, self.grads, self.out, self.lead = dims, me, grads, out, lead
        self.pair, self.by_inner, self.by_across, self.by_outer, self.last = held
        self.send, self.recv = sems

    def at(self, *index):
        return (ALL,) * self.lead + index

    def remote(self, slot, src, dst, peer):
        return pltpu.make_async_remote_copy(
            src_ref=src, dst_ref=dst, send_sem=self.send.at[slot], recv_sem=self.recv.at[slot],
            device_id=device(self.dims, *peer), device_id_type=MESH)

    def swap(self):
        a, b, x, c = self.me
        return [self.remote(0, self.grads.at[self.at(ALL, ALL, ALL, 1 - c)], self.pair, (a, b, x, 1 - c))]

    def along_inner(self, core):
        a, b, x, c = self.me
        inner = self.dims[1]
        res = []
        for k in range(1, inner):
            peer = lax.rem(b + k, inner)
            src = self.pair.at[self.at(ALL, peer)] if core == 0 else self.by_across.at[0].at[self.at(ALL, peer)]
            dst = self.by_inner.at[k - 1] if core == 0 else self.by_outer.at[k - 1]
            res.append(self.remote(k, src, dst, (a, peer, x, c)))
        return res

    def along_across(self, core):
        a, b, x, c = self.me
        _, inner, across = self.dims
        res = []
        for k in range(1, across):
            peer = lax.rem(x + k, across)
            src = self.pair.at[self.at(ALL, ALL, peer)] if core == 1 else self.by_inner.at[0].at[self.at(ALL, peer)]
            dst = self.by_across.at[k - 1] if core == 1 else self.by_outer.at[k - 1]
            res.append(self.remote(inner - 1 + k, src, dst, (a, b, peer, c)))
        return res

    def second(self, core):
        return self.along_inner(core) if core == 0 else self.along_across(core)

    def third(self, core):
        return self.along_across(core) if core == 0 else self.along_inner(core)

    def along_outer(self):
        a, b, x, c = self.me
        outer, inner, across = self.dims
        return [
            self.remote(inner + across - 2 + k, self.by_outer.at[0].at[self.at(lax.rem(a + k, outer))], self.last.at[k - 1],
                        (lax.rem(a + k, outer), b, x, c))
            for k in range(1, outer)
        ]

    def begin(self):
        for copy in self.swap():
            copy.start()

    def advance(self, stage):
        a, b, x, c = self.me
        _, inner, across = self.dims

        def up(value):
            return value.astype(f32)

        def act(core):
            for copy in (self.swap(), self.second(core), self.third(core), self.along_outer())[stage - 1]:
                copy.wait_recv()
            if stage == 1:
                self.pair[...] = (up(self.grads[self.at(ALL, ALL, ALL, c)]) + up(self.pair[...])).astype(bf16)
                following = self.second(core)
            elif stage == 2:
                held = self.by_inner if core == 0 else self.by_across
                total = up(self.pair[self.at(ALL, b) if core == 0 else self.at(ALL, ALL, x)])
                for k in range((inner if core == 0 else across) - 1):
                    total = total + up(held[k])
                held[0] = total.astype(bf16)
                following = self.third(core)
            elif stage == 3:
                held = self.by_inner if core == 0 else self.by_across
                total = up(held[(0,) + self.at(ALL, x if core == 0 else b)])
                for k in range((across if core == 0 else inner) - 1):
                    total = total + up(self.by_outer[k])
                self.by_outer[0] = total.astype(bf16)
                following = self.along_outer()
            else:
                total = up(self.by_outer[(0,) + self.at(a)])
                for k in range(self.dims[0] - 1):
                    total = total + up(self.last[k])
                self.out[...] = total
                following = []
            for copy in following:
                copy.start()

        for core in (0, 1):
            pl.when(c == core)(functools.partial(act, core))

    def drain(self):
        def act(core):
            for copy in self.swap() + self.second(core) + self.third(core) + self.along_outer():
                copy.wait_send()

        for core in (0, 1):
            pl.when(self.me[3] == core)(functools.partial(act, core))


def scatter_slots(dims):
    return dims[0] + dims[1] + dims[2] - 2


def scatter_space(dims, lead, tail):
    outer, inner, across = dims
    return [
        lead + (outer, inner, across) + tail,
        (inner - 1,) + lead + (outer, across) + tail,
        (across - 1,) + lead + (outer, inner) + tail,
        (max(inner, across) - 1,) + lead + (outer,) + tail,
        (outer - 1,) + lead + tail,
    ]


def collect(rows, row_lanes, devices):
    width = rows.shape[1]
    many = jnp.broadcast_to(rows[None], (devices, 16, width)).reshape(devices * 16, width)
    owner = lax.broadcasted_iota(jnp.int32, many.shape, 0) // 16
    at = lax.broadcasted_iota(jnp.int32, many.shape, 1)
    many = jnp.where(at // row_lanes == owner, many, 0.0).astype(bf16)
    lane = lax.broadcasted_iota(jnp.int32, (128, width), 0)
    at = lax.broadcasted_iota(jnp.int32, (128, width), 1)
    pick = jnp.where(lax.rem(at, row_lanes) == lane, 1.0, 0.0).astype(bf16)
    return dot(many, pick, 1, 1)


G_OUT, G_IN, G_ONE, G_CROSS, G_ZERO, G_HALF, G_REST, G_SMALL = range(8)
EVENTS = {
    (0, 0): ((G_OUT, 0), (G_IN, 0), (G_ONE, 0)),
    (0, 3): ((G_OUT, 1),),
    (0, 4): ((G_IN, 1), (G_ONE, 1)),
    (0, 6): ((G_OUT, 2), (G_CROSS, 0)),
    (0, 7): ((G_IN, 2), (G_ZERO, 0)),
    (1, 1): ((G_ONE, 2), (G_OUT, 3)),
    (2, 1): ((G_IN, 3), (G_CROSS, 1), (G_ONE, 3), (G_ZERO, 1)),
    (3, 1): ((G_HALF, 0), (G_OUT, 4)),
    (4, 1): ((G_IN, 4), (G_ONE, 4)),
    (5, 1): ((G_HALF, 1), (G_CROSS, 2)),
    (6, 1): ((G_REST, 0), (G_SMALL, 0), (G_ZERO, 2)),
    (7, 1): ((G_HALF, 2),),
    (8, 1): ((G_CROSS, 3), (G_ZERO, 3), (G_REST, 1), (G_SMALL, 1)),
    (9, 0): ((G_HALF, 3),),
    (9, 1): ((G_REST, 2), (G_SMALL, 2), (G_CROSS, 4), (G_ZERO, 4), (G_HALF, 4), (G_REST, 3), (G_SMALL, 3), (G_REST, 4), (G_SMALL, 4)),
}


def closing(dims, x_ref, qkv_ref, near_ref, far_ref, inv_ref, mix_ref, gmix_ref, gres_ref, ckv_ref, q_ref, inv_two, mix_two, gmix_two,
            vectors, g_vec, g_bin, scale_one, low_out, low_in, low_one,
            e_any, mix_any, two_any, one_any, wc_any, mem_any, ac_any, ap_any, wp_any, ws_any,
            g_tags, sh_out, sh_in, sh_one, sh_cross, sh_zero, sh_half, sh_rest, sh_small, dkv_ref,
            e_ref, mix_one, g_two, n_one, wt_cross, mem_ref, acc_cross, acc_zero, w_zero, wt_self,
            dq_ref, gmix_last, gres_last, gmix_now, acc, add_vec, acc_col, low_cross, low_zero, low_half, low_rest, low_small, head_sem, in_sem, *rest):
    tags, width = x_ref.shape[1:]
    cells = mem_ref.shape[0]
    half = tags // 2
    some = HEADS // 2
    step = pl.program_id(0)
    images = pl.num_programs(0) // 3
    me = place(dims)
    devices = dims[0] * dims[1] * dims[2] * 2
    held, (send, recv) = rest[:-2], rest[-2:]
    pairs = ((low_out, sh_out), (low_in, sh_in), (low_one, sh_one), (low_cross, sh_cross), (low_zero, sh_zero), (low_half, sh_half),
             (low_rest, sh_rest), (low_small, sh_small))
    every = [Scattering(dims, me, grads, out, 0, held[5 * k : 5 * k + 5], (send.at[k], recv.at[k])) for k, (grads, out) in enumerate(pairs)]
    fetches = [
        pltpu.make_async_copy(src, dst, in_sem.at[k])
        for k, (src, dst) in enumerate((
            (mix_any.at[images - 1], mix_one), (two_any, g_two), (one_any, n_one), (wc_any, wt_cross), (mem_any.at[images - 1], mem_ref),
            (ac_any, acc_cross), (ap_any, acc_zero), (wp_any.at[0], w_zero), (ws_any, wt_self)))
    ]

    def e_rows(h):
        return e_ref.at[pl.ds(pl.multiple_of(h * cells, 16), cells)]

    def e_fetch(h):
        return pltpu.make_async_copy(e_any.at[h], e_rows(h), head_sem.at[h])

    def play(number, where):
        for item, stage in EVENTS.get((number, where), ()):
            item = every[item]
            item.begin() if stage == 0 else item.advance(stage)

    def events(where):
        for number in sorted(number for number, at in EVENTS if at == where and number > 0):
            pl.when(step == number)(functools.partial(play, number, where))

    def vec(k):
        return vectors[k : k + 1, :]

    @pl.when(step == 0)
    def _():
        for h in range(HEADS):
            e_fetch(h).start()
        for fetch in fetches:
            fetch.start()
        acc_col[...] = jnp.zeros_like(acc_col)
        greet(dims, me)
        play(0, 0)

        def pair(p, _):
            for k in range(1, 4):
                pl.when(p == k)(functools.partial(play, 0, k + 1))
            for h in (2 * p, 2 * p + 1):
                e_fetch(h).wait()
            for h in (2 * p, 2 * p + 1):
                dq_ref[h], dkv_ref[h], dkv_ref[HEADS + h] = cross_back(
                    h, e_rows(h)[...], ckv_ref[0, h], ckv_ref[0, HEADS + h], q_ref[h], gmix_two[h], mix_two[h], inv_two[pl.ds(h, 1), :])
            return 0

        lax.fori_loop(0, HEADS // 2, pair, 0)
        for fetch in fetches:
            fetch.wait()
        dq = dq_ref[...].reshape(width, tags)
        dkv = dkv_ref[...].reshape(2 * width, cells)
        one_low = (n_one[...] * vec(10) + vec(6)).astype(bf16)
        acc_cross[:width] += dot(dq, one_low, 1, 0)
        acc_cross[width:] += dot(dkv, mem_ref[...], 1, 0)
        low_cross[...] = acc_cross[...].astype(bf16).T.reshape(low_cross.shape)
        play(0, 6)
        g_one = g_two[...] + dot(dq, wt_cross[:width], 0, 0)
        sum_gain, sum_shift = column_sums(g_one * n_one[...]), column_sums(g_one)
        g_one = norm_back(g_one, n_one[...], scale_one[...], vec(10))
        gres_last[...] = g_one
        g_low = g_one.astype(bf16)
        acc_zero[...] += dot(mix_one[...].reshape(width, tags), g_low, 1, 0)
        low_zero[...] = acc_zero[...].astype(bf16).reshape(low_zero.shape)
        play(0, 7)
        gmix_last[...] = dot(w_zero[...], g_low, 1, 1).astype(bf16).reshape(gmix_last.shape)
        at = lax.broadcasted_iota(jnp.int32, add_vec.shape, 0)
        total = g_vec[...]
        for k, row in ((2, column_sums(g_one)), (3, column_sums(lane_groups(dq.astype(f32)).T)),
                       (4, column_sums(memory_lanes(dkv[width:].astype(f32)).T)), (6, sum_shift), (10, sum_gain)):
            total = total + jnp.where(at == k, row, 0.0)
        add_vec[...] = total

    turn = jnp.maximum(step - 1, 0)
    part = jnp.minimum(turn // images, 1)
    now = lax.rem(turn, images)
    backward = jnp.logical_and(step >= 1, step <= 2 * images)

    @pl.when(jnp.logical_and(backward, now < images - 1))
    def _():
        gmix_now[...] = gmix_ref[0]

    @pl.when(jnp.logical_and(backward, now == images - 1))
    def _():
        gmix_now[...] = gmix_last[pl.ds(part * some, some)]

    def d_rows(image, kind, h, count=1):
        return pl.ds(pl.multiple_of(((image * 3 + kind) * HEADS + h) * HEAD_DIM, HEAD_DIM), count * HEAD_DIM)

    def head(h, _):
        grad = gmix_now[h].astype(f32)
        inv = inv_ref[0, pl.ds(part * some + h, 1), :]
        delta = jnp.sum(grad * mix_ref[0, h].astype(f32), 0, keepdims=True) * inv
        grad = (grad * inv).astype(bf16)
        ext = with_delta(grad, delta)
        qt, kt, vt = qkv_ref[0, 0, h], qkv_ref[0, 1, h], with_ones(qkv_ref[0, 2, h])
        near, far = near_ref[0, h], far_ref[0, h]
        ds_near = near * dot(vt[:, :half], ext[:, :half], 0, 0).astype(bf16)
        ds_far = far * dot(vt, ext[:, half:], 0, 0).astype(bf16)
        dv = dot(grad[:, half:], far, 1, 1)
        dk = dot(qt[:, half:], ds_far, 1, 1)
        dv = jnp.concatenate([dv[:, :half] + dot(grad[:, :half], near, 1, 1), dv[:, half:]], 1)
        dk = jnp.concatenate([dk[:, :half] + dot(qt[:, :half], ds_near, 1, 1), dk[:, half:]], 1)
        dq = jnp.concatenate([dot(kt[:, :half], ds_near, 1, 0), dot(kt, ds_far, 1, 0)], 1) * HEAD_DIM ** -0.5
        at = part * some + h
        e_ref[d_rows(now, 0, at)] = dq.astype(bf16)
        e_ref[d_rows(now, 1, at)] = dk.astype(bf16)
        e_ref[d_rows(now, 2, at)] = dv.astype(bf16)
        return 0

    @pl.when(backward)
    def _():
        lax.fori_loop(0, some, head, 0, unroll=2)
        d = [e_ref[d_rows(now, kind, part * some, some)] for kind in range(3)]
        rows = some * HEAD_DIM
        acc_col[0, pl.ds(part * rows, rows)] += lane_groups(d[0].astype(f32))
        acc_col[1, pl.ds(part * rows, rows)] += lane_groups(d[2].astype(f32))
        fresh = now == 0
        for kind in range(3):
            product = dot(d[kind], x_ref[0], 1, 0)

            @pl.when(fresh)
            def _():
                acc[kind * rows : (kind + 1) * rows] = product

            @pl.when(jnp.logical_not(fresh))
            def _():
                acc[kind * rows : (kind + 1) * rows] += product

    @pl.when(step == images)
    def _():
        low_half[...] = acc[...].astype(bf16).T.reshape(low_half.shape)

    @pl.when(step == 2 * images)
    def _():
        low_rest[...] = acc[...].astype(bf16).T.reshape(low_rest.shape)
        at = lax.broadcasted_iota(jnp.int32, add_vec.shape, 0)
        rows = jnp.where(at == 0, column_sums(acc_col[0].T), jnp.where(at == 1, column_sums(acc_col[1].T), add_vec[...]))
        at = lax.broadcasted_iota(jnp.int32, (16, g_bin.shape[1]), 0)
        hidden = jnp.where(at == 13, g_bin[...], 0.0)
        small = collect(rows, width // devices, devices) + collect(hidden, g_bin.shape[1] // devices, devices)
        low_small[...] = small.astype(bf16).reshape(low_small.shape)

    events(0)

    @pl.when(step > 2 * images)
    def _():
        image = jnp.maximum(step - 2 * images - 1, 0)
        d = e_ref[d_rows(image, 0, 0, 3 * HEADS)]
        product = dot(d, wt_self[...], 0, 0)

        @pl.when(image < images - 1)
        def _():
            g_tags[0] = gres_ref[0] + product

        @pl.when(image == images - 1)
        def _():
            g_tags[0] = gres_last[...] + product

    events(1)

    @pl.when(step == 3 * images)
    def _():
        for item in every:
            item.drain()


def run_closing(dims, x, qkv, near, far, inv, mix, gmix, g_resid, ckv, mem, vectors, wt_self, wt_cross, w_proj, g_one, g_in, g_out, g_vec, g_bin, kept):
    scale_one, e, q, inv_two, mix_two, gmix_two, n_one, g_two, acc_cross, acc_zero = kept
    images, tags, width = x.shape
    memory = mem.shape[1]
    half, some = tags // 2, HEADS // 2
    sds = jax.ShapeDtypeStruct
    cells = dims + (2,)
    devices = dims[0] * dims[1] * dims[2] * 2

    def parts(grad):
        return grad.reshape(cells + (grad.shape[0] // devices, grad.shape[1]))

    low = [parts(g_out), parts(g_in), parts(g_one)]
    rows = width // devices
    lows = [cells + (rows, 3 * width), cells + (rows, width)] + [cells + (rows, 3 * width // 2)] * 2 + [cells + (16, 128)]

    def turn(i):
        t = jnp.clip(i - 1, 0, 2 * images - 1)
        return lax.rem(t, images), lax.div(t, images)

    def by_turn(shape, split):
        def index(i):
            image, part = turn(i)
            return (image,) + tuple(part if k == split else 0 for k in range(len(shape)))
        return pl.BlockSpec((1,) + shape, index)

    def gmix_index(i):
        image, part = turn(i)
        return jnp.minimum(image, images - 2), part, 0, 0

    def one(*shape):
        return pl.BlockSpec(shape, lambda i: (0,) * len(shape), pipeline_mode=pl.Buffered(1))

    def out(*shape):
        return pl.BlockSpec(shape, lambda i: (0,) * len(shape))

    anywhere = pl.BlockSpec(memory_space=pl.ANY)
    shares = [g.shape[4:] for g in low] + [s[4:] for s in lows]
    space = []
    for shape in [g.shape for g in low] + lows:
        space += [pltpu.VMEM(s, bf16) for s in scatter_space(dims, (), shape[4:])]
    slots = scatter_slots(dims)
    qkv = qkv.reshape(images, 3, HEADS, HEAD_DIM, tags)
    heads = (HEADS, HEAD_DIM, tags)
    return pl.pallas_call(
        functools.partial(closing, dims),
        grid=(3 * images + 1,),
        in_specs=[
            by_turn((tags, width), None), by_turn((3, some, HEAD_DIM, tags), 1), by_turn((some, half, half), 0), by_turn((some, tags, half), 0),
            by_turn((HEADS, tags), None), by_turn((some, HEAD_DIM, tags), 0), pl.BlockSpec((1, some, HEAD_DIM, tags), gmix_index),
            pl.BlockSpec((1, tags, width), lambda i: (jnp.clip(i - 2 * images - 1, 0, images - 2), 0, 0)),
            pl.BlockSpec((1, 2 * HEADS, HEAD_DIM, memory), lambda i: (images - 1, 0, 0, 0), pipeline_mode=pl.Buffered(1)),
            one(*heads), one(HEADS, tags), one(*heads), one(*heads), one(16, width), one(16, width), one(*g_bin.shape), one(tags, 1),
        ] + [one(*g.shape) for g in low] + [anywhere] * 10,
        out_specs=[pl.BlockSpec((1, tags, width), lambda i: (jnp.clip(i - 2 * images - 1, 0, images - 1), 0, 0))]
        + [out(*s) for s in shares] + [pl.BlockSpec((2 * HEADS, HEAD_DIM, memory), lambda i: (0, 0, 0))],
        out_shape=[sds((images, tags, width), f32)] + [sds(s, f32) for s in shares] + [sds((2 * HEADS, HEAD_DIM, memory), bf16)],
        scratch_shapes=[
            pltpu.VMEM((HEADS * memory, tags), bf16), pltpu.VMEM(heads, bf16), pltpu.VMEM((tags, width), f32), pltpu.VMEM((tags, width), f32),
            pltpu.VMEM((3 * width, width), bf16), pltpu.VMEM((memory, width), bf16), pltpu.VMEM((3 * width, width), f32), pltpu.VMEM((width, width), f32),
            pltpu.VMEM((width, width), bf16), pltpu.VMEM((3 * width, width), bf16),
            pltpu.VMEM(heads, bf16), pltpu.VMEM(heads, bf16), pltpu.VMEM((tags, width), f32), pltpu.VMEM((some, HEAD_DIM, tags), bf16),
            pltpu.VMEM((3 * width // 2, width), f32), pltpu.VMEM((16, width), f32), pltpu.VMEM((2, width, 128), f32),
        ] + [pltpu.VMEM(s, bf16) for s in lows] + [pltpu.SemaphoreType.DMA((HEADS,)), pltpu.SemaphoreType.DMA((9,))] + space
        + [pltpu.SemaphoreType.DMA((8, slots)), pltpu.SemaphoreType.DMA((8, slots))],
        compiler_params=pltpu.CompilerParams(collective_id=1, has_side_effects=True, vmem_limit_bytes=62 * MIB),
        name="closing",
    )(x, qkv, near, far, inv, mix, gmix, g_resid, ckv, q, inv_two, mix_two, gmix_two, vectors, g_vec, g_bin, scale_one, *low,
      e, mix, g_two, n_one, wt_cross, mem, acc_cross, acc_zero, w_proj, wt_self)


def settle(lanes, hidden_lanes, images, g_mem_in, dkv, wt_cross, tags, s_out, s_in, s_one, s_cross, s_zero, s_half, s_rest, small,
           g_mem, o_tags, o_self, o_cross, o_proj, o_in, o_out, o_bin, o_gains, o_biases):
    width = o_tags.shape[2]
    o_tags[...] = tags[...]

    @pl.when(pl.program_id(0) == 0)
    def _():
        g_mem[0] = dot(dkv[...].reshape(2 * width, -1), wt_cross[...], 0, 0)
        part = width // 2
        for kind in range(3):
            o_self[:, kind * width : kind * width + part] = s_half[:, kind * part : (kind + 1) * part]
            o_self[:, kind * width + part : (kind + 1) * width] = s_rest[:, kind * part : (kind + 1) * part]
        o_cross[...] = s_cross[...]
        o_proj[0] = s_zero[...]
        o_proj[1] = s_one[...]
        o_in[...] = s_in[...]
        o_out[...] = s_out[...]
        o_biases[...] = small[:10, :lanes]
        o_gains[...] = small[10:13, :lanes]
        o_bin[...] = small[13:14, :hidden_lanes]


def run_settle(lanes, hidden_lanes, g_mem, dkv, wt_cross, g_tags, shares):
    images, tags, width = g_tags.shape
    sds = jax.ShapeDtypeStruct
    s_out, s_in, s_one, s_cross, s_zero, s_half, s_rest, small = shares

    def one(*shape):
        return pl.BlockSpec(shape, lambda i: (0,) * len(shape), pipeline_mode=pl.Buffered(1))

    def out(*shape):
        return pl.BlockSpec(shape, lambda i: (0,) * len(shape))

    rows = s_cross.shape[0]
    shapes = [s_cross.shape, s_cross.shape, (2, rows, width), s_in.shape, s_out.shape, (1, hidden_lanes), (3, lanes), (10, lanes)]
    image = pl.BlockSpec((1, tags, width), lambda i: (i, 0, 0))
    return pl.pallas_call(
        functools.partial(settle, lanes, hidden_lanes, images),
        grid=(images,),
        in_specs=[pl.BlockSpec(memory_space=pl.ANY), one(*dkv.shape),
                  pl.BlockSpec((2 * width, width), lambda i: (0, 0), pipeline_mode=pl.Buffered(1)), image] + [one(*s.shape) for s in shares],
        out_specs=[pl.BlockSpec((1,) + g_mem.shape[1:], lambda i: (images - 1, 0, 0)), image] + [out(*s) for s in shapes],
        out_shape=[sds(g_mem.shape, f32), sds(g_tags.shape, f32)] + [sds(s, f32) for s in shapes],
        input_output_aliases={0: 0},
        compiler_params=pltpu.CompilerParams(vmem_limit_bytes=62 * MIB),
        name="settle",
    )(g_mem, dkv, wt_cross[width:], g_tags, *shares)


AXES = ("wide", "narrow")
LEADS = (0, 0, 1, 0, 0, 0)


def fold(block, rows, columns):
    if rows % 16 == 0:
        return block
    return block.reshape(block.shape[:-2] + (16, rows * columns // 16))


def per_device(dims, tag_states, image_memory, tag_lengths, w_self, w_cross, w_proj, w_in, b_in, w_out, ln_gains, biases, out_grad):
    cells = dims + (2,)
    fused = w_self.shape[0] % 16 == 0 and tag_states.shape[0] == 3
    devices = dims[0] * dims[1] * dims[2] * 2
    width = tag_states.shape[2]
    lanes, hidden_lanes = biases.shape[1], b_in.shape[0]
    if fused:
        qkv, ckv, near, far, inv, mix, wt_self, wt_cross, vectors, hidden_bias, full_proj, full_in, full_out = run_opening(
            dims, tag_lengths, tag_states, image_memory, biases, ln_gains, b_in[None], (w_cross, w_self, w_proj, w_in, w_out))
        full_proj, full_in, full_out = full_proj.reshape(2, width, width), full_in.reshape(width, -1), full_out.reshape(-1, width)
        layer_out, g_resid, gmix, g_mem, _, g_one, g_in, g_out, g_vec, g_bin, *kept = run_middle(
            tag_lengths, tag_states, image_memory, out_grad, mix, ckv, wt_cross, full_proj, full_in, full_out, vectors, hidden_bias, True)
        g_tags, *shares, dkv = run_closing(
            dims, tag_states, qkv, near, far, inv, mix, gmix, g_resid, ckv, image_memory, vectors, wt_self, wt_cross, full_proj,
            g_one, g_in, g_out, g_vec, g_bin, kept)
        grad_memory, grad_tags, s_self, s_cross, s_proj, s_in, s_out, s_bin, s_gains, s_biases = run_settle(
            lanes, hidden_lanes, g_mem, dkv, wt_cross, g_tags, shares)
        return layer_out, grad_tags, grad_memory, s_self, s_cross, s_proj, s_in, s_bin[0], s_out, s_gains, s_biases
    small = jnp.concatenate(
        [
            jnp.pad(jnp.concatenate([biases, ln_gains]), ((0, 0), (0, 128 - lanes))),
            jnp.pad(b_in[None], ((0, 2), (0, 128 - hidden_lanes))),
        ]
    )
    shards = (w_self, w_cross, w_proj, w_in, w_out, small)
    gathered = gather(dims, [fold(s, *s.shape[-2:]) for s in shards], LEADS)

    def whole(held, shard):
        lead = shard.shape[:-2]
        rows, columns = shard.shape[-2:]
        return held.reshape(lead + (devices * rows, columns))

    full_self, full_cross, full_proj, full_in, full_out, full_small = [whole(h, s) for h, s in zip(gathered, shards)]
    by_device = full_small.reshape(devices, 16, 128)
    vectors = by_device[:, :, :lanes].transpose(1, 0, 2).reshape(16, width).astype(f32)
    hidden_bias = by_device[:, 13, :hidden_lanes].reshape(1, -1).astype(f32)
    layer_out, grad_tags, grad_memory, g_self, g_cross, g_proj, g_in, g_out, g_vec, g_bin = layer(
        tag_lengths, tag_states, image_memory, out_grad, full_self, full_cross, full_proj, full_in, full_out, vectors, hidden_bias)
    g_small = jnp.pad(g_vec.reshape(16, devices, lanes).transpose(1, 0, 2)[:, :13], ((0, 0), (0, 0), (0, 128 - lanes)))
    g_hidden = jnp.pad(g_bin.reshape(devices, 1, hidden_lanes), ((0, 0), (0, 2), (0, 128 - hidden_lanes)))
    g_small = jnp.concatenate([g_small, g_hidden], 1).astype(bf16).reshape(devices * 16, 128)

    def parts(grad, shard):
        lead = shard.shape[:-2]
        rows, columns = shard.shape[-2:]
        return fold(grad.reshape(lead + cells + (rows, columns)), rows, columns)

    shards = (w_self, w_cross, w_proj, w_in, w_out, jax.ShapeDtypeStruct((16, 128), bf16))
    shares = scatter(dims, [parts(g, s) for g, s in zip((g_self, g_cross, g_proj, g_in, g_out, g_small), shards)], LEADS)
    s_self, s_cross, s_proj, s_in, s_out, s_small = [v.reshape(s.shape) for v, s in zip(shares, shards)]
    return (layer_out, grad_tags, grad_memory, s_self, s_cross, s_proj, s_in, s_small[13, :hidden_lanes], s_out,
            s_small[10:13, :lanes], s_small[:10, :lanes])


def solution(mesh):
    dims = grid_of(mesh.shape["wide"], mesh.shape["narrow"])
    rows, matrix, stack, columns = P(AXES, None, None), P(AXES, None), P(None, AXES, None), P(None, AXES)
    return jax.shard_map(
        functools.partial(per_device, dims),
        mesh=mesh,
        in_specs=(rows, rows, P(AXES), matrix, matrix, stack, matrix, P(AXES), matrix, columns, columns, rows),
        out_specs=(rows, rows, rows, matrix, matrix, stack, matrix, P(AXES), matrix, columns, columns),
        check_vma=False,
    )
```

```python
import functools

import jax
import jax.numpy as jnp
from jax import lax
from jax.experimental import pallas as pl
from jax.experimental.pallas import tpu as pltpu
from jax.sharding import PartitionSpec as P


MESH = pl.DeviceIdType.MESH
f32, bf16 = jnp.float32, jnp.bfloat16


def grid_of(mesh_wide, mesh_narrow):
    outer = 4
    return outer, mesh_wide // outer, mesh_narrow // 2


def place(dims):
    outer, inner, across = dims
    wide, narrow = lax.axis_index("wide"), lax.axis_index("narrow")
    return wide // inner, lax.rem(wide, inner), narrow // 2, lax.rem(narrow, 2)


def device(dims, a, b, x, c):
    return {"wide": a * dims[1] + b, "narrow": x * 2 + c}


def greet(dims, me):
    a, b, x, c = me
    outer, inner, across = dims
    barrier = pltpu.get_barrier_semaphore()
    peers = [(lax.rem(a + k, outer), b, x, c) for k in range(1, outer)]
    peers += [(a, lax.rem(b + k, inner), x, c) for k in range(1, inner)]
    peers += [(a, b, lax.rem(x + k, across), c) for k in range(1, across)]
    peers += [(a, b, x, 1 - c)]
    for peer in peers:
        pl.semaphore_signal(barrier, inc=1, device_id=device(dims, *peer), device_id_type=MESH)
    pl.semaphore_wait(barrier, len(peers))


ALL = slice(None)


def gather_kernel(dims, leads, *refs):
    count = len(leads)
    shards, outs = refs[:count], refs[count : 2 * count]
    local_sem, send_sem, recv_sem = refs[2 * count :]
    outer, inner, across = dims
    me = place(dims)
    a, b, x, c = me
    greet(dims, me)

    def cell(ref, lead, *index):
        return ref.at[(ALL,) * lead + index]

    def remote(g, slot, src, dst, peer):
        return pltpu.make_async_remote_copy(
            src_ref=src, dst_ref=dst, send_sem=send_sem.at[g, slot], recv_sem=recv_sem.at[g, slot],
            device_id=device(dims, *peer), device_id_type=MESH)

    n_in, n_ac = inner - 1, across - 1

    def first(g):
        lead = leads[g]
        mine = cell(outs[g], lead, a, b, x, c)
        return [remote(g, k - 1, shards[g], mine, (lax.rem(a + k, outer), b, x, c)) for k in range(1, outer)]

    def keep(g):
        return pltpu.make_async_copy(shards[g], cell(outs[g], leads[g], a, b, x, c), local_sem.at[g])

    base = outer - 1

    def via_inner(g, core):
        lead = leads[g]
        column = ALL if core == 0 else x
        piece = cell(outs[g], lead, ALL, b, column, c)
        return [remote(g, base + k - 1, piece, piece, (a, lax.rem(b + k, inner), x, c)) for k in range(1, inner)]

    def via_across(g, core):
        lead = leads[g]
        row = b if core == 0 else ALL
        piece = cell(outs[g], lead, ALL, row, x, c)
        return [remote(g, base + n_in + k - 1, piece, piece, (a, b, lax.rem(x + k, across), c)) for k in range(1, across)]

    share = base + n_in + n_ac

    def to_partner(g, core, holder):
        lead = leads[g]
        def piece(slot, row, column):
            ref = cell(outs[g], lead, ALL, row, column, holder)
            return remote(g, share + slot, ref, ref, (a, b, x, 1 - c))
        own = [piece(0, b, x)]
        by_inner = [piece(1 + k - 1, lax.rem(b + k, inner), ALL if core == 0 else x) for k in range(1, inner)]
        by_across = [piece(1 + n_in + k - 1, b if core == 0 else ALL, lax.rem(x + k, across)) for k in range(1, across)]
        return (own, by_across, by_inner) if core == 0 else (own, by_inner, by_across)

    def start(copies):
        for copy in copies:
            copy.start()

    def arrived(copies):
        for copy in copies:
            copy.wait_recv()

    for g in range(count):
        keep(g).start()
        start(first(g))

    def body(core):
        second, third = (via_across, via_inner) if core == 0 else (via_inner, via_across)
        for step in range(count + 2):
            g = step
            if g < count:
                keep(g).wait()
                arrived(first(g))
                start(second(g, core))
                start(to_partner(g, core, c)[0])
            g = step - 1
            if 0 <= g < count:
                arrived(second(g, core))
                start(third(g, core))
                start(to_partner(g, core, c)[1])
            g = step - 2
            if 0 <= g < count:
                arrived(third(g, core))
                start(to_partner(g, core, c)[2])
        for g in range(count):
            for group in to_partner(g, 1 - core, 1 - c):
                arrived(group)
        for g in range(count):
            for copy in first(g) + second(g, core) + third(g, core):
                copy.wait_send()
            for group in to_partner(g, core, c):
                for copy in group:
                    copy.wait_send()

    @pl.when(c == 0)
    def _():
        body(0)

    @pl.when(c == 1)
    def _():
        body(1)


def gather(dims, shards, leads):
    outer, inner, across = dims
    def shape(s, lead):
        return jax.ShapeDtypeStruct(s.shape[:lead] + (outer, inner, across, 2) + s.shape[lead:], s.dtype)
    slots = (outer - 1) + 2 * (inner - 1) + 2 * (across - 1) + 1
    n = len(shards)
    return pl.pallas_call(
        functools.partial(gather_kernel, dims, leads),
        out_shape=[shape(s, l) for s, l in zip(shards, leads)],
        in_specs=[pl.BlockSpec(memory_space=pl.ANY)] * n,
        out_specs=[pl.BlockSpec(memory_space=pl.ANY)] * n,
        scratch_shapes=[pltpu.SemaphoreType.DMA((n,)), pltpu.SemaphoreType.DMA((n, slots)), pltpu.SemaphoreType.DMA((n, slots))],
        compiler_params=pltpu.CompilerParams(collective_id=0, has_side_effects=True),
        name="gather_weights",
    )(*shards)


def scatter_kernel(dims, leads, *refs):
    count = len(leads)
    grads, outs = refs[:count], refs[count : 2 * count]
    rest = refs[2 * count :]
    r0, r1i, r1a, r2a, r2i, r3 = (rest[k * count : (k + 1) * count] for k in range(6))
    send_sem, recv_sem = rest[6 * count :]
    outer, inner, across = dims
    me = place(dims)
    a, b, x, c = me
    greet(dims, me)
    n_in, n_ac = inner - 1, across - 1

    def cell(ref, lead, *index):
        return ref.at[(ALL,) * lead + index]

    def remote(g, slot, src, dst, peer):
        return pltpu.make_async_remote_copy(
            src_ref=src, dst_ref=dst, send_sem=send_sem.at[g, slot], recv_sem=recv_sem.at[g, slot],
            device_id=device(dims, *peer), device_id_type=MESH)

    def swap(g):
        return [remote(g, 0, cell(grads[g], leads[g], ALL, ALL, ALL, 1 - c), r0[g], (a, b, x, 1 - c))]

    def via_inner(g, core):
        lead = leads[g]
        res = []
        for k in range(1, inner):
            peer = lax.rem(b + k, inner)
            if core == 0:
                src, dst = cell(r0[g], lead, ALL, peer), r1i[g].at[k - 1]
            else:
                src, dst = cell(r1a[g].at[0], lead, ALL, peer), r2i[g].at[k - 1]
            res.append(remote(g, k, src, dst, (a, peer, x, c)))
        return res

    def via_across(g, core):
        lead = leads[g]
        res = []
        for k in range(1, across):
            peer = lax.rem(x + k, across)
            if core == 1:
                src, dst = cell(r0[g], lead, ALL, ALL, peer), r1a[g].at[k - 1]
            else:
                src, dst = cell(r1i[g].at[0], lead, ALL, peer), r2a[g].at[k - 1]
            res.append(remote(g, 1 + n_in + k - 1, src, dst, (a, b, peer, c)))
        return res

    def last(g, core):
        lead = leads[g]
        held = (r2a if core == 0 else r2i)[g].at[0]
        res = []
        for k in range(1, outer):
            peer = lax.rem(a + k, outer)
            res.append(remote(g, 1 + n_in + n_ac + k - 1, cell(held, lead, peer), r3[g].at[k - 1], (peer, b, x, c)))
        return res

    def start(copies):
        for copy in copies:
            copy.start()

    def arrived(copies):
        for copy in copies:
            copy.wait_recv()

    def up(v):
        return v.astype(f32)

    for g in range(count):
        start(swap(g))

    def body(core):
        second, third = (via_inner, via_across) if core == 0 else (via_across, via_inner)
        def at(lead, *index):
            return (ALL,) * lead + index
        for step in range(count + 3):
            g = step
            if g < count:
                arrived(swap(g))
                lead = leads[g]
                r0[g][...] = (up(grads[g][at(lead, ALL, ALL, ALL, c)]) + up(r0[g][...])).astype(bf16)
                start(second(g, core))
            g = step - 1
            if 0 <= g < count:
                arrived(second(g, core))
                lead = leads[g]
                if core == 0:
                    total = up(r0[g][at(lead, ALL, b)])
                    held = r1i[g]
                else:
                    total = up(r0[g][at(lead, ALL, ALL, x)])
                    held = r1a[g]
                for k in range(held.shape[0]):
                    total = total + up(held[k])
                held[0] = total.astype(bf16)
                start(third(g, core))
            g = step - 2
            if 0 <= g < count:
                arrived(third(g, core))
                lead = leads[g]
                if core == 0:
                    total = up(r1i[g][(0,) + at(lead, ALL, x)])
                    held = r2a[g]
                else:
                    total = up(r1a[g][(0,) + at(lead, ALL, b)])
                    held = r2i[g]
                for k in range(held.shape[0]):
                    total = total + up(held[k])
                held[0] = total.astype(bf16)
                start(last(g, core))
            g = step - 3
            if 0 <= g < count:
                arrived(last(g, core))
                lead = leads[g]
                held = (r2a if core == 0 else r2i)[g]
                total = up(held[(0,) + at(lead, a)])
                for k in range(outer - 1):
                    total = total + up(r3[g][k])
                outs[g][...] = total
        for g in range(count):
            for copy in swap(g) + second(g, core) + third(g, core) + last(g, core):
                copy.wait_send()

    @pl.when(c == 0)
    def _():
        body(0)

    @pl.when(c == 1)
    def _():
        body(1)


def scatter(dims, grads, leads):
    outer, inner, across = dims
    n = len(grads)
    outs, shapes = [], [[] for _ in range(6)]
    for g, lead in zip(grads, leads):
        head, tail = g.shape[:lead], g.shape[lead + 4 :]
        outs.append(jax.ShapeDtypeStruct(head + tail, f32))
        shapes[0].append(head + (outer, inner, across) + tail)
        shapes[1].append((inner - 1,) + head + (outer, across) + tail)
        shapes[2].append((across - 1,) + head + (outer, inner) + tail)
        shapes[3].append((across - 1,) + head + (outer,) + tail)
        shapes[4].append((inner - 1,) + head + (outer,) + tail)
        shapes[5].append((outer - 1,) + head + tail)
    slots = 1 + (inner - 1) + (across - 1) + (outer - 1)
    return pl.pallas_call(
        functools.partial(scatter_kernel, dims, leads),
        out_shape=outs,
        in_specs=[pl.BlockSpec(memory_space=pltpu.VMEM)] * n,
        out_specs=[pl.BlockSpec(memory_space=pltpu.VMEM)] * n,
        scratch_shapes=[pltpu.VMEM(s, bf16) for group in shapes for s in group]
        + [pltpu.SemaphoreType.DMA((n, slots)), pltpu.SemaphoreType.DMA((n, slots))],
        compiler_params=pltpu.CompilerParams(collective_id=1, has_side_effects=True, vmem_limit_bytes=48 * 2**20),
        name="scatter_grads",
    )(*grads)

HEADS, HEAD_DIM = 8, 64
EPS = 1e-5
MASKED = -1e9
TAME = 30.0
CHUNKS = 1
MIB = 2**20


def dot(left, right, left_dim, right_dim):
    return lax.dot_general(left, right, (((left_dim,), (right_dim,)), ((), ())), preferred_element_type=f32)


def full(shape):
    return pl.BlockSpec(shape, lambda i: (0,) * len(shape))


def image(shape):
    return pl.BlockSpec((1,) + shape, lambda i: (i,) + (0,) * len(shape))


def with_ones(rows):
    return jnp.concatenate([rows, jnp.ones((16, rows.shape[1]), bf16)], 0)


def with_delta(rows, delta):
    high = delta.astype(bf16).astype(f32)
    low = delta - high
    at = lax.broadcasted_iota(jnp.int32, (16, rows.shape[1]), 0)
    extra = jnp.where(at == 0, -high, jnp.where(at == 1, -low, 0.0))
    return jnp.concatenate([rows, extra.astype(bf16)], 0)


def self_forward(lens, x_ref, mem_ref, w_self, w_cross, bias_qkv, bias_kv,
                 qkv_ref, ckv_ref, near_ref, far_ref, inv_ref, mix_ref, wt_self, wt_cross):
    width = x_ref.shape[2]
    tags = x_ref.shape[1]
    half = tags // 2
    i = pl.program_id(0)

    @pl.when(i == 0)
    def _():
        wt_self[...] = w_self[...].T
        wt_cross[...] = w_cross[...].T

    ckv = dot(wt_cross[width:], mem_ref[0], 1, 1) + bias_kv[...]
    ckv_ref[0] = ckv.astype(bf16).reshape(ckv_ref.shape[1:])
    qkv = dot(wt_self[...], x_ref[0], 1, 1) + bias_qkv[...]
    q = qkv[:width].astype(bf16) * bf16(HEAD_DIM ** -0.5)
    qkv_ref[0, :HEADS] = q.reshape(HEADS, HEAD_DIM, tags)
    qkv_ref[0, HEADS:] = qkv[width:].astype(bf16).reshape(2 * HEADS, HEAD_DIM, tags)
    last = lens[i] - 1

    def head(h, _):
        qt, kt, vt = qkv_ref[0, h], qkv_ref[0, HEADS + h], with_ones(qkv_ref[0, 2 * HEADS + h])

        def part(keys, first, out):
            s = dot(kt[:, :keys], qt[:, first : first + half], 0, 0)
            key_at = lax.broadcasted_iota(jnp.int32, (keys, half), 0)
            query_at = lax.broadcasted_iota(jnp.int32, (1, half), 1) + first
            s = jnp.where(key_at <= jnp.minimum(query_at, last), s, MASKED)
            e = jnp.exp(s - jnp.max(s, 0, keepdims=True)).astype(bf16)
            out[0, h] = e
            mixed = dot(vt[:, :keys], e, 1, 0)
            inv = 1.0 / mixed[HEAD_DIM : HEAD_DIM + 1]
            inv_ref[0, pl.ds(h, 1), first : first + half] = inv
            mix_ref[0, h, :, first : first + half] = (mixed[:HEAD_DIM] * inv).astype(bf16)

        part(half, 0, near_ref)
        part(tags, half, far_ref)
        return 0

    lax.fori_loop(0, HEADS, head, 0)


def run_self_forward(lens, x, mem, w_self, w_cross, bias_qkv, bias_kv):
    images, tags, width = x.shape
    cells = mem.shape[1]
    half = tags // 2
    sds = jax.ShapeDtypeStruct
    return pl.pallas_call(
        self_forward,
        grid_spec=pltpu.PrefetchScalarGridSpec(
            num_scalar_prefetch=1,
            grid=(images,),
            in_specs=[pl.BlockSpec((1, tags, width), lambda i, n: (i, 0, 0)), pl.BlockSpec((1, cells, width), lambda i, n: (i, 0, 0))]
            + [pl.BlockSpec(v.shape, lambda i, n: (0, 0)) for v in (w_self, w_cross, bias_qkv, bias_kv)],
            out_specs=[
                pl.BlockSpec((1, 3 * HEADS, HEAD_DIM, tags), lambda i, n: (i, 0, 0, 0)),
                pl.BlockSpec((1, 2 * HEADS, HEAD_DIM, cells), lambda i, n: (i, 0, 0, 0)),
                pl.BlockSpec((1, HEADS, half, half), lambda i, n: (i, 0, 0, 0)),
                pl.BlockSpec((1, HEADS, tags, half), lambda i, n: (i, 0, 0, 0)),
                pl.BlockSpec((1, HEADS, tags), lambda i, n: (i, 0, 0)),
                pl.BlockSpec((1, HEADS, HEAD_DIM, tags), lambda i, n: (i, 0, 0, 0)),
                pl.BlockSpec((3 * width, width), lambda i, n: (0, 0)),
                pl.BlockSpec((3 * width, width), lambda i, n: (0, 0)),
            ],
        ),
        out_shape=[
            sds((images, 3 * HEADS, HEAD_DIM, tags), bf16),
            sds((images, 2 * HEADS, HEAD_DIM, cells), bf16),
            sds((images, HEADS, half, half), bf16),
            sds((images, HEADS, tags, half), bf16),
            sds((images, HEADS, tags), f32),
            sds((images, HEADS, HEAD_DIM, tags), bf16),
            sds((3 * width, width), bf16),
            sds((3 * width, width), bf16),
        ],
        compiler_params=pltpu.CompilerParams(vmem_limit_bytes=58 * MIB),
        name="self_forward",
    )(lens, x, mem, w_self, w_cross, bias_qkv, bias_kv)


def norm(resid):
    centred = resid - jnp.mean(resid, -1, keepdims=True)
    scale = lax.rsqrt(jnp.mean(centred * centred, -1, keepdims=True) + EPS)
    return centred * scale, scale


def norm_back(grad, normed, scale, gain):
    scaled = grad * gain
    mean_one = jnp.mean(scaled, -1, keepdims=True)
    mean_two = jnp.mean(scaled * normed, -1, keepdims=True)
    return scale * (scaled - mean_one - normed * mean_two)


def column_sums(rows):
    return jnp.sum(rows, 0, keepdims=True)


def lane_groups(rows):
    total = rows[:, :128]
    for k in range(1, rows.shape[1] // 128):
        total = total + rows[:, 128 * k : 128 * (k + 1)]
    return total


def cross_back(h, e, keys, values, queries, grad, mixed, inv):
    grad = grad.astype(f32)
    delta = jnp.sum(grad * mixed.astype(f32), 0, keepdims=True) * inv
    grad = (grad * inv).astype(bf16)
    dp = dot(with_ones(values), with_delta(grad, delta), 0, 0)
    ds = e * dp.astype(bf16)
    dv = dot(grad, e, 1, 1).astype(bf16)
    dk = dot(queries, ds, 1, 1).astype(bf16)
    dq = (dot(keys, ds, 1, 0) * HEAD_DIM ** -0.5).astype(bf16)
    return dq, dk, dv


def memory_lanes(rows):
    cells = rows.shape[1]
    body = cells // 128 * 128
    total = lane_groups(rows[:, :body])
    if body < cells:
        total = total + jnp.concatenate([rows[:, body:], jnp.zeros((rows.shape[0], 128 - cells + body), f32)], 1)
    return total


def middle(held_back, lens, x_ref, mem_ref, gout_ref, mix_one, ckv_ref, wt_cross, w_proj, w_in, w_out, vectors, b_in,
           out_ref, g_resid, g_mix, g_mem, gw_cross, gw_proj, gw_in, gw_out, g_vec, g_bin, *rest):
    if held_back:
        o_scale, o_e, o_q, o_inv, o_mix, o_gmix, o_one, o_two, o_cross, o_proj = rest[:10]
        gone = rest[-1]
        rest = rest[10:-1]
    middle_body(held_back and (o_scale, o_e, o_q, o_inv, o_mix, o_gmix, o_one, o_two, o_cross, o_proj, gone),
                lens, x_ref, mem_ref, gout_ref, mix_one, ckv_ref, wt_cross, w_proj, w_in, w_out, vectors, b_in,
                out_ref, g_resid, g_mix, g_mem, gw_cross, gw_proj, gw_in, gw_out, g_vec, g_bin, *rest)


def middle_body(held_back, lens, x_ref, mem_ref, gout_ref, mix_one, ckv_ref, wt_cross, w_proj, w_in, w_out, vectors, b_in,
           out_ref, g_resid, g_mix, g_mem, gw_cross, gw_proj, gw_in, gw_out, g_vec, g_bin,
           dkv_ref, cols,
           e_ref, q_ref, inv_ref, mix_two, gmix_two, dq_ref, acc_cross, acc_proj, acc_in, acc_out, acc_vec, acc_bin, acc_col,
           n_one, n_two, scale_two, two_low, act, g_inner, g_ff, g_cross, g_two):
    tags, width = x_ref.shape[1:]
    cells = mem_ref.shape[1]
    i = pl.program_id(0)
    count = pl.num_programs(0)

    @pl.when(i == 0)
    def _():
        for ref in (acc_cross, acc_proj, acc_in, acc_out, acc_vec, acc_bin, acc_col):
            ref[...] = jnp.zeros_like(ref)
        cols[...] = vectors[...].T

    def vec(k):
        return vectors[k : k + 1, :]

    def add(k, value):
        acc_vec[k : k + 1, :] += value

    if held_back:
        scale_out, *places, gone = held_back
        sources = (e_ref, q_ref, inv_ref, mix_two, gmix_two, n_one, g_two, acc_cross, acc_proj.at[0])
        copies = [pltpu.make_async_copy(src, dst, gone.at[k]) for k, (src, dst) in enumerate(zip(sources, places))]

    def leave(*numbers):
        if held_back:
            @pl.when(i == count - 1)
            def _():
                for number in numbers:
                    copies[number].start()

    leave(7, 8)
    mix_one_t = mix_one[0].reshape(width, tags)
    resid = x_ref[0].astype(f32) + dot(mix_one_t, w_proj[0], 0, 0) + vec(2)
    normed, scale_one = norm(resid)
    n_one[...] = normed
    one = normed * vec(10) + vec(6)
    one_low = one.astype(bf16)
    cq = (dot(wt_cross[:width], one_low, 1, 1) + cols[:, 3:4]).astype(bf16) * bf16(HEAD_DIM ** -0.5)
    q_ref[...] = cq.reshape(q_ref.shape)
    leave(1, 5)

    keys = ckv_ref[0, :HEADS].astype(f32)
    queries = q_ref[...].astype(f32)
    bound = jnp.max(jnp.sum(keys * keys, 1)) * jnp.max(jnp.sum(queries * queries, 1))
    tame = bound < TAME * TAME

    def forward(shifted, h, _):
        s = dot(ckv_ref[0, h], q_ref[h], 0, 0)
        if shifted:
            s = s - jnp.max(s, 0, keepdims=True)
        e = jnp.exp(s).astype(bf16)
        e_ref[h] = e
        mixed = dot(with_ones(ckv_ref[0, HEADS + h]), e, 1, 0)
        inv = 1.0 / mixed[HEAD_DIM : HEAD_DIM + 1]
        inv_ref[pl.ds(h, 1), :] = inv
        mix_two[h] = (mixed[:HEAD_DIM] * inv).astype(bf16)
        return 0

    @pl.when(tame)
    def _():
        lax.fori_loop(0, HEADS, functools.partial(forward, False), 0, unroll=4)

    @pl.when(jnp.logical_not(tame))
    def _():
        lax.fori_loop(0, HEADS, functools.partial(forward, True), 0)

    leave(0, 2, 3)
    mix_two_t = mix_two[...].reshape(width, tags)
    root = 0.7978845608028654
    rows = tags // CHUNKS
    totals = {}

    def tally(k, value):
        totals[k] = totals[k] + column_sums(value) if k in totals else column_sums(value)

    for first in range(0, tags, rows):
        at = slice(first, first + rows)
        resid = n_one[at] * vec(10) + vec(6) + dot(mix_two_t[:, at], w_proj[1], 0, 0) + vec(5)
        normed, scale = norm(resid)
        n_two[at] = normed
        scale_two[at] = scale
        two = normed * vec(11) + vec(7)
        two_low[at] = two.astype(bf16)
        inner = dot(two_low[at], w_in[...], 1, 0) + b_in[...]
        square = inner * inner
        tanh = jnp.tanh(inner * (root + (root * 0.044715) * square))
        half_more = 0.5 + 0.5 * tanh
        act[at] = (inner * half_more).astype(bf16)
        slope = half_more + inner * (half_more * (1.0 - tanh)) * (root + (3 * 0.044715 * root) * square)
        resid = two + dot(act[at], w_out[...], 1, 0) + vec(9)
        three, scale = norm(resid)
        valid = lax.broadcasted_iota(jnp.int32, (rows, 1), 0) + first < lens[i]
        out_ref[0, at] = jnp.where(valid, three * vec(12) + vec(8), 0.0).astype(bf16)
        grad = jnp.where(valid, gout_ref[0, at].astype(f32), 0.0)
        tally(12, grad * three)
        tally(8, grad)
        g_three = norm_back(grad, three, scale, vec(12))
        g_ff[at] = g_three.astype(bf16)
        tally(9, g_three)
        back = dot(g_ff[at], w_out[...], 1, 1) * slope
        tally(-1, back)
        g_inner[at] = back.astype(bf16)
        back = g_three + dot(g_inner[at], w_in[...], 1, 1)
        tally(11, back * n_two[at])
        tally(7, back)
        back = norm_back(back, n_two[at], scale_two[at], vec(11))
        tally(5, back)
        g_two[at] = back
        g_cross[at] = back.astype(bf16)

    for k, value in totals.items():
        if k >= 0:
            add(k, value)
    acc_bin[...] += totals[-1]
    acc_out[...] += dot(act[...], g_ff[...], 0, 0)
    acc_in[...] += dot(two_low[...], g_inner[...], 0, 0)
    acc_proj[1] += dot(mix_two_t, g_cross[...], 1, 0)
    gmix_two[...] = dot(w_proj[1], g_cross[...], 1, 1).astype(bf16).reshape(gmix_two.shape)

    def rest_of_image():
        def backward(h, _):
            dq_ref[h], dkv_ref[h], dkv_ref[HEADS + h] = cross_back(
                h, e_ref[h], ckv_ref[0, h], ckv_ref[0, HEADS + h], q_ref[h], gmix_two[h], mix_two[h], inv_ref[pl.ds(h, 1), :])
            return 0

        lax.fori_loop(0, HEADS, backward, 0, unroll=4)
        dq = dq_ref[...].reshape(width, tags)
        dkv = dkv_ref[...].reshape(2 * width, cells)
        acc_col[0] += lane_groups(dq.astype(f32))
        acc_col[1] += memory_lanes(dkv[width:].astype(f32))
        acc_cross[:width] += dot(dq, one_low, 1, 0)
        acc_cross[width:] += dot(dkv, mem_ref[0], 1, 0)
        g_mem[0] = dot(dkv, wt_cross[width:], 0, 0)
        g_one = g_two[...] + dot(dq, wt_cross[:width], 0, 0)
        add(10, column_sums(g_one * n_one[...]))
        add(6, column_sums(g_one))
        g_one = norm_back(g_one, n_one[...], scale_one, vec(10))
        add(2, column_sums(g_one))
        g_resid[0] = g_one
        g_low = g_one.astype(bf16)
        acc_proj[0] += dot(mix_one_t, g_low, 1, 0)
        g_mix[0] = dot(w_proj[0], g_low, 1, 1).astype(bf16).reshape(g_mix.shape[1:])

    if held_back:
        pl.when(i < count - 1)(rest_of_image)

        @pl.when(i == count - 1)
        def _():
            scale_out[...] = scale_one

        leave(4, 6)
    else:
        rest_of_image()

    @pl.when(i == count - 1)
    def _():
        if held_back:
            gw_proj[...] = acc_proj[1].astype(bf16)
        else:
            gw_cross[...] = acc_cross[...].astype(bf16).T
            gw_proj[...] = acc_proj[...].astype(bf16)
        gw_in[...] = acc_in[...].astype(bf16)
        gw_out[...] = acc_out[...].astype(bf16)
        add(3, column_sums(acc_col[0].T))
        add(4, column_sums(acc_col[1].T))
        g_vec[...] = acc_vec[...]
        g_bin[...] = acc_bin[...]
        if held_back:
            for copy in copies:
                copy.wait()


def run_middle(lens, x, mem, gout, mix_one, ckv, wt_cross, w_proj, w_in, w_out, vectors, b_in, held_back=False):
    images, tags, width = x.shape
    cells = mem.shape[1]
    hidden = w_in.shape[1]
    sds = jax.ShapeDtypeStruct

    def per(*shape):
        return pl.BlockSpec((1,) + shape, lambda i, n: (i,) + (0,) * len(shape))

    def one(*shape):
        return pl.BlockSpec(shape, lambda i, n: (0,) * len(shape), pipeline_mode=pl.Buffered(1))

    def out(*shape):
        return pl.BlockSpec(shape, lambda i, n: (0,) * len(shape))

    def early(*shape):
        return pl.BlockSpec((1,) + shape, lambda i, n: (jnp.minimum(i, images - 2),) + (0,) * len(shape)) if held_back else per(*shape)

    done = images - 1 if held_back else images
    out_specs = [
        per(tags, width), early(tags, width), early(HEADS, HEAD_DIM, tags), early(cells, width),
        out(width, 3 * width), out(2, width, width), out(width, hidden), out(hidden, width), out(16, width), out(1, hidden),
    ]
    out_shape = [
        sds((images, tags, width), bf16), sds((done, tags, width), f32), sds((done, HEADS, HEAD_DIM, tags), bf16),
        sds((images, cells, width), f32),
        sds((width, 3 * width), bf16), sds((2, width, width), bf16), sds((width, hidden), bf16), sds((hidden, width), bf16),
        sds((16, width), f32), sds((1, hidden), f32),
    ]
    scratch = [
        pltpu.VMEM((2 * HEADS, HEAD_DIM, cells), bf16),
        pltpu.VMEM((width, 16), f32),
        pltpu.VMEM((HEADS, cells, tags), bf16),
        pltpu.VMEM((HEADS, HEAD_DIM, tags), bf16),
        pltpu.VMEM((HEADS, tags), f32),
        pltpu.VMEM((HEADS, HEAD_DIM, tags), bf16),
        pltpu.VMEM((HEADS, HEAD_DIM, tags), bf16),
        pltpu.VMEM((HEADS, HEAD_DIM, tags), bf16),
        pltpu.VMEM((3 * width, width), f32),
        pltpu.VMEM((2, width, width), f32),
        pltpu.VMEM((width, hidden), f32),
        pltpu.VMEM((hidden, width), f32),
        pltpu.VMEM((16, width), f32),
        pltpu.VMEM((1, hidden), f32),
        pltpu.VMEM((2, width, 128), f32),
        pltpu.VMEM((tags, width), f32),
        pltpu.VMEM((tags, width), f32),
        pltpu.VMEM((tags, 1), f32),
        pltpu.VMEM((tags, width), bf16),
        pltpu.VMEM((tags, hidden), bf16),
        pltpu.VMEM((tags, hidden), bf16),
        pltpu.VMEM((tags, width), bf16),
        pltpu.VMEM((tags, width), bf16),
        pltpu.VMEM((tags, width), f32),
    ]
    if held_back:
        out_specs[4], out_shape[4] = out(8, 128), sds((8, 128), bf16)
        out_specs[5], out_shape[5] = out(width, width), sds((width, width), bf16)
        kept = [((HEADS, cells, tags), bf16), ((HEADS, HEAD_DIM, tags), bf16), ((HEADS, tags), f32), ((HEADS, HEAD_DIM, tags), bf16),
                ((HEADS, HEAD_DIM, tags), bf16), ((tags, width), f32), ((tags, width), f32), ((3 * width, width), f32), ((width, width), f32)]
        out_specs += [out(tags, 1)] + [pl.BlockSpec(memory_space=pl.ANY)] * len(kept)
        out_shape += [sds((tags, 1), f32)] + [sds(*k) for k in kept]
        scratch.append(pltpu.SemaphoreType.DMA((len(kept),)))
    return pl.pallas_call(
        functools.partial(middle, held_back),
        grid_spec=pltpu.PrefetchScalarGridSpec(
            num_scalar_prefetch=1,
            grid=(images,),
            in_specs=[
                per(tags, width), per(cells, width), per(tags, width), per(HEADS, HEAD_DIM, tags), per(2 * HEADS, HEAD_DIM, cells),
                one(3 * width, width), one(2, width, width), one(width, hidden), one(hidden, width), one(16, width), one(1, hidden),
            ],
            out_specs=out_specs,
            scratch_shapes=scratch,
        ),
        out_shape=out_shape,
        compiler_params=pltpu.CompilerParams(vmem_limit_bytes=62 * MIB),
        name="middle",
    )(lens, x, mem, gout, mix_one, ckv, wt_cross, w_proj, w_in, w_out, vectors, b_in)


def self_backward(x_ref, qkv_ref, near_ref, far_ref, inv_ref, mix_ref, gmix_ref, g_resid, wt_self,
                  g_tags, gw_self, g_col, d_ref, acc, acc_col):
    tags, width = x_ref.shape[1:]
    half = tags // 2
    i = pl.program_id(0)

    @pl.when(i == 0)
    def _():
        acc[...] = jnp.zeros_like(acc)
        acc_col[...] = jnp.zeros_like(acc_col)

    def head(h, _):
        grad = gmix_ref[0, h].astype(f32)
        inv = inv_ref[0, pl.ds(h, 1), :]
        delta = jnp.sum(grad * mix_ref[0, h].astype(f32), 0, keepdims=True) * inv
        grad = (grad * inv).astype(bf16)
        ext = with_delta(grad, delta)
        qt, kt, vt = qkv_ref[0, h], qkv_ref[0, HEADS + h], with_ones(qkv_ref[0, 2 * HEADS + h])
        near, far = near_ref[0, h], far_ref[0, h]
        ds_near = near * dot(vt[:, :half], ext[:, :half], 0, 0).astype(bf16)
        ds_far = far * dot(vt, ext[:, half:], 0, 0).astype(bf16)
        dv = dot(grad[:, half:], far, 1, 1)
        dk = dot(qt[:, half:], ds_far, 1, 1)
        d_ref[2 * HEADS + h, :, half:] = dv[:, half:].astype(bf16)
        d_ref[2 * HEADS + h, :, :half] = (dv[:, :half] + dot(grad[:, :half], near, 1, 1)).astype(bf16)
        d_ref[HEADS + h, :, half:] = dk[:, half:].astype(bf16)
        d_ref[HEADS + h, :, :half] = (dk[:, :half] + dot(qt[:, :half], ds_near, 1, 1)).astype(bf16)
        d_ref[h, :, :half] = (dot(kt[:, :half], ds_near, 1, 0) * HEAD_DIM ** -0.5).astype(bf16)
        d_ref[h, :, half:] = (dot(kt, ds_far, 1, 0) * HEAD_DIM ** -0.5).astype(bf16)
        return 0

    lax.fori_loop(0, HEADS, head, 0)
    d = d_ref[...].reshape(3 * width, tags)
    acc_col[0] += lane_groups(d[:width].astype(f32))
    acc_col[1] += lane_groups(d[2 * width :].astype(f32))
    acc[...] += dot(d, x_ref[0], 1, 0)
    g_tags[0] = g_resid[0] + dot(d, wt_self[...], 0, 0)

    @pl.when(i == pl.num_programs(0) - 1)
    def _():
        gw_self[...] = acc[...].astype(bf16).T
        g_col[0:1] = column_sums(acc_col[0].T)
        g_col[1:2] = column_sums(acc_col[1].T)


def run_self_backward(x, qkv, near, far, inv, mix, gmix, g_resid, wt_self):
    images, tags, width = x.shape
    half = tags // 2
    sds = jax.ShapeDtypeStruct

    def per(*shape):
        return pl.BlockSpec((1,) + shape, lambda i: (i,) + (0,) * len(shape))

    def one(*shape):
        return pl.BlockSpec(shape, lambda i: (0,) * len(shape))

    return pl.pallas_call(
        self_backward,
        grid=(images,),
        in_specs=[per(tags, width), per(3 * HEADS, HEAD_DIM, tags), per(HEADS, half, half), per(HEADS, tags, half), per(HEADS, tags),
                  per(HEADS, HEAD_DIM, tags), per(HEADS, HEAD_DIM, tags), per(tags, width),
                  one(3 * width, width)],
        out_specs=[per(tags, width), one(width, 3 * width), one(8, width)],
        out_shape=[sds((images, tags, width), f32), sds((width, 3 * width), bf16), sds((8, width), f32)],
        scratch_shapes=[pltpu.VMEM((3 * HEADS, HEAD_DIM, tags), bf16), pltpu.VMEM((3 * width, width), f32), pltpu.VMEM((2, width, 128), f32)],
        compiler_params=pltpu.CompilerParams(vmem_limit_bytes=60 * MIB),
        name="self_backward",
    )(x, qkv, near, far, inv, mix, gmix, g_resid, wt_self)


def layer(lens, x, mem, gout, w_self, w_cross, w_proj, w_in, w_out, vectors, b_in):
    width = x.shape[2]
    zero = jnp.zeros((width,), f32)
    bias_qkv = jnp.concatenate([vectors[0], zero, vectors[1]])[:, None]
    bias_kv = jnp.concatenate([zero, vectors[4]])[:, None]
    qkv, ckv, near, far, inv, mix, wt_self, wt_cross = run_self_forward(lens, x, mem, w_self, w_cross, bias_qkv, bias_kv)
    out, g_resid, gmix, g_mem, gw_cross, gw_proj, gw_in, gw_out, g_vec, g_bin = run_middle(
        lens, x, mem, gout, mix, ckv, wt_cross, w_proj, w_in, w_out, vectors, b_in)
    g_tags, gw_self, g_col = run_self_backward(x, qkv, near, far, inv, mix, gmix, g_resid, wt_self)
    g_vec = g_vec.at[0:2].set(g_col[0:2])
    return out, g_tags, g_mem, gw_self, gw_cross, gw_proj, gw_in, gw_out, g_vec, g_bin


ALL = slice(None)


SMALL, SELF, PROJ, CROSS, IN, OUT = range(6)
PLAN = (
    ((SMALL, 0), (SELF, 0), (PROJ, 0), (CROSS, 0), (IN, 0), (OUT, 0),
     (SMALL, 1), (SELF, 1), (SMALL, 2), (PROJ, 1), (SELF, 2), (SMALL, 3), (CROSS, 1), (PROJ, 2), (IN, 1), (SELF, 3), (CROSS, 2), (OUT, 1),
     (PROJ, 3), (SMALL, 4), (SELF, 4)),
    ((IN, 2),),
    ((OUT, 2),),
    ((CROSS, 3),),
    ((IN, 3),),
    ((OUT, 3),),
    (),
    ((CROSS, 4),),
    ((PROJ, 4), (IN, 4), (OUT, 4)),
)
MEANTIME = {2: (0, 4), 3: (1, 0), 4: (1, 4), 5: (2, 4)}


class Gathering:
    def __init__(self, dims, me, shard, held, lead, sems):
        self.dims, self.me, self.shard, self.held, self.lead = dims, me, shard, held, lead
        self.local, self.send, self.recv = sems

    def cell(self, *index):
        return self.held.at[(ALL,) * self.lead + index]

    def remote(self, slot, src, dst, peer):
        return pltpu.make_async_remote_copy(
            src_ref=src, dst_ref=dst, send_sem=self.send.at[slot], recv_sem=self.recv.at[slot],
            device_id=device(self.dims, *peer), device_id_type=MESH)

    def keep(self):
        return pltpu.make_async_copy(self.shard, self.cell(*self.me), self.local)

    def first(self):
        a, b, x, c = self.me
        outer = self.dims[0]
        return [self.remote(k - 1, self.shard, self.cell(a, b, x, c), (lax.rem(a + k, outer), b, x, c)) for k in range(1, outer)]

    def along_inner(self, core):
        a, b, x, c = self.me
        outer, inner, _ = self.dims
        piece = self.cell(ALL, b, ALL if core == 0 else x, c)
        return [self.remote(outer - 2 + k, piece, piece, (a, lax.rem(b + k, inner), x, c)) for k in range(1, inner)]

    def along_across(self, core):
        a, b, x, c = self.me
        outer, inner, across = self.dims
        piece = self.cell(ALL, b if core == 0 else ALL, x, c)
        return [self.remote(outer + inner - 3 + k, piece, piece, (a, b, lax.rem(x + k, across), c)) for k in range(1, across)]

    def second(self, core):
        return self.along_across(core) if core == 0 else self.along_inner(core)

    def third(self, core):
        return self.along_inner(core) if core == 0 else self.along_across(core)

    def handed(self, core, holder):
        a, b, x, c = self.me
        outer, inner, across = self.dims
        base = outer + inner + across - 3

        def piece(slot, row, column):
            ref = self.cell(ALL, row, column, holder)
            return self.remote(base + slot, ref, ref, (a, b, x, 1 - c))

        own = [piece(0, b, x)]
        by_inner = [piece(k, lax.rem(b + k, inner), ALL if core == 0 else x) for k in range(1, inner)]
        by_across = [piece(inner - 1 + k, b if core == 0 else ALL, lax.rem(x + k, across)) for k in range(1, across)]
        return (own, by_across, by_inner) if core == 0 else (own, by_inner, by_across)

    def begin(self):
        self.keep().start()
        for copy in self.first():
            copy.start()

    def each_core(self, act):
        for core in (0, 1):
            pl.when(self.me[3] == core)(functools.partial(act, core))

    def advance(self, stage):
        def act(core):
            if stage == 1:
                self.keep().wait()
            for copy in (self.first(), self.second(core), self.third(core))[stage - 1]:
                copy.wait_recv()
            following = (self.second(core), self.third(core), [])[stage - 1]
            for copy in following + self.handed(core, self.me[3])[stage - 1]:
                copy.start()
        self.each_core(act)

    def finish(self):
        def act(core):
            for group in self.handed(1 - core, 1 - self.me[3]):
                for copy in group:
                    copy.wait_recv()
        self.each_core(act)

    def drain(self):
        def act(core):
            for copy in self.first() + self.second(core) + self.third(core) + sum(self.handed(core, self.me[3]), []):
                copy.wait_send()
        self.each_core(act)


def gather_slots(dims):
    outer, inner, across = dims
    return outer + 2 * (inner + across) - 4


def spread(held, row_lanes, width, rows):
    devices = held.shape[0] // 16
    lane = lax.broadcasted_iota(jnp.int32, (128, width), 0)
    at = lax.broadcasted_iota(jnp.int32, (128, width), 1)
    pick = jnp.where((lax.rem(at, row_lanes) == lane), 1.0, 0.0).astype(bf16)
    wide = dot(held, pick, 1, 0)
    owner = lax.broadcasted_iota(jnp.int32, (devices * 16, width), 0) // 16
    at = lax.broadcasted_iota(jnp.int32, (devices * 16, width), 1)
    wide = jnp.where(at // row_lanes == owner, wide, 0.0)
    return jnp.sum(wide.reshape(devices, 16, width), 0)


def opening(dims, lens, x_ref, mem_ref, b_ref, g_ref, h_ref, s_cross, s_self, s_proj, s_in, s_out,
            qkv_ref, ckv_ref, low_ref, high_ref, inv_ref, mix_ref, out_self, out_cross, vec_ref, bin_ref, o_proj, o_in, o_out,
            small, small_low, h_small, h_self, h_cross, wt_self, wt_cross, cols, low_a, high_a, low_b, high_b, tile, beyond, gone, local, send, recv):
    width = x_ref.shape[2]
    tags = x_ref.shape[1]
    half = tags // 2
    step = pl.program_id(0)
    images = pl.num_programs(0) // 2
    me = place(dims)
    pairs = ((small_low, h_small, 0), (s_self, h_self, 0), (s_proj, o_proj, 1), (s_cross, h_cross, 0), (s_in, o_in, 0), (s_out, o_out, 0))
    gs = [Gathering(dims, me, shard, held, lead, (local.at[k], send.at[k], recv.at[k])) for k, (shard, held, lead) in enumerate(pairs)]
    keep_self = pltpu.make_async_copy(wt_self, out_self, gone.at[0])
    keep_cross = pltpu.make_async_copy(wt_cross, out_cross, gone.at[1])

    def play(slot):
        for item, stage in PLAN[slot]:
            item = gs[item]
            item.begin() if stage == 0 else item.finish() if stage == 4 else item.advance(stage)

    def slot_at(number, slot):
        @pl.when(step == number)
        def _():
            play(slot)

    @pl.when(step == 0)
    def _():
        small[...] = jnp.zeros_like(small)
        small[0:10, : b_ref.shape[1]] = b_ref[...].astype(f32)
        small[10:13, : g_ref.shape[1]] = g_ref[...].astype(f32)
        small[13:14, : h_ref.shape[1]] = h_ref[...].astype(f32)
        small_low[...] = small[...].astype(bf16)
        greet(dims, me)
        play(0)
        vectors = spread(h_small[...].reshape(-1, 128), b_ref.shape[1], width, 16)
        vec_ref[...] = vectors
        bin_ref[...] = spread(h_small[...].reshape(-1, 128), h_ref.shape[1], bin_ref.shape[1], 16)[13:14]
        cols[...] = vectors.T
        wt_self[...] = h_self[...].reshape(width, 3 * width).T
        keep_self.start()

    @pl.when(step < images)
    def _():
        qkv = dot(wt_self[...], x_ref[0], 1, 1)
        qkv_ref[0, :HEADS] = ((qkv[:width] + cols[:, 0:1]).astype(bf16) * bf16(HEAD_DIM ** -0.5)).reshape(HEADS, HEAD_DIM, tags)
        qkv_ref[0, HEADS : 2 * HEADS] = qkv[width : 2 * width].astype(bf16).reshape(HEADS, HEAD_DIM, tags)
        qkv_ref[0, 2 * HEADS :] = (qkv[2 * width :] + cols[:, 1:2]).astype(bf16).reshape(HEADS, HEAD_DIM, tags)

    @pl.when(step < images)
    def _():
        key_at, query_at = lax.broadcasted_iota(jnp.int32, (half, half), 0), lax.broadcasted_iota(jnp.int32, (half, half), 1)
        tile[...] = jnp.where(key_at <= query_at, 0.0, MASKED)
        row, key_at = lax.broadcasted_iota(jnp.int32, beyond.shape, 0), lax.broadcasted_iota(jnp.int32, beyond.shape, 1)
        hidden = jnp.logical_and(row == 0, key_at >= lens[jnp.minimum(step, images - 1)])
        beyond[...] = jnp.where(hidden, MASKED, 0.0).astype(bf16)

    def scores(h, low, high):
        qt, kt = with_ones(qkv_ref[0, h]), jnp.concatenate([qkv_ref[0, HEADS + h], beyond[...]], 0)
        s = dot(kt[:, :half], qt, 0, 0)
        left, right = s[:, :half] + tile[...], s[:, half:]
        under = dot(kt[:, half:], qt[:, half:], 0, 0) + tile[...]
        low[:, :half] = left
        low[:, half:] = right
        high[...] = under
        return jnp.max(left, 0, keepdims=True), jnp.maximum(jnp.max(right, 0, keepdims=True), jnp.max(under, 0, keepdims=True))

    def mix(h, low, high, tops):
        vt = with_ones(qkv_ref[0, 2 * HEADS + h])
        e_low = jnp.concatenate([jnp.exp(low[:, :half] - tops[0]).astype(bf16), jnp.exp(low[:, half:] - tops[1]).astype(bf16)], 1)
        e_high = jnp.exp(high[...] - tops[1]).astype(bf16)
        low_ref[0, h] = e_low
        high_ref[0, h] = e_high
        mixed = dot(vt[:, :half], e_low, 1, 0)
        mixed = jnp.concatenate([mixed[:, :half], mixed[:, half:] + dot(vt[:, half:], e_high, 1, 0)], 1)
        inv = 1.0 / mixed[HEAD_DIM : HEAD_DIM + 1]
        inv_ref[0, h : h + 1] = inv
        mix_ref[0, h] = (mixed[:HEAD_DIM] * inv).astype(bf16)

    def pair(h, tops):
        following = scores(h + 1, low_b, high_b)
        mix(h, low_a, high_a, tops)
        if h + 2 < HEADS:
            tops = scores(h + 2, low_a, high_a)
        mix(h + 1, low_b, high_b, following)
        return tops

    slot_at(0, 1)

    @pl.when(step < images)
    def _():
        tops = scores(0, low_a, high_a)
        for h in range(0, HEADS, 2):
            for slot, (image, number) in MEANTIME.items():
                if number == h:
                    pl.when(step == image)(functools.partial(play, slot))
            tops = pair(h, tops)

    @pl.when(step == images)
    def _():
        play(7)
        wt_cross[...] = h_cross[...].reshape(width, 3 * width).T
        keep_cross.start()

    @pl.when(step >= images)
    def _():
        kv = dot(wt_cross[width:], mem_ref[0], 1, 1)
        ckv_ref[0, :HEADS] = kv[:width].astype(bf16).reshape(HEADS, HEAD_DIM, -1)
        ckv_ref[0, HEADS:] = (kv[width:] + cols[:, 4:5]).astype(bf16).reshape(HEADS, HEAD_DIM, -1)

    @pl.when(step == 2 * images - 1)
    def _():
        play(8)
        for g in gs:
            g.drain()
        keep_self.wait()
        keep_cross.wait()


def run_opening(dims, lens, x, mem, biases, gains, b_in, shards):
    images, tags, width = x.shape
    cells = mem.shape[1]
    half = tags // 2
    hidden = b_in.shape[1] * dims[0] * dims[1] * dims[2] * 2
    sds = jax.ShapeDtypeStruct

    def early(*shape):
        return pl.BlockSpec((1,) + shape, lambda i: (jnp.minimum(i, images - 1),) + (0,) * len(shape))

    def late(*shape):
        return pl.BlockSpec((1,) + shape, lambda i: (jnp.maximum(i - images, 0),) + (0,) * len(shape))

    def one(*shape):
        return pl.BlockSpec(shape, lambda i: (0,) * len(shape))

    def held(shard, lead):
        return shard.shape[:lead] + dims + (2,) + shard.shape[lead:]

    s_cross, s_self, s_proj, s_in, s_out = shards
    rows = s_cross.shape[0]
    cell = dims + (2, rows)
    anywhere = pl.BlockSpec(memory_space=pl.ANY)
    n = len(shards) + 1
    slots = gather_slots(dims)
    return pl.pallas_call(
        functools.partial(opening, dims),
        grid=(2 * images,),
        in_specs=[pl.BlockSpec(memory_space=pltpu.SMEM), early(tags, width), late(cells, width), one(*biases.shape), one(*gains.shape), one(*b_in.shape)]
        + [anywhere] * len(shards),
        out_specs=[
            early(3 * HEADS, HEAD_DIM, tags), late(2 * HEADS, HEAD_DIM, cells), early(HEADS, half, tags), early(HEADS, half, half),
            early(HEADS, tags), early(HEADS, HEAD_DIM, tags), anywhere, anywhere, one(16, width), one(1, hidden),
            anywhere, anywhere, anywhere,
        ],
        out_shape=[
            sds((images, 3 * HEADS, HEAD_DIM, tags), bf16),
            sds((images, 2 * HEADS, HEAD_DIM, cells), bf16),
            sds((images, HEADS, half, tags), bf16),
            sds((images, HEADS, half, half), bf16),
            sds((images, HEADS, tags), f32),
            sds((images, HEADS, HEAD_DIM, tags), bf16),
            sds((3 * width, width), bf16),
            sds((3 * width, width), bf16),
            sds((16, width), f32),
            sds((1, hidden), f32),
            sds(held(s_proj, 1), bf16),
            sds(held(s_in, 0), bf16),
            sds(held(s_out, 0), bf16),
        ],
        scratch_shapes=[
            pltpu.VMEM((16, 128), f32), pltpu.VMEM((16, 128), bf16), pltpu.VMEM(dims + (2, 16, 128), bf16),
            pltpu.VMEM(cell + (3 * width,), bf16), pltpu.VMEM(cell + (3 * width,), bf16),
            pltpu.VMEM((3 * width, width), bf16), pltpu.VMEM((3 * width, width), bf16),
            pltpu.VMEM((width, 16), f32), pltpu.VMEM((half, tags), f32), pltpu.VMEM((half, half), f32), pltpu.VMEM((half, tags), f32), pltpu.VMEM((half, half), f32),
            pltpu.VMEM((half, half), f32), pltpu.VMEM((16, tags), bf16),
            pltpu.SemaphoreType.DMA((2,)),
            pltpu.SemaphoreType.DMA((n,)), pltpu.SemaphoreType.DMA((n, slots)), pltpu.SemaphoreType.DMA((n, slots)),
        ],
        compiler_params=pltpu.CompilerParams(collective_id=0, has_side_effects=True, vmem_limit_bytes=58 * MIB),
        name="opening",
    )(lens, x, mem, biases, gains, b_in, *shards)


class Scattering:
    def __init__(self, dims, me, grads, mine, out, lead, held, sems):
        self.dims, self.me, self.grads, self.mine, self.out, self.lead = dims, me, grads, mine, out, lead
        self.pair, self.by_inner, self.by_across, self.by_outer, self.last = held
        self.send, self.recv = sems

    def at(self, *index):
        return (ALL,) * self.lead + index

    def remote(self, slot, src, dst, peer):
        return pltpu.make_async_remote_copy(
            src_ref=src, dst_ref=dst, send_sem=self.send.at[slot], recv_sem=self.recv.at[slot],
            device_id=device(self.dims, *peer), device_id_type=MESH)

    def swap(self):
        a, b, x, c = self.me
        return [self.remote(0, self.grads.at[self.at(ALL, ALL, ALL, 1 - c)], self.pair, (a, b, x, 1 - c))]

    def along_inner(self, core):
        a, b, x, c = self.me
        inner = self.dims[1]
        res = []
        for k in range(1, inner):
            peer = lax.rem(b + k, inner)
            src = self.pair.at[self.at(ALL, peer)] if core == 0 else self.by_across.at[0].at[self.at(ALL, peer)]
            dst = self.by_inner.at[k - 1] if core == 0 else self.by_outer.at[k - 1]
            res.append(self.remote(k, src, dst, (a, peer, x, c)))
        return res

    def along_across(self, core):
        a, b, x, c = self.me
        _, inner, across = self.dims
        res = []
        for k in range(1, across):
            peer = lax.rem(x + k, across)
            src = self.pair.at[self.at(ALL, ALL, peer)] if core == 1 else self.by_inner.at[0].at[self.at(ALL, peer)]
            dst = self.by_across.at[k - 1] if core == 1 else self.by_outer.at[k - 1]
            res.append(self.remote(inner - 1 + k, src, dst, (a, b, peer, c)))
        return res

    def second(self, core):
        return self.along_inner(core) if core == 0 else self.along_across(core)

    def third(self, core):
        return self.along_across(core) if core == 0 else self.along_inner(core)

    def along_outer(self):
        a, b, x, c = self.me
        outer, inner, across = self.dims
        return [
            self.remote(inner + across - 2 + k, self.by_outer.at[0].at[self.at(lax.rem(a + k, outer))], self.last.at[k - 1],
                        (lax.rem(a + k, outer), b, x, c))
            for k in range(1, outer)
        ]

    def begin(self):
        for copy in self.swap():
            copy.start()

    def advance(self, stage):
        a, b, x, c = self.me
        _, inner, across = self.dims

        def up(value):
            return value.astype(f32)

        def act(core):
            for copy in (self.swap(), self.second(core), self.third(core), self.along_outer())[stage - 1]:
                copy.wait_recv()
            if stage == 1:
                def add(k, _):
                    self.pair[k] = (up(self.grads[k, :, :, c]) + up(self.pair[k])).astype(bf16)
                    return 0
                following = self.second(core)
            elif stage == 2:
                held = self.by_inner if core == 0 else self.by_across

                def add(k, _):
                    total = up(self.pair[k, b] if core == 0 else self.pair[k, :, x])
                    for j in range((inner if core == 0 else across) - 1):
                        total = total + up(held[j, k])
                    held[0, k] = total.astype(bf16)
                    return 0
                following = self.third(core)
            elif stage == 3:
                held = self.by_inner if core == 0 else self.by_across

                def add(k, _):
                    total = up(held[0, k, x if core == 0 else b])
                    for j in range((across if core == 0 else inner) - 1):
                        total = total + up(self.by_outer[j, k])
                    self.by_outer[0, k] = total.astype(bf16)
                    return 0
                following = self.along_outer()
            else:
                total = up(self.by_outer[(0,) + self.at(a)])
                for k in range(self.dims[0] - 1):
                    total = total + up(self.last[k])
                self.out[...] = total
                following = []
            if stage < 4:
                lax.fori_loop(0, self.dims[0], add, 0)
            for copy in following:
                copy.start()

        for core in (0, 1):
            pl.when(c == core)(functools.partial(act, core))

    def drain(self):
        def act(core):
            for copy in self.swap() + self.second(core) + self.third(core) + self.along_outer():
                copy.wait_send()

        for core in (0, 1):
            pl.when(self.me[3] == core)(functools.partial(act, core))


def scatter_slots(dims):
    return dims[0] + dims[1] + dims[2] - 2


def scatter_space(dims, lead, tail):
    outer, inner, across = dims
    return [
        lead + (outer, inner, across) + tail,
        (inner - 1,) + lead + (outer, across) + tail,
        (across - 1,) + lead + (outer, inner) + tail,
        (max(inner, across) - 1,) + lead + (outer,) + tail,
        (outer - 1,) + lead + tail,
    ]


def collect(rows, row_lanes, devices):
    width = rows.shape[1]
    many = jnp.broadcast_to(rows[None], (devices, 16, width)).reshape(devices * 16, width)
    owner = lax.broadcasted_iota(jnp.int32, many.shape, 0) // 16
    at = lax.broadcasted_iota(jnp.int32, many.shape, 1)
    many = jnp.where(at // row_lanes == owner, many, 0.0).astype(bf16)
    lane = lax.broadcasted_iota(jnp.int32, (128, width), 0)
    at = lax.broadcasted_iota(jnp.int32, (128, width), 1)
    pick = jnp.where(lax.rem(at, row_lanes) == lane, 1.0, 0.0).astype(bf16)
    return dot(many, pick, 1, 1)


G_OUT, G_IN, G_ONE, G_CROSS, G_ZERO, G_HALF, G_REST, G_SMALL = range(8)
EVENTS = {
    (0, 0): ((G_OUT, 0), (G_IN, 0), (G_ONE, 0)),
    (0, 1): ((G_OUT, 1),),
    (0, 2): ((G_IN, 1), (G_ONE, 1)),
    (0, 6): ((G_CROSS, 0),),
    (0, 7): ((G_ZERO, 0), (G_OUT, 2)),
    (1, 1): ((G_IN, 2),),
    (2, 1): ((G_CROSS, 1), (G_ONE, 2), (G_ZERO, 1)),
    (3, 1): ((G_HALF, 0), (G_OUT, 3), (G_IN, 3)),
    (5, 1): ((G_OUT, 4), (G_CROSS, 2), (G_HALF, 1), (G_ONE, 3)),
    (6, 1): ((G_REST, 0), (G_SMALL, 0), (G_ZERO, 2), (G_IN, 4)),
    (8, 1): ((G_ONE, 4), (G_CROSS, 3)),
    (9, 1): ((G_HALF, 2), (G_REST, 1), (G_SMALL, 1), (G_ZERO, 3)),
    (9, 2): ((G_HALF, 3), (G_CROSS, 4), (G_REST, 2), (G_SMALL, 2), (G_ZERO, 4), (G_HALF, 4), (G_REST, 3), (G_SMALL, 3), (G_REST, 4), (G_SMALL, 4)),
}


def closing(dims, x_ref, qkv_ref, low_ref, high_ref, inv_ref, mix_ref, gmix_ref, inv_two, vectors, g_vec, g_bin, scale_one,
            low_out, low_in, low_one, e_any, ckv_any, q_any, mix_two_any, gmix_two_any, mix_any, two_any, one_any, wc_any, mem_any, ac_any, ap_any, wp_any, ws_any, gres_any,
            g_tags, sh_out, sh_in, sh_one, sh_cross, sh_zero, sh_half, sh_rest, sh_small, g_mem,
            e_ref, ckv_ref, q_ref, mix_two, gmix_two, mine_out, mine_in, mine_one, gres_ref, dkv_ref,
            mix_one, g_two, n_one, wt_cross, mem_ref, acc_cross, acc_zero, w_zero, wt_self,
            dq_ref, gmix_last, gres_last, gmix_now, acc, add_vec, acc_col, low_cross, low_zero, low_half, low_rest, low_small, head_sem, in_sem, *rest):
    tags, width = x_ref.shape[1:]
    cells = mem_ref.shape[0]
    half = tags // 2
    some = HEADS // 2
    step = pl.program_id(0)
    images = pl.num_programs(0) // 3
    me = place(dims)
    devices = dims[0] * dims[1] * dims[2] * 2
    held, (send, recv) = rest[:-2], rest[-2:]
    triples = ((mine_out, None, sh_out), (mine_in, None, sh_in), (mine_one, None, sh_one), (low_cross, None, sh_cross),
               (low_zero, None, sh_zero), (low_half, None, sh_half), (low_rest, None, sh_rest), (low_small, None, sh_small))
    every = [Scattering(dims, me, grads, mine, out, 0, held[5 * k : 5 * k + 5], (send.at[k], recv.at[k])) for k, (grads, mine, out) in enumerate(triples)]
    fetches = [
        pltpu.make_async_copy(src, dst, in_sem.at[k])
        for k, (src, dst) in enumerate((
            (low_out, mine_out), (low_in, mine_in), (low_one, mine_one),
            (one_any, n_one), (mem_any.at[images - 1], mem_ref), (ac_any, acc_cross), (two_any, g_two), (wc_any, wt_cross),
            (mix_any.at[images - 1], mix_one), (ap_any, acc_zero), (wp_any.at[0], w_zero), (gres_any, gres_ref), (ws_any, wt_self)))
    ]

    def e_rows(h):
        return e_ref.at[pl.ds(pl.multiple_of(h * cells, 16), cells)]

    def head_fetches(h):
        pairs = ((e_any.at[h], e_rows(h)), (ckv_any.at[images - 1, h], ckv_ref.at[h]), (ckv_any.at[images - 1, HEADS + h], ckv_ref.at[HEADS + h]),
                 (q_any.at[h], q_ref.at[h]), (mix_two_any.at[h], mix_two.at[h]), (gmix_two_any.at[h], gmix_two.at[h]))
        return [pltpu.make_async_copy(src, dst, head_sem.at[h, k]) for k, (src, dst) in enumerate(pairs)]

    def play(number, where):
        for item, stage in EVENTS.get((number, where), ()):
            item = every[item]
            item.begin() if stage == 0 else item.advance(stage)

    def events(where):
        for number in sorted(number for number, at in EVENTS if at == where and number > 0):
            pl.when(step == number)(functools.partial(play, number, where))

    def vec(k):
        return vectors[k : k + 1, :]

    @pl.when(step == 0)
    def _():
        for fetch in fetches[:3]:
            fetch.start()
        for h in range(HEADS):
            for fetch in head_fetches(h):
                fetch.start()
        for fetch in fetches[3:]:
            fetch.start()
        acc_col[...] = jnp.zeros_like(acc_col)
        greet(dims, me)
        for fetch in fetches[:3]:
            fetch.wait()
        play(0, 0)

        for first in (0, some):
            for h in range(first, first + some):
                for fetch in head_fetches(h):
                    fetch.wait()
            for h in range(first, first + some):
                dq_ref[h], dkv_ref[h], dkv_ref[HEADS + h] = cross_back(
                    h, e_rows(h)[...], ckv_ref[h], ckv_ref[HEADS + h], q_ref[h], gmix_two[h], mix_two[h], inv_two[h : h + 1, :])
            play(0, 1 + first // some)
        for fetch in fetches[3:11]:
            fetch.wait()
        dq = dq_ref[...].reshape(width, tags)
        dkv = dkv_ref[...].reshape(2 * width, cells)
        one_low = (n_one[...] * vec(10) + vec(6)).astype(bf16)
        acc_cross[:width] += dot(dq, one_low, 1, 0)
        acc_cross[width:] += dot(dkv, mem_ref[...], 1, 0)
        low_cross[...] = acc_cross[...].astype(bf16).T.reshape(low_cross.shape)
        play(0, 6)
        g_one = g_two[...] + dot(dq, wt_cross[:width], 0, 0)
        sum_gain, sum_shift = column_sums(g_one * n_one[...]), column_sums(g_one)
        g_one = norm_back(g_one, n_one[...], scale_one[...], vec(10))
        gres_last[...] = g_one
        g_low = g_one.astype(bf16)
        acc_zero[...] += dot(mix_one[...].reshape(width, tags), g_low, 1, 0)
        low_zero[...] = acc_zero[...].astype(bf16).reshape(low_zero.shape)
        play(0, 7)
        gmix_last[...] = dot(w_zero[...], g_low, 1, 1).astype(bf16).reshape(gmix_last.shape)
        at = lax.broadcasted_iota(jnp.int32, add_vec.shape, 0)
        total = g_vec[...]
        for k, row in ((2, column_sums(g_one)), (3, column_sums(lane_groups(dq.astype(f32)).T)),
                       (4, column_sums(memory_lanes(dkv[width:].astype(f32)).T)), (6, sum_shift), (10, sum_gain)):
            total = total + jnp.where(at == k, row, 0.0)
        add_vec[...] = total

    turn = jnp.maximum(step - 1, 0)
    part = jnp.minimum(turn // images, 1)
    now = lax.rem(turn, images)
    backward = jnp.logical_and(step >= 1, step <= 2 * images)

    @pl.when(jnp.logical_and(backward, now < images - 1))
    def _():
        gmix_now[...] = gmix_ref[0]

    @pl.when(jnp.logical_and(backward, now == images - 1))
    def _():
        gmix_now[...] = gmix_last[pl.ds(part * some, some)]

    def d_rows(image, kind, h, count=1):
        return pl.ds(pl.multiple_of(((image * 3 + kind) * HEADS + h) * HEAD_DIM, HEAD_DIM), count * HEAD_DIM)

    def head(h, _):
        grad = gmix_now[h].astype(f32)
        inv = inv_ref[0, pl.ds(part * some + h, 1), :]
        delta = jnp.sum(grad * mix_ref[0, h].astype(f32), 0, keepdims=True) * inv
        grad = (grad * inv).astype(bf16)
        ext = with_delta(grad, delta)
        qt, kt, vt = qkv_ref[0, 0, h], qkv_ref[0, 1, h], with_ones(qkv_ref[0, 2, h])
        e_low, e_high = low_ref[0, h], high_ref[0, h]
        ds_low = e_low * dot(vt[:, :half], ext, 0, 0).astype(bf16)
        ds_high = e_high * dot(vt[:, half:], ext[:, half:], 0, 0).astype(bf16)
        dv = jnp.concatenate([dot(grad, e_low, 1, 1), dot(grad[:, half:], e_high, 1, 1)], 1)
        dk = jnp.concatenate([dot(qt, ds_low, 1, 1), dot(qt[:, half:], ds_high, 1, 1)], 1)
        dq = dot(kt[:, :half], ds_low, 1, 0)
        dq = jnp.concatenate([dq[:, :half], dq[:, half:] + dot(kt[:, half:], ds_high, 1, 0)], 1) * HEAD_DIM ** -0.5
        at = part * some + h
        e_ref[d_rows(now, 0, at)] = dq.astype(bf16)
        e_ref[d_rows(now, 1, at)] = dk.astype(bf16)
        e_ref[d_rows(now, 2, at)] = dv.astype(bf16)
        return 0

    @pl.when(backward)
    def _():
        lax.fori_loop(0, some, head, 0, unroll=some)
        d = [e_ref[d_rows(now, kind, part * some, some)] for kind in range(3)]
        rows = some * HEAD_DIM
        acc_col[0, pl.ds(part * rows, rows)] += lane_groups(d[0].astype(f32))
        acc_col[1, pl.ds(part * rows, rows)] += lane_groups(d[2].astype(f32))
        fresh = now == 0
        for kind in range(3):
            product = dot(d[kind], x_ref[0], 1, 0)

            @pl.when(fresh)
            def _():
                acc[kind * rows : (kind + 1) * rows] = product

            @pl.when(jnp.logical_not(fresh))
            def _():
                acc[kind * rows : (kind + 1) * rows] += product

    @pl.when(step == images)
    def _():
        low_half[...] = acc[...].astype(bf16).T.reshape(low_half.shape)

    @pl.when(step == 2 * images)
    def _():
        low_rest[...] = acc[...].astype(bf16).T.reshape(low_rest.shape)
        at = lax.broadcasted_iota(jnp.int32, add_vec.shape, 0)
        rows = jnp.where(at == 0, column_sums(acc_col[0].T), jnp.where(at == 1, column_sums(acc_col[1].T), add_vec[...]))
        at = lax.broadcasted_iota(jnp.int32, (16, g_bin.shape[1]), 0)
        hidden = jnp.where(at == 13, g_bin[...], 0.0)
        small = collect(rows, width // devices, devices) + collect(hidden, g_bin.shape[1] // devices, devices)
        low_small[...] = small.astype(bf16).reshape(low_small.shape)

    events(0)

    @pl.when(step == 2 * images + 1)
    def _():
        for fetch in fetches[11:]:
            fetch.wait()

    @pl.when(step > 2 * images)
    def _():
        image = jnp.maximum(step - 2 * images - 1, 0)
        d = e_ref[d_rows(image, 0, 0, 3 * HEADS)]
        product = dot(d, wt_self[...], 0, 0)

        @pl.when(image < images - 1)
        def _():
            g_tags[0] = gres_ref[jnp.minimum(image, images - 2)] + product

        @pl.when(image == images - 1)
        def _():
            g_tags[0] = gres_last[...] + product

    events(1)

    @pl.when(step == 3 * images)
    def _():
        g_mem[...] = dot(dkv_ref[...].reshape(2 * width, cells), wt_cross[width:], 0, 0)

    events(2)

    @pl.when(step == 3 * images)
    def _():
        for item in every:
            item.drain()


def run_closing(dims, x, qkv, e_low, e_high, inv, mix, gmix, g_resid, ckv, mem, vectors, wt_self, wt_cross, w_proj, g_one, g_in, g_out, g_vec, g_bin, kept):
    scale_one, e, q, inv_two, mix_two, gmix_two, n_one, g_two, acc_cross, acc_zero = kept
    images, tags, width = x.shape
    memory = mem.shape[1]
    half, some = tags // 2, HEADS // 2
    sds = jax.ShapeDtypeStruct
    cells = dims + (2,)
    devices = dims[0] * dims[1] * dims[2] * 2

    def parts(grad):
        return grad.reshape(cells + (grad.shape[0] // devices, grad.shape[1]))

    low = [parts(g_out), parts(g_in), parts(g_one)]
    rows = width // devices
    lows = [cells + (rows, 3 * width), cells + (rows, width)] + [cells + (rows, 3 * width // 2)] * 2 + [cells + (16, 128)]

    def turn(i):
        t = jnp.clip(i - 1, 0, 2 * images - 1)
        return lax.rem(t, images), lax.div(t, images)

    def by_turn(shape, split):
        def index(i):
            image, part = turn(i)
            return (image,) + tuple(part if k == split else 0 for k in range(len(shape)))
        return pl.BlockSpec((1,) + shape, index)

    def gmix_index(i):
        image, part = turn(i)
        return jnp.minimum(image, images - 2), part, 0, 0

    def one(*shape):
        return pl.BlockSpec(shape, lambda i: (0,) * len(shape), pipeline_mode=pl.Buffered(1))

    def out(*shape):
        return pl.BlockSpec(shape, lambda i: (0,) * len(shape))

    anywhere = pl.BlockSpec(memory_space=pl.ANY)
    shares = [g.shape[4:] for g in low] + [s[4:] for s in lows]
    space = []
    for shape in [g.shape for g in low] + lows:
        space += [pltpu.VMEM(s, bf16) for s in scatter_space(dims, (), shape[4:])]
    slots = scatter_slots(dims)
    qkv = qkv.reshape(images, 3, HEADS, HEAD_DIM, tags)
    heads = (HEADS, HEAD_DIM, tags)
    return pl.pallas_call(
        functools.partial(closing, dims),
        grid=(3 * images + 1,),
        in_specs=[
            by_turn((tags, width), None), by_turn((3, some, HEAD_DIM, tags), 1), by_turn((some, half, tags), 0), by_turn((some, half, half), 0),
            by_turn((HEADS, tags), None), by_turn((some, HEAD_DIM, tags), 0), pl.BlockSpec((1, some, HEAD_DIM, tags), gmix_index),
            one(HEADS, tags), one(16, width), one(16, width), one(*g_bin.shape), one(tags, 1),
        ] + [anywhere] * 18,
        out_specs=[pl.BlockSpec((1, tags, width), lambda i: (jnp.clip(i - 2 * images - 1, 0, images - 1), 0, 0))]
        + [out(*s) for s in shares] + [out(memory, width)],
        out_shape=[sds((images, tags, width), f32)] + [sds(s, f32) for s in shares] + [sds((memory, width), f32)],
        scratch_shapes=[
            pltpu.VMEM((HEADS * memory, tags), bf16), pltpu.VMEM((2 * HEADS, HEAD_DIM, memory), bf16), pltpu.VMEM(heads, bf16), pltpu.VMEM(heads, bf16), pltpu.VMEM(heads, bf16),
        ] + [pltpu.VMEM(g.shape, bf16) for g in low] + [
            pltpu.VMEM((images - 1, tags, width), f32), pltpu.VMEM((2 * HEADS, HEAD_DIM, memory), bf16),
            pltpu.VMEM(heads, bf16), pltpu.VMEM((tags, width), f32), pltpu.VMEM((tags, width), f32),
            pltpu.VMEM((3 * width, width), bf16), pltpu.VMEM((memory, width), bf16), pltpu.VMEM((3 * width, width), f32), pltpu.VMEM((width, width), f32),
            pltpu.VMEM((width, width), bf16), pltpu.VMEM((3 * width, width), bf16),
            pltpu.VMEM(heads, bf16), pltpu.VMEM(heads, bf16), pltpu.VMEM((tags, width), f32), pltpu.VMEM((some, HEAD_DIM, tags), bf16),
            pltpu.VMEM((3 * width // 2, width), f32), pltpu.VMEM((16, width), f32), pltpu.VMEM((2, width, 128), f32),
        ] + [pltpu.VMEM(s, bf16) for s in lows] + [pltpu.SemaphoreType.DMA((HEADS, 6)), pltpu.SemaphoreType.DMA((13,))] + space
        + [pltpu.SemaphoreType.DMA((8, slots)), pltpu.SemaphoreType.DMA((8, slots))],
        compiler_params=pltpu.CompilerParams(collective_id=1, has_side_effects=True, vmem_limit_bytes=62 * MIB),
        name="closing",
    )(x, qkv, e_low, e_high, inv, mix, gmix, inv_two, vectors, g_vec, g_bin, scale_one, *low,
      e, ckv, q, mix_two, gmix_two, mix, g_two, n_one, wt_cross, mem, acc_cross, acc_zero, w_proj, wt_self, g_resid)


def settle(lanes, hidden_lanes, images, g_mem_in, m_last, tags, s_out, s_in, s_one, s_cross, s_zero, s_half, s_rest, small,
           g_mem, o_tags, o_self, o_cross, o_proj, o_in, o_out, o_bin, o_gains, o_biases):
    width = o_tags.shape[2]
    o_tags[...] = tags[...]

    @pl.when(pl.program_id(0) == 0)
    def _():
        g_mem[0] = m_last[...]
        part = width // 2
        for kind in range(3):
            o_self[:, kind * width : kind * width + part] = s_half[:, kind * part : (kind + 1) * part]
            o_self[:, kind * width + part : (kind + 1) * width] = s_rest[:, kind * part : (kind + 1) * part]
        o_cross[...] = s_cross[...]
        o_proj[0] = s_zero[...]
        o_proj[1] = s_one[...]
        o_in[...] = s_in[...]
        o_out[...] = s_out[...]
        o_biases[...] = small[:10, :lanes]
        o_gains[...] = small[10:13, :lanes]
        o_bin[...] = small[13:14, :hidden_lanes]


def run_settle(lanes, hidden_lanes, g_mem, m_last, g_tags, shares):
    images, tags, width = g_tags.shape
    sds = jax.ShapeDtypeStruct
    s_out, s_in, s_one, s_cross, s_zero, s_half, s_rest, small = shares

    def one(*shape):
        return pl.BlockSpec(shape, lambda i: (0,) * len(shape), pipeline_mode=pl.Buffered(1))

    def out(*shape):
        return pl.BlockSpec(shape, lambda i: (0,) * len(shape))

    rows = s_cross.shape[0]
    shapes = [s_cross.shape, s_cross.shape, (2, rows, width), s_in.shape, s_out.shape, (1, hidden_lanes), (3, lanes), (10, lanes)]
    image = pl.BlockSpec((1, tags, width), lambda i: (i, 0, 0))
    return pl.pallas_call(
        functools.partial(settle, lanes, hidden_lanes, images),
        grid=(images,),
        in_specs=[pl.BlockSpec(memory_space=pl.ANY), one(*m_last.shape), image] + [one(*s.shape) for s in shares],
        out_specs=[pl.BlockSpec((1,) + g_mem.shape[1:], lambda i: (images - 1, 0, 0)), image] + [out(*s) for s in shapes],
        out_shape=[sds(g_mem.shape, f32), sds(g_tags.shape, f32)] + [sds(s, f32) for s in shapes],
        input_output_aliases={0: 0},
        compiler_params=pltpu.CompilerParams(vmem_limit_bytes=62 * MIB),
        name="settle",
    )(g_mem, m_last, g_tags, *shares)


AXES = ("wide", "narrow")
LEADS = (0, 0, 1, 0, 0, 0)


def fold(block, rows, columns):
    if rows % 16 == 0:
        return block
    return block.reshape(block.shape[:-2] + (16, rows * columns // 16))


def per_device(dims, tag_states, image_memory, tag_lengths, w_self, w_cross, w_proj, w_in, b_in, w_out, ln_gains, biases, out_grad):
    cells = dims + (2,)
    fused = w_self.shape[0] % 16 == 0 and tag_states.shape[0] == 3
    devices = dims[0] * dims[1] * dims[2] * 2
    width = tag_states.shape[2]
    lanes, hidden_lanes = biases.shape[1], b_in.shape[0]
    if fused:
        qkv, ckv, near, far, inv, mix, wt_self, wt_cross, vectors, hidden_bias, full_proj, full_in, full_out = run_opening(
            dims, tag_lengths, tag_states, image_memory, biases, ln_gains, b_in[None], (w_cross, w_self, w_proj, w_in, w_out))
        full_proj, full_in, full_out = full_proj.reshape(2, width, width), full_in.reshape(width, -1), full_out.reshape(-1, width)
        layer_out, g_resid, gmix, g_mem, _, g_one, g_in, g_out, g_vec, g_bin, *kept = run_middle(
            tag_lengths, tag_states, image_memory, out_grad, mix, ckv, wt_cross, full_proj, full_in, full_out, vectors, hidden_bias, True)
        g_tags, *shares, m_last = run_closing(
            dims, tag_states, qkv, near, far, inv, mix, gmix, g_resid, ckv, image_memory, vectors, wt_self, wt_cross, full_proj,
            g_one, g_in, g_out, g_vec, g_bin, kept)
        grad_memory, grad_tags, s_self, s_cross, s_proj, s_in, s_out, s_bin, s_gains, s_biases = run_settle(
            lanes, hidden_lanes, g_mem, m_last, g_tags, shares)
        return layer_out, grad_tags, grad_memory, s_self, s_cross, s_proj, s_in, s_bin[0], s_out, s_gains, s_biases
    small = jnp.concatenate(
        [
            jnp.pad(jnp.concatenate([biases, ln_gains]), ((0, 0), (0, 128 - lanes))),
            jnp.pad(b_in[None], ((0, 2), (0, 128 - hidden_lanes))),
        ]
    )
    shards = (w_self, w_cross, w_proj, w_in, w_out, small)
    gathered = gather(dims, [fold(s, *s.shape[-2:]) for s in shards], LEADS)

    def whole(held, shard):
        lead = shard.shape[:-2]
        rows, columns = shard.shape[-2:]
        return held.reshape(lead + (devices * rows, columns))

    full_self, full_cross, full_proj, full_in, full_out, full_small = [whole(h, s) for h, s in zip(gathered, shards)]
    by_device = full_small.reshape(devices, 16, 128)
    vectors = by_device[:, :, :lanes].transpose(1, 0, 2).reshape(16, width).astype(f32)
    hidden_bias = by_device[:, 13, :hidden_lanes].reshape(1, -1).astype(f32)
    layer_out, grad_tags, grad_memory, g_self, g_cross, g_proj, g_in, g_out, g_vec, g_bin = layer(
        tag_lengths, tag_states, image_memory, out_grad, full_self, full_cross, full_proj, full_in, full_out, vectors, hidden_bias)
    g_small = jnp.pad(g_vec.reshape(16, devices, lanes).transpose(1, 0, 2)[:, :13], ((0, 0), (0, 0), (0, 128 - lanes)))
    g_hidden = jnp.pad(g_bin.reshape(devices, 1, hidden_lanes), ((0, 0), (0, 2), (0, 128 - hidden_lanes)))
    g_small = jnp.concatenate([g_small, g_hidden], 1).astype(bf16).reshape(devices * 16, 128)

    def parts(grad, shard):
        lead = shard.shape[:-2]
        rows, columns = shard.shape[-2:]
        return fold(grad.reshape(lead + cells + (rows, columns)), rows, columns)

    shards = (w_self, w_cross, w_proj, w_in, w_out, jax.ShapeDtypeStruct((16, 128), bf16))
    shares = scatter(dims, [parts(g, s) for g, s in zip((g_self, g_cross, g_proj, g_in, g_out, g_small), shards)], LEADS)
    s_self, s_cross, s_proj, s_in, s_out, s_small = [v.reshape(s.shape) for v, s in zip(shares, shards)]
    return (layer_out, grad_tags, grad_memory, s_self, s_cross, s_proj, s_in, s_small[13, :hidden_lanes], s_out,
            s_small[10:13, :lanes], s_small[:10, :lanes])


def solution(mesh):
    dims = grid_of(mesh.shape["wide"], mesh.shape["narrow"])
    rows, matrix, stack, columns = P(AXES, None, None), P(AXES, None), P(None, AXES, None), P(None, AXES)
    return jax.shard_map(
        functools.partial(per_device, dims),
        mesh=mesh,
        in_specs=(rows, rows, P(AXES), matrix, matrix, stack, matrix, P(AXES), matrix, columns, columns, rows),
        out_specs=(rows, rows, rows, matrix, matrix, stack, matrix, P(AXES), matrix, columns, columns),
        check_vma=False,
    )
```

```python
import functools

import jax
import jax.numpy as jnp
from jax import lax
from jax.experimental import pallas as pl
from jax.experimental.pallas import tpu as pltpu
from jax.sharding import PartitionSpec as P


MESH = pl.DeviceIdType.MESH
f32, bf16 = jnp.float32, jnp.bfloat16


def grid_of(mesh_wide, mesh_narrow):
    outer = 4
    return outer, mesh_wide // outer, mesh_narrow // 2


def place(dims):
    outer, inner, across = dims
    wide, narrow = lax.axis_index("wide"), lax.axis_index("narrow")
    return wide // inner, lax.rem(wide, inner), narrow // 2, lax.rem(narrow, 2)


def device(dims, a, b, x, c):
    return {"wide": a * dims[1] + b, "narrow": x * 2 + c}


def greet(dims, me, diagonal=False):
    a, b, x, c = me
    outer, inner, across = dims
    barrier = pltpu.get_barrier_semaphore()
    peers = [(lax.rem(a + k, outer), b, x, c) for k in range(1, outer)]
    peers += [(a, lax.rem(b + k, inner), x, c) for k in range(1, inner)]
    peers += [(a, b, lax.rem(x + k, across), c) for k in range(1, across)]
    peers += [(a, b, x, 1 - c)]
    if diagonal:
        peers += [(a, lax.rem(b + j, inner), lax.rem(x + k, across), c) for j in range(1, inner) for k in range(1, across)]
    for peer in peers:
        pl.semaphore_signal(barrier, inc=1, device_id=device(dims, *peer), device_id_type=MESH)
    pl.semaphore_wait(barrier, len(peers))


ALL = slice(None)


def gather_kernel(dims, leads, *refs):
    count = len(leads)
    shards, outs = refs[:count], refs[count : 2 * count]
    local_sem, send_sem, recv_sem = refs[2 * count :]
    outer, inner, across = dims
    me = place(dims)
    a, b, x, c = me
    greet(dims, me)

    def cell(ref, lead, *index):
        return ref.at[(ALL,) * lead + index]

    def remote(g, slot, src, dst, peer):
        return pltpu.make_async_remote_copy(
            src_ref=src, dst_ref=dst, send_sem=send_sem.at[g, slot], recv_sem=recv_sem.at[g, slot],
            device_id=device(dims, *peer), device_id_type=MESH)

    n_in, n_ac = inner - 1, across - 1

    def first(g):
        lead = leads[g]
        mine = cell(outs[g], lead, a, b, x, c)
        return [remote(g, k - 1, shards[g], mine, (lax.rem(a + k, outer), b, x, c)) for k in range(1, outer)]

    def keep(g):
        return pltpu.make_async_copy(shards[g], cell(outs[g], leads[g], a, b, x, c), local_sem.at[g])

    base = outer - 1

    def via_inner(g, core):
        lead = leads[g]
        column = ALL if core == 0 else x
        piece = cell(outs[g], lead, ALL, b, column, c)
        return [remote(g, base + k - 1, piece, piece, (a, lax.rem(b + k, inner), x, c)) for k in range(1, inner)]

    def via_across(g, core):
        lead = leads[g]
        row = b if core == 0 else ALL
        piece = cell(outs[g], lead, ALL, row, x, c)
        return [remote(g, base + n_in + k - 1, piece, piece, (a, b, lax.rem(x + k, across), c)) for k in range(1, across)]

    share = base + n_in + n_ac

    def to_partner(g, core, holder):
        lead = leads[g]
        def piece(slot, row, column):
            ref = cell(outs[g], lead, ALL, row, column, holder)
            return remote(g, share + slot, ref, ref, (a, b, x, 1 - c))
        own = [piece(0, b, x)]
        by_inner = [piece(1 + k - 1, lax.rem(b + k, inner), ALL if core == 0 else x) for k in range(1, inner)]
        by_across = [piece(1 + n_in + k - 1, b if core == 0 else ALL, lax.rem(x + k, across)) for k in range(1, across)]
        return (own, by_across, by_inner) if core == 0 else (own, by_inner, by_across)

    def start(copies):
        for copy in copies:
            copy.start()

    def arrived(copies):
        for copy in copies:
            copy.wait_recv()

    for g in range(count):
        keep(g).start()
        start(first(g))

    def body(core):
        second, third = (via_across, via_inner) if core == 0 else (via_inner, via_across)
        for step in range(count + 2):
            g = step
            if g < count:
                keep(g).wait()
                arrived(first(g))
                start(second(g, core))
                start(to_partner(g, core, c)[0])
            g = step - 1
            if 0 <= g < count:
                arrived(second(g, core))
                start(third(g, core))
                start(to_partner(g, core, c)[1])
            g = step - 2
            if 0 <= g < count:
                arrived(third(g, core))
                start(to_partner(g, core, c)[2])
        for g in range(count):
            for group in to_partner(g, 1 - core, 1 - c):
                arrived(group)
        for g in range(count):
            for copy in first(g) + second(g, core) + third(g, core):
                copy.wait_send()
            for group in to_partner(g, core, c):
                for copy in group:
                    copy.wait_send()

    @pl.when(c == 0)
    def _():
        body(0)

    @pl.when(c == 1)
    def _():
        body(1)


def gather(dims, shards, leads):
    outer, inner, across = dims
    def shape(s, lead):
        return jax.ShapeDtypeStruct(s.shape[:lead] + (outer, inner, across, 2) + s.shape[lead:], s.dtype)
    slots = (outer - 1) + 2 * (inner - 1) + 2 * (across - 1) + 1
    n = len(shards)
    return pl.pallas_call(
        functools.partial(gather_kernel, dims, leads),
        out_shape=[shape(s, l) for s, l in zip(shards, leads)],
        in_specs=[pl.BlockSpec(memory_space=pl.ANY)] * n,
        out_specs=[pl.BlockSpec(memory_space=pl.ANY)] * n,
        scratch_shapes=[pltpu.SemaphoreType.DMA((n,)), pltpu.SemaphoreType.DMA((n, slots)), pltpu.SemaphoreType.DMA((n, slots))],
        compiler_params=pltpu.CompilerParams(collective_id=0, has_side_effects=True),
        name="gather_weights",
    )(*shards)


def scatter_kernel(dims, leads, *refs):
    count = len(leads)
    grads, outs = refs[:count], refs[count : 2 * count]
    rest = refs[2 * count :]
    r0, r1i, r1a, r2a, r2i, r3 = (rest[k * count : (k + 1) * count] for k in range(6))
    send_sem, recv_sem = rest[6 * count :]
    outer, inner, across = dims
    me = place(dims)
    a, b, x, c = me
    greet(dims, me)
    n_in, n_ac = inner - 1, across - 1

    def cell(ref, lead, *index):
        return ref.at[(ALL,) * lead + index]

    def remote(g, slot, src, dst, peer):
        return pltpu.make_async_remote_copy(
            src_ref=src, dst_ref=dst, send_sem=send_sem.at[g, slot], recv_sem=recv_sem.at[g, slot],
            device_id=device(dims, *peer), device_id_type=MESH)

    def swap(g):
        return [remote(g, 0, cell(grads[g], leads[g], ALL, ALL, ALL, 1 - c), r0[g], (a, b, x, 1 - c))]

    def via_inner(g, core):
        lead = leads[g]
        res = []
        for k in range(1, inner):
            peer = lax.rem(b + k, inner)
            if core == 0:
                src, dst = cell(r0[g], lead, ALL, peer), r1i[g].at[k - 1]
            else:
                src, dst = cell(r1a[g].at[0], lead, ALL, peer), r2i[g].at[k - 1]
            res.append(remote(g, k, src, dst, (a, peer, x, c)))
        return res

    def via_across(g, core):
        lead = leads[g]
        res = []
        for k in range(1, across):
            peer = lax.rem(x + k, across)
            if core == 1:
                src, dst = cell(r0[g], lead, ALL, ALL, peer), r1a[g].at[k - 1]
            else:
                src, dst = cell(r1i[g].at[0], lead, ALL, peer), r2a[g].at[k - 1]
            res.append(remote(g, 1 + n_in + k - 1, src, dst, (a, b, peer, c)))
        return res

    def last(g, core):
        lead = leads[g]
        held = (r2a if core == 0 else r2i)[g].at[0]
        res = []
        for k in range(1, outer):
            peer = lax.rem(a + k, outer)
            res.append(remote(g, 1 + n_in + n_ac + k - 1, cell(held, lead, peer), r3[g].at[k - 1], (peer, b, x, c)))
        return res

    def start(copies):
        for copy in copies:
            copy.start()

    def arrived(copies):
        for copy in copies:
            copy.wait_recv()

    def up(v):
        return v.astype(f32)

    for g in range(count):
        start(swap(g))

    def body(core):
        second, third = (via_inner, via_across) if core == 0 else (via_across, via_inner)
        def at(lead, *index):
            return (ALL,) * lead + index
        for step in range(count + 3):
            g = step
            if g < count:
                arrived(swap(g))
                lead = leads[g]
                r0[g][...] = (up(grads[g][at(lead, ALL, ALL, ALL, c)]) + up(r0[g][...])).astype(bf16)
                start(second(g, core))
            g = step - 1
            if 0 <= g < count:
                arrived(second(g, core))
                lead = leads[g]
                if core == 0:
                    total = up(r0[g][at(lead, ALL, b)])
                    held = r1i[g]
                else:
                    total = up(r0[g][at(lead, ALL, ALL, x)])
                    held = r1a[g]
                for k in range(held.shape[0]):
                    total = total + up(held[k])
                held[0] = total.astype(bf16)
                start(third(g, core))
            g = step - 2
            if 0 <= g < count:
                arrived(third(g, core))
                lead = leads[g]
                if core == 0:
                    total = up(r1i[g][(0,) + at(lead, ALL, x)])
                    held = r2a[g]
                else:
                    total = up(r1a[g][(0,) + at(lead, ALL, b)])
                    held = r2i[g]
                for k in range(held.shape[0]):
                    total = total + up(held[k])
                held[0] = total.astype(bf16)
                start(last(g, core))
            g = step - 3
            if 0 <= g < count:
                arrived(last(g, core))
                lead = leads[g]
                held = (r2a if core == 0 else r2i)[g]
                total = up(held[(0,) + at(lead, a)])
                for k in range(outer - 1):
                    total = total + up(r3[g][k])
                outs[g][...] = total
        for g in range(count):
            for copy in swap(g) + second(g, core) + third(g, core) + last(g, core):
                copy.wait_send()

    @pl.when(c == 0)
    def _():
        body(0)

    @pl.when(c == 1)
    def _():
        body(1)


def scatter(dims, grads, leads):
    outer, inner, across = dims
    n = len(grads)
    outs, shapes = [], [[] for _ in range(6)]
    for g, lead in zip(grads, leads):
        head, tail = g.shape[:lead], g.shape[lead + 4 :]
        outs.append(jax.ShapeDtypeStruct(head + tail, f32))
        shapes[0].append(head + (outer, inner, across) + tail)
        shapes[1].append((inner - 1,) + head + (outer, across) + tail)
        shapes[2].append((across - 1,) + head + (outer, inner) + tail)
        shapes[3].append((across - 1,) + head + (outer,) + tail)
        shapes[4].append((inner - 1,) + head + (outer,) + tail)
        shapes[5].append((outer - 1,) + head + tail)
    slots = 1 + (inner - 1) + (across - 1) + (outer - 1)
    return pl.pallas_call(
        functools.partial(scatter_kernel, dims, leads),
        out_shape=outs,
        in_specs=[pl.BlockSpec(memory_space=pltpu.VMEM)] * n,
        out_specs=[pl.BlockSpec(memory_space=pltpu.VMEM)] * n,
        scratch_shapes=[pltpu.VMEM(s, bf16) for group in shapes for s in group]
        + [pltpu.SemaphoreType.DMA((n, slots)), pltpu.SemaphoreType.DMA((n, slots))],
        compiler_params=pltpu.CompilerParams(collective_id=1, has_side_effects=True, vmem_limit_bytes=48 * 2**20),
        name="scatter_grads",
    )(*grads)

HEADS, HEAD_DIM = 8, 64
EPS = 1e-5
MASKED = -1e9
TAME = 30.0
CHUNKS = 1
MIB = 2**20


def dot(left, right, left_dim, right_dim):
    return lax.dot_general(left, right, (((left_dim,), (right_dim,)), ((), ())), preferred_element_type=f32)


def full(shape):
    return pl.BlockSpec(shape, lambda i: (0,) * len(shape))


def image(shape):
    return pl.BlockSpec((1,) + shape, lambda i: (i,) + (0,) * len(shape))


def with_ones(rows):
    return jnp.concatenate([rows, jnp.ones((16, rows.shape[1]), bf16)], 0)


def with_delta(rows, delta):
    high = delta.astype(bf16).astype(f32)
    low = delta - high
    at = lax.broadcasted_iota(jnp.int32, (16, rows.shape[1]), 0)
    extra = jnp.where(at == 0, -high, jnp.where(at == 1, -low, 0.0))
    return jnp.concatenate([rows, extra.astype(bf16)], 0)


def self_forward(lens, x_ref, mem_ref, w_self, w_cross, bias_qkv, bias_kv,
                 qkv_ref, ckv_ref, near_ref, far_ref, inv_ref, mix_ref, wt_self, wt_cross):
    width = x_ref.shape[2]
    tags = x_ref.shape[1]
    half = tags // 2
    i = pl.program_id(0)

    @pl.when(i == 0)
    def _():
        wt_self[...] = w_self[...].T
        wt_cross[...] = w_cross[...].T

    ckv = dot(wt_cross[width:], mem_ref[0], 1, 1) + bias_kv[...]
    ckv_ref[0] = ckv.astype(bf16).reshape(ckv_ref.shape[1:])
    qkv = dot(wt_self[...], x_ref[0], 1, 1) + bias_qkv[...]
    q = qkv[:width].astype(bf16) * bf16(HEAD_DIM ** -0.5)
    qkv_ref[0, :HEADS] = q.reshape(HEADS, HEAD_DIM, tags)
    qkv_ref[0, HEADS:] = qkv[width:].astype(bf16).reshape(2 * HEADS, HEAD_DIM, tags)
    last = lens[i] - 1

    def head(h, _):
        qt, kt, vt = qkv_ref[0, h], qkv_ref[0, HEADS + h], with_ones(qkv_ref[0, 2 * HEADS + h])

        def part(keys, first, out):
            s = dot(kt[:, :keys], qt[:, first : first + half], 0, 0)
            key_at = lax.broadcasted_iota(jnp.int32, (keys, half), 0)
            query_at = lax.broadcasted_iota(jnp.int32, (1, half), 1) + first
            s = jnp.where(key_at <= jnp.minimum(query_at, last), s, MASKED)
            e = jnp.exp(s - jnp.max(s, 0, keepdims=True)).astype(bf16)
            out[0, h] = e
            mixed = dot(vt[:, :keys], e, 1, 0)
            inv = 1.0 / mixed[HEAD_DIM : HEAD_DIM + 1]
            inv_ref[0, pl.ds(h, 1), first : first + half] = inv
            mix_ref[0, h, :, first : first + half] = (mixed[:HEAD_DIM] * inv).astype(bf16)

        part(half, 0, near_ref)
        part(tags, half, far_ref)
        return 0

    lax.fori_loop(0, HEADS, head, 0)


def run_self_forward(lens, x, mem, w_self, w_cross, bias_qkv, bias_kv):
    images, tags, width = x.shape
    cells = mem.shape[1]
    half = tags // 2
    sds = jax.ShapeDtypeStruct
    return pl.pallas_call(
        self_forward,
        grid_spec=pltpu.PrefetchScalarGridSpec(
            num_scalar_prefetch=1,
            grid=(images,),
            in_specs=[pl.BlockSpec((1, tags, width), lambda i, n: (i, 0, 0)), pl.BlockSpec((1, cells, width), lambda i, n: (i, 0, 0))]
            + [pl.BlockSpec(v.shape, lambda i, n: (0, 0)) for v in (w_self, w_cross, bias_qkv, bias_kv)],
            out_specs=[
                pl.BlockSpec((1, 3 * HEADS, HEAD_DIM, tags), lambda i, n: (i, 0, 0, 0)),
                pl.BlockSpec((1, 2 * HEADS, HEAD_DIM, cells), lambda i, n: (i, 0, 0, 0)),
                pl.BlockSpec((1, HEADS, half, half), lambda i, n: (i, 0, 0, 0)),
                pl.BlockSpec((1, HEADS, tags, half), lambda i, n: (i, 0, 0, 0)),
                pl.BlockSpec((1, HEADS, tags), lambda i, n: (i, 0, 0)),
                pl.BlockSpec((1, HEADS, HEAD_DIM, tags), lambda i, n: (i, 0, 0, 0)),
                pl.BlockSpec((3 * width, width), lambda i, n: (0, 0)),
                pl.BlockSpec((3 * width, width), lambda i, n: (0, 0)),
            ],
        ),
        out_shape=[
            sds((images, 3 * HEADS, HEAD_DIM, tags), bf16),
            sds((images, 2 * HEADS, HEAD_DIM, cells), bf16),
            sds((images, HEADS, half, half), bf16),
            sds((images, HEADS, tags, half), bf16),
            sds((images, HEADS, tags), f32),
            sds((images, HEADS, HEAD_DIM, tags), bf16),
            sds((3 * width, width), bf16),
            sds((3 * width, width), bf16),
        ],
        compiler_params=pltpu.CompilerParams(vmem_limit_bytes=58 * MIB),
        name="self_forward",
    )(lens, x, mem, w_self, w_cross, bias_qkv, bias_kv)


def norm(resid):
    centred = resid - jnp.mean(resid, -1, keepdims=True)
    scale = lax.rsqrt(jnp.mean(centred * centred, -1, keepdims=True) + EPS)
    return centred * scale, scale


def norm_back(grad, normed, scale, gain):
    scaled = grad * gain
    mean_one = jnp.mean(scaled, -1, keepdims=True)
    mean_two = jnp.mean(scaled * normed, -1, keepdims=True)
    return scale * (scaled - mean_one - normed * mean_two)


def column_sums(rows):
    return jnp.sum(rows, 0, keepdims=True)


def lane_groups(rows):
    total = rows[:, :128]
    for k in range(1, rows.shape[1] // 128):
        total = total + rows[:, 128 * k : 128 * (k + 1)]
    return total


def cross_back(h, e, keys, values, queries, grad, mixed, inv):
    grad = grad.astype(f32)
    delta = jnp.sum(grad * mixed.astype(f32), 0, keepdims=True) * inv
    grad = (grad * inv).astype(bf16)
    dp = dot(with_ones(values), with_delta(grad, delta), 0, 0)
    ds = e * dp.astype(bf16)
    dv = dot(grad, e, 1, 1).astype(bf16)
    dk = dot(queries, ds, 1, 1).astype(bf16)
    dq = (dot(keys, ds, 1, 0) * HEAD_DIM ** -0.5).astype(bf16)
    return dq, dk, dv


def memory_lanes(rows):
    cells = rows.shape[1]
    body = cells // 128 * 128
    total = lane_groups(rows[:, :body])
    if body < cells:
        total = total + jnp.concatenate([rows[:, body:], jnp.zeros((rows.shape[0], 128 - cells + body), f32)], 1)
    return total


def middle(held_back, lens, x_ref, mem_ref, gout_ref, mix_one, ckv_ref, wt_cross, w_proj, w_in, w_out, vectors, b_in,
           out_ref, g_resid, g_mix, g_mem, gw_cross, gw_proj, gw_in, gw_out, g_vec, g_bin, *rest):
    if held_back:
        o_scale, o_e, o_q, o_inv, o_mix, o_gmix, o_one, o_two, o_cross, o_proj = rest[:10]
        gone = rest[-1]
        rest = rest[10:-1]
    middle_body(held_back and (o_scale, o_e, o_q, o_inv, o_mix, o_gmix, o_one, o_two, o_cross, o_proj, gone),
                lens, x_ref, mem_ref, gout_ref, mix_one, ckv_ref, wt_cross, w_proj, w_in, w_out, vectors, b_in,
                out_ref, g_resid, g_mix, g_mem, gw_cross, gw_proj, gw_in, gw_out, g_vec, g_bin, *rest)


def middle_body(held_back, lens, x_ref, mem_ref, gout_ref, mix_one, ckv_ref, wt_cross, w_proj, far_in, far_out, vectors, b_in,
           out_ref, g_resid, g_mix, g_mem, gw_cross, gw_proj, gw_in, gw_out, g_vec, g_bin,
           dkv_ref, cols,
           e_ref, q_ref, inv_ref, mix_two, gmix_two, dq_ref, acc_cross, acc_proj, acc_in, acc_out, acc_vec, acc_bin, acc_col,
           n_one, n_two, scale_two, two_low, act, g_inner, g_ff, g_cross, g_two, w_in, w_out, come):
    tags, width = x_ref.shape[1:]
    cells = mem_ref.shape[1]
    i = pl.program_id(0)
    count = pl.num_programs(0)
    arrivals = [pltpu.make_async_copy(src, dst, come.at[k]) for k, (src, dst) in enumerate(((far_in, w_in), (far_out, w_out)))]

    @pl.when(i == 0)
    def _():
        for ref in (acc_cross, acc_proj, acc_in, acc_out, acc_vec, acc_bin, acc_col):
            ref[...] = jnp.zeros_like(ref)
        cols[...] = vectors[...].T
        for copy in arrivals:
            copy.start()

    def vec(k):
        return vectors[k : k + 1, :]

    def add(k, value):
        acc_vec[k : k + 1, :] += value

    if held_back:
        scale_out, *places, gone = held_back
        sources = (e_ref, q_ref, inv_ref, mix_two, gmix_two, n_one, g_two, acc_cross, acc_proj.at[0])
        copies = [pltpu.make_async_copy(src, dst, gone.at[k]) for k, (src, dst) in enumerate(zip(sources, places))]

    def leave(*numbers):
        if held_back:
            @pl.when(i == count - 1)
            def _():
                for number in numbers:
                    copies[number].start()

    leave(7, 8)
    mix_one_t = mix_one[0].reshape(width, tags)
    resid = x_ref[0].astype(f32) + dot(mix_one_t, w_proj[0], 0, 0) + vec(2)
    normed, scale_one = norm(resid)
    n_one[...] = normed
    one = normed * vec(10) + vec(6)
    one_low = one.astype(bf16)
    cq = (dot(wt_cross[:width], one_low, 1, 1) + cols[:, 3:4]).astype(bf16) * bf16(HEAD_DIM ** -0.5)
    q_ref[...] = cq.reshape(q_ref.shape)
    leave(1, 5)

    keys = ckv_ref[0, :HEADS].astype(f32)
    queries = q_ref[...].astype(f32)
    bound = jnp.max(jnp.sum(keys * keys, 1)) * jnp.max(jnp.sum(queries * queries, 1))
    tame = bound < TAME * TAME

    def forward(shifted, h, _):
        s = dot(ckv_ref[0, h], q_ref[h], 0, 0)
        if shifted:
            s = s - jnp.max(s, 0, keepdims=True)
        e = jnp.exp(s).astype(bf16)
        e_ref[h] = e
        mixed = dot(with_ones(ckv_ref[0, HEADS + h]), e, 1, 0)
        inv = 1.0 / mixed[HEAD_DIM : HEAD_DIM + 1]
        inv_ref[pl.ds(h, 1), :] = inv
        mix_two[h] = (mixed[:HEAD_DIM] * inv).astype(bf16)
        return 0

    @pl.when(tame)
    def _():
        lax.fori_loop(0, HEADS, functools.partial(forward, False), 0, unroll=4)

    @pl.when(jnp.logical_not(tame))
    def _():
        lax.fori_loop(0, HEADS, functools.partial(forward, True), 0)

    leave(0, 2, 3)
    @pl.when(i == 0)
    def _():
        for copy in arrivals:
            copy.wait()

    mix_two_t = mix_two[...].reshape(width, tags)
    root = 0.7978845608028654
    rows = tags // CHUNKS
    totals = {}

    def tally(k, value):
        totals[k] = totals[k] + column_sums(value) if k in totals else column_sums(value)

    for first in range(0, tags, rows):
        at = slice(first, first + rows)
        resid = n_one[at] * vec(10) + vec(6) + dot(mix_two_t[:, at], w_proj[1], 0, 0) + vec(5)
        normed, scale = norm(resid)
        n_two[at] = normed
        scale_two[at] = scale
        two = normed * vec(11) + vec(7)
        two_low[at] = two.astype(bf16)
        inner = dot(two_low[at], w_in[...], 1, 0) + b_in[...]
        square = inner * inner
        tanh = jnp.tanh(inner * (root + (root * 0.044715) * square))
        half_more = 0.5 + 0.5 * tanh
        act[at] = (inner * half_more).astype(bf16)
        slope = half_more + inner * (half_more * (1.0 - tanh)) * (root + (3 * 0.044715 * root) * square)
        resid = two + dot(act[at], w_out[...], 1, 0) + vec(9)
        three, scale = norm(resid)
        valid = lax.broadcasted_iota(jnp.int32, (rows, 1), 0) + first < lens[i]
        out_ref[0, at] = jnp.where(valid, three * vec(12) + vec(8), 0.0).astype(bf16)
        grad = jnp.where(valid, gout_ref[0, at].astype(f32), 0.0)
        tally(12, grad * three)
        tally(8, grad)
        g_three = norm_back(grad, three, scale, vec(12))
        g_ff[at] = g_three.astype(bf16)
        tally(9, g_three)
        back = dot(g_ff[at], w_out[...], 1, 1) * slope
        tally(-1, back)
        g_inner[at] = back.astype(bf16)
        back = g_three + dot(g_inner[at], w_in[...], 1, 1)
        tally(11, back * n_two[at])
        tally(7, back)
        back = norm_back(back, n_two[at], scale_two[at], vec(11))
        tally(5, back)
        g_two[at] = back
        g_cross[at] = back.astype(bf16)

    for k, value in totals.items():
        if k >= 0:
            add(k, value)
    acc_bin[...] += totals[-1]
    acc_out[...] += dot(act[...], g_ff[...], 0, 0)
    acc_in[...] += dot(two_low[...], g_inner[...], 0, 0)
    acc_proj[1] += dot(mix_two_t, g_cross[...], 1, 0)
    gmix_two[...] = dot(w_proj[1], g_cross[...], 1, 1).astype(bf16).reshape(gmix_two.shape)

    def rest_of_image():
        def backward(h, _):
            dq_ref[h], dkv_ref[h], dkv_ref[HEADS + h] = cross_back(
                h, e_ref[h], ckv_ref[0, h], ckv_ref[0, HEADS + h], q_ref[h], gmix_two[h], mix_two[h], inv_ref[pl.ds(h, 1), :])
            return 0

        lax.fori_loop(0, HEADS, backward, 0, unroll=4)
        dq = dq_ref[...].reshape(width, tags)
        dkv = dkv_ref[...].reshape(2 * width, cells)
        acc_col[0] += lane_groups(dq.astype(f32))
        acc_col[1] += memory_lanes(dkv[width:].astype(f32))
        acc_cross[:width] += dot(dq, one_low, 1, 0)
        acc_cross[width:] += dot(dkv, mem_ref[0], 1, 0)
        g_mem[0] = dot(dkv, wt_cross[width:], 0, 0)
        g_one = g_two[...] + dot(dq, wt_cross[:width], 0, 0)
        add(10, column_sums(g_one * n_one[...]))
        add(6, column_sums(g_one))
        g_one = norm_back(g_one, n_one[...], scale_one, vec(10))
        add(2, column_sums(g_one))
        g_resid[0] = g_one
        g_low = g_one.astype(bf16)
        acc_proj[0] += dot(mix_one_t, g_low, 1, 0)
        g_mix[0] = dot(w_proj[0], g_low, 1, 1).astype(bf16).reshape(g_mix.shape[1:])

    if held_back:
        pl.when(i < count - 1)(rest_of_image)

        @pl.when(i == count - 1)
        def _():
            scale_out[...] = scale_one

        leave(4, 6)
    else:
        rest_of_image()

    @pl.when(i == count - 1)
    def _():
        if held_back:
            gw_proj[...] = acc_proj[1].astype(bf16)
        else:
            gw_cross[...] = acc_cross[...].astype(bf16).T
            gw_proj[...] = acc_proj[...].astype(bf16)
        gw_in[...] = acc_in[...].astype(bf16)
        gw_out[...] = acc_out[...].astype(bf16)
        add(3, column_sums(acc_col[0].T))
        add(4, column_sums(acc_col[1].T))
        g_vec[...] = acc_vec[...]
        g_bin[...] = acc_bin[...]
        if held_back:
            for copy in copies:
                copy.wait()


def run_middle(lens, x, mem, gout, mix_one, ckv, wt_cross, w_proj, w_in, w_out, vectors, b_in, held_back=False):
    images, tags, width = x.shape
    cells = mem.shape[1]
    hidden = w_in.shape[1]
    sds = jax.ShapeDtypeStruct

    def per(*shape):
        return pl.BlockSpec((1,) + shape, lambda i, n: (i,) + (0,) * len(shape))

    def one(*shape):
        return pl.BlockSpec(shape, lambda i, n: (0,) * len(shape), pipeline_mode=pl.Buffered(1))

    def out(*shape):
        return pl.BlockSpec(shape, lambda i, n: (0,) * len(shape))

    def early(*shape):
        return pl.BlockSpec((1,) + shape, lambda i, n: (jnp.minimum(i, images - 2),) + (0,) * len(shape)) if held_back else per(*shape)

    done = images - 1 if held_back else images
    out_specs = [
        per(tags, width), early(tags, width), early(HEADS, HEAD_DIM, tags), early(cells, width),
        out(width, 3 * width), out(2, width, width), out(width, hidden), out(hidden, width), out(16, width), out(1, hidden),
    ]
    out_shape = [
        sds((images, tags, width), bf16), sds((done, tags, width), f32), sds((done, HEADS, HEAD_DIM, tags), bf16),
        sds((images, cells, width), f32),
        sds((width, 3 * width), bf16), sds((2, width, width), bf16), sds((width, hidden), bf16), sds((hidden, width), bf16),
        sds((16, width), f32), sds((1, hidden), f32),
    ]
    scratch = [
        pltpu.VMEM((2 * HEADS, HEAD_DIM, cells), bf16),
        pltpu.VMEM((width, 16), f32),
        pltpu.VMEM((HEADS, cells, tags), bf16),
        pltpu.VMEM((HEADS, HEAD_DIM, tags), bf16),
        pltpu.VMEM((HEADS, tags), f32),
        pltpu.VMEM((HEADS, HEAD_DIM, tags), bf16),
        pltpu.VMEM((HEADS, HEAD_DIM, tags), bf16),
        pltpu.VMEM((HEADS, HEAD_DIM, tags), bf16),
        pltpu.VMEM((3 * width, width), f32),
        pltpu.VMEM((2, width, width), f32),
        pltpu.VMEM((width, hidden), f32),
        pltpu.VMEM((hidden, width), f32),
        pltpu.VMEM((16, width), f32),
        pltpu.VMEM((1, hidden), f32),
        pltpu.VMEM((2, width, 128), f32),
        pltpu.VMEM((tags, width), f32),
        pltpu.VMEM((tags, width), f32),
        pltpu.VMEM((tags, 1), f32),
        pltpu.VMEM((tags, width), bf16),
        pltpu.VMEM((tags, hidden), bf16),
        pltpu.VMEM((tags, hidden), bf16),
        pltpu.VMEM((tags, width), bf16),
        pltpu.VMEM((tags, width), bf16),
        pltpu.VMEM((tags, width), f32),
        pltpu.VMEM((width, hidden), bf16),
        pltpu.VMEM((hidden, width), bf16),
        pltpu.SemaphoreType.DMA((2,)),
    ]
    if held_back:
        out_specs[4], out_shape[4] = out(8, 128), sds((8, 128), bf16)
        out_specs[5], out_shape[5] = out(width, width), sds((width, width), bf16)
        kept = [((HEADS, cells, tags), bf16), ((HEADS, HEAD_DIM, tags), bf16), ((HEADS, tags), f32), ((HEADS, HEAD_DIM, tags), bf16),
                ((HEADS, HEAD_DIM, tags), bf16), ((tags, width), f32), ((tags, width), f32), ((3 * width, width), f32), ((width, width), f32)]
        out_specs += [out(tags, 1)] + [pl.BlockSpec(memory_space=pl.ANY)] * len(kept)
        out_shape += [sds((tags, 1), f32)] + [sds(*k) for k in kept]
        scratch.append(pltpu.SemaphoreType.DMA((len(kept),)))
    return pl.pallas_call(
        functools.partial(middle, held_back),
        grid_spec=pltpu.PrefetchScalarGridSpec(
            num_scalar_prefetch=1,
            grid=(images,),
            in_specs=[
                per(tags, width), per(cells, width), per(tags, width), per(HEADS, HEAD_DIM, tags), per(2 * HEADS, HEAD_DIM, cells),
                one(3 * width, width), one(2, width, width), pl.BlockSpec(memory_space=pl.ANY), pl.BlockSpec(memory_space=pl.ANY), one(16, width), one(1, hidden),
            ],
            out_specs=out_specs,
            scratch_shapes=scratch,
        ),
        out_shape=out_shape,
        compiler_params=pltpu.CompilerParams(vmem_limit_bytes=62 * MIB),
        name="middle",
    )(lens, x, mem, gout, mix_one, ckv, wt_cross, w_proj, w_in, w_out, vectors, b_in)


def self_backward(x_ref, qkv_ref, near_ref, far_ref, inv_ref, mix_ref, gmix_ref, g_resid, wt_self,
                  g_tags, gw_self, g_col, d_ref, acc, acc_col):
    tags, width = x_ref.shape[1:]
    half = tags // 2
    i = pl.program_id(0)

    @pl.when(i == 0)
    def _():
        acc[...] = jnp.zeros_like(acc)
        acc_col[...] = jnp.zeros_like(acc_col)

    def head(h, _):
        grad = gmix_ref[0, h].astype(f32)
        inv = inv_ref[0, pl.ds(h, 1), :]
        delta = jnp.sum(grad * mix_ref[0, h].astype(f32), 0, keepdims=True) * inv
        grad = (grad * inv).astype(bf16)
        ext = with_delta(grad, delta)
        qt, kt, vt = qkv_ref[0, h], qkv_ref[0, HEADS + h], with_ones(qkv_ref[0, 2 * HEADS + h])
        near, far = near_ref[0, h], far_ref[0, h]
        ds_near = near * dot(vt[:, :half], ext[:, :half], 0, 0).astype(bf16)
        ds_far = far * dot(vt, ext[:, half:], 0, 0).astype(bf16)
        dv = dot(grad[:, half:], far, 1, 1)
        dk = dot(qt[:, half:], ds_far, 1, 1)
        d_ref[2 * HEADS + h, :, half:] = dv[:, half:].astype(bf16)
        d_ref[2 * HEADS + h, :, :half] = (dv[:, :half] + dot(grad[:, :half], near, 1, 1)).astype(bf16)
        d_ref[HEADS + h, :, half:] = dk[:, half:].astype(bf16)
        d_ref[HEADS + h, :, :half] = (dk[:, :half] + dot(qt[:, :half], ds_near, 1, 1)).astype(bf16)
        d_ref[h, :, :half] = (dot(kt[:, :half], ds_near, 1, 0) * HEAD_DIM ** -0.5).astype(bf16)
        d_ref[h, :, half:] = (dot(kt, ds_far, 1, 0) * HEAD_DIM ** -0.5).astype(bf16)
        return 0

    lax.fori_loop(0, HEADS, head, 0)
    d = d_ref[...].reshape(3 * width, tags)
    acc_col[0] += lane_groups(d[:width].astype(f32))
    acc_col[1] += lane_groups(d[2 * width :].astype(f32))
    acc[...] += dot(d, x_ref[0], 1, 0)
    g_tags[0] = g_resid[0] + dot(d, wt_self[...], 0, 0)

    @pl.when(i == pl.num_programs(0) - 1)
    def _():
        gw_self[...] = acc[...].astype(bf16).T
        g_col[0:1] = column_sums(acc_col[0].T)
        g_col[1:2] = column_sums(acc_col[1].T)


def run_self_backward(x, qkv, near, far, inv, mix, gmix, g_resid, wt_self):
    images, tags, width = x.shape
    half = tags // 2
    sds = jax.ShapeDtypeStruct

    def per(*shape):
        return pl.BlockSpec((1,) + shape, lambda i: (i,) + (0,) * len(shape))

    def one(*shape):
        return pl.BlockSpec(shape, lambda i: (0,) * len(shape))

    return pl.pallas_call(
        self_backward,
        grid=(images,),
        in_specs=[per(tags, width), per(3 * HEADS, HEAD_DIM, tags), per(HEADS, half, half), per(HEADS, tags, half), per(HEADS, tags),
                  per(HEADS, HEAD_DIM, tags), per(HEADS, HEAD_DIM, tags), per(tags, width),
                  one(3 * width, width)],
        out_specs=[per(tags, width), one(width, 3 * width), one(8, width)],
        out_shape=[sds((images, tags, width), f32), sds((width, 3 * width), bf16), sds((8, width), f32)],
        scratch_shapes=[pltpu.VMEM((3 * HEADS, HEAD_DIM, tags), bf16), pltpu.VMEM((3 * width, width), f32), pltpu.VMEM((2, width, 128), f32)],
        compiler_params=pltpu.CompilerParams(vmem_limit_bytes=60 * MIB),
        name="self_backward",
    )(x, qkv, near, far, inv, mix, gmix, g_resid, wt_self)


def layer(lens, x, mem, gout, w_self, w_cross, w_proj, w_in, w_out, vectors, b_in):
    width = x.shape[2]
    zero = jnp.zeros((width,), f32)
    bias_qkv = jnp.concatenate([vectors[0], zero, vectors[1]])[:, None]
    bias_kv = jnp.concatenate([zero, vectors[4]])[:, None]
    qkv, ckv, near, far, inv, mix, wt_self, wt_cross = run_self_forward(lens, x, mem, w_self, w_cross, bias_qkv, bias_kv)
    out, g_resid, gmix, g_mem, gw_cross, gw_proj, gw_in, gw_out, g_vec, g_bin = run_middle(
        lens, x, mem, gout, mix, ckv, wt_cross, w_proj, w_in, w_out, vectors, b_in)
    g_tags, gw_self, g_col = run_self_backward(x, qkv, near, far, inv, mix, gmix, g_resid, wt_self)
    g_vec = g_vec.at[0:2].set(g_col[0:2])
    return out, g_tags, g_mem, gw_self, gw_cross, gw_proj, gw_in, gw_out, g_vec, g_bin


ALL = slice(None)


SMALL, SELF, PROJ, CROSS, IN, OUT = range(6)
PLAN = (
    ((SMALL, 0), (SELF, 0), (PROJ, 0), (CROSS, 0), (IN, 0), (OUT, 0),
     (SMALL, 1), (SELF, 1), (SMALL, 2), (PROJ, 1), (SELF, 2), (SMALL, 3), (CROSS, 1), (PROJ, 2), (IN, 1), (SELF, 3), (CROSS, 2), (OUT, 1),
     (PROJ, 3), (SMALL, 4), (SELF, 4)),
    ((IN, 2),),
    ((OUT, 2),),
    ((CROSS, 3),),
    ((IN, 3),),
    ((OUT, 3),),
    (),
    ((CROSS, 4),),
    ((PROJ, 4), (IN, 4), (OUT, 4)),
)
MEANTIME = {2: (0, 4), 3: (1, 0), 4: (1, 4), 5: (2, 4)}


class Gathering:
    def __init__(self, dims, me, shard, held, lead, sems):
        self.dims, self.me, self.shard, self.held, self.lead = dims, me, shard, held, lead
        self.local, self.send, self.recv = sems

    def cell(self, *index):
        return self.held.at[(ALL,) * self.lead + index]

    def remote(self, slot, src, dst, peer):
        return pltpu.make_async_remote_copy(
            src_ref=src, dst_ref=dst, send_sem=self.send.at[slot], recv_sem=self.recv.at[slot],
            device_id=device(self.dims, *peer), device_id_type=MESH)

    def keep(self):
        return pltpu.make_async_copy(self.shard, self.cell(*self.me), self.local)

    def first(self):
        a, b, x, c = self.me
        outer = self.dims[0]
        return [self.remote(k - 1, self.shard, self.cell(a, b, x, c), (lax.rem(a + k, outer), b, x, c)) for k in range(1, outer)]

    def along_inner(self, core):
        a, b, x, c = self.me
        outer, inner, _ = self.dims
        piece = self.cell(ALL, b, ALL if core == 0 else x, c)
        return [self.remote(outer - 2 + k, piece, piece, (a, lax.rem(b + k, inner), x, c)) for k in range(1, inner)]

    def along_across(self, core):
        a, b, x, c = self.me
        outer, inner, across = self.dims
        piece = self.cell(ALL, b if core == 0 else ALL, x, c)
        return [self.remote(outer + inner - 3 + k, piece, piece, (a, b, lax.rem(x + k, across), c)) for k in range(1, across)]

    def second(self, core):
        return self.along_across(core) if core == 0 else self.along_inner(core)

    def third(self, core):
        return self.along_inner(core) if core == 0 else self.along_across(core)

    def handed(self, core, holder):
        a, b, x, c = self.me
        outer, inner, across = self.dims
        base = outer + inner + across - 3

        def piece(slot, row, column):
            ref = self.cell(ALL, row, column, holder)
            return self.remote(base + slot, ref, ref, (a, b, x, 1 - c))

        own = [piece(0, b, x)]
        by_inner = [piece(k, lax.rem(b + k, inner), ALL if core == 0 else x) for k in range(1, inner)]
        by_across = [piece(inner - 1 + k, b if core == 0 else ALL, lax.rem(x + k, across)) for k in range(1, across)]
        return (own, by_across, by_inner) if core == 0 else (own, by_inner, by_across)

    def begin(self):
        self.keep().start()
        for copy in self.first():
            copy.start()

    def each_core(self, act):
        for core in (0, 1):
            pl.when(self.me[3] == core)(functools.partial(act, core))

    def advance(self, stage):
        def act(core):
            if stage == 1:
                self.keep().wait()
            for copy in (self.first(), self.second(core), self.third(core))[stage - 1]:
                copy.wait_recv()
            following = (self.second(core), self.third(core), [])[stage - 1]
            for copy in following + self.handed(core, self.me[3])[stage - 1]:
                copy.start()
        self.each_core(act)

    def finish(self):
        def act(core):
            for group in self.handed(1 - core, 1 - self.me[3]):
                for copy in group:
                    copy.wait_recv()
        self.each_core(act)

    def drain(self):
        def act(core):
            for copy in self.first() + self.second(core) + self.third(core) + sum(self.handed(core, self.me[3]), []):
                copy.wait_send()
        self.each_core(act)


def gather_slots(dims):
    outer, inner, across = dims
    return outer + 2 * (inner + across) - 4


def spread(held, row_lanes, width, rows):
    devices = held.shape[0] // 16
    lane = lax.broadcasted_iota(jnp.int32, (128, width), 0)
    at = lax.broadcasted_iota(jnp.int32, (128, width), 1)
    pick = jnp.where((lax.rem(at, row_lanes) == lane), 1.0, 0.0).astype(bf16)
    wide = dot(held, pick, 1, 0)
    owner = lax.broadcasted_iota(jnp.int32, (devices * 16, width), 0) // 16
    at = lax.broadcasted_iota(jnp.int32, (devices * 16, width), 1)
    wide = jnp.where(at // row_lanes == owner, wide, 0.0)
    return jnp.sum(wide.reshape(devices, 16, width), 0)


def opening(dims, lens, x_ref, mem_ref, b_ref, g_ref, h_ref, s_cross, s_self, s_proj, s_in, s_out,
            qkv_ref, ckv_ref, low_ref, high_ref, inv_ref, mix_ref, out_self, out_cross, vec_ref, bin_ref, o_proj, o_in, o_out,
            small, small_low, h_small, h_self, h_cross, wt_self, wt_cross, cols, low_a, high_a, low_b, high_b, tile, beyond, gone, local, send, recv):
    width = x_ref.shape[2]
    tags = x_ref.shape[1]
    half = tags // 2
    step = pl.program_id(0)
    images = pl.num_programs(0) // 2
    me = place(dims)
    pairs = ((small_low, h_small, 0), (s_self, h_self, 0), (s_proj, o_proj, 1), (s_cross, h_cross, 0), (s_in, o_in, 0), (s_out, o_out, 0))
    gs = [Gathering(dims, me, shard, held, lead, (local.at[k], send.at[k], recv.at[k])) for k, (shard, held, lead) in enumerate(pairs)]
    keep_self = pltpu.make_async_copy(wt_self, out_self, gone.at[0])
    keep_cross = pltpu.make_async_copy(wt_cross, out_cross, gone.at[1])

    def play(slot):
        for item, stage in PLAN[slot]:
            item = gs[item]
            item.begin() if stage == 0 else item.finish() if stage == 4 else item.advance(stage)

    def slot_at(number, slot):
        @pl.when(step == number)
        def _():
            play(slot)

    @pl.when(step == 0)
    def _():
        small[...] = jnp.zeros_like(small)
        small[0:10, : b_ref.shape[1]] = b_ref[...].astype(f32)
        small[10:13, : g_ref.shape[1]] = g_ref[...].astype(f32)
        small[13:14, : h_ref.shape[1]] = h_ref[...].astype(f32)
        small_low[...] = small[...].astype(bf16)
        greet(dims, me)
        play(0)
        vectors = spread(h_small[...].reshape(-1, 128), b_ref.shape[1], width, 16)
        vec_ref[...] = vectors
        bin_ref[...] = spread(h_small[...].reshape(-1, 128), h_ref.shape[1], bin_ref.shape[1], 16)[13:14]
        cols[...] = vectors.T
        wt_self[...] = h_self[...].reshape(width, 3 * width).T
        keep_self.start()

    @pl.when(step < images)
    def _():
        qkv = dot(wt_self[...], x_ref[0], 1, 1)
        qkv_ref[0, :HEADS] = ((qkv[:width] + cols[:, 0:1]).astype(bf16) * bf16(HEAD_DIM ** -0.5)).reshape(HEADS, HEAD_DIM, tags)
        qkv_ref[0, HEADS : 2 * HEADS] = qkv[width : 2 * width].astype(bf16).reshape(HEADS, HEAD_DIM, tags)
        qkv_ref[0, 2 * HEADS :] = (qkv[2 * width :] + cols[:, 1:2]).astype(bf16).reshape(HEADS, HEAD_DIM, tags)

    @pl.when(step < images)
    def _():
        key_at, query_at = lax.broadcasted_iota(jnp.int32, (half, half), 0), lax.broadcasted_iota(jnp.int32, (half, half), 1)
        tile[...] = jnp.where(key_at <= query_at, 0.0, MASKED)
        row, key_at = lax.broadcasted_iota(jnp.int32, beyond.shape, 0), lax.broadcasted_iota(jnp.int32, beyond.shape, 1)
        hidden = jnp.logical_and(row == 0, key_at >= lens[jnp.minimum(step, images - 1)])
        beyond[...] = jnp.where(hidden, MASKED, 0.0).astype(bf16)

    def scores(h, low, high):
        qt, kt = with_ones(qkv_ref[0, h]), jnp.concatenate([qkv_ref[0, HEADS + h], beyond[...]], 0)
        s = dot(kt[:, :half], qt, 0, 0)
        left, right = s[:, :half] + tile[...], s[:, half:]
        under = dot(kt[:, half:], qt[:, half:], 0, 0) + tile[...]
        low[:, :half] = left
        low[:, half:] = right
        high[...] = under
        return jnp.max(left, 0, keepdims=True), jnp.maximum(jnp.max(right, 0, keepdims=True), jnp.max(under, 0, keepdims=True))

    def mix(h, low, high, tops):
        vt = with_ones(qkv_ref[0, 2 * HEADS + h])
        e_low = jnp.concatenate([jnp.exp(low[:, :half] - tops[0]).astype(bf16), jnp.exp(low[:, half:] - tops[1]).astype(bf16)], 1)
        e_high = jnp.exp(high[...] - tops[1]).astype(bf16)
        low_ref[0, h] = e_low
        high_ref[0, h] = e_high
        mixed = dot(vt[:, :half], e_low, 1, 0)
        mixed = jnp.concatenate([mixed[:, :half], mixed[:, half:] + dot(vt[:, half:], e_high, 1, 0)], 1)
        inv = 1.0 / mixed[HEAD_DIM : HEAD_DIM + 1]
        inv_ref[0, h : h + 1] = inv
        mix_ref[0, h] = (mixed[:HEAD_DIM] * inv).astype(bf16)

    def pair(h, tops):
        following = scores(h + 1, low_b, high_b)
        mix(h, low_a, high_a, tops)
        if h + 2 < HEADS:
            tops = scores(h + 2, low_a, high_a)
        mix(h + 1, low_b, high_b, following)
        return tops

    slot_at(0, 1)

    @pl.when(step < images)
    def _():
        tops = scores(0, low_a, high_a)
        for h in range(0, HEADS, 2):
            for slot, (image, number) in MEANTIME.items():
                if number == h:
                    pl.when(step == image)(functools.partial(play, slot))
            tops = pair(h, tops)

    @pl.when(step == images)
    def _():
        play(7)
        wt_cross[...] = h_cross[...].reshape(width, 3 * width).T
        keep_cross.start()

    @pl.when(step >= images)
    def _():
        kv = dot(wt_cross[width:], mem_ref[0], 1, 1)
        ckv_ref[0, :HEADS] = kv[:width].astype(bf16).reshape(HEADS, HEAD_DIM, -1)
        ckv_ref[0, HEADS:] = (kv[width:] + cols[:, 4:5]).astype(bf16).reshape(HEADS, HEAD_DIM, -1)

    @pl.when(step == 2 * images - 1)
    def _():
        play(8)
        for g in gs:
            g.drain()
        keep_self.wait()
        keep_cross.wait()


def run_opening(dims, lens, x, mem, biases, gains, b_in, shards):
    images, tags, width = x.shape
    cells = mem.shape[1]
    half = tags // 2
    hidden = b_in.shape[1] * dims[0] * dims[1] * dims[2] * 2
    sds = jax.ShapeDtypeStruct

    def early(*shape):
        return pl.BlockSpec((1,) + shape, lambda i: (jnp.minimum(i, images - 1),) + (0,) * len(shape))

    def late(*shape):
        return pl.BlockSpec((1,) + shape, lambda i: (jnp.maximum(i - images, 0),) + (0,) * len(shape))

    def one(*shape):
        return pl.BlockSpec(shape, lambda i: (0,) * len(shape))

    def held(shard, lead):
        return shard.shape[:lead] + dims + (2,) + shard.shape[lead:]

    s_cross, s_self, s_proj, s_in, s_out = shards
    rows = s_cross.shape[0]
    cell = dims + (2, rows)
    anywhere = pl.BlockSpec(memory_space=pl.ANY)
    n = len(shards) + 1
    slots = gather_slots(dims)
    return pl.pallas_call(
        functools.partial(opening, dims),
        grid=(2 * images,),
        in_specs=[pl.BlockSpec(memory_space=pltpu.SMEM), early(tags, width), late(cells, width), one(*biases.shape), one(*gains.shape), one(*b_in.shape)]
        + [anywhere] * len(shards),
        out_specs=[
            early(3 * HEADS, HEAD_DIM, tags), late(2 * HEADS, HEAD_DIM, cells), early(HEADS, half, tags), early(HEADS, half, half),
            early(HEADS, tags), early(HEADS, HEAD_DIM, tags), anywhere, anywhere, one(16, width), one(1, hidden),
            anywhere, anywhere, anywhere,
        ],
        out_shape=[
            sds((images, 3 * HEADS, HEAD_DIM, tags), bf16),
            sds((images, 2 * HEADS, HEAD_DIM, cells), bf16),
            sds((images, HEADS, half, tags), bf16),
            sds((images, HEADS, half, half), bf16),
            sds((images, HEADS, tags), f32),
            sds((images, HEADS, HEAD_DIM, tags), bf16),
            sds((3 * width, width), bf16),
            sds((3 * width, width), bf16),
            sds((16, width), f32),
            sds((1, hidden), f32),
            sds(held(s_proj, 1), bf16),
            sds(held(s_in, 0), bf16),
            sds(held(s_out, 0), bf16),
        ],
        scratch_shapes=[
            pltpu.VMEM((16, 128), f32), pltpu.VMEM((16, 128), bf16), pltpu.VMEM(dims + (2, 16, 128), bf16),
            pltpu.VMEM(cell + (3 * width,), bf16), pltpu.VMEM(cell + (3 * width,), bf16),
            pltpu.VMEM((3 * width, width), bf16), pltpu.VMEM((3 * width, width), bf16),
            pltpu.VMEM((width, 16), f32), pltpu.VMEM((half, tags), f32), pltpu.VMEM((half, half), f32), pltpu.VMEM((half, tags), f32), pltpu.VMEM((half, half), f32),
            pltpu.VMEM((half, half), f32), pltpu.VMEM((16, tags), bf16),
            pltpu.SemaphoreType.DMA((2,)),
            pltpu.SemaphoreType.DMA((n,)), pltpu.SemaphoreType.DMA((n, slots)), pltpu.SemaphoreType.DMA((n, slots)),
        ],
        compiler_params=pltpu.CompilerParams(collective_id=0, has_side_effects=True, vmem_limit_bytes=58 * MIB),
        name="opening",
    )(lens, x, mem, biases, gains, b_in, *shards)


class Scattering:
    def __init__(self, dims, me, grads, short, out, lead, held, sems):
        self.dims, self.me, self.grads, self.short, self.out, self.lead = dims, me, grads, short, out, lead
        self.pair, self.by_inner, self.by_across, self.by_outer, self.last = held
        self.send, self.recv = sems

    def at(self, *index):
        return (ALL,) * self.lead + index

    def remote(self, slot, src, dst, peer):
        return pltpu.make_async_remote_copy(
            src_ref=src, dst_ref=dst, send_sem=self.send.at[slot], recv_sem=self.recv.at[slot],
            device_id=device(self.dims, *peer), device_id_type=MESH)

    def swap(self):
        a, b, x, c = self.me
        return [self.remote(0, self.grads.at[self.at(ALL, ALL, ALL, 1 - c)], self.pair, (a, b, x, 1 - c))]

    def along_inner(self, core):
        a, b, x, c = self.me
        inner = self.dims[1]
        res = []
        for k in range(1, inner):
            peer = lax.rem(b + k, inner)
            src = self.pair.at[self.at(ALL, peer)] if core == 0 else self.by_across.at[0].at[self.at(ALL, peer)]
            dst = self.by_inner.at[k - 1] if core == 0 else self.by_outer.at[k - 1]
            res.append(self.remote(k, src, dst, (a, peer, x, c)))
        return res

    def along_across(self, core):
        a, b, x, c = self.me
        _, inner, across = self.dims
        res = []
        for k in range(1, across):
            peer = lax.rem(x + k, across)
            src = self.pair.at[self.at(ALL, ALL, peer)] if core == 1 else self.by_inner.at[0].at[self.at(ALL, peer)]
            dst = self.by_across.at[k - 1] if core == 1 else self.by_outer.at[k - 1]
            res.append(self.remote(inner - 1 + k, src, dst, (a, b, peer, c)))
        return res

    def second(self, core):
        return self.along_inner(core) if core == 0 else self.along_across(core)

    def third(self, core):
        return self.along_across(core) if core == 0 else self.along_inner(core)

    def along_outer(self):
        a, b, x, c = self.me
        outer, inner, across = self.dims
        return [
            self.remote(inner + across - 2 + k, self.by_outer.at[0].at[self.at(lax.rem(a + k, outer))], self.last.at[k - 1],
                        (lax.rem(a + k, outer), b, x, c))
            for k in range(1, outer)
        ]

    def over_plane(self):
        a, b, x, c = self.me
        _, inner, across = self.dims
        res = []
        for k in range(1, inner * across):
            row, column = lax.rem(b + k // across, inner), lax.rem(x + k % across, across)
            res.append(self.remote(k, self.pair.at[:, row, column], self.by_inner.at[k - 1], (a, row, column, c)))
        return res

    def from_plane(self):
        a, b, x, c = self.me
        outer, inner, across = self.dims
        return [
            self.remote(inner * across - 1 + k, self.by_outer.at[0, lax.rem(a + k, outer)], self.last.at[k - 1], (lax.rem(a + k, outer), b, x, c))
            for k in range(1, outer)
        ]

    def begin(self):
        for copy in self.swap():
            copy.start()

    def advance_short(self, stage):
        a, b, x, c = self.me
        outer, inner, across = self.dims

        def up(value):
            return value.astype(f32)

        for copy in (self.swap(), self.over_plane(), self.from_plane())[stage - 1]:
            copy.wait_recv()
        if stage == 1:
            self.pair[...] = (up(self.grads[:, :, :, c]) + up(self.pair[...])).astype(bf16)
            following = self.over_plane()
        elif stage == 2:
            total = up(self.pair[:, b, x])
            for k in range(inner * across - 1):
                total = total + up(self.by_inner[k])
            self.by_outer[0] = total.astype(bf16)
            following = self.from_plane()
        else:
            total = up(self.by_outer[0, a])
            for k in range(outer - 1):
                total = total + up(self.last[k])
            self.out[...] = total
            following = []
        for copy in following:
            copy.start()

    def advance(self, stage):
        if self.short:
            return self.advance_short(stage)
        a, b, x, c = self.me
        _, inner, across = self.dims

        def up(value):
            return value.astype(f32)

        def act(core):
            for copy in (self.swap(), self.second(core), self.third(core), self.along_outer())[stage - 1]:
                copy.wait_recv()
            if stage == 1:
                def add(k, _):
                    self.pair[k] = (up(self.grads[k, :, :, c]) + up(self.pair[k])).astype(bf16)
                    return 0
                following = self.second(core)
            elif stage == 2:
                held = self.by_inner if core == 0 else self.by_across

                def add(k, _):
                    total = up(self.pair[k, b] if core == 0 else self.pair[k, :, x])
                    for j in range((inner if core == 0 else across) - 1):
                        total = total + up(held[j, k])
                    held[0, k] = total.astype(bf16)
                    return 0
                following = self.third(core)
            elif stage == 3:
                held = self.by_inner if core == 0 else self.by_across

                def add(k, _):
                    total = up(held[0, k, x if core == 0 else b])
                    for j in range((across if core == 0 else inner) - 1):
                        total = total + up(self.by_outer[j, k])
                    self.by_outer[0, k] = total.astype(bf16)
                    return 0
                following = self.along_outer()
            else:
                total = up(self.by_outer[(0,) + self.at(a)])
                for k in range(self.dims[0] - 1):
                    total = total + up(self.last[k])
                self.out[...] = total
                following = []
            if stage < 4:
                lax.fori_loop(0, self.dims[0], add, 0)
            for copy in following:
                copy.start()

        for core in (0, 1):
            pl.when(c == core)(functools.partial(act, core))

    def drain(self):
        def act(core):
            for copy in self.swap() + self.second(core) + self.third(core) + self.along_outer():
                copy.wait_send()

        if self.short:
            for copy in self.swap() + self.over_plane() + self.from_plane():
                copy.wait_send()
            return
        for core in (0, 1):
            pl.when(self.me[3] == core)(functools.partial(act, core))


def scatter_slots(dims):
    return max(dims[0] + dims[1] + dims[2] - 2, dims[0] + dims[1] * dims[2] - 1)


def scatter_space(dims, lead, tail, short=False):
    outer, inner, across = dims
    if short:
        return [(outer, inner, across) + tail, (inner * across - 1, outer) + tail, (1,) + tail, (1, outer) + tail, (outer - 1,) + tail]
    return [
        lead + (outer, inner, across) + tail,
        (inner - 1,) + lead + (outer, across) + tail,
        (across - 1,) + lead + (outer, inner) + tail,
        (max(inner, across) - 1,) + lead + (outer,) + tail,
        (outer - 1,) + lead + tail,
    ]


def collect(rows, row_lanes, devices):
    width = rows.shape[1]
    many = jnp.broadcast_to(rows[None], (devices, 16, width)).reshape(devices * 16, width)
    owner = lax.broadcasted_iota(jnp.int32, many.shape, 0) // 16
    at = lax.broadcasted_iota(jnp.int32, many.shape, 1)
    many = jnp.where(at // row_lanes == owner, many, 0.0).astype(bf16)
    lane = lax.broadcasted_iota(jnp.int32, (128, width), 0)
    at = lax.broadcasted_iota(jnp.int32, (128, width), 1)
    pick = jnp.where(lax.rem(at, row_lanes) == lane, 1.0, 0.0).astype(bf16)
    return dot(many, pick, 1, 1)


G_OUT, G_IN, G_ONE, G_CROSS, G_ZERO, G_HALF, G_REST, G_SMALL = range(8)
SHORT = (G_REST, G_SMALL)
EVENTS = {
    (0, 0): ((G_OUT, 0), (G_IN, 0), (G_ONE, 0)),
    (0, 1): ((G_OUT, 1),),
    (0, 2): ((G_IN, 1), (G_ONE, 1)),
    (0, 6): ((G_CROSS, 0),),
    (0, 7): ((G_ZERO, 0), (G_OUT, 2)),
    (1, 1): ((G_IN, 2),),
    (2, 1): ((G_CROSS, 1), (G_ONE, 2), (G_ZERO, 1)),
    (3, 1): ((G_HALF, 0), (G_OUT, 3), (G_IN, 3)),
    (5, 1): ((G_OUT, 4), (G_CROSS, 2), (G_HALF, 1), (G_ONE, 3)),
    (6, 1): ((G_REST, 0), (G_SMALL, 0), (G_ZERO, 2), (G_IN, 4)),
    (8, 1): ((G_ONE, 4), (G_CROSS, 3)),
    (9, 1): ((G_HALF, 2), (G_REST, 1), (G_SMALL, 1), (G_ZERO, 3)),
    (9, 2): ((G_HALF, 3), (G_REST, 2), (G_SMALL, 2), (G_CROSS, 4), (G_ZERO, 4), (G_HALF, 4), (G_REST, 3), (G_SMALL, 3)),
}


def closing(dims, x_ref, qkv_ref, low_ref, high_ref, inv_ref, mix_ref, gmix_ref, inv_two, vectors, g_vec, g_bin, scale_one,
            low_out, low_in, low_one, e_any, ckv_any, q_any, mix_two_any, gmix_two_any, mix_any, two_any, one_any, wc_any, mem_any, ac_any, ap_any, wp_any, ws_any, gres_any,
            g_tags, sh_out, sh_in, sh_one, sh_cross, sh_zero, sh_half, sh_rest, sh_small, g_mem,
            e_ref, ckv_ref, q_ref, mix_two, gmix_two, mine_out, mine_in, mine_one, gres_ref, dkv_ref,
            mix_one, g_two, n_one, wt_cross, mem_ref, acc_cross, acc_zero, w_zero, wt_self,
            dq_ref, gmix_last, gres_last, gmix_now, acc, add_vec, acc_col, low_cross, low_zero, low_half, low_rest, low_small, head_sem, in_sem, *rest):
    tags, width = x_ref.shape[1:]
    cells = mem_ref.shape[0]
    half = tags // 2
    some = HEADS // 2
    step = pl.program_id(0)
    images = pl.num_programs(0) // 3
    me = place(dims)
    devices = dims[0] * dims[1] * dims[2] * 2
    held, (send, recv) = rest[:-2], rest[-2:]
    triples = ((mine_out, None, sh_out), (mine_in, None, sh_in), (mine_one, None, sh_one), (low_cross, None, sh_cross),
               (low_zero, None, sh_zero), (low_half, None, sh_half), (low_rest, None, sh_rest), (low_small, None, sh_small))
    every = [Scattering(dims, me, grads, k in SHORT, out, 0, held[5 * k : 5 * k + 5], (send.at[k], recv.at[k])) for k, (grads, _, out) in enumerate(triples)]
    fetches = [
        pltpu.make_async_copy(src, dst, in_sem.at[k])
        for k, (src, dst) in enumerate((
            (low_out, mine_out), (low_in, mine_in), (low_one, mine_one),
            (one_any, n_one), (mem_any.at[images - 1], mem_ref), (ac_any, acc_cross), (two_any, g_two), (wc_any, wt_cross),
            (mix_any.at[images - 1], mix_one), (ap_any, acc_zero), (wp_any.at[0], w_zero), (gres_any, gres_ref), (ws_any, wt_self)))
    ]

    def e_rows(h):
        return e_ref.at[pl.ds(pl.multiple_of(h * cells, 16), cells)]

    def head_fetches(h):
        pairs = ((e_any.at[h], e_rows(h)), (ckv_any.at[images - 1, h], ckv_ref.at[h]), (ckv_any.at[images - 1, HEADS + h], ckv_ref.at[HEADS + h]),
                 (q_any.at[h], q_ref.at[h]), (mix_two_any.at[h], mix_two.at[h]), (gmix_two_any.at[h], gmix_two.at[h]))
        return [pltpu.make_async_copy(src, dst, head_sem.at[h, k]) for k, (src, dst) in enumerate(pairs)]

    def play(number, where):
        for item, stage in EVENTS.get((number, where), ()):
            item = every[item]
            item.begin() if stage == 0 else item.advance(stage)

    def events(where):
        for number in sorted(number for number, at in EVENTS if at == where and number > 0):
            pl.when(step == number)(functools.partial(play, number, where))

    def vec(k):
        return vectors[k : k + 1, :]

    @pl.when(step == 0)
    def _():
        for fetch in fetches[:3]:
            fetch.start()
        for h in range(HEADS):
            for fetch in head_fetches(h):
                fetch.start()
        for fetch in fetches[3:]:
            fetch.start()
        acc_col[...] = jnp.zeros_like(acc_col)
        greet(dims, me, True)
        for fetch in fetches[:3]:
            fetch.wait()
        play(0, 0)

        for first in (0, some):
            for h in range(first, first + some):
                for fetch in head_fetches(h):
                    fetch.wait()
            for h in range(first, first + some):
                dq_ref[h], dkv_ref[h], dkv_ref[HEADS + h] = cross_back(
                    h, e_rows(h)[...], ckv_ref[h], ckv_ref[HEADS + h], q_ref[h], gmix_two[h], mix_two[h], inv_two[h : h + 1, :])
            play(0, 1 + first // some)
        for fetch in fetches[3:11]:
            fetch.wait()
        dq = dq_ref[...].reshape(width, tags)
        dkv = dkv_ref[...].reshape(2 * width, cells)
        one_low = (n_one[...] * vec(10) + vec(6)).astype(bf16)
        acc_cross[:width] += dot(dq, one_low, 1, 0)
        acc_cross[width:] += dot(dkv, mem_ref[...], 1, 0)
        low_cross[...] = acc_cross[...].astype(bf16).T.reshape(low_cross.shape)
        play(0, 6)
        g_one = g_two[...] + dot(dq, wt_cross[:width], 0, 0)
        sum_gain, sum_shift = column_sums(g_one * n_one[...]), column_sums(g_one)
        g_one = norm_back(g_one, n_one[...], scale_one[...], vec(10))
        gres_last[...] = g_one
        g_low = g_one.astype(bf16)
        acc_zero[...] += dot(mix_one[...].reshape(width, tags), g_low, 1, 0)
        low_zero[...] = acc_zero[...].astype(bf16).reshape(low_zero.shape)
        play(0, 7)
        gmix_last[...] = dot(w_zero[...], g_low, 1, 1).astype(bf16).reshape(gmix_last.shape)
        at = lax.broadcasted_iota(jnp.int32, add_vec.shape, 0)
        total = g_vec[...]
        for k, row in ((2, column_sums(g_one)), (3, column_sums(lane_groups(dq.astype(f32)).T)),
                       (4, column_sums(memory_lanes(dkv[width:].astype(f32)).T)), (6, sum_shift), (10, sum_gain)):
            total = total + jnp.where(at == k, row, 0.0)
        add_vec[...] = total

    turn = jnp.maximum(step - 1, 0)
    part = jnp.minimum(turn // images, 1)
    now = lax.rem(turn, images)
    backward = jnp.logical_and(step >= 1, step <= 2 * images)

    @pl.when(jnp.logical_and(backward, now < images - 1))
    def _():
        gmix_now[...] = gmix_ref[0]

    @pl.when(jnp.logical_and(backward, now == images - 1))
    def _():
        gmix_now[...] = gmix_last[pl.ds(part * some, some)]

    def d_rows(image, kind, h, count=1):
        return pl.ds(pl.multiple_of(((image * 3 + kind) * HEADS + h) * HEAD_DIM, HEAD_DIM), count * HEAD_DIM)

    def head(h, _):
        grad = gmix_now[h].astype(f32)
        inv = inv_ref[0, pl.ds(part * some + h, 1), :]
        delta = jnp.sum(grad * mix_ref[0, h].astype(f32), 0, keepdims=True) * inv
        grad = (grad * inv).astype(bf16)
        ext = with_delta(grad, delta)
        qt, kt, vt = qkv_ref[0, 0, h], qkv_ref[0, 1, h], with_ones(qkv_ref[0, 2, h])
        e_low, e_high = low_ref[0, h], high_ref[0, h]
        ds_low = e_low * dot(vt[:, :half], ext, 0, 0).astype(bf16)
        ds_high = e_high * dot(vt[:, half:], ext[:, half:], 0, 0).astype(bf16)
        dv = jnp.concatenate([dot(grad, e_low, 1, 1), dot(grad[:, half:], e_high, 1, 1)], 1)
        dk = jnp.concatenate([dot(qt, ds_low, 1, 1), dot(qt[:, half:], ds_high, 1, 1)], 1)
        dq = dot(kt[:, :half], ds_low, 1, 0)
        dq = jnp.concatenate([dq[:, :half], dq[:, half:] + dot(kt[:, half:], ds_high, 1, 0)], 1) * HEAD_DIM ** -0.5
        at = part * some + h
        e_ref[d_rows(now, 0, at)] = dq.astype(bf16)
        e_ref[d_rows(now, 1, at)] = dk.astype(bf16)
        e_ref[d_rows(now, 2, at)] = dv.astype(bf16)
        return 0

    @pl.when(backward)
    def _():
        lax.fori_loop(0, some, head, 0, unroll=some)
        d = [e_ref[d_rows(now, kind, part * some, some)] for kind in range(3)]
        rows = some * HEAD_DIM
        acc_col[0, pl.ds(part * rows, rows)] += lane_groups(d[0].astype(f32))
        acc_col[1, pl.ds(part * rows, rows)] += lane_groups(d[2].astype(f32))
        fresh = now == 0
        for kind in range(3):
            product = dot(d[kind], x_ref[0], 1, 0)

            @pl.when(fresh)
            def _():
                acc[kind * rows : (kind + 1) * rows] = product

            @pl.when(jnp.logical_not(fresh))
            def _():
                acc[kind * rows : (kind + 1) * rows] += product

    @pl.when(step == images)
    def _():
        low_half[...] = acc[...].astype(bf16).T.reshape(low_half.shape)

    @pl.when(step == 2 * images)
    def _():
        low_rest[...] = acc[...].astype(bf16).T.reshape(low_rest.shape)
        at = lax.broadcasted_iota(jnp.int32, add_vec.shape, 0)
        rows = jnp.where(at == 0, column_sums(acc_col[0].T), jnp.where(at == 1, column_sums(acc_col[1].T), add_vec[...]))
        at = lax.broadcasted_iota(jnp.int32, (16, g_bin.shape[1]), 0)
        hidden = jnp.where(at == 13, g_bin[...], 0.0)
        small = collect(rows, width // devices, devices) + collect(hidden, g_bin.shape[1] // devices, devices)
        low_small[...] = small.astype(bf16).reshape(low_small.shape)

    events(0)

    @pl.when(step == 2 * images + 1)
    def _():
        for fetch in fetches[11:]:
            fetch.wait()

    @pl.when(step > 2 * images)
    def _():
        image = jnp.maximum(step - 2 * images - 1, 0)
        d = e_ref[d_rows(image, 0, 0, 3 * HEADS)]
        product = dot(d, wt_self[...], 0, 0)

        @pl.when(image < images - 1)
        def _():
            g_tags[0] = (gres_ref[jnp.minimum(image, images - 2)] + product).astype(bf16)

        @pl.when(image == images - 1)
        def _():
            g_tags[0] = (gres_last[...] + product).astype(bf16)

    events(1)

    @pl.when(step == 3 * images)
    def _():
        g_mem[...] = dot(dkv_ref[...].reshape(2 * width, cells), wt_cross[width:], 0, 0).astype(bf16)

    events(2)

    @pl.when(step == 3 * images)
    def _():
        for item in every:
            item.drain()


def run_closing(dims, x, qkv, e_low, e_high, inv, mix, gmix, g_resid, ckv, mem, vectors, wt_self, wt_cross, w_proj, g_one, g_in, g_out, g_vec, g_bin, kept):
    scale_one, e, q, inv_two, mix_two, gmix_two, n_one, g_two, acc_cross, acc_zero = kept
    images, tags, width = x.shape
    memory = mem.shape[1]
    half, some = tags // 2, HEADS // 2
    sds = jax.ShapeDtypeStruct
    cells = dims + (2,)
    devices = dims[0] * dims[1] * dims[2] * 2

    def parts(grad):
        return grad.reshape(cells + (grad.shape[0] // devices, grad.shape[1]))

    low = [parts(g_out), parts(g_in), parts(g_one)]
    rows = width // devices
    lows = [cells + (rows, 3 * width), cells + (rows, width)] + [cells + (rows, 3 * width // 2)] * 2 + [cells + (16, 128)]

    def turn(i):
        t = jnp.clip(i - 1, 0, 2 * images - 1)
        return lax.rem(t, images), lax.div(t, images)

    def by_turn(shape, split):
        def index(i):
            image, part = turn(i)
            return (image,) + tuple(part if k == split else 0 for k in range(len(shape)))
        return pl.BlockSpec((1,) + shape, index)

    def gmix_index(i):
        image, part = turn(i)
        return jnp.minimum(image, images - 2), part, 0, 0

    def one(*shape):
        return pl.BlockSpec(shape, lambda i: (0,) * len(shape), pipeline_mode=pl.Buffered(1))

    def out(*shape):
        return pl.BlockSpec(shape, lambda i: (0,) * len(shape))

    anywhere = pl.BlockSpec(memory_space=pl.ANY)
    shares = [g.shape[4:] for g in low] + [s[4:] for s in lows]
    space = []
    for k, shape in enumerate([g.shape for g in low] + lows):
        space += [pltpu.VMEM(s, bf16) for s in scatter_space(dims, (), shape[4:], k in SHORT)]
    slots = scatter_slots(dims)
    qkv = qkv.reshape(images, 3, HEADS, HEAD_DIM, tags)
    heads = (HEADS, HEAD_DIM, tags)
    return pl.pallas_call(
        functools.partial(closing, dims),
        grid=(3 * images + 1,),
        in_specs=[
            by_turn((tags, width), None), by_turn((3, some, HEAD_DIM, tags), 1), by_turn((some, half, tags), 0), by_turn((some, half, half), 0),
            by_turn((HEADS, tags), None), by_turn((some, HEAD_DIM, tags), 0), pl.BlockSpec((1, some, HEAD_DIM, tags), gmix_index),
            one(HEADS, tags), one(16, width), one(16, width), one(*g_bin.shape), one(tags, 1),
        ] + [anywhere] * 18,
        out_specs=[pl.BlockSpec((1, tags, width), lambda i: (jnp.clip(i - 2 * images - 1, 0, images - 1), 0, 0))]
        + [out(*s) for s in shares] + [out(memory, width)],
        out_shape=[sds((images, tags, width), bf16)] + [sds(s, f32) for s in shares] + [sds((memory, width), bf16)],
        scratch_shapes=[
            pltpu.VMEM((HEADS * memory, tags), bf16), pltpu.VMEM((2 * HEADS, HEAD_DIM, memory), bf16), pltpu.VMEM(heads, bf16), pltpu.VMEM(heads, bf16), pltpu.VMEM(heads, bf16),
        ] + [pltpu.VMEM(g.shape, bf16) for g in low] + [
            pltpu.VMEM((images - 1, tags, width), f32), pltpu.VMEM((2 * HEADS, HEAD_DIM, memory), bf16),
            pltpu.VMEM(heads, bf16), pltpu.VMEM((tags, width), f32), pltpu.VMEM((tags, width), f32),
            pltpu.VMEM((3 * width, width), bf16), pltpu.VMEM((memory, width), bf16), pltpu.VMEM((3 * width, width), f32), pltpu.VMEM((width, width), f32),
            pltpu.VMEM((width, width), bf16), pltpu.VMEM((3 * width, width), bf16),
            pltpu.VMEM(heads, bf16), pltpu.VMEM(heads, bf16), pltpu.VMEM((tags, width), f32), pltpu.VMEM((some, HEAD_DIM, tags), bf16),
            pltpu.VMEM((3 * width // 2, width), f32), pltpu.VMEM((16, width), f32), pltpu.VMEM((2, width, 128), f32),
        ] + [pltpu.VMEM(s, bf16) for s in lows] + [pltpu.SemaphoreType.DMA((HEADS, 6)), pltpu.SemaphoreType.DMA((13,))] + space
        + [pltpu.SemaphoreType.DMA((8, slots)), pltpu.SemaphoreType.DMA((8, slots))],
        compiler_params=pltpu.CompilerParams(collective_id=1, has_side_effects=True, vmem_limit_bytes=62 * MIB),
        name="closing",
    )(x, qkv, e_low, e_high, inv, mix, gmix, inv_two, vectors, g_vec, g_bin, scale_one, *low,
      e, ckv, q, mix_two, gmix_two, mix, g_two, n_one, wt_cross, mem, acc_cross, acc_zero, w_proj, wt_self, g_resid)


def settle(lanes, hidden_lanes, images, g_mem_in, m_last, tags, s_out, s_in, s_one, s_cross, s_zero, s_half, s_rest, small,
           g_mem, o_tags, o_self, o_cross, o_proj, o_in, o_out, o_bin, o_gains, o_biases):
    width = o_tags.shape[2]
    o_tags[...] = tags[...].astype(f32)

    @pl.when(pl.program_id(0) == 0)
    def _():
        g_mem[0] = m_last[...].astype(f32)
        part = width // 2
        for kind in range(3):
            o_self[:, kind * width : kind * width + part] = s_half[:, kind * part : (kind + 1) * part]
            o_self[:, kind * width + part : (kind + 1) * width] = s_rest[:, kind * part : (kind + 1) * part]
        o_cross[...] = s_cross[...]
        o_proj[0] = s_zero[...]
        o_proj[1] = s_one[...]
        o_in[...] = s_in[...]
        o_out[...] = s_out[...]
        o_biases[...] = small[:10, :lanes]
        o_gains[...] = small[10:13, :lanes]
        o_bin[...] = small[13:14, :hidden_lanes]


def run_settle(lanes, hidden_lanes, g_mem, m_last, g_tags, shares):
    images, tags, width = g_tags.shape
    sds = jax.ShapeDtypeStruct
    s_out, s_in, s_one, s_cross, s_zero, s_half, s_rest, small = shares

    def one(*shape):
        return pl.BlockSpec(shape, lambda i: (0,) * len(shape), pipeline_mode=pl.Buffered(1))

    def out(*shape):
        return pl.BlockSpec(shape, lambda i: (0,) * len(shape))

    rows = s_cross.shape[0]
    shapes = [s_cross.shape, s_cross.shape, (2, rows, width), s_in.shape, s_out.shape, (1, hidden_lanes), (3, lanes), (10, lanes)]
    image = pl.BlockSpec((1, tags, width), lambda i: (i, 0, 0))
    return pl.pallas_call(
        functools.partial(settle, lanes, hidden_lanes, images),
        grid=(images,),
        in_specs=[pl.BlockSpec(memory_space=pl.ANY), one(*m_last.shape), image] + [one(*s.shape) for s in shares],
        out_specs=[pl.BlockSpec((1,) + g_mem.shape[1:], lambda i: (images - 1, 0, 0)), image] + [out(*s) for s in shapes],
        out_shape=[sds(g_mem.shape, f32), sds(g_tags.shape, f32)] + [sds(s, f32) for s in shapes],
        input_output_aliases={0: 0},
        compiler_params=pltpu.CompilerParams(vmem_limit_bytes=62 * MIB),
        name="settle",
    )(g_mem, m_last, g_tags, *shares)


AXES = ("wide", "narrow")
LEADS = (0, 0, 1, 0, 0, 0)


def fold(block, rows, columns):
    if rows % 16 == 0:
        return block
    return block.reshape(block.shape[:-2] + (16, rows * columns // 16))


def per_device(dims, tag_states, image_memory, tag_lengths, w_self, w_cross, w_proj, w_in, b_in, w_out, ln_gains, biases, out_grad):
    cells = dims + (2,)
    fused = w_self.shape[0] % 16 == 0 and tag_states.shape[0] == 3
    devices = dims[0] * dims[1] * dims[2] * 2
    width = tag_states.shape[2]
    lanes, hidden_lanes = biases.shape[1], b_in.shape[0]
    if fused:
        qkv, ckv, near, far, inv, mix, wt_self, wt_cross, vectors, hidden_bias, full_proj, full_in, full_out = run_opening(
            dims, tag_lengths, tag_states, image_memory, biases, ln_gains, b_in[None], (w_cross, w_self, w_proj, w_in, w_out))
        full_proj, full_in, full_out = full_proj.reshape(2, width, width), full_in.reshape(width, -1), full_out.reshape(-1, width)
        layer_out, g_resid, gmix, g_mem, _, g_one, g_in, g_out, g_vec, g_bin, *kept = run_middle(
            tag_lengths, tag_states, image_memory, out_grad, mix, ckv, wt_cross, full_proj, full_in, full_out, vectors, hidden_bias, True)
        g_tags, *shares, m_last = run_closing(
            dims, tag_states, qkv, near, far, inv, mix, gmix, g_resid, ckv, image_memory, vectors, wt_self, wt_cross, full_proj,
            g_one, g_in, g_out, g_vec, g_bin, kept)
        grad_memory, grad_tags, s_self, s_cross, s_proj, s_in, s_out, s_bin, s_gains, s_biases = run_settle(
            lanes, hidden_lanes, g_mem, m_last, g_tags, shares)
        return layer_out, grad_tags, grad_memory, s_self, s_cross, s_proj, s_in, s_bin[0], s_out, s_gains, s_biases
    small = jnp.concatenate(
        [
            jnp.pad(jnp.concatenate([biases, ln_gains]), ((0, 0), (0, 128 - lanes))),
            jnp.pad(b_in[None], ((0, 2), (0, 128 - hidden_lanes))),
        ]
    )
    shards = (w_self, w_cross, w_proj, w_in, w_out, small)
    gathered = gather(dims, [fold(s, *s.shape[-2:]) for s in shards], LEADS)

    def whole(held, shard):
        lead = shard.shape[:-2]
        rows, columns = shard.shape[-2:]
        return held.reshape(lead + (devices * rows, columns))

    full_self, full_cross, full_proj, full_in, full_out, full_small = [whole(h, s) for h, s in zip(gathered, shards)]
    by_device = full_small.reshape(devices, 16, 128)
    vectors = by_device[:, :, :lanes].transpose(1, 0, 2).reshape(16, width).astype(f32)
    hidden_bias = by_device[:, 13, :hidden_lanes].reshape(1, -1).astype(f32)
    layer_out, grad_tags, grad_memory, g_self, g_cross, g_proj, g_in, g_out, g_vec, g_bin = layer(
        tag_lengths, tag_states, image_memory, out_grad, full_self, full_cross, full_proj, full_in, full_out, vectors, hidden_bias)
    g_small = jnp.pad(g_vec.reshape(16, devices, lanes).transpose(1, 0, 2)[:, :13], ((0, 0), (0, 0), (0, 128 - lanes)))
    g_hidden = jnp.pad(g_bin.reshape(devices, 1, hidden_lanes), ((0, 0), (0, 2), (0, 128 - hidden_lanes)))
    g_small = jnp.concatenate([g_small, g_hidden], 1).astype(bf16).reshape(devices * 16, 128)

    def parts(grad, shard):
        lead = shard.shape[:-2]
        rows, columns = shard.shape[-2:]
        return fold(grad.reshape(lead + cells + (rows, columns)), rows, columns)

    shards = (w_self, w_cross, w_proj, w_in, w_out, jax.ShapeDtypeStruct((16, 128), bf16))
    shares = scatter(dims, [parts(g, s) for g, s in zip((g_self, g_cross, g_proj, g_in, g_out, g_small), shards)], LEADS)
    s_self, s_cross, s_proj, s_in, s_out, s_small = [v.reshape(s.shape) for v, s in zip(shares, shards)]
    return (layer_out, grad_tags, grad_memory, s_self, s_cross, s_proj, s_in, s_small[13, :hidden_lanes], s_out,
            s_small[10:13, :lanes], s_small[:10, :lanes])


def solution(mesh):
    dims = grid_of(mesh.shape["wide"], mesh.shape["narrow"])
    rows, matrix, stack, columns = P(AXES, None, None), P(AXES, None), P(None, AXES, None), P(None, AXES)
    return jax.shard_map(
        functools.partial(per_device, dims),
        mesh=mesh,
        in_specs=(rows, rows, P(AXES), matrix, matrix, stack, matrix, P(AXES), matrix, columns, columns, rows),
        out_specs=(rows, rows, rows, matrix, matrix, stack, matrix, P(AXES), matrix, columns, columns),
        check_vma=False,
    )
```

```python
import functools

import jax
import jax.numpy as jnp
from jax import lax
from jax.experimental import pallas as pl
from jax.experimental.pallas import tpu as pltpu
from jax.sharding import PartitionSpec as P


MESH = pl.DeviceIdType.MESH
f32, bf16 = jnp.float32, jnp.bfloat16


def grid_of(mesh_wide, mesh_narrow):
    outer = 4
    return outer, mesh_wide // outer, mesh_narrow // 2


def place(dims):
    outer, inner, across = dims
    wide, narrow = lax.axis_index("wide"), lax.axis_index("narrow")
    return wide // inner, lax.rem(wide, inner), narrow // 2, lax.rem(narrow, 2)


def device(dims, a, b, x, c):
    return {"wide": a * dims[1] + b, "narrow": x * 2 + c}


def hail(dims, me, diagonal=False):
    a, b, x, c = me
    outer, inner, across = dims
    barrier = pltpu.get_barrier_semaphore()
    peers = [(lax.rem(a + k, outer), b, x, c) for k in range(1, outer)]
    peers += [(a, lax.rem(b + k, inner), x, c) for k in range(1, inner)]
    peers += [(a, b, lax.rem(x + k, across), c) for k in range(1, across)]
    peers += [(a, b, x, 1 - c)]
    if diagonal:
        peers += [(a, lax.rem(b + j, inner), lax.rem(x + k, across), c) for j in range(1, inner) for k in range(1, across)]
    for peer in peers:
        pl.semaphore_signal(barrier, inc=1, device_id=device(dims, *peer), device_id_type=MESH)
    return len(peers)


def greet(dims, me, count=0):
    pl.semaphore_wait(pltpu.get_barrier_semaphore(), count or hail(dims, me))


ALL = slice(None)


def gather_kernel(dims, leads, *refs):
    count = len(leads)
    shards, outs = refs[:count], refs[count : 2 * count]
    local_sem, send_sem, recv_sem = refs[2 * count :]
    outer, inner, across = dims
    me = place(dims)
    a, b, x, c = me
    greet(dims, me)

    def cell(ref, lead, *index):
        return ref.at[(ALL,) * lead + index]

    def remote(g, slot, src, dst, peer):
        return pltpu.make_async_remote_copy(
            src_ref=src, dst_ref=dst, send_sem=send_sem.at[g, slot], recv_sem=recv_sem.at[g, slot],
            device_id=device(dims, *peer), device_id_type=MESH)

    n_in, n_ac = inner - 1, across - 1

    def first(g):
        lead = leads[g]
        mine = cell(outs[g], lead, a, b, x, c)
        return [remote(g, k - 1, shards[g], mine, (lax.rem(a + k, outer), b, x, c)) for k in range(1, outer)]

    def keep(g):
        return pltpu.make_async_copy(shards[g], cell(outs[g], leads[g], a, b, x, c), local_sem.at[g])

    base = outer - 1

    def via_inner(g, core):
        lead = leads[g]
        column = ALL if core == 0 else x
        piece = cell(outs[g], lead, ALL, b, column, c)
        return [remote(g, base + k - 1, piece, piece, (a, lax.rem(b + k, inner), x, c)) for k in range(1, inner)]

    def via_across(g, core):
        lead = leads[g]
        row = b if core == 0 else ALL
        piece = cell(outs[g], lead, ALL, row, x, c)
        return [remote(g, base + n_in + k - 1, piece, piece, (a, b, lax.rem(x + k, across), c)) for k in range(1, across)]

    share = base + n_in + n_ac

    def to_partner(g, core, holder):
        lead = leads[g]
        def piece(slot, row, column):
            ref = cell(outs[g], lead, ALL, row, column, holder)
            return remote(g, share + slot, ref, ref, (a, b, x, 1 - c))
        own = [piece(0, b, x)]
        by_inner = [piece(1 + k - 1, lax.rem(b + k, inner), ALL if core == 0 else x) for k in range(1, inner)]
        by_across = [piece(1 + n_in + k - 1, b if core == 0 else ALL, lax.rem(x + k, across)) for k in range(1, across)]
        return (own, by_across, by_inner) if core == 0 else (own, by_inner, by_across)

    def start(copies):
        for copy in copies:
            copy.start()

    def arrived(copies):
        for copy in copies:
            copy.wait_recv()

    for g in range(count):
        keep(g).start()
        start(first(g))

    def body(core):
        second, third = (via_across, via_inner) if core == 0 else (via_inner, via_across)
        for step in range(count + 2):
            g = step
            if g < count:
                keep(g).wait()
                arrived(first(g))
                start(second(g, core))
                start(to_partner(g, core, c)[0])
            g = step - 1
            if 0 <= g < count:
                arrived(second(g, core))
                start(third(g, core))
                start(to_partner(g, core, c)[1])
            g = step - 2
            if 0 <= g < count:
                arrived(third(g, core))
                start(to_partner(g, core, c)[2])
        for g in range(count):
            for group in to_partner(g, 1 - core, 1 - c):
                arrived(group)
        for g in range(count):
            for copy in first(g) + second(g, core) + third(g, core):
                copy.wait_send()
            for group in to_partner(g, core, c):
                for copy in group:
                    copy.wait_send()

    @pl.when(c == 0)
    def _():
        body(0)

    @pl.when(c == 1)
    def _():
        body(1)


def gather(dims, shards, leads):
    outer, inner, across = dims
    def shape(s, lead):
        return jax.ShapeDtypeStruct(s.shape[:lead] + (outer, inner, across, 2) + s.shape[lead:], s.dtype)
    slots = (outer - 1) + 2 * (inner - 1) + 2 * (across - 1) + 1
    n = len(shards)
    return pl.pallas_call(
        functools.partial(gather_kernel, dims, leads),
        out_shape=[shape(s, l) for s, l in zip(shards, leads)],
        in_specs=[pl.BlockSpec(memory_space=pl.ANY)] * n,
        out_specs=[pl.BlockSpec(memory_space=pl.ANY)] * n,
        scratch_shapes=[pltpu.SemaphoreType.DMA((n,)), pltpu.SemaphoreType.DMA((n, slots)), pltpu.SemaphoreType.DMA((n, slots))],
        compiler_params=pltpu.CompilerParams(collective_id=0, has_side_effects=True),
        name="gather_weights",
    )(*shards)


def scatter_kernel(dims, leads, *refs):
    count = len(leads)
    grads, outs = refs[:count], refs[count : 2 * count]
    rest = refs[2 * count :]
    r0, r1i, r1a, r2a, r2i, r3 = (rest[k * count : (k + 1) * count] for k in range(6))
    send_sem, recv_sem = rest[6 * count :]
    outer, inner, across = dims
    me = place(dims)
    a, b, x, c = me
    greet(dims, me)
    n_in, n_ac = inner - 1, across - 1

    def cell(ref, lead, *index):
        return ref.at[(ALL,) * lead + index]

    def remote(g, slot, src, dst, peer):
        return pltpu.make_async_remote_copy(
            src_ref=src, dst_ref=dst, send_sem=send_sem.at[g, slot], recv_sem=recv_sem.at[g, slot],
            device_id=device(dims, *peer), device_id_type=MESH)

    def swap(g):
        return [remote(g, 0, cell(grads[g], leads[g], ALL, ALL, ALL, 1 - c), r0[g], (a, b, x, 1 - c))]

    def via_inner(g, core):
        lead = leads[g]
        res = []
        for k in range(1, inner):
            peer = lax.rem(b + k, inner)
            if core == 0:
                src, dst = cell(r0[g], lead, ALL, peer), r1i[g].at[k - 1]
            else:
                src, dst = cell(r1a[g].at[0], lead, ALL, peer), r2i[g].at[k - 1]
            res.append(remote(g, k, src, dst, (a, peer, x, c)))
        return res

    def via_across(g, core):
        lead = leads[g]
        res = []
        for k in range(1, across):
            peer = lax.rem(x + k, across)
            if core == 1:
                src, dst = cell(r0[g], lead, ALL, ALL, peer), r1a[g].at[k - 1]
            else:
                src, dst = cell(r1i[g].at[0], lead, ALL, peer), r2a[g].at[k - 1]
            res.append(remote(g, 1 + n_in + k - 1, src, dst, (a, b, peer, c)))
        return res

    def last(g, core):
        lead = leads[g]
        held = (r2a if core == 0 else r2i)[g].at[0]
        res = []
        for k in range(1, outer):
            peer = lax.rem(a + k, outer)
            res.append(remote(g, 1 + n_in + n_ac + k - 1, cell(held, lead, peer), r3[g].at[k - 1], (peer, b, x, c)))
        return res

    def start(copies):
        for copy in copies:
            copy.start()

    def arrived(copies):
        for copy in copies:
            copy.wait_recv()

    def up(v):
        return v.astype(f32)

    for g in range(count):
        start(swap(g))

    def body(core):
        second, third = (via_inner, via_across) if core == 0 else (via_across, via_inner)
        def at(lead, *index):
            return (ALL,) * lead + index
        for step in range(count + 3):
            g = step
            if g < count:
                arrived(swap(g))
                lead = leads[g]
                r0[g][...] = (up(grads[g][at(lead, ALL, ALL, ALL, c)]) + up(r0[g][...])).astype(bf16)
                start(second(g, core))
            g = step - 1
            if 0 <= g < count:
                arrived(second(g, core))
                lead = leads[g]
                if core == 0:
                    total = up(r0[g][at(lead, ALL, b)])
                    held = r1i[g]
                else:
                    total = up(r0[g][at(lead, ALL, ALL, x)])
                    held = r1a[g]
                for k in range(held.shape[0]):
                    total = total + up(held[k])
                held[0] = total.astype(bf16)
                start(third(g, core))
            g = step - 2
            if 0 <= g < count:
                arrived(third(g, core))
                lead = leads[g]
                if core == 0:
                    total = up(r1i[g][(0,) + at(lead, ALL, x)])
                    held = r2a[g]
                else:
                    total = up(r1a[g][(0,) + at(lead, ALL, b)])
                    held = r2i[g]
                for k in range(held.shape[0]):
                    total = total + up(held[k])
                held[0] = total.astype(bf16)
                start(last(g, core))
            g = step - 3
            if 0 <= g < count:
                arrived(last(g, core))
                lead = leads[g]
                held = (r2a if core == 0 else r2i)[g]
                total = up(held[(0,) + at(lead, a)])
                for k in range(outer - 1):
                    total = total + up(r3[g][k])
                outs[g][...] = total
        for g in range(count):
            for copy in swap(g) + second(g, core) + third(g, core) + last(g, core):
                copy.wait_send()

    @pl.when(c == 0)
    def _():
        body(0)

    @pl.when(c == 1)
    def _():
        body(1)


def scatter(dims, grads, leads):
    outer, inner, across = dims
    n = len(grads)
    outs, shapes = [], [[] for _ in range(6)]
    for g, lead in zip(grads, leads):
        head, tail = g.shape[:lead], g.shape[lead + 4 :]
        outs.append(jax.ShapeDtypeStruct(head + tail, f32))
        shapes[0].append(head + (outer, inner, across) + tail)
        shapes[1].append((inner - 1,) + head + (outer, across) + tail)
        shapes[2].append((across - 1,) + head + (outer, inner) + tail)
        shapes[3].append((across - 1,) + head + (outer,) + tail)
        shapes[4].append((inner - 1,) + head + (outer,) + tail)
        shapes[5].append((outer - 1,) + head + tail)
    slots = 1 + (inner - 1) + (across - 1) + (outer - 1)
    return pl.pallas_call(
        functools.partial(scatter_kernel, dims, leads),
        out_shape=outs,
        in_specs=[pl.BlockSpec(memory_space=pltpu.VMEM)] * n,
        out_specs=[pl.BlockSpec(memory_space=pltpu.VMEM)] * n,
        scratch_shapes=[pltpu.VMEM(s, bf16) for group in shapes for s in group]
        + [pltpu.SemaphoreType.DMA((n, slots)), pltpu.SemaphoreType.DMA((n, slots))],
        compiler_params=pltpu.CompilerParams(collective_id=1, has_side_effects=True, vmem_limit_bytes=48 * 2**20),
        name="scatter_grads",
    )(*grads)

HEADS, HEAD_DIM = 8, 64
EPS = 1e-5
MASKED = -1e9
TAME = 30.0
CHUNKS = 1
MIB = 2**20


def dot(left, right, left_dim, right_dim):
    return lax.dot_general(left, right, (((left_dim,), (right_dim,)), ((), ())), preferred_element_type=f32)


def full(shape):
    return pl.BlockSpec(shape, lambda i: (0,) * len(shape))


def image(shape):
    return pl.BlockSpec((1,) + shape, lambda i: (i,) + (0,) * len(shape))


def with_ones(rows):
    return jnp.concatenate([rows, jnp.ones((16, rows.shape[1]), bf16)], 0)


def with_delta(rows, delta):
    high = delta.astype(bf16).astype(f32)
    low = delta - high
    at = lax.broadcasted_iota(jnp.int32, (16, rows.shape[1]), 0)
    extra = jnp.where(at == 0, -high, jnp.where(at == 1, -low, 0.0))
    return jnp.concatenate([rows, extra.astype(bf16)], 0)


def self_forward(lens, x_ref, mem_ref, w_self, w_cross, bias_qkv, bias_kv,
                 qkv_ref, ckv_ref, near_ref, far_ref, inv_ref, mix_ref, wt_self, wt_cross):
    width = x_ref.shape[2]
    tags = x_ref.shape[1]
    half = tags // 2
    i = pl.program_id(0)

    @pl.when(i == 0)
    def _():
        wt_self[...] = w_self[...].T
        wt_cross[...] = w_cross[...].T

    ckv = dot(wt_cross[width:], mem_ref[0], 1, 1) + bias_kv[...]
    ckv_ref[0] = ckv.astype(bf16).reshape(ckv_ref.shape[1:])
    qkv = dot(wt_self[...], x_ref[0], 1, 1) + bias_qkv[...]
    q = qkv[:width].astype(bf16) * bf16(HEAD_DIM ** -0.5)
    qkv_ref[0, :HEADS] = q.reshape(HEADS, HEAD_DIM, tags)
    qkv_ref[0, HEADS:] = qkv[width:].astype(bf16).reshape(2 * HEADS, HEAD_DIM, tags)
    last = lens[i] - 1

    def head(h, _):
        qt, kt, vt = qkv_ref[0, h], qkv_ref[0, HEADS + h], with_ones(qkv_ref[0, 2 * HEADS + h])

        def part(keys, first, out):
            s = dot(kt[:, :keys], qt[:, first : first + half], 0, 0)
            key_at = lax.broadcasted_iota(jnp.int32, (keys, half), 0)
            query_at = lax.broadcasted_iota(jnp.int32, (1, half), 1) + first
            s = jnp.where(key_at <= jnp.minimum(query_at, last), s, MASKED)
            e = jnp.exp(s - jnp.max(s, 0, keepdims=True)).astype(bf16)
            out[0, h] = e
            mixed = dot(vt[:, :keys], e, 1, 0)
            inv = 1.0 / mixed[HEAD_DIM : HEAD_DIM + 1]
            inv_ref[0, pl.ds(h, 1), first : first + half] = inv
            mix_ref[0, h, :, first : first + half] = (mixed[:HEAD_DIM] * inv).astype(bf16)

        part(half, 0, near_ref)
        part(tags, half, far_ref)
        return 0

    lax.fori_loop(0, HEADS, head, 0)


def run_self_forward(lens, x, mem, w_self, w_cross, bias_qkv, bias_kv):
    images, tags, width = x.shape
    cells = mem.shape[1]
    half = tags // 2
    sds = jax.ShapeDtypeStruct
    return pl.pallas_call(
        self_forward,
        grid_spec=pltpu.PrefetchScalarGridSpec(
            num_scalar_prefetch=1,
            grid=(images,),
            in_specs=[pl.BlockSpec((1, tags, width), lambda i, n: (i, 0, 0)), pl.BlockSpec((1, cells, width), lambda i, n: (i, 0, 0))]
            + [pl.BlockSpec(v.shape, lambda i, n: (0, 0)) for v in (w_self, w_cross, bias_qkv, bias_kv)],
            out_specs=[
                pl.BlockSpec((1, 3 * HEADS, HEAD_DIM, tags), lambda i, n: (i, 0, 0, 0)),
                pl.BlockSpec((1, 2 * HEADS, HEAD_DIM, cells), lambda i, n: (i, 0, 0, 0)),
                pl.BlockSpec((1, HEADS, half, half), lambda i, n: (i, 0, 0, 0)),
                pl.BlockSpec((1, HEADS, tags, half), lambda i, n: (i, 0, 0, 0)),
                pl.BlockSpec((1, HEADS, tags), lambda i, n: (i, 0, 0)),
                pl.BlockSpec((1, HEADS, HEAD_DIM, tags), lambda i, n: (i, 0, 0, 0)),
                pl.BlockSpec((3 * width, width), lambda i, n: (0, 0)),
                pl.BlockSpec((3 * width, width), lambda i, n: (0, 0)),
            ],
        ),
        out_shape=[
            sds((images, 3 * HEADS, HEAD_DIM, tags), bf16),
            sds((images, 2 * HEADS, HEAD_DIM, cells), bf16),
            sds((images, HEADS, half, half), bf16),
            sds((images, HEADS, tags, half), bf16),
            sds((images, HEADS, tags), f32),
            sds((images, HEADS, HEAD_DIM, tags), bf16),
            sds((3 * width, width), bf16),
            sds((3 * width, width), bf16),
        ],
        compiler_params=pltpu.CompilerParams(vmem_limit_bytes=58 * MIB),
        name="self_forward",
    )(lens, x, mem, w_self, w_cross, bias_qkv, bias_kv)


def norm(resid):
    centred = resid - jnp.mean(resid, -1, keepdims=True)
    scale = lax.rsqrt(jnp.mean(centred * centred, -1, keepdims=True) + EPS)
    return centred * scale, scale


def norm_back(grad, normed, scale, gain):
    scaled = grad * gain
    mean_one = jnp.mean(scaled, -1, keepdims=True)
    mean_two = jnp.mean(scaled * normed, -1, keepdims=True)
    return scale * (scaled - mean_one - normed * mean_two)


def column_sums(rows):
    return jnp.sum(rows, 0, keepdims=True)


def lane_groups(rows):
    total = rows[:, :128]
    for k in range(1, rows.shape[1] // 128):
        total = total + rows[:, 128 * k : 128 * (k + 1)]
    return total


def cross_back(h, e, keys, values, queries, grad, mixed, inv):
    grad = grad.astype(f32)
    delta = jnp.sum(grad * mixed.astype(f32), 0, keepdims=True) * inv
    grad = (grad * inv).astype(bf16)
    dp = dot(with_ones(values), with_delta(grad, delta), 0, 0)
    ds = e * dp.astype(bf16)
    dv = dot(grad, e, 1, 1).astype(bf16)
    dk = dot(queries, ds, 1, 1).astype(bf16)
    dq = (dot(keys, ds, 1, 0) * HEAD_DIM ** -0.5).astype(bf16)
    return dq, dk, dv


def memory_lanes(rows):
    cells = rows.shape[1]
    body = cells // 128 * 128
    total = lane_groups(rows[:, :body])
    if body < cells:
        total = total + jnp.concatenate([rows[:, body:], jnp.zeros((rows.shape[0], 128 - cells + body), f32)], 1)
    return total


def middle(held_back, lens, x_ref, mem_ref, gout_ref, mix_one, ckv_ref, wt_cross, w_proj, w_in, w_out, vectors, b_in,
           out_ref, g_resid, g_mix, g_mem, gw_cross, gw_proj, gw_in, gw_out, g_vec, g_bin, *rest):
    if held_back:
        o_scale, o_e, o_q, o_inv, o_mix, o_gmix, o_one, o_two, o_cross, o_proj = rest[:10]
        gone = rest[-1]
        rest = rest[10:-1]
    middle_body(held_back and (o_scale, o_e, o_q, o_inv, o_mix, o_gmix, o_one, o_two, o_cross, o_proj, gone),
                lens, x_ref, mem_ref, gout_ref, mix_one, ckv_ref, wt_cross, w_proj, w_in, w_out, vectors, b_in,
                out_ref, g_resid, g_mix, g_mem, gw_cross, gw_proj, gw_in, gw_out, g_vec, g_bin, *rest)


def middle_body(held_back, lens, x_ref, mem_ref, gout_ref, mix_one, ckv_ref, wt_cross, w_proj, far_in, far_out, vectors, b_in,
           out_ref, g_resid, g_mix, g_mem, gw_cross, gw_proj, gw_in, gw_out, g_vec, g_bin,
           dkv_ref, cols,
           e_ref, q_ref, inv_ref, mix_two, gmix_two, dq_ref, acc_cross, acc_proj, acc_in, acc_out, acc_vec, acc_bin, acc_col,
           n_one, n_two, scale_two, two_low, act, g_inner, g_ff, g_cross, g_two, w_in, w_out, come):
    tags, width = x_ref.shape[1:]
    cells = mem_ref.shape[1]
    i = pl.program_id(0)
    count = pl.num_programs(0)
    arrivals = [pltpu.make_async_copy(src, dst, come.at[k]) for k, (src, dst) in enumerate(((far_in, w_in), (far_out, w_out)))]

    @pl.when(i == 0)
    def _():
        for ref in (acc_cross, acc_proj, acc_in, acc_out, acc_vec, acc_bin, acc_col):
            ref[...] = jnp.zeros_like(ref)
        cols[...] = vectors[...].T
        for copy in arrivals:
            copy.start()

    def vec(k):
        return vectors[k : k + 1, :]

    def add(k, value):
        acc_vec[k : k + 1, :] += value

    if held_back:
        scale_out, *places, gone = held_back
        sources = (e_ref, q_ref, inv_ref, mix_two, gmix_two, n_one, g_two, acc_cross, acc_proj.at[0])
        copies = [pltpu.make_async_copy(src, dst, gone.at[k]) for k, (src, dst) in enumerate(zip(sources, places))]

    def leave(*numbers):
        if held_back:
            @pl.when(i == count - 1)
            def _():
                for number in numbers:
                    copies[number].start()

    leave(7, 8)
    mix_one_t = mix_one[0].reshape(width, tags)
    resid = x_ref[0].astype(f32) + dot(mix_one_t, w_proj[0], 0, 0) + vec(2)
    normed, scale_one = norm(resid)
    n_one[...] = normed
    one = normed * vec(10) + vec(6)
    one_low = one.astype(bf16)
    cq = (dot(wt_cross[:width], one_low, 1, 1) + cols[:, 3:4]).astype(bf16) * bf16(HEAD_DIM ** -0.5)
    q_ref[...] = cq.reshape(q_ref.shape)
    leave(1, 5)

    keys = ckv_ref[0, :HEADS].astype(f32)
    queries = q_ref[...].astype(f32)
    bound = jnp.max(jnp.sum(keys * keys, 1)) * jnp.max(jnp.sum(queries * queries, 1))
    tame = bound < TAME * TAME

    def forward(shifted, h, _):
        s = dot(ckv_ref[0, h], q_ref[h], 0, 0)
        if shifted:
            s = s - jnp.max(s, 0, keepdims=True)
        e = jnp.exp(s).astype(bf16)
        e_ref[h] = e
        mixed = dot(with_ones(ckv_ref[0, HEADS + h]), e, 1, 0)
        inv = 1.0 / mixed[HEAD_DIM : HEAD_DIM + 1]
        inv_ref[pl.ds(h, 1), :] = inv
        mix_two[h] = (mixed[:HEAD_DIM] * inv).astype(bf16)
        return 0

    @pl.when(tame)
    def _():
        lax.fori_loop(0, HEADS, functools.partial(forward, False), 0, unroll=8)

    @pl.when(jnp.logical_not(tame))
    def _():
        lax.fori_loop(0, HEADS, functools.partial(forward, True), 0)

    leave(0, 2, 3)
    @pl.when(i == 0)
    def _():
        for copy in arrivals:
            copy.wait()

    mix_two_t = mix_two[...].reshape(width, tags)
    root = 0.7978845608028654
    rows = tags // CHUNKS
    totals = {}

    def tally(k, value):
        totals[k] = totals[k] + column_sums(value) if k in totals else column_sums(value)

    for first in range(0, tags, rows):
        at = slice(first, first + rows)
        resid = n_one[at] * vec(10) + vec(6) + dot(mix_two_t[:, at], w_proj[1], 0, 0) + vec(5)
        normed, scale = norm(resid)
        n_two[at] = normed
        scale_two[at] = scale
        two = normed * vec(11) + vec(7)
        two_low[at] = two.astype(bf16)
        inner = dot(two_low[at], w_in[...], 1, 0) + b_in[...]
        square = inner * inner
        tanh = jnp.tanh(inner * (root + (root * 0.044715) * square))
        half_more = 0.5 + 0.5 * tanh
        act[at] = (inner * half_more).astype(bf16)
        slope = half_more + inner * (half_more * (1.0 - tanh)) * (root + (3 * 0.044715 * root) * square)
        resid = two + dot(act[at], w_out[...], 1, 0) + vec(9)
        three, scale = norm(resid)
        valid = lax.broadcasted_iota(jnp.int32, (rows, 1), 0) + first < lens[i]
        out_ref[0, at] = jnp.where(valid, three * vec(12) + vec(8), 0.0).astype(bf16)
        grad = jnp.where(valid, gout_ref[0, at].astype(f32), 0.0)
        tally(12, grad * three)
        tally(8, grad)
        g_three = norm_back(grad, three, scale, vec(12))
        g_ff[at] = g_three.astype(bf16)
        tally(9, g_three)
        back = dot(g_ff[at], w_out[...], 1, 1) * slope
        tally(-1, back)
        g_inner[at] = back.astype(bf16)
        back = g_three + dot(g_inner[at], w_in[...], 1, 1)
        tally(11, back * n_two[at])
        tally(7, back)
        back = norm_back(back, n_two[at], scale_two[at], vec(11))
        tally(5, back)
        g_two[at] = back
        g_cross[at] = back.astype(bf16)

    for k, value in totals.items():
        if k >= 0:
            add(k, value)
    acc_bin[...] += totals[-1]
    acc_out[...] += dot(act[...], g_ff[...], 0, 0)
    acc_in[...] += dot(two_low[...], g_inner[...], 0, 0)
    acc_proj[1] += dot(mix_two_t, g_cross[...], 1, 0)
    gmix_two[...] = dot(w_proj[1], g_cross[...], 1, 1).astype(bf16).reshape(gmix_two.shape)

    def rest_of_image():
        def backward(h, _):
            dq_ref[h], dkv_ref[h], dkv_ref[HEADS + h] = cross_back(
                h, e_ref[h], ckv_ref[0, h], ckv_ref[0, HEADS + h], q_ref[h], gmix_two[h], mix_two[h], inv_ref[pl.ds(h, 1), :])
            return 0

        lax.fori_loop(0, HEADS, backward, 0, unroll=4)
        dq = dq_ref[...].reshape(width, tags)
        dkv = dkv_ref[...].reshape(2 * width, cells)
        acc_col[0] += lane_groups(dq.astype(f32))
        acc_col[1] += memory_lanes(dkv[width:].astype(f32))
        acc_cross[:width] += dot(dq, one_low, 1, 0)
        acc_cross[width:] += dot(dkv, mem_ref[0], 1, 0)
        g_mem[0] = dot(dkv, wt_cross[width:], 0, 0)
        g_one = g_two[...] + dot(dq, wt_cross[:width], 0, 0)
        add(10, column_sums(g_one * n_one[...]))
        add(6, column_sums(g_one))
        g_one = norm_back(g_one, n_one[...], scale_one, vec(10))
        add(2, column_sums(g_one))
        g_resid[0] = g_one
        g_low = g_one.astype(bf16)
        acc_proj[0] += dot(mix_one_t, g_low, 1, 0)
        g_mix[0] = dot(w_proj[0], g_low, 1, 1).astype(bf16).reshape(g_mix.shape[1:])

    if held_back:
        pl.when(i < count - 1)(rest_of_image)

        @pl.when(i == count - 1)
        def _():
            scale_out[...] = scale_one

        leave(4, 6)
    else:
        rest_of_image()

    @pl.when(i == count - 1)
    def _():
        if held_back:
            gw_proj[...] = acc_proj[1].astype(bf16)
        else:
            gw_cross[...] = acc_cross[...].astype(bf16).T
            gw_proj[...] = acc_proj[...].astype(bf16)
        gw_in[...] = acc_in[...].astype(bf16)
        gw_out[...] = acc_out[...].astype(bf16)
        add(3, column_sums(acc_col[0].T))
        add(4, column_sums(acc_col[1].T))
        g_vec[...] = acc_vec[...]
        g_bin[...] = acc_bin[...]
        if held_back:
            for copy in copies:
                copy.wait()


def run_middle(lens, x, mem, gout, mix_one, ckv, wt_cross, w_proj, w_in, w_out, vectors, b_in, held_back=False):
    images, tags, width = x.shape
    cells = mem.shape[1]
    hidden = w_in.shape[1]
    sds = jax.ShapeDtypeStruct

    def per(*shape):
        return pl.BlockSpec((1,) + shape, lambda i, n: (i,) + (0,) * len(shape))

    def one(*shape):
        return pl.BlockSpec(shape, lambda i, n: (0,) * len(shape), pipeline_mode=pl.Buffered(1))

    def out(*shape):
        return pl.BlockSpec(shape, lambda i, n: (0,) * len(shape))

    def early(*shape):
        return pl.BlockSpec((1,) + shape, lambda i, n: (jnp.minimum(i, images - 2),) + (0,) * len(shape)) if held_back else per(*shape)

    done = images - 1 if held_back else images
    out_specs = [
        per(tags, width), early(tags, width), early(HEADS, HEAD_DIM, tags), early(cells, width),
        out(width, 3 * width), out(2, width, width), out(width, hidden), out(hidden, width), out(16, width), out(1, hidden),
    ]
    out_shape = [
        sds((images, tags, width), bf16), sds((done, tags, width), f32), sds((done, HEADS, HEAD_DIM, tags), bf16),
        sds((images, cells, width), f32),
        sds((width, 3 * width), bf16), sds((2, width, width), bf16), sds((width, hidden), bf16), sds((hidden, width), bf16),
        sds((16, width), f32), sds((1, hidden), f32),
    ]
    scratch = [
        pltpu.VMEM((2 * HEADS, HEAD_DIM, cells), bf16),
        pltpu.VMEM((width, 16), f32),
        pltpu.VMEM((HEADS, cells, tags), bf16),
        pltpu.VMEM((HEADS, HEAD_DIM, tags), bf16),
        pltpu.VMEM((HEADS, tags), f32),
        pltpu.VMEM((HEADS, HEAD_DIM, tags), bf16),
        pltpu.VMEM((HEADS, HEAD_DIM, tags), bf16),
        pltpu.VMEM((HEADS, HEAD_DIM, tags), bf16),
        pltpu.VMEM((3 * width, width), f32),
        pltpu.VMEM((2, width, width), f32),
        pltpu.VMEM((width, hidden), f32),
        pltpu.VMEM((hidden, width), f32),
        pltpu.VMEM((16, width), f32),
        pltpu.VMEM((1, hidden), f32),
        pltpu.VMEM((2, width, 128), f32),
        pltpu.VMEM((tags, width), f32),
        pltpu.VMEM((tags, width), f32),
        pltpu.VMEM((tags, 1), f32),
        pltpu.VMEM((tags, width), bf16),
        pltpu.VMEM((tags, hidden), bf16),
        pltpu.VMEM((tags, hidden), bf16),
        pltpu.VMEM((tags, width), bf16),
        pltpu.VMEM((tags, width), bf16),
        pltpu.VMEM((tags, width), f32),
        pltpu.VMEM((width, hidden), bf16),
        pltpu.VMEM((hidden, width), bf16),
        pltpu.SemaphoreType.DMA((2,)),
    ]
    if held_back:
        out_specs[4], out_shape[4] = out(8, 128), sds((8, 128), bf16)
        out_specs[5], out_shape[5] = out(width, width), sds((width, width), bf16)
        kept = [((HEADS, cells, tags), bf16), ((HEADS, HEAD_DIM, tags), bf16), ((HEADS, tags), f32), ((HEADS, HEAD_DIM, tags), bf16),
                ((HEADS, HEAD_DIM, tags), bf16), ((tags, width), f32), ((tags, width), f32), ((3 * width, width), f32), ((width, width), f32)]
        out_specs += [out(tags, 1)] + [pl.BlockSpec(memory_space=pl.ANY)] * len(kept)
        out_shape += [sds((tags, 1), f32)] + [sds(*k) for k in kept]
        scratch.append(pltpu.SemaphoreType.DMA((len(kept),)))
    return pl.pallas_call(
        functools.partial(middle, held_back),
        grid_spec=pltpu.PrefetchScalarGridSpec(
            num_scalar_prefetch=1,
            grid=(images,),
            in_specs=[
                per(tags, width), per(cells, width), per(tags, width), per(HEADS, HEAD_DIM, tags), per(2 * HEADS, HEAD_DIM, cells),
                one(3 * width, width), one(2, width, width), pl.BlockSpec(memory_space=pl.ANY), pl.BlockSpec(memory_space=pl.ANY), one(16, width), one(1, hidden),
            ],
            out_specs=out_specs,
            scratch_shapes=scratch,
        ),
        out_shape=out_shape,
        compiler_params=pltpu.CompilerParams(vmem_limit_bytes=62 * MIB),
        name="middle",
    )(lens, x, mem, gout, mix_one, ckv, wt_cross, w_proj, w_in, w_out, vectors, b_in)


def self_backward(x_ref, qkv_ref, near_ref, far_ref, inv_ref, mix_ref, gmix_ref, g_resid, wt_self,
                  g_tags, gw_self, g_col, d_ref, acc, acc_col):
    tags, width = x_ref.shape[1:]
    half = tags // 2
    i = pl.program_id(0)

    @pl.when(i == 0)
    def _():
        acc[...] = jnp.zeros_like(acc)
        acc_col[...] = jnp.zeros_like(acc_col)

    def head(h, _):
        grad = gmix_ref[0, h].astype(f32)
        inv = inv_ref[0, pl.ds(h, 1), :]
        delta = jnp.sum(grad * mix_ref[0, h].astype(f32), 0, keepdims=True) * inv
        grad = (grad * inv).astype(bf16)
        ext = with_delta(grad, delta)
        qt, kt, vt = qkv_ref[0, h], qkv_ref[0, HEADS + h], with_ones(qkv_ref[0, 2 * HEADS + h])
        near, far = near_ref[0, h], far_ref[0, h]
        ds_near = near * dot(vt[:, :half], ext[:, :half], 0, 0).astype(bf16)
        ds_far = far * dot(vt, ext[:, half:], 0, 0).astype(bf16)
        dv = dot(grad[:, half:], far, 1, 1)
        dk = dot(qt[:, half:], ds_far, 1, 1)
        d_ref[2 * HEADS + h, :, half:] = dv[:, half:].astype(bf16)
        d_ref[2 * HEADS + h, :, :half] = (dv[:, :half] + dot(grad[:, :half], near, 1, 1)).astype(bf16)
        d_ref[HEADS + h, :, half:] = dk[:, half:].astype(bf16)
        d_ref[HEADS + h, :, :half] = (dk[:, :half] + dot(qt[:, :half], ds_near, 1, 1)).astype(bf16)
        d_ref[h, :, :half] = (dot(kt[:, :half], ds_near, 1, 0) * HEAD_DIM ** -0.5).astype(bf16)
        d_ref[h, :, half:] = (dot(kt, ds_far, 1, 0) * HEAD_DIM ** -0.5).astype(bf16)
        return 0

    lax.fori_loop(0, HEADS, head, 0)
    d = d_ref[...].reshape(3 * width, tags)
    acc_col[0] += lane_groups(d[:width].astype(f32))
    acc_col[1] += lane_groups(d[2 * width :].astype(f32))
    acc[...] += dot(d, x_ref[0], 1, 0)
    g_tags[0] = g_resid[0] + dot(d, wt_self[...], 0, 0)

    @pl.when(i == pl.num_programs(0) - 1)
    def _():
        gw_self[...] = acc[...].astype(bf16).T
        g_col[0:1] = column_sums(acc_col[0].T)
        g_col[1:2] = column_sums(acc_col[1].T)


def run_self_backward(x, qkv, near, far, inv, mix, gmix, g_resid, wt_self):
    images, tags, width = x.shape
    half = tags // 2
    sds = jax.ShapeDtypeStruct

    def per(*shape):
        return pl.BlockSpec((1,) + shape, lambda i: (i,) + (0,) * len(shape))

    def one(*shape):
        return pl.BlockSpec(shape, lambda i: (0,) * len(shape))

    return pl.pallas_call(
        self_backward,
        grid=(images,),
        in_specs=[per(tags, width), per(3 * HEADS, HEAD_DIM, tags), per(HEADS, half, half), per(HEADS, tags, half), per(HEADS, tags),
                  per(HEADS, HEAD_DIM, tags), per(HEADS, HEAD_DIM, tags), per(tags, width),
                  one(3 * width, width)],
        out_specs=[per(tags, width), one(width, 3 * width), one(8, width)],
        out_shape=[sds((images, tags, width), f32), sds((width, 3 * width), bf16), sds((8, width), f32)],
        scratch_shapes=[pltpu.VMEM((3 * HEADS, HEAD_DIM, tags), bf16), pltpu.VMEM((3 * width, width), f32), pltpu.VMEM((2, width, 128), f32)],
        compiler_params=pltpu.CompilerParams(vmem_limit_bytes=60 * MIB),
        name="self_backward",
    )(x, qkv, near, far, inv, mix, gmix, g_resid, wt_self)


def layer(lens, x, mem, gout, w_self, w_cross, w_proj, w_in, w_out, vectors, b_in):
    width = x.shape[2]
    zero = jnp.zeros((width,), f32)
    bias_qkv = jnp.concatenate([vectors[0], zero, vectors[1]])[:, None]
    bias_kv = jnp.concatenate([zero, vectors[4]])[:, None]
    qkv, ckv, near, far, inv, mix, wt_self, wt_cross = run_self_forward(lens, x, mem, w_self, w_cross, bias_qkv, bias_kv)
    out, g_resid, gmix, g_mem, gw_cross, gw_proj, gw_in, gw_out, g_vec, g_bin = run_middle(
        lens, x, mem, gout, mix, ckv, wt_cross, w_proj, w_in, w_out, vectors, b_in)
    g_tags, gw_self, g_col = run_self_backward(x, qkv, near, far, inv, mix, gmix, g_resid, wt_self)
    g_vec = g_vec.at[0:2].set(g_col[0:2])
    return out, g_tags, g_mem, gw_self, gw_cross, gw_proj, gw_in, gw_out, g_vec, g_bin


ALL = slice(None)


SMALL, SELF, PROJ, CROSS, IN, OUT = range(6)
PLAN = (
    ((SMALL, 0), (SELF, 0), (PROJ, 0), (CROSS, 0), (IN, 0), (OUT, 0),
     (SMALL, 1), (SELF, 1), (SMALL, 2), (PROJ, 1), (SELF, 2), (SMALL, 3), (CROSS, 1), (PROJ, 2), (IN, 1), (SELF, 3), (CROSS, 2), (OUT, 1),
     (PROJ, 3), (SMALL, 4), (SELF, 4)),
    ((IN, 2),),
    ((OUT, 2),),
    ((CROSS, 3),),
    ((IN, 3),),
    ((OUT, 3),),
    (),
    ((CROSS, 4),),
    ((PROJ, 4), (IN, 4), (OUT, 4)),
)
MEANTIME = {2: (0, 6), 3: (1, 2), 4: (2, 0), 5: (2, 6)}


class Gathering:
    def __init__(self, dims, me, shard, held, lead, sems):
        self.dims, self.me, self.shard, self.held, self.lead = dims, me, shard, held, lead
        self.local, self.send, self.recv = sems

    def cell(self, *index):
        return self.held.at[(ALL,) * self.lead + index]

    def remote(self, slot, src, dst, peer):
        return pltpu.make_async_remote_copy(
            src_ref=src, dst_ref=dst, send_sem=self.send.at[slot], recv_sem=self.recv.at[slot],
            device_id=device(self.dims, *peer), device_id_type=MESH)

    def keep(self):
        return pltpu.make_async_copy(self.shard, self.cell(*self.me), self.local)

    def first(self):
        a, b, x, c = self.me
        outer = self.dims[0]
        return [self.remote(k - 1, self.shard, self.cell(a, b, x, c), (lax.rem(a + k, outer), b, x, c)) for k in range(1, outer)]

    def along_inner(self, core):
        a, b, x, c = self.me
        outer, inner, _ = self.dims
        piece = self.cell(ALL, b, ALL if core == 0 else x, c)
        return [self.remote(outer - 2 + k, piece, piece, (a, lax.rem(b + k, inner), x, c)) for k in range(1, inner)]

    def along_across(self, core):
        a, b, x, c = self.me
        outer, inner, across = self.dims
        piece = self.cell(ALL, b if core == 0 else ALL, x, c)
        return [self.remote(outer + inner - 3 + k, piece, piece, (a, b, lax.rem(x + k, across), c)) for k in range(1, across)]

    def second(self, core):
        return self.along_across(core) if core == 0 else self.along_inner(core)

    def third(self, core):
        return self.along_inner(core) if core == 0 else self.along_across(core)

    def handed(self, core, holder):
        a, b, x, c = self.me
        outer, inner, across = self.dims
        base = outer + inner + across - 3

        def piece(slot, row, column):
            ref = self.cell(ALL, row, column, holder)
            return self.remote(base + slot, ref, ref, (a, b, x, 1 - c))

        own = [piece(0, b, x)]
        by_inner = [piece(k, lax.rem(b + k, inner), ALL if core == 0 else x) for k in range(1, inner)]
        by_across = [piece(inner - 1 + k, b if core == 0 else ALL, lax.rem(x + k, across)) for k in range(1, across)]
        return (own, by_across, by_inner) if core == 0 else (own, by_inner, by_across)

    def begin(self):
        self.keep().start()
        for copy in self.first():
            copy.start()

    def each_core(self, act):
        for core in (0, 1):
            pl.when(self.me[3] == core)(functools.partial(act, core))

    def advance(self, stage):
        def act(core):
            if stage == 1:
                self.keep().wait()
            for copy in (self.first(), self.second(core), self.third(core))[stage - 1]:
                copy.wait_recv()
            following = (self.second(core), self.third(core), [])[stage - 1]
            for copy in following + self.handed(core, self.me[3])[stage - 1]:
                copy.start()
        self.each_core(act)

    def finish(self):
        def act(core):
            for group in self.handed(1 - core, 1 - self.me[3]):
                for copy in group:
                    copy.wait_recv()
        self.each_core(act)

    def drain(self):
        def act(core):
            for copy in self.first() + self.second(core) + self.third(core) + sum(self.handed(core, self.me[3]), []):
                copy.wait_send()
        self.each_core(act)


def gather_slots(dims):
    outer, inner, across = dims
    return outer + 2 * (inner + across) - 4


def spread(held, row_lanes, width, rows):
    devices = held.shape[0] // 16
    lane = lax.broadcasted_iota(jnp.int32, (128, width), 0)
    at = lax.broadcasted_iota(jnp.int32, (128, width), 1)
    pick = jnp.where((lax.rem(at, row_lanes) == lane), 1.0, 0.0).astype(bf16)
    wide = dot(held, pick, 1, 0)
    owner = lax.broadcasted_iota(jnp.int32, (devices * 16, width), 0) // 16
    at = lax.broadcasted_iota(jnp.int32, (devices * 16, width), 1)
    wide = jnp.where(at // row_lanes == owner, wide, 0.0)
    return jnp.sum(wide.reshape(devices, 16, width), 0)


def opening(dims, lens, x_ref, mem_ref, b_ref, g_ref, h_ref, s_cross, s_self, s_proj, s_in, s_out,
            qkv_ref, ckv_ref, low_ref, high_ref, inv_ref, mix_ref, out_self, out_cross, vec_ref, bin_ref, o_proj, o_in, o_out,
            small, small_low, h_small, h_self, h_cross, wt_self, wt_cross, cols, low_a, high_a, low_b, high_b, tile, beyond, gone, local, send, recv):
    width = x_ref.shape[2]
    tags = x_ref.shape[1]
    half = tags // 2
    step = pl.program_id(0)
    images = pl.num_programs(0) // 2
    me = place(dims)
    pairs = ((small_low, h_small, 0), (s_self, h_self, 0), (s_proj, o_proj, 1), (s_cross, h_cross, 0), (s_in, o_in, 0), (s_out, o_out, 0))
    gs = [Gathering(dims, me, shard, held, lead, (local.at[k], send.at[k], recv.at[k])) for k, (shard, held, lead) in enumerate(pairs)]
    keep_self = pltpu.make_async_copy(wt_self, out_self, gone.at[0])
    keep_cross = pltpu.make_async_copy(wt_cross, out_cross, gone.at[1])

    def play(slot):
        for item, stage in PLAN[slot]:
            item = gs[item]
            item.begin() if stage == 0 else item.finish() if stage == 4 else item.advance(stage)

    def slot_at(number, slot):
        @pl.when(step == number)
        def _():
            play(slot)

    @pl.when(step == 0)
    def _():
        hails = hail(dims, me)
        small[...] = jnp.zeros_like(small)
        small[0:10, : b_ref.shape[1]] = b_ref[...].astype(f32)
        small[10:13, : g_ref.shape[1]] = g_ref[...].astype(f32)
        small[13:14, : h_ref.shape[1]] = h_ref[...].astype(f32)
        small_low[...] = small[...].astype(bf16)
        greet(dims, me, hails)
        play(0)
        vectors = spread(h_small[...].reshape(-1, 128), b_ref.shape[1], width, 16)
        vec_ref[...] = vectors
        bin_ref[...] = spread(h_small[...].reshape(-1, 128), h_ref.shape[1], bin_ref.shape[1], 16)[13:14]
        cols[...] = vectors.T
        wt_self[...] = h_self[...].reshape(width, 3 * width).T
        keep_self.start()

    @pl.when(step < images)
    def _():
        qkv = dot(wt_self[...], x_ref[0], 1, 1)
        qkv_ref[0, :HEADS] = ((qkv[:width] + cols[:, 0:1]).astype(bf16) * bf16(HEAD_DIM ** -0.5)).reshape(HEADS, HEAD_DIM, tags)
        qkv_ref[0, HEADS : 2 * HEADS] = qkv[width : 2 * width].astype(bf16).reshape(HEADS, HEAD_DIM, tags)
        qkv_ref[0, 2 * HEADS :] = (qkv[2 * width :] + cols[:, 1:2]).astype(bf16).reshape(HEADS, HEAD_DIM, tags)

    @pl.when(step < images)
    def _():
        key_at, query_at = lax.broadcasted_iota(jnp.int32, (half, half), 0), lax.broadcasted_iota(jnp.int32, (half, half), 1)
        tile[...] = jnp.where(key_at <= query_at, 0.0, MASKED)
        row, key_at = lax.broadcasted_iota(jnp.int32, beyond.shape, 0), lax.broadcasted_iota(jnp.int32, beyond.shape, 1)
        hidden = jnp.logical_and(row == 0, key_at >= lens[jnp.minimum(step, images - 1)])
        beyond[...] = jnp.where(hidden, MASKED, 0.0).astype(bf16)

    def scores(h, low, high):
        qt, kt = with_ones(qkv_ref[0, h]), jnp.concatenate([qkv_ref[0, HEADS + h], beyond[...]], 0)
        s = dot(kt[:, :half], qt, 0, 0)
        left, right = s[:, :half] + tile[...], s[:, half:]
        under = dot(kt[:, half:], qt[:, half:], 0, 0) + tile[...]
        low[:, :half] = left
        low[:, half:] = right
        high[...] = under
        return jnp.max(left, 0, keepdims=True), jnp.maximum(jnp.max(right, 0, keepdims=True), jnp.max(under, 0, keepdims=True))

    def mix(h, low, high, tops):
        vt = with_ones(qkv_ref[0, 2 * HEADS + h])
        e_low = jnp.concatenate([jnp.exp(low[:, :half] - tops[0]).astype(bf16), jnp.exp(low[:, half:] - tops[1]).astype(bf16)], 1)
        e_high = jnp.exp(high[...] - tops[1]).astype(bf16)
        low_ref[0, h] = e_low
        high_ref[0, h] = e_high
        mixed = dot(vt[:, :half], e_low, 1, 0)
        mixed = jnp.concatenate([mixed[:, :half], mixed[:, half:] + dot(vt[:, half:], e_high, 1, 0)], 1)
        inv = 1.0 / mixed[HEAD_DIM : HEAD_DIM + 1]
        inv_ref[0, h : h + 1] = inv
        mix_ref[0, h] = (mixed[:HEAD_DIM] * inv).astype(bf16)

    def pair(h, tops):
        following = scores(h + 1, low_b, high_b)
        mix(h, low_a, high_a, tops)
        if h + 2 < HEADS:
            tops = scores(h + 2, low_a, high_a)
        mix(h + 1, low_b, high_b, following)
        return tops

    slot_at(0, 1)

    @pl.when(step < images)
    def _():
        tops = scores(0, low_a, high_a)
        for h in range(0, HEADS, 2):
            for slot, (image, number) in MEANTIME.items():
                if number == h:
                    pl.when(step == image)(functools.partial(play, slot))
            tops = pair(h, tops)

    @pl.when(step == images)
    def _():
        play(7)
        wt_cross[...] = h_cross[...].reshape(width, 3 * width).T
        keep_cross.start()

    @pl.when(step >= images)
    def _():
        kv = dot(wt_cross[width:], mem_ref[0], 1, 1)
        ckv_ref[0, :HEADS] = kv[:width].astype(bf16).reshape(HEADS, HEAD_DIM, -1)
        ckv_ref[0, HEADS:] = (kv[width:] + cols[:, 4:5]).astype(bf16).reshape(HEADS, HEAD_DIM, -1)

    @pl.when(step == 2 * images - 1)
    def _():
        play(8)
        for g in gs:
            g.drain()
        keep_self.wait()
        keep_cross.wait()


def run_opening(dims, lens, x, mem, biases, gains, b_in, shards):
    images, tags, width = x.shape
    cells = mem.shape[1]
    half = tags // 2
    hidden = b_in.shape[1] * dims[0] * dims[1] * dims[2] * 2
    sds = jax.ShapeDtypeStruct

    def early(*shape):
        return pl.BlockSpec((1,) + shape, lambda i: (jnp.minimum(i, images - 1),) + (0,) * len(shape))

    def late(*shape):
        return pl.BlockSpec((1,) + shape, lambda i: (jnp.maximum(i - images, 0),) + (0,) * len(shape))

    def one(*shape):
        return pl.BlockSpec(shape, lambda i: (0,) * len(shape))

    def held(shard, lead):
        return shard.shape[:lead] + dims + (2,) + shard.shape[lead:]

    s_cross, s_self, s_proj, s_in, s_out = shards
    rows = s_cross.shape[0]
    cell = dims + (2, rows)
    anywhere = pl.BlockSpec(memory_space=pl.ANY)
    n = len(shards) + 1
    slots = gather_slots(dims)
    return pl.pallas_call(
        functools.partial(opening, dims),
        grid=(2 * images,),
        in_specs=[pl.BlockSpec(memory_space=pltpu.SMEM), early(tags, width), late(cells, width), one(*biases.shape), one(*gains.shape), one(*b_in.shape)]
        + [anywhere] * len(shards),
        out_specs=[
            early(3 * HEADS, HEAD_DIM, tags), late(2 * HEADS, HEAD_DIM, cells), early(HEADS, half, tags), early(HEADS, half, half),
            early(HEADS, tags), early(HEADS, HEAD_DIM, tags), anywhere, anywhere, one(16, width), one(1, hidden),
            anywhere, anywhere, anywhere,
        ],
        out_shape=[
            sds((images, 3 * HEADS, HEAD_DIM, tags), bf16),
            sds((images, 2 * HEADS, HEAD_DIM, cells), bf16),
            sds((images, HEADS, half, tags), bf16),
            sds((images, HEADS, half, half), bf16),
            sds((images, HEADS, tags), f32),
            sds((images, HEADS, HEAD_DIM, tags), bf16),
            sds((3 * width, width), bf16),
            sds((3 * width, width), bf16),
            sds((16, width), f32),
            sds((1, hidden), f32),
            sds(held(s_proj, 1), bf16),
            sds(held(s_in, 0), bf16),
            sds(held(s_out, 0), bf16),
        ],
        scratch_shapes=[
            pltpu.VMEM((16, 128), f32), pltpu.VMEM((16, 128), bf16), pltpu.VMEM(dims + (2, 16, 128), bf16),
            pltpu.VMEM(cell + (3 * width,), bf16), pltpu.VMEM(cell + (3 * width,), bf16),
            pltpu.VMEM((3 * width, width), bf16), pltpu.VMEM((3 * width, width), bf16),
            pltpu.VMEM((width, 16), f32), pltpu.VMEM((half, tags), f32), pltpu.VMEM((half, half), f32), pltpu.VMEM((half, tags), f32), pltpu.VMEM((half, half), f32),
            pltpu.VMEM((half, half), f32), pltpu.VMEM((16, tags), bf16),
            pltpu.SemaphoreType.DMA((2,)),
            pltpu.SemaphoreType.DMA((n,)), pltpu.SemaphoreType.DMA((n, slots)), pltpu.SemaphoreType.DMA((n, slots)),
        ],
        compiler_params=pltpu.CompilerParams(collective_id=0, has_side_effects=True, vmem_limit_bytes=58 * MIB),
        name="opening",
    )(lens, x, mem, biases, gains, b_in, *shards)


class Scattering:
    def __init__(self, dims, me, grads, short, out, lead, held, sems):
        self.dims, self.me, self.grads, self.short, self.out, self.lead = dims, me, grads, short, out, lead
        self.pair, self.by_inner, self.by_across, self.by_outer, self.last = held
        self.send, self.recv = sems

    def at(self, *index):
        return (ALL,) * self.lead + index

    def remote(self, slot, src, dst, peer):
        return pltpu.make_async_remote_copy(
            src_ref=src, dst_ref=dst, send_sem=self.send.at[slot], recv_sem=self.recv.at[slot],
            device_id=device(self.dims, *peer), device_id_type=MESH)

    def swap(self):
        a, b, x, c = self.me
        return [self.remote(0, self.grads.at[self.at(ALL, ALL, ALL, 1 - c)], self.pair, (a, b, x, 1 - c))]

    def along_inner(self, core):
        a, b, x, c = self.me
        inner = self.dims[1]
        res = []
        for k in range(1, inner):
            peer = lax.rem(b + k, inner)
            src = self.pair.at[self.at(ALL, peer)] if core == 0 else self.by_across.at[0].at[self.at(ALL, peer)]
            dst = self.by_inner.at[k - 1] if core == 0 else self.by_outer.at[k - 1]
            res.append(self.remote(k, src, dst, (a, peer, x, c)))
        return res

    def along_across(self, core):
        a, b, x, c = self.me
        _, inner, across = self.dims
        res = []
        for k in range(1, across):
            peer = lax.rem(x + k, across)
            src = self.pair.at[self.at(ALL, ALL, peer)] if core == 1 else self.by_inner.at[0].at[self.at(ALL, peer)]
            dst = self.by_across.at[k - 1] if core == 1 else self.by_outer.at[k - 1]
            res.append(self.remote(inner - 1 + k, src, dst, (a, b, peer, c)))
        return res

    def second(self, core):
        return self.along_inner(core) if core == 0 else self.along_across(core)

    def third(self, core):
        return self.along_across(core) if core == 0 else self.along_inner(core)

    def along_outer(self):
        a, b, x, c = self.me
        outer, inner, across = self.dims
        return [
            self.remote(inner + across - 2 + k, self.by_outer.at[0].at[self.at(lax.rem(a + k, outer))], self.last.at[k - 1],
                        (lax.rem(a + k, outer), b, x, c))
            for k in range(1, outer)
        ]

    def over_plane(self):
        a, b, x, c = self.me
        _, inner, across = self.dims
        res = []
        for k in range(1, inner * across):
            row, column = lax.rem(b + k // across, inner), lax.rem(x + k % across, across)
            res.append(self.remote(k, self.pair.at[:, row, column], self.by_inner.at[k - 1], (a, row, column, c)))
        return res

    def from_plane(self):
        a, b, x, c = self.me
        outer, inner, across = self.dims
        return [
            self.remote(inner * across - 1 + k, self.by_outer.at[0, lax.rem(a + k, outer)], self.last.at[k - 1], (lax.rem(a + k, outer), b, x, c))
            for k in range(1, outer)
        ]

    def begin(self):
        for copy in self.swap():
            copy.start()

    def advance_short(self, stage):
        a, b, x, c = self.me
        outer, inner, across = self.dims

        def up(value):
            return value.astype(f32)

        for copy in (self.swap(), self.over_plane(), self.from_plane())[stage - 1]:
            copy.wait_recv()
        if stage == 1:
            self.pair[...] = (up(self.grads[:, :, :, c]) + up(self.pair[...])).astype(bf16)
            following = self.over_plane()
        elif stage == 2:
            total = up(self.pair[:, b, x])
            for k in range(inner * across - 1):
                total = total + up(self.by_inner[k])
            self.by_outer[0] = total.astype(bf16)
            following = self.from_plane()
        else:
            total = up(self.by_outer[0, a])
            for k in range(outer - 1):
                total = total + up(self.last[k])
            self.out[...] = total
            following = []
        for copy in following:
            copy.start()

    def advance(self, stage):
        if self.short:
            return self.advance_short(stage)
        a, b, x, c = self.me
        _, inner, across = self.dims

        def up(value):
            return value.astype(f32)

        def act(core):
            for copy in (self.swap(), self.second(core), self.third(core), self.along_outer())[stage - 1]:
                copy.wait_recv()
            if stage == 1:
                def add(k, _):
                    self.pair[k] = (up(self.grads[k, :, :, c]) + up(self.pair[k])).astype(bf16)
                    return 0
                following = self.second(core)
            elif stage == 2:
                held = self.by_inner if core == 0 else self.by_across

                def add(k, _):
                    total = up(self.pair[k, b] if core == 0 else self.pair[k, :, x])
                    for j in range((inner if core == 0 else across) - 1):
                        total = total + up(held[j, k])
                    held[0, k] = total.astype(bf16)
                    return 0
                following = self.third(core)
            elif stage == 3:
                held = self.by_inner if core == 0 else self.by_across

                def add(k, _):
                    total = up(held[0, k, x if core == 0 else b])
                    for j in range((across if core == 0 else inner) - 1):
                        total = total + up(self.by_outer[j, k])
                    self.by_outer[0, k] = total.astype(bf16)
                    return 0
                following = self.along_outer()
            else:
                total = up(self.by_outer[(0,) + self.at(a)])
                for k in range(self.dims[0] - 1):
                    total = total + up(self.last[k])
                self.out[...] = total
                following = []
            if stage < 4:
                lax.fori_loop(0, self.dims[0], add, 0)
            for copy in following:
                copy.start()

        for core in (0, 1):
            pl.when(c == core)(functools.partial(act, core))

    def drain(self):
        def act(core):
            for copy in self.swap() + self.second(core) + self.third(core) + self.along_outer():
                copy.wait_send()

        if self.short:
            for copy in self.swap() + self.over_plane() + self.from_plane():
                copy.wait_send()
            return
        for core in (0, 1):
            pl.when(self.me[3] == core)(functools.partial(act, core))


def scatter_slots(dims):
    return max(dims[0] + dims[1] + dims[2] - 2, dims[0] + dims[1] * dims[2] - 1)


def scatter_space(dims, lead, tail, short=False):
    outer, inner, across = dims
    if short:
        return [(outer, inner, across) + tail, (inner * across - 1, outer) + tail, (1,) + tail, (1, outer) + tail, (outer - 1,) + tail]
    return [
        lead + (outer, inner, across) + tail,
        (inner - 1,) + lead + (outer, across) + tail,
        (across - 1,) + lead + (outer, inner) + tail,
        (max(inner, across) - 1,) + lead + (outer,) + tail,
        (outer - 1,) + lead + tail,
    ]


def collect(rows, row_lanes, devices):
    width = rows.shape[1]
    many = jnp.broadcast_to(rows[None], (devices, 16, width)).reshape(devices * 16, width)
    owner = lax.broadcasted_iota(jnp.int32, many.shape, 0) // 16
    at = lax.broadcasted_iota(jnp.int32, many.shape, 1)
    many = jnp.where(at // row_lanes == owner, many, 0.0).astype(bf16)
    lane = lax.broadcasted_iota(jnp.int32, (128, width), 0)
    at = lax.broadcasted_iota(jnp.int32, (128, width), 1)
    pick = jnp.where(lax.rem(at, row_lanes) == lane, 1.0, 0.0).astype(bf16)
    return dot(many, pick, 1, 1)


G_OUT, G_IN, G_ONE, G_CROSS, G_ZERO, G_HALF, G_REST, G_SMALL = range(8)
SHORT = (G_REST, G_SMALL)
FEW = 2
EVENTS = {
    (0, 0): ((G_OUT, 0), (G_IN, 0), (G_ONE, 0)),
    (0, 1): ((G_OUT, 1),),
    (0, 2): ((G_IN, 1), (G_ONE, 1)),
    (0, 6): ((G_CROSS, 0),),
    (0, 7): ((G_ZERO, 0), (G_OUT, 2)),
    (1, 1): ((G_IN, 2),),
    (2, 1): ((G_CROSS, 1), (G_ONE, 2), (G_ZERO, 1)),
    (3, 1): ((G_HALF, 0), (G_OUT, 3), (G_IN, 3)),
    (5, 1): ((G_OUT, 4), (G_CROSS, 2), (G_HALF, 1), (G_ONE, 3)),
    (6, 1): ((G_REST, 0), (G_SMALL, 0), (G_ZERO, 2), (G_IN, 4)),
    (8, 1): ((G_ONE, 4), (G_CROSS, 3)),
    (9, 1): ((G_HALF, 2), (G_REST, 1), (G_SMALL, 1), (G_ZERO, 3)),
    (9, 2): ((G_HALF, 3), (G_REST, 2), (G_SMALL, 2), (G_CROSS, 4), (G_ZERO, 4), (G_HALF, 4), (G_REST, 3), (G_SMALL, 3)),
}


def closing(dims, x_ref, qkv_ref, low_ref, high_ref, inv_ref, mix_ref, gmix_ref, inv_two, vectors, g_vec, g_bin, scale_one,
            low_out, low_in, low_one, e_any, ckv_any, q_any, mix_two_any, gmix_two_any, mix_any, two_any, one_any, wc_any, mem_any, ac_any, ap_any, wp_any, ws_any, gres_any,
            g_tags, sh_out, sh_in, sh_one, sh_cross, sh_zero, sh_half, sh_rest, sh_small, g_mem,
            e_ref, ckv_ref, q_ref, mix_two, gmix_two, mine_out, mine_in, mine_one, gres_ref, dkv_ref,
            mix_one, g_two, n_one, wt_cross, mem_ref, acc_cross, acc_zero, w_zero, wt_self,
            dq_ref, gmix_last, gres_last, gmix_now, acc, add_vec, acc_col, low_cross, low_zero, low_half, low_rest, low_small, head_sem, in_sem, *rest):
    tags, width = x_ref.shape[1:]
    cells = mem_ref.shape[0]
    half = tags // 2
    some = HEADS // 2
    step = pl.program_id(0)
    images = pl.num_programs(0) // 3
    me = place(dims)
    devices = dims[0] * dims[1] * dims[2] * 2
    held, (send, recv) = rest[:-2], rest[-2:]
    triples = ((mine_out, None, sh_out), (mine_in, None, sh_in), (mine_one, None, sh_one), (low_cross, None, sh_cross),
               (low_zero, None, sh_zero), (low_half, None, sh_half), (low_rest, None, sh_rest), (low_small, None, sh_small))
    every = [Scattering(dims, me, grads, k in SHORT, out, 0, held[5 * k : 5 * k + 5], (send.at[k], recv.at[k])) for k, (grads, _, out) in enumerate(triples)]
    fetches = [
        pltpu.make_async_copy(src, dst, in_sem.at[k])
        for k, (src, dst) in enumerate((
            (low_out, mine_out), (low_in, mine_in), (low_one, mine_one),
            (one_any, n_one), (mem_any.at[images - 1], mem_ref), (ac_any, acc_cross), (two_any, g_two), (wc_any, wt_cross),
            (mix_any.at[images - 1], mix_one), (ap_any, acc_zero), (wp_any.at[0], w_zero), (gres_any, gres_ref), (ws_any, wt_self)))
    ]

    def e_rows(h):
        return e_ref.at[pl.ds(pl.multiple_of(h * cells, 16), cells)]

    def few_fetches(k):
        few = pl.ds(k * FEW, FEW)
        rows = pl.ds(k * FEW * cells, FEW * cells)
        pairs = ((e_any.at[rows], e_ref.at[rows]), (ckv_any.at[images - 1, few], ckv_ref.at[few]),
                 (ckv_any.at[images - 1, pl.ds(HEADS + k * FEW, FEW)], ckv_ref.at[pl.ds(HEADS + k * FEW, FEW)]),
                 (q_any.at[few], q_ref.at[few]), (mix_two_any.at[few], mix_two.at[few]), (gmix_two_any.at[few], gmix_two.at[few]))
        return [pltpu.make_async_copy(src, dst, head_sem.at[k, j]) for j, (src, dst) in enumerate(pairs)]

    def play(number, where):
        for item, stage in EVENTS.get((number, where), ()):
            item = every[item]
            item.begin() if stage == 0 else item.advance(stage)

    def events(where):
        for number in sorted(number for number, at in EVENTS if at == where and number > 0):
            pl.when(step == number)(functools.partial(play, number, where))

    def vec(k):
        return vectors[k : k + 1, :]

    @pl.when(step == 0)
    def _():
        hails = hail(dims, me, True)
        for fetch in fetches[:3] + few_fetches(0):
            fetch.start()
        greet(dims, me, hails)
        for fetch in fetches[:3]:
            fetch.wait()
        play(0, 0)
        for k in range(1, HEADS // FEW):
            for fetch in few_fetches(k):
                fetch.start()
        for fetch in fetches[3:]:
            fetch.start()
        acc_col[...] = jnp.zeros_like(acc_col)
        def few_heads(k, _):
            for fetch in few_fetches(k):
                fetch.wait()
            for j in range(FEW):
                h = k * FEW + j
                dq_ref[h], dkv_ref[h], dkv_ref[HEADS + h] = cross_back(
                    h, e_rows(h)[...], ckv_ref[h], ckv_ref[HEADS + h], q_ref[h], gmix_two[h], mix_two[h], inv_two[pl.ds(h, 1), :])
            for half_done in (1, 2):
                pl.when((k + 1) * FEW == some * half_done)(functools.partial(play, 0, half_done))
            return 0

        lax.fori_loop(0, HEADS // FEW, few_heads, 0)
        for fetch in fetches[3:11]:
            fetch.wait()
        dq = dq_ref[...].reshape(width, tags)
        dkv = dkv_ref[...].reshape(2 * width, cells)
        one_low = (n_one[...] * vec(10) + vec(6)).astype(bf16)
        acc_cross[:width] += dot(dq, one_low, 1, 0)
        acc_cross[width:] += dot(dkv, mem_ref[...], 1, 0)
        low_cross[...] = acc_cross[...].astype(bf16).T.reshape(low_cross.shape)
        play(0, 6)
        g_one = g_two[...] + dot(dq, wt_cross[:width], 0, 0)
        sum_gain, sum_shift = column_sums(g_one * n_one[...]), column_sums(g_one)
        g_one = norm_back(g_one, n_one[...], scale_one[...], vec(10))
        gres_last[...] = g_one
        g_low = g_one.astype(bf16)
        acc_zero[...] += dot(mix_one[...].reshape(width, tags), g_low, 1, 0)
        low_zero[...] = acc_zero[...].astype(bf16).reshape(low_zero.shape)
        play(0, 7)
        gmix_last[...] = dot(w_zero[...], g_low, 1, 1).astype(bf16).reshape(gmix_last.shape)
        at = lax.broadcasted_iota(jnp.int32, add_vec.shape, 0)
        total = g_vec[...]
        for k, row in ((2, column_sums(g_one)), (3, column_sums(lane_groups(dq.astype(f32)).T)),
                       (4, column_sums(memory_lanes(dkv[width:].astype(f32)).T)), (6, sum_shift), (10, sum_gain)):
            total = total + jnp.where(at == k, row, 0.0)
        add_vec[...] = total

    turn = jnp.maximum(step - 1, 0)
    part = jnp.minimum(turn // images, 1)
    now = lax.rem(turn, images)
    backward = jnp.logical_and(step >= 1, step <= 2 * images)

    @pl.when(jnp.logical_and(backward, now < images - 1))
    def _():
        gmix_now[...] = gmix_ref[0]

    @pl.when(jnp.logical_and(backward, now == images - 1))
    def _():
        gmix_now[...] = gmix_last[pl.ds(part * some, some)]

    def d_rows(image, kind, h, count=1):
        return pl.ds(pl.multiple_of(((image * 3 + kind) * HEADS + h) * HEAD_DIM, HEAD_DIM), count * HEAD_DIM)

    def head(h, _):
        grad = gmix_now[h].astype(f32)
        inv = inv_ref[0, pl.ds(part * some + h, 1), :]
        delta = jnp.sum(grad * mix_ref[0, h].astype(f32), 0, keepdims=True) * inv
        grad = (grad * inv).astype(bf16)
        ext = with_delta(grad, delta)
        qt, kt, vt = qkv_ref[0, 0, h], qkv_ref[0, 1, h], with_ones(qkv_ref[0, 2, h])
        e_low, e_high = low_ref[0, h], high_ref[0, h]
        ds_low = e_low * dot(vt[:, :half], ext, 0, 0).astype(bf16)
        ds_high = e_high * dot(vt[:, half:], ext[:, half:], 0, 0).astype(bf16)
        dv = jnp.concatenate([dot(grad, e_low, 1, 1), dot(grad[:, half:], e_high, 1, 1)], 1)
        dk = jnp.concatenate([dot(qt, ds_low, 1, 1), dot(qt[:, half:], ds_high, 1, 1)], 1)
        dq = dot(kt[:, :half], ds_low, 1, 0)
        dq = jnp.concatenate([dq[:, :half], dq[:, half:] + dot(kt[:, half:], ds_high, 1, 0)], 1) * HEAD_DIM ** -0.5
        at = part * some + h
        e_ref[d_rows(now, 0, at)] = dq.astype(bf16)
        e_ref[d_rows(now, 1, at)] = dk.astype(bf16)
        e_ref[d_rows(now, 2, at)] = dv.astype(bf16)
        return 0

    @pl.when(backward)
    def _():
        lax.fori_loop(0, some, head, 0, unroll=some)
        d = [e_ref[d_rows(now, kind, part * some, some)] for kind in range(3)]
        rows = some * HEAD_DIM
        acc_col[0, pl.ds(part * rows, rows)] += lane_groups(d[0].astype(f32))
        acc_col[1, pl.ds(part * rows, rows)] += lane_groups(d[2].astype(f32))
        fresh = now == 0
        for kind in range(3):
            product = dot(d[kind], x_ref[0], 1, 0)

            @pl.when(fresh)
            def _():
                acc[kind * rows : (kind + 1) * rows] = product

            @pl.when(jnp.logical_not(fresh))
            def _():
                acc[kind * rows : (kind + 1) * rows] += product

    @pl.when(step == images)
    def _():
        low_half[...] = acc[...].astype(bf16).T.reshape(low_half.shape)

    @pl.when(step == 2 * images)
    def _():
        low_rest[...] = acc[...].astype(bf16).T.reshape(low_rest.shape)
        at = lax.broadcasted_iota(jnp.int32, add_vec.shape, 0)
        rows = jnp.where(at == 0, column_sums(acc_col[0].T), jnp.where(at == 1, column_sums(acc_col[1].T), add_vec[...]))
        at = lax.broadcasted_iota(jnp.int32, (16, g_bin.shape[1]), 0)
        hidden = jnp.where(at == 13, g_bin[...], 0.0)
        small = collect(rows, width // devices, devices) + collect(hidden, g_bin.shape[1] // devices, devices)
        low_small[...] = small.astype(bf16).reshape(low_small.shape)

    events(0)

    @pl.when(step == 2 * images + 1)
    def _():
        for fetch in fetches[11:]:
            fetch.wait()

    @pl.when(step > 2 * images)
    def _():
        image = jnp.maximum(step - 2 * images - 1, 0)
        d = e_ref[d_rows(image, 0, 0, 3 * HEADS)]
        product = dot(d, wt_self[...], 0, 0)

        @pl.when(image < images - 1)
        def _():
            g_tags[0] = (gres_ref[jnp.minimum(image, images - 2)] + product).astype(bf16)

        @pl.when(image == images - 1)
        def _():
            g_tags[0] = (gres_last[...] + product).astype(bf16)

    events(1)

    @pl.when(step == 3 * images)
    def _():
        g_mem[...] = dot(dkv_ref[...].reshape(2 * width, cells), wt_cross[width:], 0, 0).astype(bf16)

    events(2)

    @pl.when(step == 3 * images)
    def _():
        for item in every:
            item.drain()


def run_closing(dims, x, qkv, e_low, e_high, inv, mix, gmix, g_resid, ckv, mem, vectors, wt_self, wt_cross, w_proj, g_one, g_in, g_out, g_vec, g_bin, kept):
    scale_one, e, q, inv_two, mix_two, gmix_two, n_one, g_two, acc_cross, acc_zero = kept
    images, tags, width = x.shape
    memory = mem.shape[1]
    half, some = tags // 2, HEADS // 2
    sds = jax.ShapeDtypeStruct
    cells = dims + (2,)
    devices = dims[0] * dims[1] * dims[2] * 2

    def parts(grad):
        return grad.reshape(cells + (grad.shape[0] // devices, grad.shape[1]))

    low = [parts(g_out), parts(g_in), parts(g_one)]
    rows = width // devices
    lows = [cells + (rows, 3 * width), cells + (rows, width)] + [cells + (rows, 3 * width // 2)] * 2 + [cells + (16, 128)]

    def turn(i):
        t = jnp.clip(i - 1, 0, 2 * images - 1)
        return lax.rem(t, images), lax.div(t, images)

    def by_turn(shape, split):
        def index(i):
            image, part = turn(i)
            return (image,) + tuple(part if k == split else 0 for k in range(len(shape)))
        return pl.BlockSpec((1,) + shape, index)

    def gmix_index(i):
        image, part = turn(i)
        return jnp.minimum(image, images - 2), part, 0, 0

    def one(*shape):
        return pl.BlockSpec(shape, lambda i: (0,) * len(shape), pipeline_mode=pl.Buffered(1))

    def out(*shape):
        return pl.BlockSpec(shape, lambda i: (0,) * len(shape))

    anywhere = pl.BlockSpec(memory_space=pl.ANY)
    shares = [g.shape[4:] for g in low] + [s[4:] for s in lows]
    space = []
    for k, shape in enumerate([g.shape for g in low] + lows):
        space += [pltpu.VMEM(s, bf16) for s in scatter_space(dims, (), shape[4:], k in SHORT)]
    slots = scatter_slots(dims)
    qkv = qkv.reshape(images, 3, HEADS, HEAD_DIM, tags)
    heads = (HEADS, HEAD_DIM, tags)
    return pl.pallas_call(
        functools.partial(closing, dims),
        grid=(3 * images + 1,),
        in_specs=[
            by_turn((tags, width), None), by_turn((3, some, HEAD_DIM, tags), 1), by_turn((some, half, tags), 0), by_turn((some, half, half), 0),
            by_turn((HEADS, tags), None), by_turn((some, HEAD_DIM, tags), 0), pl.BlockSpec((1, some, HEAD_DIM, tags), gmix_index),
            one(HEADS, tags), one(16, width), one(16, width), one(*g_bin.shape), one(tags, 1),
        ] + [anywhere] * 18,
        out_specs=[pl.BlockSpec((1, tags, width), lambda i: (jnp.clip(i - 2 * images - 1, 0, images - 1), 0, 0))]
        + [out(*s) for s in shares] + [out(memory, width)],
        out_shape=[sds((images, tags, width), bf16)] + [sds(s, f32) for s in shares] + [sds((memory, width), bf16)],
        scratch_shapes=[
            pltpu.VMEM((HEADS * memory, tags), bf16), pltpu.VMEM((2 * HEADS, HEAD_DIM, memory), bf16), pltpu.VMEM(heads, bf16), pltpu.VMEM(heads, bf16), pltpu.VMEM(heads, bf16),
        ] + [pltpu.VMEM(g.shape, bf16) for g in low] + [
            pltpu.VMEM((images - 1, tags, width), f32), pltpu.VMEM((2 * HEADS, HEAD_DIM, memory), bf16),
            pltpu.VMEM(heads, bf16), pltpu.VMEM((tags, width), f32), pltpu.VMEM((tags, width), f32),
            pltpu.VMEM((3 * width, width), bf16), pltpu.VMEM((memory, width), bf16), pltpu.VMEM((3 * width, width), f32), pltpu.VMEM((width, width), f32),
            pltpu.VMEM((width, width), bf16), pltpu.VMEM((3 * width, width), bf16),
            pltpu.VMEM(heads, bf16), pltpu.VMEM(heads, bf16), pltpu.VMEM((tags, width), f32), pltpu.VMEM((some, HEAD_DIM, tags), bf16),
            pltpu.VMEM((3 * width // 2, width), f32), pltpu.VMEM((16, width), f32), pltpu.VMEM((2, width, 128), f32),
        ] + [pltpu.VMEM(s, bf16) for s in lows] + [pltpu.SemaphoreType.DMA((HEADS // FEW, 6)), pltpu.SemaphoreType.DMA((13,))] + space
        + [pltpu.SemaphoreType.DMA((8, slots)), pltpu.SemaphoreType.DMA((8, slots))],
        compiler_params=pltpu.CompilerParams(collective_id=1, has_side_effects=True, vmem_limit_bytes=62 * MIB),
        name="closing",
    )(x, qkv, e_low, e_high, inv, mix, gmix, inv_two, vectors, g_vec, g_bin, scale_one, *low,
      e.reshape(HEADS * memory, tags), ckv, q, mix_two, gmix_two, mix, g_two, n_one, wt_cross, mem, acc_cross, acc_zero, w_proj, wt_self, g_resid)


def settle(lanes, hidden_lanes, images, g_mem_in, m_last, tags, s_out, s_in, s_one, s_cross, s_zero, s_half, s_rest, small,
           g_mem, o_tags, o_self, o_cross, o_proj, o_in, o_out, o_bin, o_gains, o_biases):
    width = o_tags.shape[2]
    o_tags[...] = tags[...].astype(f32)

    @pl.when(pl.program_id(0) == 0)
    def _():
        g_mem[0] = m_last[...].astype(f32)
        part = width // 2
        for kind in range(3):
            o_self[:, kind * width : kind * width + part] = s_half[:, kind * part : (kind + 1) * part]
            o_self[:, kind * width + part : (kind + 1) * width] = s_rest[:, kind * part : (kind + 1) * part]
        o_cross[...] = s_cross[...]
        o_proj[0] = s_zero[...]
        o_proj[1] = s_one[...]
        o_in[...] = s_in[...]
        o_out[...] = s_out[...]
        o_biases[...] = small[:10, :lanes]
        o_gains[...] = small[10:13, :lanes]
        o_bin[...] = small[13:14, :hidden_lanes]


def run_settle(lanes, hidden_lanes, g_mem, m_last, g_tags, shares):
    images, tags, width = g_tags.shape
    sds = jax.ShapeDtypeStruct
    s_out, s_in, s_one, s_cross, s_zero, s_half, s_rest, small = shares

    def one(*shape):
        return pl.BlockSpec(shape, lambda i: (0,) * len(shape), pipeline_mode=pl.Buffered(1))

    def out(*shape):
        return pl.BlockSpec(shape, lambda i: (0,) * len(shape))

    rows = s_cross.shape[0]
    shapes = [s_cross.shape, s_cross.shape, (2, rows, width), s_in.shape, s_out.shape, (1, hidden_lanes), (3, lanes), (10, lanes)]
    image = pl.BlockSpec((1, tags, width), lambda i: (i, 0, 0))
    return pl.pallas_call(
        functools.partial(settle, lanes, hidden_lanes, images),
        grid=(images,),
        in_specs=[pl.BlockSpec(memory_space=pl.ANY), one(*m_last.shape), image] + [one(*s.shape) for s in shares],
        out_specs=[pl.BlockSpec((1,) + g_mem.shape[1:], lambda i: (images - 1, 0, 0)), image] + [out(*s) for s in shapes],
        out_shape=[sds(g_mem.shape, f32), sds(g_tags.shape, f32)] + [sds(s, f32) for s in shapes],
        input_output_aliases={0: 0},
        compiler_params=pltpu.CompilerParams(vmem_limit_bytes=62 * MIB),
        name="settle",
    )(g_mem, m_last, g_tags, *shares)


AXES = ("wide", "narrow")
LEADS = (0, 0, 1, 0, 0, 0)


def fold(block, rows, columns):
    if rows % 16 == 0:
        return block
    return block.reshape(block.shape[:-2] + (16, rows * columns // 16))


def per_device(dims, tag_states, image_memory, tag_lengths, w_self, w_cross, w_proj, w_in, b_in, w_out, ln_gains, biases, out_grad):
    cells = dims + (2,)
    fused = w_self.shape[0] % 16 == 0 and tag_states.shape[0] == 3
    devices = dims[0] * dims[1] * dims[2] * 2
    width = tag_states.shape[2]
    lanes, hidden_lanes = biases.shape[1], b_in.shape[0]
    if fused:
        qkv, ckv, near, far, inv, mix, wt_self, wt_cross, vectors, hidden_bias, full_proj, full_in, full_out = run_opening(
            dims, tag_lengths, tag_states, image_memory, biases, ln_gains, b_in[None], (w_cross, w_self, w_proj, w_in, w_out))
        full_proj, full_in, full_out = full_proj.reshape(2, width, width), full_in.reshape(width, -1), full_out.reshape(-1, width)
        layer_out, g_resid, gmix, g_mem, _, g_one, g_in, g_out, g_vec, g_bin, *kept = run_middle(
            tag_lengths, tag_states, image_memory, out_grad, mix, ckv, wt_cross, full_proj, full_in, full_out, vectors, hidden_bias, True)
        g_tags, *shares, m_last = run_closing(
            dims, tag_states, qkv, near, far, inv, mix, gmix, g_resid, ckv, image_memory, vectors, wt_self, wt_cross, full_proj,
            g_one, g_in, g_out, g_vec, g_bin, kept)
        grad_memory, grad_tags, s_self, s_cross, s_proj, s_in, s_out, s_bin, s_gains, s_biases = run_settle(
            lanes, hidden_lanes, g_mem, m_last, g_tags, shares)
        return layer_out, grad_tags, grad_memory, s_self, s_cross, s_proj, s_in, s_bin[0], s_out, s_gains, s_biases
    small = jnp.concatenate(
        [
            jnp.pad(jnp.concatenate([biases, ln_gains]), ((0, 0), (0, 128 - lanes))),
            jnp.pad(b_in[None], ((0, 2), (0, 128 - hidden_lanes))),
        ]
    )
    shards = (w_self, w_cross, w_proj, w_in, w_out, small)
    gathered = gather(dims, [fold(s, *s.shape[-2:]) for s in shards], LEADS)

    def whole(held, shard):
        lead = shard.shape[:-2]
        rows, columns = shard.shape[-2:]
        return held.reshape(lead + (devices * rows, columns))

    full_self, full_cross, full_proj, full_in, full_out, full_small = [whole(h, s) for h, s in zip(gathered, shards)]
    by_device = full_small.reshape(devices, 16, 128)
    vectors = by_device[:, :, :lanes].transpose(1, 0, 2).reshape(16, width).astype(f32)
    hidden_bias = by_device[:, 13, :hidden_lanes].reshape(1, -1).astype(f32)
    layer_out, grad_tags, grad_memory, g_self, g_cross, g_proj, g_in, g_out, g_vec, g_bin = layer(
        tag_lengths, tag_states, image_memory, out_grad, full_self, full_cross, full_proj, full_in, full_out, vectors, hidden_bias)
    g_small = jnp.pad(g_vec.reshape(16, devices, lanes).transpose(1, 0, 2)[:, :13], ((0, 0), (0, 0), (0, 128 - lanes)))
    g_hidden = jnp.pad(g_bin.reshape(devices, 1, hidden_lanes), ((0, 0), (0, 2), (0, 128 - hidden_lanes)))
    g_small = jnp.concatenate([g_small, g_hidden], 1).astype(bf16).reshape(devices * 16, 128)

    def parts(grad, shard):
        lead = shard.shape[:-2]
        rows, columns = shard.shape[-2:]
        return fold(grad.reshape(lead + cells + (rows, columns)), rows, columns)

    shards = (w_self, w_cross, w_proj, w_in, w_out, jax.ShapeDtypeStruct((16, 128), bf16))
    shares = scatter(dims, [parts(g, s) for g, s in zip((g_self, g_cross, g_proj, g_in, g_out, g_small), shards)], LEADS)
    s_self, s_cross, s_proj, s_in, s_out, s_small = [v.reshape(s.shape) for v, s in zip(shares, shards)]
    return (layer_out, grad_tags, grad_memory, s_self, s_cross, s_proj, s_in, s_small[13, :hidden_lanes], s_out,
            s_small[10:13, :lanes], s_small[:10, :lanes])


def solution(mesh):
    dims = grid_of(mesh.shape["wide"], mesh.shape["narrow"])
    rows, matrix, stack, columns = P(AXES, None, None), P(AXES, None), P(None, AXES, None), P(None, AXES)
    return jax.shard_map(
        functools.partial(per_device, dims),
        mesh=mesh,
        in_specs=(rows, rows, P(AXES), matrix, matrix, stack, matrix, P(AXES), matrix, columns, columns, rows),
        out_specs=(rows, rows, rows, matrix, matrix, stack, matrix, P(AXES), matrix, columns, columns),
        check_vma=False,
    )
```

```python
import functools

import jax
import jax.numpy as jnp
from jax import lax
from jax.experimental import pallas as pl
from jax.experimental.pallas import tpu as pltpu
from jax.sharding import PartitionSpec as P


MESH = pl.DeviceIdType.MESH
f32, bf16 = jnp.float32, jnp.bfloat16


def grid_of(mesh_wide, mesh_narrow):
    outer = 4
    return outer, mesh_wide // outer, mesh_narrow // 2


def place(dims):
    outer, inner, across = dims
    wide, narrow = lax.axis_index("wide"), lax.axis_index("narrow")
    return wide // inner, lax.rem(wide, inner), narrow // 2, lax.rem(narrow, 2)


def device(dims, a, b, x, c):
    return {"wide": a * dims[1] + b, "narrow": x * 2 + c}


def hail(dims, me, diagonal=False):
    a, b, x, c = me
    outer, inner, across = dims
    barrier = pltpu.get_barrier_semaphore()
    peers = [(lax.rem(a + k, outer), b, x, c) for k in range(1, outer)]
    peers += [(a, lax.rem(b + k, inner), x, c) for k in range(1, inner)]
    peers += [(a, b, lax.rem(x + k, across), c) for k in range(1, across)]
    peers += [(a, b, x, 1 - c)]
    if diagonal:
        peers += [(a, lax.rem(b + j, inner), lax.rem(x + k, across), c) for j in range(1, inner) for k in range(1, across)]
    for peer in peers:
        pl.semaphore_signal(barrier, inc=1, device_id=device(dims, *peer), device_id_type=MESH)
    return len(peers)


def greet(dims, me, count=0):
    pl.semaphore_wait(pltpu.get_barrier_semaphore(), count or hail(dims, me))


ALL = slice(None)


def gather_kernel(dims, leads, *refs):
    count = len(leads)
    shards, outs = refs[:count], refs[count : 2 * count]
    local_sem, send_sem, recv_sem = refs[2 * count :]
    outer, inner, across = dims
    me = place(dims)
    a, b, x, c = me
    greet(dims, me)

    def cell(ref, lead, *index):
        return ref.at[(ALL,) * lead + index]

    def remote(g, slot, src, dst, peer):
        return pltpu.make_async_remote_copy(
            src_ref=src, dst_ref=dst, send_sem=send_sem.at[g, slot], recv_sem=recv_sem.at[g, slot],
            device_id=device(dims, *peer), device_id_type=MESH)

    n_in, n_ac = inner - 1, across - 1

    def first(g):
        lead = leads[g]
        mine = cell(outs[g], lead, a, b, x, c)
        return [remote(g, k - 1, shards[g], mine, (lax.rem(a + k, outer), b, x, c)) for k in range(1, outer)]

    def keep(g):
        return pltpu.make_async_copy(shards[g], cell(outs[g], leads[g], a, b, x, c), local_sem.at[g])

    base = outer - 1

    def via_inner(g, core):
        lead = leads[g]
        column = ALL if core == 0 else x
        piece = cell(outs[g], lead, ALL, b, column, c)
        return [remote(g, base + k - 1, piece, piece, (a, lax.rem(b + k, inner), x, c)) for k in range(1, inner)]

    def via_across(g, core):
        lead = leads[g]
        row = b if core == 0 else ALL
        piece = cell(outs[g], lead, ALL, row, x, c)
        return [remote(g, base + n_in + k - 1, piece, piece, (a, b, lax.rem(x + k, across), c)) for k in range(1, across)]

    share = base + n_in + n_ac

    def to_partner(g, core, holder):
        lead = leads[g]
        def piece(slot, row, column):
            ref = cell(outs[g], lead, ALL, row, column, holder)
            return remote(g, share + slot, ref, ref, (a, b, x, 1 - c))
        own = [piece(0, b, x)]
        by_inner = [piece(1 + k - 1, lax.rem(b + k, inner), ALL if core == 0 else x) for k in range(1, inner)]
        by_across = [piece(1 + n_in + k - 1, b if core == 0 else ALL, lax.rem(x + k, across)) for k in range(1, across)]
        return (own, by_across, by_inner) if core == 0 else (own, by_inner, by_across)

    def start(copies):
        for copy in copies:
            copy.start()

    def arrived(copies):
        for copy in copies:
            copy.wait_recv()

    for g in range(count):
        keep(g).start()
        start(first(g))

    def body(core):
        second, third = (via_across, via_inner) if core == 0 else (via_inner, via_across)
        for step in range(count + 2):
            g = step
            if g < count:
                keep(g).wait()
                arrived(first(g))
                start(second(g, core))
                start(to_partner(g, core, c)[0])
            g = step - 1
            if 0 <= g < count:
                arrived(second(g, core))
                start(third(g, core))
                start(to_partner(g, core, c)[1])
            g = step - 2
            if 0 <= g < count:
                arrived(third(g, core))
                start(to_partner(g, core, c)[2])
        for g in range(count):
            for group in to_partner(g, 1 - core, 1 - c):
                arrived(group)
        for g in range(count):
            for copy in first(g) + second(g, core) + third(g, core):
                copy.wait_send()
            for group in to_partner(g, core, c):
                for copy in group:
                    copy.wait_send()

    @pl.when(c == 0)
    def _():
        body(0)

    @pl.when(c == 1)
    def _():
        body(1)


def gather(dims, shards, leads):
    outer, inner, across = dims
    def shape(s, lead):
        return jax.ShapeDtypeStruct(s.shape[:lead] + (outer, inner, across, 2) + s.shape[lead:], s.dtype)
    slots = (outer - 1) + 2 * (inner - 1) + 2 * (across - 1) + 1
    n = len(shards)
    return pl.pallas_call(
        functools.partial(gather_kernel, dims, leads),
        out_shape=[shape(s, l) for s, l in zip(shards, leads)],
        in_specs=[pl.BlockSpec(memory_space=pl.ANY)] * n,
        out_specs=[pl.BlockSpec(memory_space=pl.ANY)] * n,
        scratch_shapes=[pltpu.SemaphoreType.DMA((n,)), pltpu.SemaphoreType.DMA((n, slots)), pltpu.SemaphoreType.DMA((n, slots))],
        compiler_params=pltpu.CompilerParams(collective_id=0, has_side_effects=True),
        name="gather_weights",
    )(*shards)


def scatter_kernel(dims, leads, *refs):
    count = len(leads)
    grads, outs = refs[:count], refs[count : 2 * count]
    rest = refs[2 * count :]
    r0, r1i, r1a, r2a, r2i, r3 = (rest[k * count : (k + 1) * count] for k in range(6))
    send_sem, recv_sem = rest[6 * count :]
    outer, inner, across = dims
    me = place(dims)
    a, b, x, c = me
    greet(dims, me)
    n_in, n_ac = inner - 1, across - 1

    def cell(ref, lead, *index):
        return ref.at[(ALL,) * lead + index]

    def remote(g, slot, src, dst, peer):
        return pltpu.make_async_remote_copy(
            src_ref=src, dst_ref=dst, send_sem=send_sem.at[g, slot], recv_sem=recv_sem.at[g, slot],
            device_id=device(dims, *peer), device_id_type=MESH)

    def swap(g):
        return [remote(g, 0, cell(grads[g], leads[g], ALL, ALL, ALL, 1 - c), r0[g], (a, b, x, 1 - c))]

    def via_inner(g, core):
        lead = leads[g]
        res = []
        for k in range(1, inner):
            peer = lax.rem(b + k, inner)
            if core == 0:
                src, dst = cell(r0[g], lead, ALL, peer), r1i[g].at[k - 1]
            else:
                src, dst = cell(r1a[g].at[0], lead, ALL, peer), r2i[g].at[k - 1]
            res.append(remote(g, k, src, dst, (a, peer, x, c)))
        return res

    def via_across(g, core):
        lead = leads[g]
        res = []
        for k in range(1, across):
            peer = lax.rem(x + k, across)
            if core == 1:
                src, dst = cell(r0[g], lead, ALL, ALL, peer), r1a[g].at[k - 1]
            else:
                src, dst = cell(r1i[g].at[0], lead, ALL, peer), r2a[g].at[k - 1]
            res.append(remote(g, 1 + n_in + k - 1, src, dst, (a, b, peer, c)))
        return res

    def last(g, core):
        lead = leads[g]
        held = (r2a if core == 0 else r2i)[g].at[0]
        res = []
        for k in range(1, outer):
            peer = lax.rem(a + k, outer)
            res.append(remote(g, 1 + n_in + n_ac + k - 1, cell(held, lead, peer), r3[g].at[k - 1], (peer, b, x, c)))
        return res

    def start(copies):
        for copy in copies:
            copy.start()

    def arrived(copies):
        for copy in copies:
            copy.wait_recv()

    def up(v):
        return v.astype(f32)

    for g in range(count):
        start(swap(g))

    def body(core):
        second, third = (via_inner, via_across) if core == 0 else (via_across, via_inner)
        def at(lead, *index):
            return (ALL,) * lead + index
        for step in range(count + 3):
            g = step
            if g < count:
                arrived(swap(g))
                lead = leads[g]
                r0[g][...] = (up(grads[g][at(lead, ALL, ALL, ALL, c)]) + up(r0[g][...])).astype(bf16)
                start(second(g, core))
            g = step - 1
            if 0 <= g < count:
                arrived(second(g, core))
                lead = leads[g]
                if core == 0:
                    total = up(r0[g][at(lead, ALL, b)])
                    held = r1i[g]
                else:
                    total = up(r0[g][at(lead, ALL, ALL, x)])
                    held = r1a[g]
                for k in range(held.shape[0]):
                    total = total + up(held[k])
                held[0] = total.astype(bf16)
                start(third(g, core))
            g = step - 2
            if 0 <= g < count:
                arrived(third(g, core))
                lead = leads[g]
                if core == 0:
                    total = up(r1i[g][(0,) + at(lead, ALL, x)])
                    held = r2a[g]
                else:
                    total = up(r1a[g][(0,) + at(lead, ALL, b)])
                    held = r2i[g]
                for k in range(held.shape[0]):
                    total = total + up(held[k])
                held[0] = total.astype(bf16)
                start(last(g, core))
            g = step - 3
            if 0 <= g < count:
                arrived(last(g, core))
                lead = leads[g]
                held = (r2a if core == 0 else r2i)[g]
                total = up(held[(0,) + at(lead, a)])
                for k in range(outer - 1):
                    total = total + up(r3[g][k])
                outs[g][...] = total
        for g in range(count):
            for copy in swap(g) + second(g, core) + third(g, core) + last(g, core):
                copy.wait_send()

    @pl.when(c == 0)
    def _():
        body(0)

    @pl.when(c == 1)
    def _():
        body(1)


def scatter(dims, grads, leads):
    outer, inner, across = dims
    n = len(grads)
    outs, shapes = [], [[] for _ in range(6)]
    for g, lead in zip(grads, leads):
        head, tail = g.shape[:lead], g.shape[lead + 4 :]
        outs.append(jax.ShapeDtypeStruct(head + tail, f32))
        shapes[0].append(head + (outer, inner, across) + tail)
        shapes[1].append((inner - 1,) + head + (outer, across) + tail)
        shapes[2].append((across - 1,) + head + (outer, inner) + tail)
        shapes[3].append((across - 1,) + head + (outer,) + tail)
        shapes[4].append((inner - 1,) + head + (outer,) + tail)
        shapes[5].append((outer - 1,) + head + tail)
    slots = 1 + (inner - 1) + (across - 1) + (outer - 1)
    return pl.pallas_call(
        functools.partial(scatter_kernel, dims, leads),
        out_shape=outs,
        in_specs=[pl.BlockSpec(memory_space=pltpu.VMEM)] * n,
        out_specs=[pl.BlockSpec(memory_space=pltpu.VMEM)] * n,
        scratch_shapes=[pltpu.VMEM(s, bf16) for group in shapes for s in group]
        + [pltpu.SemaphoreType.DMA((n, slots)), pltpu.SemaphoreType.DMA((n, slots))],
        compiler_params=pltpu.CompilerParams(collective_id=1, has_side_effects=True, vmem_limit_bytes=48 * 2**20),
        name="scatter_grads",
    )(*grads)

HEADS, HEAD_DIM = 8, 64
EPS = 1e-5
MASKED = -1e9
TAME = 30.0
CHUNKS = 1
MIB = 2**20


def dot(left, right, left_dim, right_dim):
    return lax.dot_general(left, right, (((left_dim,), (right_dim,)), ((), ())), preferred_element_type=f32)


def full(shape):
    return pl.BlockSpec(shape, lambda i: (0,) * len(shape))


def image(shape):
    return pl.BlockSpec((1,) + shape, lambda i: (i,) + (0,) * len(shape))


def with_ones(rows):
    return jnp.concatenate([rows, jnp.ones((16, rows.shape[1]), bf16)], 0)


def with_delta(rows, delta):
    high = delta.astype(bf16).astype(f32)
    low = delta - high
    at = lax.broadcasted_iota(jnp.int32, (16, rows.shape[1]), 0)
    extra = jnp.where(at == 0, -high, jnp.where(at == 1, -low, 0.0))
    return jnp.concatenate([rows, extra.astype(bf16)], 0)


def self_forward(lens, x_ref, mem_ref, w_self, w_cross, bias_qkv, bias_kv,
                 qkv_ref, ckv_ref, near_ref, far_ref, inv_ref, mix_ref, wt_self, wt_cross):
    width = x_ref.shape[2]
    tags = x_ref.shape[1]
    half = tags // 2
    i = pl.program_id(0)

    @pl.when(i == 0)
    def _():
        wt_self[...] = w_self[...].T
        wt_cross[...] = w_cross[...].T

    ckv = dot(wt_cross[width:], mem_ref[0], 1, 1) + bias_kv[...]
    ckv_ref[0] = ckv.astype(bf16).reshape(ckv_ref.shape[1:])
    qkv = dot(wt_self[...], x_ref[0], 1, 1) + bias_qkv[...]
    q = qkv[:width].astype(bf16) * bf16(HEAD_DIM ** -0.5)
    qkv_ref[0, :HEADS] = q.reshape(HEADS, HEAD_DIM, tags)
    qkv_ref[0, HEADS:] = qkv[width:].astype(bf16).reshape(2 * HEADS, HEAD_DIM, tags)
    last = lens[i] - 1

    def head(h, _):
        qt, kt, vt = qkv_ref[0, h], qkv_ref[0, HEADS + h], with_ones(qkv_ref[0, 2 * HEADS + h])

        def part(keys, first, out):
            s = dot(kt[:, :keys], qt[:, first : first + half], 0, 0)
            key_at = lax.broadcasted_iota(jnp.int32, (keys, half), 0)
            query_at = lax.broadcasted_iota(jnp.int32, (1, half), 1) + first
            s = jnp.where(key_at <= jnp.minimum(query_at, last), s, MASKED)
            e = jnp.exp(s - jnp.max(s, 0, keepdims=True)).astype(bf16)
            out[0, h] = e
            mixed = dot(vt[:, :keys], e, 1, 0)
            inv = 1.0 / mixed[HEAD_DIM : HEAD_DIM + 1]
            inv_ref[0, pl.ds(h, 1), first : first + half] = inv
            mix_ref[0, h, :, first : first + half] = (mixed[:HEAD_DIM] * inv).astype(bf16)

        part(half, 0, near_ref)
        part(tags, half, far_ref)
        return 0

    lax.fori_loop(0, HEADS, head, 0)


def run_self_forward(lens, x, mem, w_self, w_cross, bias_qkv, bias_kv):
    images, tags, width = x.shape
    cells = mem.shape[1]
    half = tags // 2
    sds = jax.ShapeDtypeStruct
    return pl.pallas_call(
        self_forward,
        grid_spec=pltpu.PrefetchScalarGridSpec(
            num_scalar_prefetch=1,
            grid=(images,),
            in_specs=[pl.BlockSpec((1, tags, width), lambda i, n: (i, 0, 0)), pl.BlockSpec((1, cells, width), lambda i, n: (i, 0, 0))]
            + [pl.BlockSpec(v.shape, lambda i, n: (0, 0)) for v in (w_self, w_cross, bias_qkv, bias_kv)],
            out_specs=[
                pl.BlockSpec((1, 3 * HEADS, HEAD_DIM, tags), lambda i, n: (i, 0, 0, 0)),
                pl.BlockSpec((1, 2 * HEADS, HEAD_DIM, cells), lambda i, n: (i, 0, 0, 0)),
                pl.BlockSpec((1, HEADS, half, half), lambda i, n: (i, 0, 0, 0)),
                pl.BlockSpec((1, HEADS, tags, half), lambda i, n: (i, 0, 0, 0)),
                pl.BlockSpec((1, HEADS, tags), lambda i, n: (i, 0, 0)),
                pl.BlockSpec((1, HEADS, HEAD_DIM, tags), lambda i, n: (i, 0, 0, 0)),
                pl.BlockSpec((3 * width, width), lambda i, n: (0, 0)),
                pl.BlockSpec((3 * width, width), lambda i, n: (0, 0)),
            ],
        ),
        out_shape=[
            sds((images, 3 * HEADS, HEAD_DIM, tags), bf16),
            sds((images, 2 * HEADS, HEAD_DIM, cells), bf16),
            sds((images, HEADS, half, half), bf16),
            sds((images, HEADS, tags, half), bf16),
            sds((images, HEADS, tags), f32),
            sds((images, HEADS, HEAD_DIM, tags), bf16),
            sds((3 * width, width), bf16),
            sds((3 * width, width), bf16),
        ],
        compiler_params=pltpu.CompilerParams(vmem_limit_bytes=58 * MIB),
        name="self_forward",
    )(lens, x, mem, w_self, w_cross, bias_qkv, bias_kv)


def norm(resid):
    centred = resid - jnp.mean(resid, -1, keepdims=True)
    scale = lax.rsqrt(jnp.mean(centred * centred, -1, keepdims=True) + EPS)
    return centred * scale, scale


def norm_back(grad, normed, scale, gain):
    scaled = grad * gain
    mean_one = jnp.mean(scaled, -1, keepdims=True)
    mean_two = jnp.mean(scaled * normed, -1, keepdims=True)
    return scale * (scaled - mean_one - normed * mean_two)


def column_sums(rows):
    return jnp.sum(rows, 0, keepdims=True)


def lane_groups(rows):
    total = rows[:, :128]
    for k in range(1, rows.shape[1] // 128):
        total = total + rows[:, 128 * k : 128 * (k + 1)]
    return total


def cross_back(h, e, keys, values, queries, grad, mixed, inv):
    grad = grad.astype(f32)
    delta = jnp.sum(grad * mixed.astype(f32), 0, keepdims=True) * inv
    grad = (grad * inv).astype(bf16)
    dp = dot(with_ones(values), with_delta(grad, delta), 0, 0)
    ds = e * dp.astype(bf16)
    dv = dot(grad, e, 1, 1).astype(bf16)
    dk = dot(queries, ds, 1, 1).astype(bf16)
    dq = (dot(keys, ds, 1, 0) * HEAD_DIM ** -0.5).astype(bf16)
    return dq, dk, dv


def memory_lanes(rows):
    cells = rows.shape[1]
    body = cells // 128 * 128
    total = lane_groups(rows[:, :body])
    if body < cells:
        total = total + jnp.concatenate([rows[:, body:], jnp.zeros((rows.shape[0], 128 - cells + body), f32)], 1)
    return total


def middle(held_back, lens, x_ref, mem_ref, gout_ref, mix_one, ckv_ref, wt_cross, w_proj, w_in, w_out, vectors, b_in,
           out_ref, g_resid, g_mix, g_mem, gw_cross, gw_proj, gw_in, gw_out, g_vec, g_bin, *rest):
    if held_back:
        o_scale, o_e, o_q, o_inv, o_mix, o_gmix, o_one, o_two, o_cross, o_proj = rest[:10]
        gone = rest[-1]
        rest = rest[10:-1]
    middle_body(held_back and (o_scale, o_e, o_q, o_inv, o_mix, o_gmix, o_one, o_two, o_cross, o_proj, gone),
                lens, x_ref, mem_ref, gout_ref, mix_one, ckv_ref, wt_cross, w_proj, w_in, w_out, vectors, b_in,
                out_ref, g_resid, g_mix, g_mem, gw_cross, gw_proj, gw_in, gw_out, g_vec, g_bin, *rest)


def middle_body(held_back, lens, x_ref, mem_ref, gout_ref, mix_one, ckv_ref, wt_cross, w_proj, far_in, far_out, vectors, b_in,
           out_ref, g_resid, g_mix, g_mem, gw_cross, gw_proj, gw_in, gw_out, g_vec, g_bin,
           dkv_ref, cols,
           e_ref, q_ref, inv_ref, mix_two, gmix_two, dq_ref, acc_cross, acc_proj, acc_in, acc_out, acc_vec, acc_bin, acc_col,
           n_one, n_two, scale_two, two_low, act, g_inner, g_ff, g_cross, g_two, w_in, w_out, come):
    tags, width = x_ref.shape[1:]
    cells = mem_ref.shape[1]
    i = pl.program_id(0)
    count = pl.num_programs(0)
    arrivals = [pltpu.make_async_copy(src, dst, come.at[k]) for k, (src, dst) in enumerate(((far_in, w_in), (far_out, w_out)))]

    @pl.when(i == 0)
    def _():
        for ref in (acc_cross, acc_proj, acc_in, acc_out, acc_vec, acc_bin, acc_col):
            ref[...] = jnp.zeros_like(ref)
        cols[...] = vectors[...].T
        for copy in arrivals:
            copy.start()

    def vec(k):
        return vectors[k : k + 1, :]

    def add(k, value):
        acc_vec[k : k + 1, :] += value

    if held_back:
        scale_out, *places, gone = held_back
        sources = (e_ref, q_ref, inv_ref, mix_two, gmix_two, n_one, g_two, acc_cross, acc_proj.at[0])
        copies = [pltpu.make_async_copy(src, dst, gone.at[k]) for k, (src, dst) in enumerate(zip(sources, places))]

    def leave(*numbers):
        if held_back:
            @pl.when(i == count - 1)
            def _():
                for number in numbers:
                    copies[number].start()

    leave(7, 8)
    mix_one_t = mix_one[0].reshape(width, tags)
    resid = x_ref[0].astype(f32) + dot(mix_one_t, w_proj[0], 0, 0) + vec(2)
    normed, scale_one = norm(resid)
    n_one[...] = normed
    one = normed * vec(10) + vec(6)
    one_low = one.astype(bf16)
    cq = (dot(wt_cross[:width], one_low, 1, 1) + cols[:, 3:4]).astype(bf16) * bf16(HEAD_DIM ** -0.5)
    q_ref[...] = cq.reshape(q_ref.shape)
    leave(1, 5)

    keys, queries = ckv_ref[0, :HEADS], q_ref[...]
    keys, queries = keys * keys, queries * queries
    bound = jnp.max(jnp.sum(keys.astype(f32), 1)) * jnp.max(jnp.sum(queries.astype(f32), 1))
    tame = bound < TAME * TAME

    def forward(shifted, h, _):
        s = dot(ckv_ref[0, h], q_ref[h], 0, 0)
        if shifted:
            s = s - jnp.max(s, 0, keepdims=True)
        e = jnp.exp(s).astype(bf16)
        e_ref[h] = e
        mixed = dot(with_ones(ckv_ref[0, HEADS + h]), e, 1, 0)
        inv = 1.0 / mixed[HEAD_DIM : HEAD_DIM + 1]
        inv_ref[pl.ds(h, 1), :] = inv
        mix_two[h] = (mixed[:HEAD_DIM] * inv).astype(bf16)
        return 0

    @pl.when(tame)
    def _():
        lax.fori_loop(0, HEADS, functools.partial(forward, False), 0, unroll=8)

    @pl.when(jnp.logical_not(tame))
    def _():
        lax.fori_loop(0, HEADS, functools.partial(forward, True), 0)

    leave(0, 2, 3)
    @pl.when(i == 0)
    def _():
        for copy in arrivals:
            copy.wait()

    mix_two_t = mix_two[...].reshape(width, tags)
    root = 0.7978845608028654
    rows = tags // CHUNKS
    totals = {}

    def tally(k, value):
        totals[k] = totals[k] + column_sums(value) if k in totals else column_sums(value)

    for first in range(0, tags, rows):
        at = slice(first, first + rows)
        resid = n_one[at] * vec(10) + vec(6) + dot(mix_two_t[:, at], w_proj[1], 0, 0) + vec(5)
        normed, scale = norm(resid)
        n_two[at] = normed
        scale_two[at] = scale
        two = normed * vec(11) + vec(7)
        two_low[at] = two.astype(bf16)
        inner = dot(two_low[at], w_in[...], 1, 0) + b_in[...]
        square = inner * inner
        tanh = jnp.tanh(inner * (root + (root * 0.044715) * square))
        half_more = 0.5 + 0.5 * tanh
        act[at] = (inner * half_more).astype(bf16)
        slope = half_more + inner * (half_more * (1.0 - tanh)) * (root + (3 * 0.044715 * root) * square)
        resid = two + dot(act[at], w_out[...], 1, 0) + vec(9)
        three, scale = norm(resid)
        valid = lax.broadcasted_iota(jnp.int32, (rows, 1), 0) + first < lens[i]
        out_ref[0, at] = jnp.where(valid, three * vec(12) + vec(8), 0.0).astype(bf16)
        grad = jnp.where(valid, gout_ref[0, at].astype(f32), 0.0)
        tally(12, grad * three)
        tally(8, grad)
        g_three = norm_back(grad, three, scale, vec(12))
        g_ff[at] = g_three.astype(bf16)
        tally(9, g_three)
        back = dot(g_ff[at], w_out[...], 1, 1) * slope
        tally(-1, back)
        g_inner[at] = back.astype(bf16)
        back = g_three + dot(g_inner[at], w_in[...], 1, 1)
        tally(11, back * n_two[at])
        tally(7, back)
        back = norm_back(back, n_two[at], scale_two[at], vec(11))
        tally(5, back)
        g_two[at] = back
        g_cross[at] = back.astype(bf16)

    for k, value in totals.items():
        if k >= 0:
            add(k, value)
    acc_bin[...] += totals[-1]
    acc_out[...] += dot(act[...], g_ff[...], 0, 0)
    acc_in[...] += dot(two_low[...], g_inner[...], 0, 0)
    acc_proj[1] += dot(mix_two_t, g_cross[...], 1, 0)
    gmix_two[...] = dot(w_proj[1], g_cross[...], 1, 1).astype(bf16).reshape(gmix_two.shape)

    def rest_of_image():
        def backward(h, _):
            dq_ref[h], dkv_ref[h], dkv_ref[HEADS + h] = cross_back(
                h, e_ref[h], ckv_ref[0, h], ckv_ref[0, HEADS + h], q_ref[h], gmix_two[h], mix_two[h], inv_ref[pl.ds(h, 1), :])
            return 0

        lax.fori_loop(0, HEADS, backward, 0, unroll=4)
        dq = dq_ref[...].reshape(width, tags)
        dkv = dkv_ref[...].reshape(2 * width, cells)
        acc_col[0] += lane_groups(dq.astype(f32))
        acc_col[1] += memory_lanes(dkv[width:].astype(f32))
        acc_cross[:width] += dot(dq, one_low, 1, 0)
        acc_cross[width:] += dot(dkv, mem_ref[0], 1, 0)
        g_mem[0] = dot(dkv, wt_cross[width:], 0, 0)
        g_one = g_two[...] + dot(dq, wt_cross[:width], 0, 0)
        add(10, column_sums(g_one * n_one[...]))
        add(6, column_sums(g_one))
        g_one = norm_back(g_one, n_one[...], scale_one, vec(10))
        add(2, column_sums(g_one))
        g_resid[0] = g_one
        g_low = g_one.astype(bf16)
        acc_proj[0] += dot(mix_one_t, g_low, 1, 0)
        g_mix[0] = dot(w_proj[0], g_low, 1, 1).astype(bf16).reshape(g_mix.shape[1:])

    if held_back:
        pl.when(i < count - 1)(rest_of_image)

        @pl.when(i == count - 1)
        def _():
            scale_out[...] = scale_one

        leave(4, 6)
    else:
        rest_of_image()

    @pl.when(i == count - 1)
    def _():
        if held_back:
            gw_proj[...] = acc_proj[1].astype(bf16)
        else:
            gw_cross[...] = acc_cross[...].astype(bf16).T
            gw_proj[...] = acc_proj[...].astype(bf16)
        gw_in[...] = acc_in[...].astype(bf16)
        gw_out[...] = acc_out[...].astype(bf16)
        add(3, column_sums(acc_col[0].T))
        add(4, column_sums(acc_col[1].T))
        g_vec[...] = acc_vec[...]
        g_bin[...] = acc_bin[...]
        if held_back:
            for copy in copies:
                copy.wait()


def run_middle(lens, x, mem, gout, mix_one, ckv, wt_cross, w_proj, w_in, w_out, vectors, b_in, held_back=False):
    images, tags, width = x.shape
    cells = mem.shape[1]
    hidden = w_in.shape[1]
    sds = jax.ShapeDtypeStruct

    def per(*shape):
        return pl.BlockSpec((1,) + shape, lambda i, n: (i,) + (0,) * len(shape))

    def one(*shape):
        return pl.BlockSpec(shape, lambda i, n: (0,) * len(shape), pipeline_mode=pl.Buffered(1))

    def out(*shape):
        return pl.BlockSpec(shape, lambda i, n: (0,) * len(shape))

    def early(*shape):
        return pl.BlockSpec((1,) + shape, lambda i, n: (jnp.minimum(i, images - 2),) + (0,) * len(shape)) if held_back else per(*shape)

    done = images - 1 if held_back else images
    out_specs = [
        per(tags, width), early(tags, width), early(HEADS, HEAD_DIM, tags), early(cells, width),
        out(width, 3 * width), out(2, width, width), out(width, hidden), out(hidden, width), out(16, width), out(1, hidden),
    ]
    out_shape = [
        sds((images, tags, width), bf16), sds((done, tags, width), f32), sds((done, HEADS, HEAD_DIM, tags), bf16),
        sds((images, cells, width), f32),
        sds((width, 3 * width), bf16), sds((2, width, width), bf16), sds((width, hidden), bf16), sds((hidden, width), bf16),
        sds((16, width), f32), sds((1, hidden), f32),
    ]
    scratch = [
        pltpu.VMEM((2 * HEADS, HEAD_DIM, cells), bf16),
        pltpu.VMEM((width, 16), f32),
        pltpu.VMEM((HEADS, cells, tags), bf16),
        pltpu.VMEM((HEADS, HEAD_DIM, tags), bf16),
        pltpu.VMEM((HEADS, tags), f32),
        pltpu.VMEM((HEADS, HEAD_DIM, tags), bf16),
        pltpu.VMEM((HEADS, HEAD_DIM, tags), bf16),
        pltpu.VMEM((HEADS, HEAD_DIM, tags), bf16),
        pltpu.VMEM((3 * width, width), f32),
        pltpu.VMEM((2, width, width), f32),
        pltpu.VMEM((width, hidden), f32),
        pltpu.VMEM((hidden, width), f32),
        pltpu.VMEM((16, width), f32),
        pltpu.VMEM((1, hidden), f32),
        pltpu.VMEM((2, width, 128), f32),
        pltpu.VMEM((tags, width), f32),
        pltpu.VMEM((tags, width), f32),
        pltpu.VMEM((tags, 1), f32),
        pltpu.VMEM((tags, width), bf16),
        pltpu.VMEM((tags, hidden), bf16),
        pltpu.VMEM((tags, hidden), bf16),
        pltpu.VMEM((tags, width), bf16),
        pltpu.VMEM((tags, width), bf16),
        pltpu.VMEM((tags, width), f32),
        pltpu.VMEM((width, hidden), bf16),
        pltpu.VMEM((hidden, width), bf16),
        pltpu.SemaphoreType.DMA((2,)),
    ]
    if held_back:
        out_specs[4], out_shape[4] = out(8, 128), sds((8, 128), bf16)
        out_specs[5], out_shape[5] = out(width, width), sds((width, width), bf16)
        kept = [((HEADS, cells, tags), bf16), ((HEADS, HEAD_DIM, tags), bf16), ((HEADS, tags), f32), ((HEADS, HEAD_DIM, tags), bf16),
                ((HEADS, HEAD_DIM, tags), bf16), ((tags, width), f32), ((tags, width), f32), ((3 * width, width), f32), ((width, width), f32)]
        out_specs += [out(tags, 1)] + [pl.BlockSpec(memory_space=pl.ANY)] * len(kept)
        out_shape += [sds((tags, 1), f32)] + [sds(*k) for k in kept]
        scratch.append(pltpu.SemaphoreType.DMA((len(kept),)))
    return pl.pallas_call(
        functools.partial(middle, held_back),
        grid_spec=pltpu.PrefetchScalarGridSpec(
            num_scalar_prefetch=1,
            grid=(images,),
            in_specs=[
                per(tags, width), per(cells, width), per(tags, width), per(HEADS, HEAD_DIM, tags), per(2 * HEADS, HEAD_DIM, cells),
                one(3 * width, width), one(2, width, width), pl.BlockSpec(memory_space=pl.ANY), pl.BlockSpec(memory_space=pl.ANY), one(16, width), one(1, hidden),
            ],
            out_specs=out_specs,
            scratch_shapes=scratch,
        ),
        out_shape=out_shape,
        compiler_params=pltpu.CompilerParams(vmem_limit_bytes=62 * MIB),
        name="middle",
    )(lens, x, mem, gout, mix_one, ckv, wt_cross, w_proj, w_in, w_out, vectors, b_in)


def self_backward(x_ref, qkv_ref, near_ref, far_ref, inv_ref, mix_ref, gmix_ref, g_resid, wt_self,
                  g_tags, gw_self, g_col, d_ref, acc, acc_col):
    tags, width = x_ref.shape[1:]
    half = tags // 2
    i = pl.program_id(0)

    @pl.when(i == 0)
    def _():
        acc[...] = jnp.zeros_like(acc)
        acc_col[...] = jnp.zeros_like(acc_col)

    def head(h, _):
        grad = gmix_ref[0, h].astype(f32)
        inv = inv_ref[0, pl.ds(h, 1), :]
        delta = jnp.sum(grad * mix_ref[0, h].astype(f32), 0, keepdims=True) * inv
        grad = (grad * inv).astype(bf16)
        ext = with_delta(grad, delta)
        qt, kt, vt = qkv_ref[0, h], qkv_ref[0, HEADS + h], with_ones(qkv_ref[0, 2 * HEADS + h])
        near, far = near_ref[0, h], far_ref[0, h]
        ds_near = near * dot(vt[:, :half], ext[:, :half], 0, 0).astype(bf16)
        ds_far = far * dot(vt, ext[:, half:], 0, 0).astype(bf16)
        dv = dot(grad[:, half:], far, 1, 1)
        dk = dot(qt[:, half:], ds_far, 1, 1)
        d_ref[2 * HEADS + h, :, half:] = dv[:, half:].astype(bf16)
        d_ref[2 * HEADS + h, :, :half] = (dv[:, :half] + dot(grad[:, :half], near, 1, 1)).astype(bf16)
        d_ref[HEADS + h, :, half:] = dk[:, half:].astype(bf16)
        d_ref[HEADS + h, :, :half] = (dk[:, :half] + dot(qt[:, :half], ds_near, 1, 1)).astype(bf16)
        d_ref[h, :, :half] = (dot(kt[:, :half], ds_near, 1, 0) * HEAD_DIM ** -0.5).astype(bf16)
        d_ref[h, :, half:] = (dot(kt, ds_far, 1, 0) * HEAD_DIM ** -0.5).astype(bf16)
        return 0

    lax.fori_loop(0, HEADS, head, 0)
    d = d_ref[...].reshape(3 * width, tags)
    acc_col[0] += lane_groups(d[:width].astype(f32))
    acc_col[1] += lane_groups(d[2 * width :].astype(f32))
    acc[...] += dot(d, x_ref[0], 1, 0)
    g_tags[0] = g_resid[0] + dot(d, wt_self[...], 0, 0)

    @pl.when(i == pl.num_programs(0) - 1)
    def _():
        gw_self[...] = acc[...].astype(bf16).T
        g_col[0:1] = column_sums(acc_col[0].T)
        g_col[1:2] = column_sums(acc_col[1].T)


def run_self_backward(x, qkv, near, far, inv, mix, gmix, g_resid, wt_self):
    images, tags, width = x.shape
    half = tags // 2
    sds = jax.ShapeDtypeStruct

    def per(*shape):
        return pl.BlockSpec((1,) + shape, lambda i: (i,) + (0,) * len(shape))

    def one(*shape):
        return pl.BlockSpec(shape, lambda i: (0,) * len(shape))

    return pl.pallas_call(
        self_backward,
        grid=(images,),
        in_specs=[per(tags, width), per(3 * HEADS, HEAD_DIM, tags), per(HEADS, half, half), per(HEADS, tags, half), per(HEADS, tags),
                  per(HEADS, HEAD_DIM, tags), per(HEADS, HEAD_DIM, tags), per(tags, width),
                  one(3 * width, width)],
        out_specs=[per(tags, width), one(width, 3 * width), one(8, width)],
        out_shape=[sds((images, tags, width), f32), sds((width, 3 * width), bf16), sds((8, width), f32)],
        scratch_shapes=[pltpu.VMEM((3 * HEADS, HEAD_DIM, tags), bf16), pltpu.VMEM((3 * width, width), f32), pltpu.VMEM((2, width, 128), f32)],
        compiler_params=pltpu.CompilerParams(vmem_limit_bytes=60 * MIB),
        name="self_backward",
    )(x, qkv, near, far, inv, mix, gmix, g_resid, wt_self)


def layer(lens, x, mem, gout, w_self, w_cross, w_proj, w_in, w_out, vectors, b_in):
    width = x.shape[2]
    zero = jnp.zeros((width,), f32)
    bias_qkv = jnp.concatenate([vectors[0], zero, vectors[1]])[:, None]
    bias_kv = jnp.concatenate([zero, vectors[4]])[:, None]
    qkv, ckv, near, far, inv, mix, wt_self, wt_cross = run_self_forward(lens, x, mem, w_self, w_cross, bias_qkv, bias_kv)
    out, g_resid, gmix, g_mem, gw_cross, gw_proj, gw_in, gw_out, g_vec, g_bin = run_middle(
        lens, x, mem, gout, mix, ckv, wt_cross, w_proj, w_in, w_out, vectors, b_in)
    g_tags, gw_self, g_col = run_self_backward(x, qkv, near, far, inv, mix, gmix, g_resid, wt_self)
    g_vec = g_vec.at[0:2].set(g_col[0:2])
    return out, g_tags, g_mem, gw_self, gw_cross, gw_proj, gw_in, gw_out, g_vec, g_bin


ALL = slice(None)


SMALL, SELF, PROJ, CROSS, IN, OUT = range(6)
PLAN = (
    ((SMALL, 0), (SELF, 0), (PROJ, 0), (CROSS, 0), (IN, 0), (OUT, 0),
     (SMALL, 1), (SELF, 1), (SMALL, 2), (PROJ, 1), (SELF, 2), (SMALL, 3), (CROSS, 1), (PROJ, 2), (IN, 1), (SELF, 3), (CROSS, 2), (OUT, 1),
     (PROJ, 3), (SMALL, 4), (SELF, 4)),
    ((IN, 2),),
    ((OUT, 2),),
    ((CROSS, 3),),
    ((IN, 3),),
    ((OUT, 3),),
    (),
    ((CROSS, 4),),
    ((PROJ, 4), (IN, 4), (OUT, 4)),
)
MEANTIME = {2: (0, 6), 3: (1, 2), 4: (2, 0), 5: (2, 6)}


class Gathering:
    def __init__(self, dims, me, shard, held, lead, sems):
        self.dims, self.me, self.shard, self.held, self.lead = dims, me, shard, held, lead
        self.local, self.send, self.recv = sems

    def cell(self, *index):
        return self.held.at[(ALL,) * self.lead + index]

    def remote(self, slot, src, dst, peer):
        return pltpu.make_async_remote_copy(
            src_ref=src, dst_ref=dst, send_sem=self.send.at[slot], recv_sem=self.recv.at[slot],
            device_id=device(self.dims, *peer), device_id_type=MESH)

    def keep(self):
        return pltpu.make_async_copy(self.shard, self.cell(*self.me), self.local)

    def first(self):
        a, b, x, c = self.me
        outer = self.dims[0]
        return [self.remote(k - 1, self.shard, self.cell(a, b, x, c), (lax.rem(a + k, outer), b, x, c)) for k in range(1, outer)]

    def along_inner(self, core):
        a, b, x, c = self.me
        outer, inner, _ = self.dims
        piece = self.cell(ALL, b, ALL if core == 0 else x, c)
        return [self.remote(outer - 2 + k, piece, piece, (a, lax.rem(b + k, inner), x, c)) for k in range(1, inner)]

    def along_across(self, core):
        a, b, x, c = self.me
        outer, inner, across = self.dims
        piece = self.cell(ALL, b if core == 0 else ALL, x, c)
        return [self.remote(outer + inner - 3 + k, piece, piece, (a, b, lax.rem(x + k, across), c)) for k in range(1, across)]

    def second(self, core):
        return self.along_across(core) if core == 0 else self.along_inner(core)

    def third(self, core):
        return self.along_inner(core) if core == 0 else self.along_across(core)

    def handed(self, core, holder):
        a, b, x, c = self.me
        outer, inner, across = self.dims
        base = outer + inner + across - 3

        def piece(slot, row, column):
            ref = self.cell(ALL, row, column, holder)
            return self.remote(base + slot, ref, ref, (a, b, x, 1 - c))

        own = [piece(0, b, x)]
        by_inner = [piece(k, lax.rem(b + k, inner), ALL if core == 0 else x) for k in range(1, inner)]
        by_across = [piece(inner - 1 + k, b if core == 0 else ALL, lax.rem(x + k, across)) for k in range(1, across)]
        return (own, by_across, by_inner) if core == 0 else (own, by_inner, by_across)

    def begin(self):
        self.keep().start()
        for copy in self.first():
            copy.start()

    def each_core(self, act):
        for core in (0, 1):
            pl.when(self.me[3] == core)(functools.partial(act, core))

    def advance(self, stage):
        def act(core):
            if stage == 1:
                self.keep().wait()
            for copy in (self.first(), self.second(core), self.third(core))[stage - 1]:
                copy.wait_recv()
            following = (self.second(core), self.third(core), [])[stage - 1]
            for copy in following + self.handed(core, self.me[3])[stage - 1]:
                copy.start()
        self.each_core(act)

    def finish(self):
        def act(core):
            for group in self.handed(1 - core, 1 - self.me[3]):
                for copy in group:
                    copy.wait_recv()
        self.each_core(act)

    def drain(self):
        def act(core):
            for copy in self.first() + self.second(core) + self.third(core) + sum(self.handed(core, self.me[3]), []):
                copy.wait_send()
        self.each_core(act)


def gather_slots(dims):
    outer, inner, across = dims
    return outer + 2 * (inner + across) - 4


def spread(held, row_lanes, width, rows):
    devices = held.shape[0] // 16
    lane = lax.broadcasted_iota(jnp.int32, (128, width), 0)
    at = lax.broadcasted_iota(jnp.int32, (128, width), 1)
    pick = jnp.where((lax.rem(at, row_lanes) == lane), 1.0, 0.0).astype(bf16)
    wide = dot(held, pick, 1, 0)
    owner = lax.broadcasted_iota(jnp.int32, (devices * 16, width), 0) // 16
    at = lax.broadcasted_iota(jnp.int32, (devices * 16, width), 1)
    wide = jnp.where(at // row_lanes == owner, wide, 0.0)
    return jnp.sum(wide.reshape(devices, 16, width), 0)


def opening(dims, lens, x_ref, mem_ref, b_ref, g_ref, h_ref, s_cross, s_self, s_proj, s_in, s_out,
            qkv_ref, ckv_ref, low_ref, high_ref, inv_ref, mix_ref, out_self, out_cross, vec_ref, bin_ref, o_proj, o_in, o_out,
            small, small_low, h_small, h_self, h_cross, wt_self, wt_cross, cols, low_a, high_a, low_b, high_b, tile, beyond, gone, local, send, recv):
    width = x_ref.shape[2]
    tags = x_ref.shape[1]
    half = tags // 2
    step = pl.program_id(0)
    images = pl.num_programs(0) // 2
    me = place(dims)
    pairs = ((small_low, h_small, 0), (s_self, h_self, 0), (s_proj, o_proj, 1), (s_cross, h_cross, 0), (s_in, o_in, 0), (s_out, o_out, 0))
    gs = [Gathering(dims, me, shard, held, lead, (local.at[k], send.at[k], recv.at[k])) for k, (shard, held, lead) in enumerate(pairs)]
    keep_self = pltpu.make_async_copy(wt_self, out_self, gone.at[0])
    keep_cross = pltpu.make_async_copy(wt_cross, out_cross, gone.at[1])

    def play(slot):
        for item, stage in PLAN[slot]:
            item = gs[item]
            item.begin() if stage == 0 else item.finish() if stage == 4 else item.advance(stage)

    def slot_at(number, slot):
        @pl.when(step == number)
        def _():
            play(slot)

    @pl.when(step == 0)
    def _():
        hails = hail(dims, me)
        small[...] = jnp.zeros_like(small)
        small[0:10, : b_ref.shape[1]] = b_ref[...].astype(f32)
        small[10:13, : g_ref.shape[1]] = g_ref[...].astype(f32)
        small[13:14, : h_ref.shape[1]] = h_ref[...].astype(f32)
        small_low[...] = small[...].astype(bf16)
        greet(dims, me, hails)
        play(0)
        vectors = spread(h_small[...].reshape(-1, 128), b_ref.shape[1], width, 16)
        vec_ref[...] = vectors
        bin_ref[...] = spread(h_small[...].reshape(-1, 128), h_ref.shape[1], bin_ref.shape[1], 16)[13:14]
        cols[...] = vectors.T
        wt_self[...] = h_self[...].reshape(width, 3 * width).T
        keep_self.start()

    @pl.when(step < images)
    def _():
        qkv = dot(wt_self[...], x_ref[0], 1, 1)
        qkv_ref[0, :HEADS] = ((qkv[:width] + cols[:, 0:1]).astype(bf16) * bf16(HEAD_DIM ** -0.5)).reshape(HEADS, HEAD_DIM, tags)
        qkv_ref[0, HEADS : 2 * HEADS] = qkv[width : 2 * width].astype(bf16).reshape(HEADS, HEAD_DIM, tags)
        qkv_ref[0, 2 * HEADS :] = (qkv[2 * width :] + cols[:, 1:2]).astype(bf16).reshape(HEADS, HEAD_DIM, tags)

    @pl.when(step < images)
    def _():
        key_at, query_at = lax.broadcasted_iota(jnp.int32, (half, half), 0), lax.broadcasted_iota(jnp.int32, (half, half), 1)
        tile[...] = jnp.where(key_at <= query_at, 0.0, MASKED)
        row, key_at = lax.broadcasted_iota(jnp.int32, beyond.shape, 0), lax.broadcasted_iota(jnp.int32, beyond.shape, 1)
        hidden = jnp.logical_and(row == 0, key_at >= lens[jnp.minimum(step, images - 1)])
        beyond[...] = jnp.where(hidden, MASKED, 0.0).astype(bf16)

    def scores(h, low, high):
        qt, kt = with_ones(qkv_ref[0, h]), jnp.concatenate([qkv_ref[0, HEADS + h], beyond[...]], 0)
        s = dot(kt[:, :half], qt, 0, 0)
        left, right = s[:, :half] + tile[...], s[:, half:]
        under = dot(kt[:, half:], qt[:, half:], 0, 0) + tile[...]
        low[:, :half] = left
        low[:, half:] = right
        high[...] = under
        return jnp.max(left, 0, keepdims=True), jnp.maximum(jnp.max(right, 0, keepdims=True), jnp.max(under, 0, keepdims=True))

    def mix(h, low, high, tops):
        vt = with_ones(qkv_ref[0, 2 * HEADS + h])
        e_low = jnp.concatenate([jnp.exp(low[:, :half] - tops[0]).astype(bf16), jnp.exp(low[:, half:] - tops[1]).astype(bf16)], 1)
        e_high = jnp.exp(high[...] - tops[1]).astype(bf16)
        low_ref[0, h] = e_low
        high_ref[0, h] = e_high
        mixed = dot(vt[:, :half], e_low, 1, 0)
        mixed = jnp.concatenate([mixed[:, :half], mixed[:, half:] + dot(vt[:, half:], e_high, 1, 0)], 1)
        inv = 1.0 / mixed[HEAD_DIM : HEAD_DIM + 1]
        inv_ref[0, h : h + 1] = inv
        mix_ref[0, h] = (mixed[:HEAD_DIM] * inv).astype(bf16)

    def pair(h, tops):
        following = scores(h + 1, low_b, high_b)
        mix(h, low_a, high_a, tops)
        if h + 2 < HEADS:
            tops = scores(h + 2, low_a, high_a)
        mix(h + 1, low_b, high_b, following)
        return tops

    slot_at(0, 1)

    @pl.when(step < images)
    def _():
        tops = scores(0, low_a, high_a)
        for h in range(0, HEADS, 2):
            for slot, (image, number) in MEANTIME.items():
                if number == h:
                    pl.when(step == image)(functools.partial(play, slot))
            tops = pair(h, tops)

    @pl.when(step == images)
    def _():
        play(7)
        wt_cross[...] = h_cross[...].reshape(width, 3 * width).T
        keep_cross.start()

    @pl.when(step >= images)
    def _():
        kv = dot(wt_cross[width:], mem_ref[0], 1, 1)
        ckv_ref[0, :HEADS] = kv[:width].astype(bf16).reshape(HEADS, HEAD_DIM, -1)
        ckv_ref[0, HEADS:] = (kv[width:] + cols[:, 4:5]).astype(bf16).reshape(HEADS, HEAD_DIM, -1)

    @pl.when(step == 2 * images - 1)
    def _():
        play(8)
        for g in gs:
            g.drain()
        keep_self.wait()
        keep_cross.wait()


def run_opening(dims, lens, x, mem, biases, gains, b_in, shards):
    images, tags, width = x.shape
    cells = mem.shape[1]
    half = tags // 2
    hidden = b_in.shape[1] * dims[0] * dims[1] * dims[2] * 2
    sds = jax.ShapeDtypeStruct

    def early(*shape):
        return pl.BlockSpec((1,) + shape, lambda i: (jnp.minimum(i, images - 1),) + (0,) * len(shape))

    def late(*shape):
        return pl.BlockSpec((1,) + shape, lambda i: (jnp.maximum(i - images, 0),) + (0,) * len(shape))

    def one(*shape):
        return pl.BlockSpec(shape, lambda i: (0,) * len(shape))

    def held(shard, lead):
        return shard.shape[:lead] + dims + (2,) + shard.shape[lead:]

    s_cross, s_self, s_proj, s_in, s_out = shards
    rows = s_cross.shape[0]
    cell = dims + (2, rows)
    anywhere = pl.BlockSpec(memory_space=pl.ANY)
    n = len(shards) + 1
    slots = gather_slots(dims)
    return pl.pallas_call(
        functools.partial(opening, dims),
        grid=(2 * images,),
        in_specs=[pl.BlockSpec(memory_space=pltpu.SMEM), early(tags, width), late(cells, width), one(*biases.shape), one(*gains.shape), one(*b_in.shape)]
        + [anywhere] * len(shards),
        out_specs=[
            early(3 * HEADS, HEAD_DIM, tags), late(2 * HEADS, HEAD_DIM, cells), early(HEADS, half, tags), early(HEADS, half, half),
            early(HEADS, tags), early(HEADS, HEAD_DIM, tags), anywhere, anywhere, one(16, width), one(1, hidden),
            anywhere, anywhere, anywhere,
        ],
        out_shape=[
            sds((images, 3 * HEADS, HEAD_DIM, tags), bf16),
            sds((images, 2 * HEADS, HEAD_DIM, cells), bf16),
            sds((images, HEADS, half, tags), bf16),
            sds((images, HEADS, half, half), bf16),
            sds((images, HEADS, tags), f32),
            sds((images, HEADS, HEAD_DIM, tags), bf16),
            sds((3 * width, width), bf16),
            sds((3 * width, width), bf16),
            sds((16, width), f32),
            sds((1, hidden), f32),
            sds(held(s_proj, 1), bf16),
            sds(held(s_in, 0), bf16),
            sds(held(s_out, 0), bf16),
        ],
        scratch_shapes=[
            pltpu.VMEM((16, 128), f32), pltpu.VMEM((16, 128), bf16), pltpu.VMEM(dims + (2, 16, 128), bf16),
            pltpu.VMEM(cell + (3 * width,), bf16), pltpu.VMEM(cell + (3 * width,), bf16),
            pltpu.VMEM((3 * width, width), bf16), pltpu.VMEM((3 * width, width), bf16),
            pltpu.VMEM((width, 16), f32), pltpu.VMEM((half, tags), f32), pltpu.VMEM((half, half), f32), pltpu.VMEM((half, tags), f32), pltpu.VMEM((half, half), f32),
            pltpu.VMEM((half, half), f32), pltpu.VMEM((16, tags), bf16),
            pltpu.SemaphoreType.DMA((2,)),
            pltpu.SemaphoreType.DMA((n,)), pltpu.SemaphoreType.DMA((n, slots)), pltpu.SemaphoreType.DMA((n, slots)),
        ],
        compiler_params=pltpu.CompilerParams(collective_id=0, has_side_effects=True, vmem_limit_bytes=58 * MIB),
        name="opening",
    )(lens, x, mem, biases, gains, b_in, *shards)


class Scattering:
    def __init__(self, dims, me, grads, short, out, lead, held, sems):
        self.dims, self.me, self.grads, self.short, self.out, self.lead = dims, me, grads, short, out, lead
        self.pair, self.by_inner, self.by_across, self.by_outer, self.last = held
        self.send, self.recv = sems

    def at(self, *index):
        return (ALL,) * self.lead + index

    def remote(self, slot, src, dst, peer):
        return pltpu.make_async_remote_copy(
            src_ref=src, dst_ref=dst, send_sem=self.send.at[slot], recv_sem=self.recv.at[slot],
            device_id=device(self.dims, *peer), device_id_type=MESH)

    def swap(self):
        a, b, x, c = self.me
        return [self.remote(0, self.grads.at[self.at(ALL, ALL, ALL, 1 - c)], self.pair, (a, b, x, 1 - c))]

    def along_inner(self, core):
        a, b, x, c = self.me
        inner = self.dims[1]
        res = []
        for k in range(1, inner):
            peer = lax.rem(b + k, inner)
            src = self.pair.at[self.at(ALL, peer)] if core == 0 else self.by_across.at[0].at[self.at(ALL, peer)]
            dst = self.by_inner.at[k - 1] if core == 0 else self.by_outer.at[k - 1]
            res.append(self.remote(k, src, dst, (a, peer, x, c)))
        return res

    def along_across(self, core):
        a, b, x, c = self.me
        _, inner, across = self.dims
        res = []
        for k in range(1, across):
            peer = lax.rem(x + k, across)
            src = self.pair.at[self.at(ALL, ALL, peer)] if core == 1 else self.by_inner.at[0].at[self.at(ALL, peer)]
            dst = self.by_across.at[k - 1] if core == 1 else self.by_outer.at[k - 1]
            res.append(self.remote(inner - 1 + k, src, dst, (a, b, peer, c)))
        return res

    def second(self, core):
        return self.along_inner(core) if core == 0 else self.along_across(core)

    def third(self, core):
        return self.along_across(core) if core == 0 else self.along_inner(core)

    def along_outer(self):
        a, b, x, c = self.me
        outer, inner, across = self.dims
        return [
            self.remote(inner + across - 2 + k, self.by_outer.at[0].at[self.at(lax.rem(a + k, outer))], self.last.at[k - 1],
                        (lax.rem(a + k, outer), b, x, c))
            for k in range(1, outer)
        ]

    def over_plane(self):
        a, b, x, c = self.me
        _, inner, across = self.dims
        res = []
        for k in range(1, inner * across):
            row, column = lax.rem(b + k // across, inner), lax.rem(x + k % across, across)
            res.append(self.remote(k, self.pair.at[:, row, column], self.by_inner.at[k - 1], (a, row, column, c)))
        return res

    def from_plane(self):
        a, b, x, c = self.me
        outer, inner, across = self.dims
        return [
            self.remote(inner * across - 1 + k, self.by_outer.at[0, lax.rem(a + k, outer)], self.last.at[k - 1], (lax.rem(a + k, outer), b, x, c))
            for k in range(1, outer)
        ]

    def begin(self):
        for copy in self.swap():
            copy.start()

    def advance_short(self, stage):
        a, b, x, c = self.me
        outer, inner, across = self.dims

        def up(value):
            return value.astype(f32)

        for copy in (self.swap(), self.over_plane(), self.from_plane())[stage - 1]:
            copy.wait_recv()
        if stage == 1:
            self.pair[...] = (up(self.grads[:, :, :, c]) + up(self.pair[...])).astype(bf16)
            following = self.over_plane()
        elif stage == 2:
            total = up(self.pair[:, b, x])
            for k in range(inner * across - 1):
                total = total + up(self.by_inner[k])
            self.by_outer[0] = total.astype(bf16)
            following = self.from_plane()
        else:
            total = up(self.by_outer[0, a])
            for k in range(outer - 1):
                total = total + up(self.last[k])
            self.out[...] = total
            following = []
        for copy in following:
            copy.start()

    def advance(self, stage):
        if self.short:
            return self.advance_short(stage)
        a, b, x, c = self.me
        _, inner, across = self.dims

        def up(value):
            return value.astype(f32)

        def act(core):
            for copy in (self.swap(), self.second(core), self.third(core), self.along_outer())[stage - 1]:
                copy.wait_recv()
            if stage == 1:
                def add(k, _):
                    self.pair[k] = (up(self.grads[k, :, :, c]) + up(self.pair[k])).astype(bf16)
                    return 0
                following = self.second(core)
            elif stage == 2:
                held = self.by_inner if core == 0 else self.by_across

                def add(k, _):
                    total = up(self.pair[k, b] if core == 0 else self.pair[k, :, x])
                    for j in range((inner if core == 0 else across) - 1):
                        total = total + up(held[j, k])
                    held[0, k] = total.astype(bf16)
                    return 0
                following = self.third(core)
            elif stage == 3:
                held = self.by_inner if core == 0 else self.by_across

                def add(k, _):
                    total = up(held[0, k, x if core == 0 else b])
                    for j in range((across if core == 0 else inner) - 1):
                        total = total + up(self.by_outer[j, k])
                    self.by_outer[0, k] = total.astype(bf16)
                    return 0
                following = self.along_outer()
            else:
                total = up(self.by_outer[(0,) + self.at(a)])
                for k in range(self.dims[0] - 1):
                    total = total + up(self.last[k])
                self.out[...] = total
                following = []
            if stage < 4:
                lax.fori_loop(0, self.dims[0], add, 0)
            for copy in following:
                copy.start()

        for core in (0, 1):
            pl.when(c == core)(functools.partial(act, core))

    def drain(self):
        def act(core):
            for copy in self.swap() + self.second(core) + self.third(core) + self.along_outer():
                copy.wait_send()

        if self.short:
            for copy in self.swap() + self.over_plane() + self.from_plane():
                copy.wait_send()
            return
        for core in (0, 1):
            pl.when(self.me[3] == core)(functools.partial(act, core))


def scatter_slots(dims):
    return max(dims[0] + dims[1] + dims[2] - 2, dims[0] + dims[1] * dims[2] - 1)


def scatter_space(dims, lead, tail, short=False):
    outer, inner, across = dims
    if short:
        return [(outer, inner, across) + tail, (inner * across - 1, outer) + tail, (1,) + tail, (1, outer) + tail, (outer - 1,) + tail]
    return [
        lead + (outer, inner, across) + tail,
        (inner - 1,) + lead + (outer, across) + tail,
        (across - 1,) + lead + (outer, inner) + tail,
        (max(inner, across) - 1,) + lead + (outer,) + tail,
        (outer - 1,) + lead + tail,
    ]


def collect(rows, row_lanes, devices):
    width = rows.shape[1]
    many = jnp.broadcast_to(rows[None], (devices, 16, width)).reshape(devices * 16, width)
    owner = lax.broadcasted_iota(jnp.int32, many.shape, 0) // 16
    at = lax.broadcasted_iota(jnp.int32, many.shape, 1)
    many = jnp.where(at // row_lanes == owner, many, 0.0).astype(bf16)
    lane = lax.broadcasted_iota(jnp.int32, (128, width), 0)
    at = lax.broadcasted_iota(jnp.int32, (128, width), 1)
    pick = jnp.where(lax.rem(at, row_lanes) == lane, 1.0, 0.0).astype(bf16)
    return dot(many, pick, 1, 1)


G_OUT, G_IN, G_ONE, G_CROSS, G_ZERO, G_HALF, G_REST, G_SMALL = range(8)
SHORT = (G_REST, G_SMALL)
FEW = 2
EVENTS = {
    (0, 0): ((G_OUT, 0), (G_IN, 0), (G_ONE, 0)),
    (0, 1): ((G_OUT, 1),),
    (0, 2): ((G_IN, 1), (G_ONE, 1)),
    (0, 6): ((G_CROSS, 0),),
    (0, 7): ((G_ZERO, 0), (G_OUT, 2)),
    (1, 1): ((G_IN, 2),),
    (2, 1): ((G_CROSS, 1), (G_ONE, 2), (G_ZERO, 1)),
    (3, 1): ((G_HALF, 0), (G_OUT, 3), (G_IN, 3)),
    (5, 1): ((G_OUT, 4), (G_CROSS, 2), (G_HALF, 1), (G_ONE, 3)),
    (6, 1): ((G_REST, 0), (G_SMALL, 0), (G_ZERO, 2), (G_IN, 4)),
    (8, 1): ((G_ONE, 4), (G_CROSS, 3)),
    (9, 1): ((G_HALF, 2), (G_REST, 1), (G_SMALL, 1), (G_ZERO, 3)),
    (9, 2): ((G_HALF, 3), (G_REST, 2), (G_SMALL, 2), (G_CROSS, 4), (G_ZERO, 4), (G_HALF, 4), (G_REST, 3), (G_SMALL, 3)),
}


def closing(dims, x_ref, qkv_ref, low_ref, high_ref, inv_ref, mix_ref, gmix_ref, inv_two, vectors, g_vec, g_bin, scale_one,
            low_out, low_in, low_one, e_any, ckv_any, q_any, mix_two_any, gmix_two_any, mix_any, two_any, one_any, wc_any, mem_any, ac_any, ap_any, wp_any, ws_any, gres_any,
            g_tags, sh_out, sh_in, sh_one, sh_cross, sh_zero, sh_half, sh_rest, sh_small, g_mem,
            e_ref, ckv_ref, q_ref, mix_two, gmix_two, mine_out, mine_in, mine_one, gres_ref, dkv_ref,
            mix_one, g_two, n_one, wt_cross, mem_ref, acc_cross, acc_zero, w_zero, wt_self,
            dq_ref, gmix_last, gres_last, gmix_now, acc, add_vec, acc_col, low_cross, low_zero, low_half, low_rest, low_small, head_sem, in_sem, *rest):
    tags, width = x_ref.shape[1:]
    cells = mem_ref.shape[0]
    half = tags // 2
    some = HEADS // 2
    step = pl.program_id(0)
    images = pl.num_programs(0) // 3
    me = place(dims)
    devices = dims[0] * dims[1] * dims[2] * 2
    held, (send, recv) = rest[:-2], rest[-2:]
    triples = ((mine_out, None, sh_out), (mine_in, None, sh_in), (mine_one, None, sh_one), (low_cross, None, sh_cross),
               (low_zero, None, sh_zero), (low_half, None, sh_half), (low_rest, None, sh_rest), (low_small, None, sh_small))
    every = [Scattering(dims, me, grads, k in SHORT, out, 0, held[5 * k : 5 * k + 5], (send.at[k], recv.at[k])) for k, (grads, _, out) in enumerate(triples)]
    fetches = [
        pltpu.make_async_copy(src, dst, in_sem.at[k])
        for k, (src, dst) in enumerate((
            (low_out, mine_out), (low_in, mine_in), (low_one, mine_one),
            (one_any, n_one), (mem_any.at[images - 1], mem_ref), (ac_any, acc_cross), (two_any, g_two), (wc_any, wt_cross),
            (mix_any.at[images - 1], mix_one), (ap_any, acc_zero), (wp_any.at[0], w_zero), (gres_any, gres_ref), (ws_any, wt_self)))
    ]

    def e_rows(h):
        return e_ref.at[pl.ds(pl.multiple_of(h * cells, 16), cells)]

    def few_fetches(k):
        few = pl.ds(k * FEW, FEW)
        rows = pl.ds(k * FEW * cells, FEW * cells)
        pairs = ((e_any.at[rows], e_ref.at[rows]), (ckv_any.at[images - 1, few], ckv_ref.at[few]),
                 (ckv_any.at[images - 1, pl.ds(HEADS + k * FEW, FEW)], ckv_ref.at[pl.ds(HEADS + k * FEW, FEW)]),
                 (q_any.at[few], q_ref.at[few]), (mix_two_any.at[few], mix_two.at[few]), (gmix_two_any.at[few], gmix_two.at[few]))
        return [pltpu.make_async_copy(src, dst, head_sem.at[k, j]) for j, (src, dst) in enumerate(pairs)]

    def play(number, where):
        for item, stage in EVENTS.get((number, where), ()):
            item = every[item]
            item.begin() if stage == 0 else item.advance(stage)

    def events(where):
        for number in sorted(number for number, at in EVENTS if at == where and number > 0):
            pl.when(step == number)(functools.partial(play, number, where))

    def vec(k):
        return vectors[k : k + 1, :]

    @pl.when(step == 0)
    def _():
        hails = hail(dims, me, True)
        for fetch in fetches[:3] + few_fetches(0):
            fetch.start()
        greet(dims, me, hails)
        for fetch in fetches[:3]:
            fetch.wait()
        play(0, 0)
        for k in range(1, HEADS // FEW):
            for fetch in few_fetches(k):
                fetch.start()
        for fetch in fetches[3:]:
            fetch.start()
        acc_col[...] = jnp.zeros_like(acc_col)
        def few_heads(k, _):
            for fetch in few_fetches(k):
                fetch.wait()
            for j in range(FEW):
                h = k * FEW + j
                dq_ref[h], dkv_ref[h], dkv_ref[HEADS + h] = cross_back(
                    h, e_rows(h)[...], ckv_ref[h], ckv_ref[HEADS + h], q_ref[h], gmix_two[h], mix_two[h], inv_two[pl.ds(h, 1), :])
            for half_done in (1, 2):
                pl.when((k + 1) * FEW == some * half_done)(functools.partial(play, 0, half_done))
            return 0

        lax.fori_loop(0, HEADS // FEW, few_heads, 0)
        for fetch in fetches[3:11]:
            fetch.wait()
        dq = dq_ref[...].reshape(width, tags)
        dkv = dkv_ref[...].reshape(2 * width, cells)
        one_low = (n_one[...] * vec(10) + vec(6)).astype(bf16)
        acc_cross[:width] += dot(dq, one_low, 1, 0)
        acc_cross[width:] += dot(dkv, mem_ref[...], 1, 0)
        low_cross[...] = acc_cross[...].astype(bf16).T.reshape(low_cross.shape)
        play(0, 6)
        g_one = g_two[...] + dot(dq, wt_cross[:width], 0, 0)
        sum_gain, sum_shift = column_sums(g_one * n_one[...]), column_sums(g_one)
        g_one = norm_back(g_one, n_one[...], scale_one[...], vec(10))
        gres_last[...] = g_one
        g_low = g_one.astype(bf16)
        acc_zero[...] += dot(mix_one[...].reshape(width, tags), g_low, 1, 0)
        low_zero[...] = acc_zero[...].astype(bf16).reshape(low_zero.shape)
        play(0, 7)
        gmix_last[...] = dot(w_zero[...], g_low, 1, 1).astype(bf16).reshape(gmix_last.shape)
        at = lax.broadcasted_iota(jnp.int32, add_vec.shape, 0)
        total = g_vec[...]
        for k, row in ((2, column_sums(g_one)), (3, column_sums(lane_groups(dq.astype(f32)).T)),
                       (4, column_sums(memory_lanes(dkv[width:].astype(f32)).T)), (6, sum_shift), (10, sum_gain)):
            total = total + jnp.where(at == k, row, 0.0)
        add_vec[...] = total

    turn = jnp.maximum(step - 1, 0)
    part = jnp.minimum(turn // images, 1)
    now = lax.rem(turn, images)
    backward = jnp.logical_and(step >= 1, step <= 2 * images)

    @pl.when(jnp.logical_and(backward, now < images - 1))
    def _():
        gmix_now[...] = gmix_ref[0]

    @pl.when(jnp.logical_and(backward, now == images - 1))
    def _():
        gmix_now[...] = gmix_last[pl.ds(part * some, some)]

    def d_rows(image, kind, h, count=1):
        return pl.ds(pl.multiple_of(((image * 3 + kind) * HEADS + h) * HEAD_DIM, HEAD_DIM), count * HEAD_DIM)

    def head(h, _):
        grad = gmix_now[h].astype(f32)
        inv = inv_ref[0, pl.ds(part * some + h, 1), :]
        delta = jnp.sum(grad * mix_ref[0, h].astype(f32), 0, keepdims=True) * inv
        grad = (grad * inv).astype(bf16)
        ext = with_delta(grad, delta)
        qt, kt, vt = qkv_ref[0, 0, h], qkv_ref[0, 1, h], with_ones(qkv_ref[0, 2, h])
        e_low, e_high = low_ref[0, h], high_ref[0, h]
        ds_low = e_low * dot(vt[:, :half], ext, 0, 0).astype(bf16)
        ds_high = e_high * dot(vt[:, half:], ext[:, half:], 0, 0).astype(bf16)
        dv = jnp.concatenate([dot(grad, e_low, 1, 1), dot(grad[:, half:], e_high, 1, 1)], 1)
        dk = jnp.concatenate([dot(qt, ds_low, 1, 1), dot(qt[:, half:], ds_high, 1, 1)], 1)
        dq = dot(kt[:, :half], ds_low, 1, 0)
        dq = jnp.concatenate([dq[:, :half], dq[:, half:] + dot(kt[:, half:], ds_high, 1, 0)], 1) * HEAD_DIM ** -0.5
        at = part * some + h
        e_ref[d_rows(now, 0, at)] = dq.astype(bf16)
        e_ref[d_rows(now, 1, at)] = dk.astype(bf16)
        e_ref[d_rows(now, 2, at)] = dv.astype(bf16)
        return 0

    @pl.when(backward)
    def _():
        lax.fori_loop(0, some, head, 0, unroll=some)
        d = [e_ref[d_rows(now, kind, part * some, some)] for kind in range(3)]
        rows = some * HEAD_DIM
        acc_col[0, pl.ds(part * rows, rows)] += lane_groups(d[0].astype(f32))
        acc_col[1, pl.ds(part * rows, rows)] += lane_groups(d[2].astype(f32))
        fresh = now == 0
        for kind in range(3):
            product = dot(d[kind], x_ref[0], 1, 0)

            @pl.when(fresh)
            def _():
                acc[kind * rows : (kind + 1) * rows] = product

            @pl.when(jnp.logical_not(fresh))
            def _():
                acc[kind * rows : (kind + 1) * rows] += product

    @pl.when(step == images)
    def _():
        low_half[...] = acc[...].astype(bf16).T.reshape(low_half.shape)

    @pl.when(step == 2 * images)
    def _():
        low_rest[...] = acc[...].astype(bf16).T.reshape(low_rest.shape)
        at = lax.broadcasted_iota(jnp.int32, add_vec.shape, 0)
        rows = jnp.where(at == 0, column_sums(acc_col[0].T), jnp.where(at == 1, column_sums(acc_col[1].T), add_vec[...]))
        at = lax.broadcasted_iota(jnp.int32, (16, g_bin.shape[1]), 0)
        hidden = jnp.where(at == 13, g_bin[...], 0.0)
        small = collect(rows, width // devices, devices) + collect(hidden, g_bin.shape[1] // devices, devices)
        low_small[...] = small.astype(bf16).reshape(low_small.shape)

    events(0)

    @pl.when(step == 2 * images + 1)
    def _():
        for fetch in fetches[11:]:
            fetch.wait()

    @pl.when(step > 2 * images)
    def _():
        image = jnp.maximum(step - 2 * images - 1, 0)
        d = e_ref[d_rows(image, 0, 0, 3 * HEADS)]
        product = dot(d, wt_self[...], 0, 0)

        @pl.when(image < images - 1)
        def _():
            g_tags[0] = (gres_ref[jnp.minimum(image, images - 2)] + product).astype(bf16)

        @pl.when(image == images - 1)
        def _():
            g_tags[0] = (gres_last[...] + product).astype(bf16)

    events(1)

    @pl.when(step == 3 * images)
    def _():
        g_mem[...] = dot(dkv_ref[...].reshape(2 * width, cells), wt_cross[width:], 0, 0).astype(bf16)

    events(2)

    @pl.when(step == 3 * images)
    def _():
        for item in every:
            item.drain()


def run_closing(dims, x, qkv, e_low, e_high, inv, mix, gmix, g_resid, ckv, mem, vectors, wt_self, wt_cross, w_proj, g_one, g_in, g_out, g_vec, g_bin, kept):
    scale_one, e, q, inv_two, mix_two, gmix_two, n_one, g_two, acc_cross, acc_zero = kept
    images, tags, width = x.shape
    memory = mem.shape[1]
    half, some = tags // 2, HEADS // 2
    sds = jax.ShapeDtypeStruct
    cells = dims + (2,)
    devices = dims[0] * dims[1] * dims[2] * 2

    def parts(grad):
        return grad.reshape(cells + (grad.shape[0] // devices, grad.shape[1]))

    low = [parts(g_out), parts(g_in), parts(g_one)]
    rows = width // devices
    lows = [cells + (rows, 3 * width), cells + (rows, width)] + [cells + (rows, 3 * width // 2)] * 2 + [cells + (16, 128)]

    def turn(i):
        t = jnp.clip(i - 1, 0, 2 * images - 1)
        return lax.rem(t, images), lax.div(t, images)

    def by_turn(shape, split):
        def index(i):
            image, part = turn(i)
            return (image,) + tuple(part if k == split else 0 for k in range(len(shape)))
        return pl.BlockSpec((1,) + shape, index)

    def gmix_index(i):
        image, part = turn(i)
        return jnp.minimum(image, images - 2), part, 0, 0

    def one(*shape):
        return pl.BlockSpec(shape, lambda i: (0,) * len(shape), pipeline_mode=pl.Buffered(1))

    def out(*shape):
        return pl.BlockSpec(shape, lambda i: (0,) * len(shape))

    anywhere = pl.BlockSpec(memory_space=pl.ANY)
    shares = [g.shape[4:] for g in low] + [s[4:] for s in lows]
    space = []
    for k, shape in enumerate([g.shape for g in low] + lows):
        space += [pltpu.VMEM(s, bf16) for s in scatter_space(dims, (), shape[4:], k in SHORT)]
    slots = scatter_slots(dims)
    qkv = qkv.reshape(images, 3, HEADS, HEAD_DIM, tags)
    heads = (HEADS, HEAD_DIM, tags)
    return pl.pallas_call(
        functools.partial(closing, dims),
        grid=(3 * images + 1,),
        in_specs=[
            by_turn((tags, width), None), by_turn((3, some, HEAD_DIM, tags), 1), by_turn((some, half, tags), 0), by_turn((some, half, half), 0),
            by_turn((HEADS, tags), None), by_turn((some, HEAD_DIM, tags), 0), pl.BlockSpec((1, some, HEAD_DIM, tags), gmix_index),
            one(HEADS, tags), one(16, width), one(16, width), one(*g_bin.shape), one(tags, 1),
        ] + [anywhere] * 18,
        out_specs=[pl.BlockSpec((1, tags, width), lambda i: (jnp.clip(i - 2 * images - 1, 0, images - 1), 0, 0))]
        + [out(*s) for s in shares] + [out(memory, width)],
        out_shape=[sds((images, tags, width), bf16)] + [sds(s, f32) for s in shares] + [sds((memory, width), bf16)],
        scratch_shapes=[
            pltpu.VMEM((HEADS * memory, tags), bf16), pltpu.VMEM((2 * HEADS, HEAD_DIM, memory), bf16), pltpu.VMEM(heads, bf16), pltpu.VMEM(heads, bf16), pltpu.VMEM(heads, bf16),
        ] + [pltpu.VMEM(g.shape, bf16) for g in low] + [
            pltpu.VMEM((images - 1, tags, width), f32), pltpu.VMEM((2 * HEADS, HEAD_DIM, memory), bf16),
            pltpu.VMEM(heads, bf16), pltpu.VMEM((tags, width), f32), pltpu.VMEM((tags, width), f32),
            pltpu.VMEM((3 * width, width), bf16), pltpu.VMEM((memory, width), bf16), pltpu.VMEM((3 * width, width), f32), pltpu.VMEM((width, width), f32),
            pltpu.VMEM((width, width), bf16), pltpu.VMEM((3 * width, width), bf16),
            pltpu.VMEM(heads, bf16), pltpu.VMEM(heads, bf16), pltpu.VMEM((tags, width), f32), pltpu.VMEM((some, HEAD_DIM, tags), bf16),
            pltpu.VMEM((3 * width // 2, width), f32), pltpu.VMEM((16, width), f32), pltpu.VMEM((2, width, 128), f32),
        ] + [pltpu.VMEM(s, bf16) for s in lows] + [pltpu.SemaphoreType.DMA((HEADS // FEW, 6)), pltpu.SemaphoreType.DMA((13,))] + space
        + [pltpu.SemaphoreType.DMA((8, slots)), pltpu.SemaphoreType.DMA((8, slots))],
        compiler_params=pltpu.CompilerParams(collective_id=1, has_side_effects=True, vmem_limit_bytes=62 * MIB),
        name="closing",
    )(x, qkv, e_low, e_high, inv, mix, gmix, inv_two, vectors, g_vec, g_bin, scale_one, *low,
      e.reshape(HEADS * memory, tags), ckv, q, mix_two, gmix_two, mix, g_two, n_one, wt_cross, mem, acc_cross, acc_zero, w_proj, wt_self, g_resid)


def settle(lanes, hidden_lanes, images, g_mem_in, m_last, tags, s_out, s_in, s_one, s_cross, s_zero, s_half, s_rest, small,
           g_mem, o_tags, o_self, o_cross, o_proj, o_in, o_out, o_bin, o_gains, o_biases):
    width = o_tags.shape[2]
    o_tags[...] = tags[...].astype(f32)

    @pl.when(pl.program_id(0) == 0)
    def _():
        g_mem[0] = m_last[...].astype(f32)
        part = width // 2
        for kind in range(3):
            o_self[:, kind * width : kind * width + part] = s_half[:, kind * part : (kind + 1) * part]
            o_self[:, kind * width + part : (kind + 1) * width] = s_rest[:, kind * part : (kind + 1) * part]
        o_cross[...] = s_cross[...]
        o_proj[0] = s_zero[...]
        o_proj[1] = s_one[...]
        o_in[...] = s_in[...]
        o_out[...] = s_out[...]
        o_biases[...] = small[:10, :lanes]
        o_gains[...] = small[10:13, :lanes]
        o_bin[...] = small[13:14, :hidden_lanes]


def run_settle(lanes, hidden_lanes, g_mem, m_last, g_tags, shares):
    images, tags, width = g_tags.shape
    sds = jax.ShapeDtypeStruct
    s_out, s_in, s_one, s_cross, s_zero, s_half, s_rest, small = shares

    def one(*shape):
        return pl.BlockSpec(shape, lambda i: (0,) * len(shape), pipeline_mode=pl.Buffered(1))

    def out(*shape):
        return pl.BlockSpec(shape, lambda i: (0,) * len(shape))

    rows = s_cross.shape[0]
    shapes = [s_cross.shape, s_cross.shape, (2, rows, width), s_in.shape, s_out.shape, (1, hidden_lanes), (3, lanes), (10, lanes)]
    image = pl.BlockSpec((1, tags // 2, width), lambda i: (lax.div(i, 2), lax.rem(i, 2), 0))
    return pl.pallas_call(
        functools.partial(settle, lanes, hidden_lanes, images),
        grid=(2 * images,),
        in_specs=[pl.BlockSpec(memory_space=pl.ANY), one(*m_last.shape), image] + [one(*s.shape) for s in shares],
        out_specs=[pl.BlockSpec((1,) + g_mem.shape[1:], lambda i: (images - 1, 0, 0)), image] + [out(*s) for s in shapes],
        out_shape=[sds(g_mem.shape, f32), sds(g_tags.shape, f32)] + [sds(s, f32) for s in shapes],
        input_output_aliases={0: 0},
        compiler_params=pltpu.CompilerParams(vmem_limit_bytes=62 * MIB),
        name="settle",
    )(g_mem, m_last, g_tags, *shares)


AXES = ("wide", "narrow")
LEADS = (0, 0, 1, 0, 0, 0)


def fold(block, rows, columns):
    if rows % 16 == 0:
        return block
    return block.reshape(block.shape[:-2] + (16, rows * columns // 16))


def per_device(dims, tag_states, image_memory, tag_lengths, w_self, w_cross, w_proj, w_in, b_in, w_out, ln_gains, biases, out_grad):
    cells = dims + (2,)
    fused = w_self.shape[0] % 16 == 0 and tag_states.shape[0] == 3
    devices = dims[0] * dims[1] * dims[2] * 2
    width = tag_states.shape[2]
    lanes, hidden_lanes = biases.shape[1], b_in.shape[0]
    if fused:
        qkv, ckv, near, far, inv, mix, wt_self, wt_cross, vectors, hidden_bias, full_proj, full_in, full_out = run_opening(
            dims, tag_lengths, tag_states, image_memory, biases, ln_gains, b_in[None], (w_cross, w_self, w_proj, w_in, w_out))
        full_proj, full_in, full_out = full_proj.reshape(2, width, width), full_in.reshape(width, -1), full_out.reshape(-1, width)
        layer_out, g_resid, gmix, g_mem, _, g_one, g_in, g_out, g_vec, g_bin, *kept = run_middle(
            tag_lengths, tag_states, image_memory, out_grad, mix, ckv, wt_cross, full_proj, full_in, full_out, vectors, hidden_bias, True)
        g_tags, *shares, m_last = run_closing(
            dims, tag_states, qkv, near, far, inv, mix, gmix, g_resid, ckv, image_memory, vectors, wt_self, wt_cross, full_proj,
            g_one, g_in, g_out, g_vec, g_bin, kept)
        grad_memory, grad_tags, s_self, s_cross, s_proj, s_in, s_out, s_bin, s_gains, s_biases = run_settle(
            lanes, hidden_lanes, g_mem, m_last, g_tags, shares)
        return layer_out, grad_tags, grad_memory, s_self, s_cross, s_proj, s_in, s_bin[0], s_out, s_gains, s_biases
    small = jnp.concatenate(
        [
            jnp.pad(jnp.concatenate([biases, ln_gains]), ((0, 0), (0, 128 - lanes))),
            jnp.pad(b_in[None], ((0, 2), (0, 128 - hidden_lanes))),
        ]
    )
    shards = (w_self, w_cross, w_proj, w_in, w_out, small)
    gathered = gather(dims, [fold(s, *s.shape[-2:]) for s in shards], LEADS)

    def whole(held, shard):
        lead = shard.shape[:-2]
        rows, columns = shard.shape[-2:]
        return held.reshape(lead + (devices * rows, columns))

    full_self, full_cross, full_proj, full_in, full_out, full_small = [whole(h, s) for h, s in zip(gathered, shards)]
    by_device = full_small.reshape(devices, 16, 128)
    vectors = by_device[:, :, :lanes].transpose(1, 0, 2).reshape(16, width).astype(f32)
    hidden_bias = by_device[:, 13, :hidden_lanes].reshape(1, -1).astype(f32)
    layer_out, grad_tags, grad_memory, g_self, g_cross, g_proj, g_in, g_out, g_vec, g_bin = layer(
        tag_lengths, tag_states, image_memory, out_grad, full_self, full_cross, full_proj, full_in, full_out, vectors, hidden_bias)
    g_small = jnp.pad(g_vec.reshape(16, devices, lanes).transpose(1, 0, 2)[:, :13], ((0, 0), (0, 0), (0, 128 - lanes)))
    g_hidden = jnp.pad(g_bin.reshape(devices, 1, hidden_lanes), ((0, 0), (0, 2), (0, 128 - hidden_lanes)))
    g_small = jnp.concatenate([g_small, g_hidden], 1).astype(bf16).reshape(devices * 16, 128)

    def parts(grad, shard):
        lead = shard.shape[:-2]
        rows, columns = shard.shape[-2:]
        return fold(grad.reshape(lead + cells + (rows, columns)), rows, columns)

    shards = (w_self, w_cross, w_proj, w_in, w_out, jax.ShapeDtypeStruct((16, 128), bf16))
    shares = scatter(dims, [parts(g, s) for g, s in zip((g_self, g_cross, g_proj, g_in, g_out, g_small), shards)], LEADS)
    s_self, s_cross, s_proj, s_in, s_out, s_small = [v.reshape(s.shape) for v, s in zip(shares, shards)]
    return (layer_out, grad_tags, grad_memory, s_self, s_cross, s_proj, s_in, s_small[13, :hidden_lanes], s_out,
            s_small[10:13, :lanes], s_small[:10, :lanes])


def solution(mesh):
    dims = grid_of(mesh.shape["wide"], mesh.shape["narrow"])
    rows, matrix, stack, columns = P(AXES, None, None), P(AXES, None), P(None, AXES, None), P(None, AXES)
    return jax.shard_map(
        functools.partial(per_device, dims),
        mesh=mesh,
        in_specs=(rows, rows, P(AXES), matrix, matrix, stack, matrix, P(AXES), matrix, columns, columns, rows),
        out_specs=(rows, rows, rows, matrix, matrix, stack, matrix, P(AXES), matrix, columns, columns),
        check_vma=False,
    )
```
